32 devices in a mesh: blk: 16 (over z, x, core), pair: 2 (over y).
Axes of the slice: x: 2, y: 2, z: 4, core: 2. Of those that a mesh axis runs over, the one named last changes fastest.
Arguments:
- tokens_in: bfloat16 [4096, 2560], P(('blk', 'pair')), may hold values from -6 to 6
- cotangent: bfloat16 [4096, 2560], P(('blk', 'pair')), may hold values from -6 to 6
- w_qkv: float32 [2560, 3072], P(('blk', 'pair')), may hold values from -0.125 to 0.125
- w_out: float32 [2560, 2560], P(None, ('blk', 'pair')), may hold values from -3.5 to 3.5
- w_gateup: float32 [2, 2560, 7680], P(None, ('blk', 'pair')), may hold values from -0.125 to 0.125
- w_down: float32 [7680, 2560], P(None, ('blk', 'pair')), may hold values from -0.125 to 0.125
- gains: float32 [2, 2560], P(None, ('blk', 'pair')), may hold values from 0.5 to 1.5
- mom_qkv: float32 [2560, 3072], P(('blk', 'pair')), may hold values from -512 to 512
- mom_out: float32 [2560, 2560], P(None, ('blk', 'pair')), may hold values from -20 to 20
- mom_gateup: float32 [2, 2560, 7680], P(None, ('blk', 'pair')), may hold values from -320 to 320
- mom_down: float32 [7680, 2560], P(None, ('blk', 'pair')), may hold values from -224 to 224
- mom_gains: float32 [2, 2560], P(None, ('blk', 'pair')), may hold values from -768 to 768
Outputs:
- block_output: bfloat16 [4096, 2560], P(('blk', 'pair'))
- input_grad: float32 [4096, 2560], P(('blk', 'pair'))
- new_w_qkv: float32 [2560, 3072], P(('blk', 'pair'))
- moment_qkv: float32 [2560, 3072], P(('blk', 'pair'))
- copy_qkv: bfloat16 [2560, 3072], P(('blk', 'pair'))
- new_w_out: float32 [2560, 2560], P(None, ('blk', 'pair'))
- moment_out: float32 [2560, 2560], P(None, ('blk', 'pair'))
- copy_out: bfloat16 [2560, 2560], P(None, ('blk', 'pair'))
- new_w_gateup: float32 [2, 2560, 7680], P(None, ('blk', 'pair'))
- moment_gateup: float32 [2, 2560, 7680], P(None, ('blk', 'pair'))
- copy_gateup: bfloat16 [2, 2560, 7680], P(None, ('blk', 'pair'))
- new_w_down: float32 [7680, 2560], P(None, ('blk', 'pair'))
- moment_down: float32 [7680, 2560], P(None, ('blk', 'pair'))
- copy_down: bfloat16 [7680, 2560], P(None, ('blk', 'pair'))
- new_gains: float32 [2, 2560], P(None, ('blk', 'pair'))
- moment_gains: float32 [2, 2560], P(None, ('blk', 'pair'))
- copy_gains: bfloat16 [2, 2560], P(None, ('blk', 'pair'))
The draws below stay inside these ranges and needn't reach their ends.
All inputs are finite; a program needn't handle non-finite values.
Results may differ from the reference program's by a relative error of at most 0.04.
Values may be sent and summed in bfloat16 or wider, within the bound.
A program may use at most 640 MiB of HBM per device.

```python
import jax
import jax.numpy as jnp
from jax import lax

D = 2560
H = 10
HEAD = 256
FF = 7680
WINDOW = 2048
NS_STEPS = 5
TOK_DEV = 128
TOKENS = 4096
N_PAIR = 2


def level_of(key, shape, split, least, largest):
    loudness, own = 1.0, jax.random.fold_in(key, 6)
    for axis_at, shards_of in split:
        steps = jnp.exp(jax.random.uniform(jax.random.fold_in(own, axis_at), (shards_of,), jnp.float32, least / len(split), largest / len(split)))
        loudness = loudness * jnp.repeat(steps, shape[axis_at] // shards_of).reshape([-1 if axis == axis_at else 1 for axis in range(len(shape))])
    return loudness


def normal_values(rng, dims, deviation, bound, cuts=(), held_as=jnp.bfloat16):
    level = level_of(rng, dims, cuts, -0.22, 0.18) if cuts else 1.0
    result = jax.random.normal(rng, dims, jnp.float32) * deviation * level
    return jnp.minimum(jnp.maximum(result, -bound), bound).astype(held_as)


def setup_inputs(seed: int = 0) -> dict:
    key_of = jax.random.split(jax.random.key(seed), 13)
    tokens_in = normal_values(key_of[0], (TOKENS, D), 1.0, 6.0, ((0, 32),))
    cotangent = normal_values(key_of[1], (TOKENS, D), 1.0, 6.0, ((0, 32),))
    w_qkv = normal_values(key_of[2], (D, (H + 2) * HEAD), D ** -0.5, 0.125, ((0, 32),), jnp.float32)
    w_out = normal_values(key_of[3], (H * HEAD, D), (3 * H * HEAD // WINDOW) ** -0.5, 3.5, ((1, 32),), jnp.float32)
    w_gateup = normal_values(key_of[4], (2, D, FF), D ** -0.5, 0.125, ((1, 32),), jnp.float32)
    w_down = normal_values(key_of[5], (FF, D), (FF // 3) ** -0.5, 0.125, ((1, 32),), jnp.float32)
    gains = jnp.clip(1.0 + 0.1 * jax.random.normal(key_of[6], (2, D), jnp.float32), 0.5, 1.5)
    mom_qkv = normal_values(key_of[7], (D, (H + 2) * HEAD), (1.5 * TOKENS ** 0.5), 512.0, ((0, 32),), jnp.float32)
    mom_out = normal_values(key_of[8], (H * HEAD, D), (0.05 * TOKENS ** 0.5), 20.0, ((1, 32),), jnp.float32)
    mom_gateup = normal_values(key_of[9], (2, D, FF), (0.8 * TOKENS ** 0.5), 320.0, ((1, 32),), jnp.float32)
    mom_down = normal_values(key_of[10], (FF, D), (0.6 * TOKENS ** 0.5), 224.0, ((1, 32),), jnp.float32)
    mom_gains = normal_values(key_of[11], (2, D), (2.0 * TOKENS ** 0.5), 768.0, ((1, 32),), jnp.float32)
    return dict(tokens_in=tokens_in, cotangent=cotangent, w_qkv=w_qkv, w_out=w_out, w_gateup=w_gateup, w_down=w_down, gains=gains, mom_qkv=mom_qkv, mom_out=mom_out, mom_gateup=mom_gateup, mom_down=mom_down, mom_gains=mom_gains)


@jax.custom_vjp
def low(v):
    return lax.optimization_barrier(v.astype(jnp.bfloat16)).astype(jnp.float32)

@jax.custom_vjp
def low_back(v):
    return v

def low_keep(v):
    return (low(v), None)

def low_pass(kept, grad):
    return (grad,)

def back_keep(v):
    return (v, None)

def back_low(kept, grad):
    return (low(grad),)
low.defvjp(low_keep, low_pass)
low_back.defvjp(back_keep, back_low)
highest = lax.Precision.HIGHEST
eps_norm = 1e-06
eps_pieces = 1e-07
ns_first = 3.4445
ns_second = -4.775
ns_third = 2.0315
momentum_decay = 0.95
matrix_rate = 0.5
output_rate = 10.0
gain_rate = 0.001
weight_shrink = 0.001
masked_score = -1e+30

def matmul(left, right):
    return jnp.dot(left, right, precision=highest, preferred_element_type=jnp.float32)

def rms_scale(stream, gain_row):
    mean_square = lax.optimization_barrier(jnp.mean(stream * stream, axis=-1, keepdims=True))
    return stream * lax.rsqrt(mean_square + eps_norm) * gain_row

def attention(queries, keys, values):
    block_rows = N_PAIR * TOK_DEV
    span = WINDOW + block_rows
    padding = jnp.zeros((WINDOW, HEAD), jnp.float32)
    keys_padded = jnp.concatenate([padding, keys], axis=0)
    values_padded = jnp.concatenate([padding, values], axis=0)
    query_index = jnp.arange(block_rows, dtype=jnp.int32)
    key_index = jnp.arange(span, dtype=jnp.int32)
    score_scale = HEAD ** (-0.5)

    def one_block(start):
        block_queries = lax.dynamic_slice_in_dim(queries, start, block_rows, 0)
        block_keys = lax.dynamic_slice_in_dim(keys_padded, start, span, 0)
        block_values = lax.dynamic_slice_in_dim(values_padded, start, span, 0)
        raw = jnp.einsum('qhd,kd->hqk', block_queries, block_keys, precision=highest)
        distance = query_index[:, None] + WINDOW - key_index[None, :]
        allowed = (distance >= 0) & (distance < WINDOW) & (start - WINDOW + key_index[None, :] >= 0)
        scores = jnp.where(allowed[None], low_back(raw) * score_scale, masked_score)
        top_score = lax.optimization_barrier(jnp.max(scores, axis=-1, keepdims=True))
        expo = jnp.exp(scores - top_score)
        probs = expo / lax.optimization_barrier(jnp.sum(expo, axis=-1, keepdims=True))
        mixed = jnp.einsum('hqk,kd->qhd', low(probs), block_values, precision=highest)
        return mixed.reshape(block_rows, H * HEAD)
    starts = jnp.arange(TOKENS // block_rows, dtype=jnp.int32) * block_rows
    return lax.map(jax.checkpoint(one_block), starts).reshape(TOKENS, H * HEAD)

def forward(stream, w_qkv, w_out, w_gateup, w_down, gains):
    gain_rows = low(gains)
    normed_attn = low(rms_scale(stream, gain_rows[0]))
    qkv = low_back(low(matmul(normed_attn, low(w_qkv))))
    queries = qkv[:, :H * HEAD].reshape(TOKENS, H, HEAD)
    keys = qkv[:, H * HEAD:(H + 1) * HEAD]
    values = qkv[:, (H + 1) * HEAD:]
    mixed = low_back(low(attention(queries, keys, values)))
    projected = low_back(matmul(mixed, low(w_out)))
    resid = stream + projected
    normed_mlp = low(rms_scale(resid, gain_rows[1]))
    gate_part = low_back(matmul(normed_mlp, low(w_gateup[0])))
    up_part = low_back(matmul(normed_mlp, low(w_gateup[1])))
    hidden = low(jax.nn.gelu(gate_part, approximate=True) * up_part)
    branch = low_back(matmul(hidden, low(w_down)))
    return resid + branch

def to_pieces(part_qkv, part_out, part_gateup, part_down):
    row_count = part_qkv.shape[0]
    blocks = FF // HEAD
    piece_qkv = part_qkv.reshape(row_count, H + 2, HEAD).transpose(1, 0, 2)
    piece_out = part_out.reshape(H, HEAD, row_count).transpose(0, 2, 1)
    piece_gateup = part_gateup.reshape(2, row_count, blocks, HEAD).transpose(0, 2, 1, 3).reshape(2 * blocks, row_count, HEAD)
    piece_down = part_down.reshape(blocks, HEAD, row_count).transpose(0, 2, 1)
    return jnp.concatenate([piece_qkv, piece_out, piece_gateup, piece_down], axis=0)

def from_pieces(stacked):
    row_count = stacked.shape[1]
    blocks = FF // HEAD
    piece_qkv = stacked[:H + 2].transpose(1, 0, 2).reshape(row_count, (H + 2) * HEAD)
    piece_out = stacked[H + 2:2 * H + 2].transpose(0, 2, 1).reshape(H * HEAD, row_count)
    piece_gateup = stacked[2 * H + 2:2 * H + 2 + 2 * blocks].reshape(2, blocks, row_count, HEAD).transpose(0, 2, 1, 3).reshape(2, row_count, FF)
    piece_down = stacked[2 * H + 2 + 2 * blocks:].transpose(0, 2, 1).reshape(FF, row_count)
    return (piece_qkv, piece_out, piece_gateup, piece_down)

def newton_schulz(piece):
    rounded = low(piece)
    norm_size = jnp.sqrt(jnp.sum(rounded * rounded))
    current = low(rounded / (norm_size + eps_pieces))
    for sweep_index in range(NS_STEPS):
        gram_matrix = low(jnp.dot(current.T, current, precision=highest, preferred_element_type=jnp.float32))
        square = jnp.dot(gram_matrix, gram_matrix, precision=highest, preferred_element_type=jnp.float32)
        mixing = low(ns_second * gram_matrix + ns_third * square)
        current = low(ns_first * current + jnp.dot(current, mixing, precision=highest, preferred_element_type=jnp.float32))
    return current

def reference(tokens_in, cotangent, w_qkv, w_out, w_gateup, w_down, gains, mom_qkv, mom_out, mom_gateup, mom_down, mom_gains):
    stream = tokens_in.astype(jnp.float32)
    output, pullback = jax.vjp(forward, stream, w_qkv, w_out, w_gateup, w_down, gains)
    grad_input, grad_qkv, grad_out, grad_gateup, grad_down, grad_gains = pullback(cotangent.astype(jnp.float32))
    moment_qkv = momentum_decay * mom_qkv + grad_qkv
    moment_out = momentum_decay * mom_out + grad_out
    moment_gateup = momentum_decay * mom_gateup + grad_gateup
    moment_down = momentum_decay * mom_down + grad_down
    moment_gains = momentum_decay * mom_gains + grad_gains
    stacked = to_pieces(moment_qkv, moment_out, moment_gateup, moment_down)
    turned = lax.map(newton_schulz, stacked)
    turn_qkv, turn_out, turn_gateup, turn_down = from_pieces(turned)
    new_qkv = (1.0 - weight_shrink) * w_qkv - matrix_rate * turn_qkv
    new_out = (1.0 - weight_shrink) * w_out - output_rate * turn_out
    new_gateup = (1.0 - weight_shrink) * w_gateup - matrix_rate * turn_gateup
    new_down = (1.0 - weight_shrink) * w_down - matrix_rate * turn_down
    new_gains = gains - gain_rate * moment_gains
    return (output.astype(jnp.bfloat16), grad_input, new_qkv, moment_qkv, new_qkv.astype(jnp.bfloat16), new_out, moment_out, new_out.astype(jnp.bfloat16), new_gateup, moment_gateup, new_gateup.astype(jnp.bfloat16), new_down, moment_down, new_down.astype(jnp.bfloat16), new_gains, moment_gains, new_gains.astype(jnp.bfloat16))
```

```python
import jax
import jax.numpy as jnp
from jax import lax
from jax.sharding import PartitionSpec as P

H = 10
HEAD = 256
FF = 7680
WINDOW = 2048
NS_STEPS = 5


eps_norm = 1e-06
eps_pieces = 1e-07
ns_first = 3.4445
ns_second = -4.775
ns_third = 2.0315
momentum_decay = 0.95
matrix_rate = 0.5
output_rate = 10.0
gain_rate = 0.001
weight_shrink = 0.001
masked_score = -1e30


def rms_scale(stream, gain_row):
    mean_square = jnp.mean(stream * stream, axis=-1, keepdims=True)
    return stream * lax.rsqrt(mean_square + eps_norm) * gain_row


def gelu_product(gate_part, up_part):
    return jax.nn.gelu(gate_part, approximate=True) * up_part


def ffn_packets(part_gateup, part_down, device_count):
    row_count = part_gateup.shape[1]
    blocks = FF // HEAD
    gateup = part_gateup.reshape(2, row_count, blocks, HEAD).transpose(2, 1, 0, 3)
    down = part_down.reshape(blocks, HEAD, row_count).transpose(0, 2, 1)[:, :, None, :]
    packets = jnp.concatenate([gateup, down], axis=2).reshape(blocks, row_count, 3 * HEAD)
    return jnp.pad(packets, ((0, device_count - blocks), (0, 0), (0, 0)))


def ffn_unpack(packets):
    row_count = packets.shape[1]
    blocks = FF // HEAD
    kept = packets[:blocks].reshape(blocks, row_count, 3, HEAD)
    gateup = kept[:, :, :2].transpose(2, 1, 0, 3).reshape(2, row_count, FF)
    down = kept[:, :, 2].transpose(0, 2, 1).reshape(FF, row_count)
    return gateup, down


def column_packets(columns, device_count):
    row_count, width = columns.shape
    blocks = width // HEAD
    packets = columns.reshape(row_count, blocks, HEAD).transpose(1, 0, 2)
    return jnp.pad(packets, ((0, device_count - blocks), (0, 0), (0, 0)))


def attn_unpack(packets):
    row_count = packets.shape[1]
    part_qkv = packets[: H + 2].transpose(1, 0, 2).reshape(row_count, (H + 2) * HEAD)
    part_out = packets[H + 2 : 2 * H + 2].transpose(0, 2, 1).reshape(H * HEAD, row_count)
    return part_qkv, part_out


def orthogonalize(piece):
    values = piece.astype(jnp.float32)
    norm_size = jnp.sqrt(jnp.sum(values * values))
    current = (values / (norm_size + eps_pieces)).astype(jnp.bfloat16)
    for sweep_index in range(NS_STEPS):
        gram_matrix = jnp.einsum(
            "di,dj->ij", current, current, preferred_element_type=jnp.float32
        ).astype(jnp.bfloat16)
        square = jnp.dot(gram_matrix, gram_matrix, preferred_element_type=jnp.float32)
        mixing = (ns_second * gram_matrix.astype(jnp.float32) + ns_third * square).astype(
            jnp.bfloat16
        )
        turned = jnp.dot(current, mixing, preferred_element_type=jnp.float32)
        current = (ns_first * current.astype(jnp.float32) + turned).astype(jnp.bfloat16)
    return current


def on_device(
    tokens_in,
    cotangent,
    w_qkv,
    w_out,
    w_gateup,
    w_down,
    gains,
    mom_qkv,
    mom_out,
    mom_gateup,
    mom_down,
    mom_gains,
):
    everyone = ("blk", "pair")
    bf16 = jnp.bfloat16
    f32 = jnp.float32
    device_count = lax.axis_size("blk") * lax.axis_size("pair")
    me = lax.axis_index("blk") * lax.axis_size("pair") + lax.axis_index("pair")
    local_rows, width = tokens_in.shape
    share_rows = w_qkv.shape[0]
    score_scale = HEAD ** (-0.5)
    span = WINDOW + local_rows

    def gather(shard):
        return lax.all_gather(shard, everyone, axis=0, tiled=True)

    def scatter_sum(partial):
        return lax.psum_scatter(partial, everyone, scatter_dimension=0, tiled=True)

    def exchange(packets):
        return lax.all_to_all(packets, everyone, split_axis=0, concat_axis=0, tiled=True)

    token_count = local_rows * device_count
    large = token_count * width * 2 > 48 * 2**20

    def after(value, earlier):
        return lax.optimization_barrier((value, earlier))[0] if large else value

    stream = tokens_in.astype(f32)
    full_gains = gather(gains.astype(bf16).T)
    full_qkv = gather(w_qkv.astype(bf16))
    gain_attn = full_gains[:, 0].astype(f32)
    gain_mlp = full_gains[:, 1].astype(f32)
    normed_attn_f, norm_back_attn = jax.vjp(rms_scale, stream, gain_attn)
    normed_attn = normed_attn_f.astype(bf16)
    qkv = jnp.dot(normed_attn, full_qkv, preferred_element_type=f32).astype(bf16)
    queries = qkv[:, : H * HEAD].reshape(local_rows, H, HEAD)
    kv_all = gather(qkv[:, H * HEAD :])
    kv_window = lax.dynamic_slice_in_dim(
        jnp.pad(kv_all, ((WINDOW, 0), (0, 0))), me * local_rows, span, 0
    )
    keys = kv_window[:, :HEAD]
    values = kv_window[:, HEAD:]
    full_out = gather(w_out.astype(bf16).T)
    ffn_weights = exchange(ffn_packets(w_gateup.astype(bf16), w_down.astype(bf16), device_count))
    ffn_weights = ffn_weights.reshape(width, 3 * HEAD)
    own_gateup = ffn_weights[:, : 2 * HEAD]
    own_down = ffn_weights[:, 2 * HEAD :]
    cotangent_all = gather(cotangent)

    key_index = jnp.arange(span, dtype=jnp.int32)[None, :]
    distance = jnp.arange(local_rows, dtype=jnp.int32)[:, None] + WINDOW - key_index
    allowed = (
        (distance >= 0) & (distance < WINDOW) & (me * local_rows - WINDOW + key_index >= 0)
    )
    raw = jnp.einsum("qhd,kd->hqk", queries, keys, preferred_element_type=f32)
    scores = jnp.where(allowed[None], raw * score_scale, masked_score)
    top_score = jnp.max(scores, axis=-1, keepdims=True)
    expo = jnp.exp(scores - top_score)
    probs = expo / jnp.sum(expo, axis=-1, keepdims=True)
    probs_low = probs.astype(bf16)
    mixed = jnp.einsum("hqk,kd->qhd", probs_low, values, preferred_element_type=f32)
    mixed = mixed.reshape(local_rows, H * HEAD).astype(bf16)
    resid = stream + jnp.einsum("tc,dc->td", mixed, full_out, preferred_element_type=f32)

    normed_mlp_f, norm_back_mlp = jax.vjp(rms_scale, resid, gain_mlp)
    normed_mlp_all = gather(normed_mlp_f.astype(bf16))
    both_parts = jnp.dot(normed_mlp_all, own_gateup, preferred_element_type=f32)
    hidden_f, geglu_back = jax.vjp(gelu_product, both_parts[:, :HEAD], both_parts[:, HEAD:])
    hidden = hidden_f.astype(bf16)
    grad_hidden = jnp.dot(cotangent_all, own_down, preferred_element_type=f32)
    grad_gate, grad_up = geglu_back(grad_hidden)
    grad_gateup = jnp.concatenate([grad_gate.astype(bf16), grad_up.astype(bf16)], axis=1)
    grad_normed_mlp = scatter_sum(
        jnp.einsum("tf,df->td", grad_gateup, own_gateup, preferred_element_type=f32).astype(bf16)
    ).astype(f32)
    resid_part, gain_grad_mlp = norm_back_mlp(grad_normed_mlp)
    grad_resid = cotangent.astype(f32) + resid_part
    grad_proj = grad_resid.astype(bf16)
    branch = scatter_sum(
        jnp.einsum("tf,df->td", after(hidden, grad_normed_mlp), own_down, preferred_element_type=f32).astype(bf16)
    ).astype(f32)
    block_output = (resid + branch).astype(bf16)

    ffn_grads = jnp.concatenate(
        [
            jnp.einsum("td,tf->df", normed_mlp_all, grad_gateup, preferred_element_type=f32),
            jnp.einsum("td,tf->df", cotangent_all, hidden, preferred_element_type=f32),
        ],
        axis=1,
    )
    ffn_moms = exchange(ffn_packets(mom_gateup.astype(bf16), mom_down.astype(bf16), device_count))
    ffn_pieces = momentum_decay * ffn_moms.reshape(width, 3 * HEAD).astype(f32) + ffn_grads
    ffn_pieces = ffn_pieces.astype(bf16)
    ffn_turned = jnp.concatenate(
        [orthogonalize(ffn_pieces[:, at * HEAD : (at + 1) * HEAD]) for at in range(3)], axis=1
    )
    ffn_shape = (device_count, share_rows, 3 * HEAD)
    grad_w_gateup, grad_w_down = ffn_unpack(exchange(ffn_grads.astype(bf16).reshape(ffn_shape)))
    turn_gateup, turn_down = ffn_unpack(exchange(ffn_turned.reshape(ffn_shape)))

    grad_mixed = jnp.dot(grad_proj, full_out, preferred_element_type=f32).astype(bf16)
    grad_mixed = grad_mixed.reshape(local_rows, H, HEAD)
    grad_probs = jnp.einsum("qhd,kd->hqk", grad_mixed, values, preferred_element_type=f32)
    row_delta = jnp.sum(probs * grad_probs, axis=-1, keepdims=True)
    grad_raw = (probs * (grad_probs - row_delta) * score_scale).astype(bf16)
    grad_query = jnp.einsum("hqk,kd->qhd", grad_raw, keys, preferred_element_type=f32)
    grad_keys = jnp.einsum("hqk,qhd->kd", grad_raw, queries, preferred_element_type=f32)
    grad_values = jnp.einsum("hqk,qhd->kd", probs_low, grad_mixed, preferred_element_type=f32)
    grad_kv = jnp.concatenate([grad_keys, grad_values], axis=1).astype(bf16)
    grad_kv_all = lax.dynamic_update_slice_in_dim(
        jnp.zeros((WINDOW + token_count, 2 * HEAD), bf16), grad_kv, me * local_rows, 0
    )[WINDOW:]
    grad_qkv = jnp.concatenate(
        [grad_query.reshape(local_rows, H * HEAD).astype(bf16), scatter_sum(grad_kv_all)], axis=1
    )
    grad_normed_attn = jnp.einsum("tc,dc->td", grad_qkv, full_qkv, preferred_element_type=f32)
    stream_part, gain_grad_attn = norm_back_attn(grad_normed_attn)
    input_grad = grad_resid + stream_part

    attn_rights = exchange(
        column_packets(jnp.concatenate([grad_qkv, mixed], axis=1), device_count)
    ).reshape(token_count, HEAD)
    normed_attn_all = gather(after(normed_attn, (ffn_grads, block_output)))
    grad_proj_all = gather(after(grad_proj, (ffn_grads, block_output)))

    def owned_gradient(lefts):
        return jnp.einsum("td,tf->df", lefts, attn_rights, preferred_element_type=f32)

    attn_grads = lax.cond(
        me < H + 2,
        lambda: owned_gradient(normed_attn_all),
        lambda: owned_gradient(grad_proj_all),
    )
    attn_moms = exchange(
        column_packets(
            jnp.concatenate([mom_qkv.astype(bf16), mom_out.astype(bf16).T], axis=1), device_count
        )
    ).reshape(width, HEAD)
    attn_piece = (momentum_decay * attn_moms.astype(f32) + attn_grads).astype(bf16)
    attn_turned = orthogonalize(attn_piece)
    attn_shape = (device_count, share_rows, HEAD)
    grad_w_qkv, grad_w_out = attn_unpack(exchange(attn_grads.astype(bf16).reshape(attn_shape)))
    turn_qkv, turn_out = attn_unpack(exchange(attn_turned.reshape(attn_shape)))

    gain_grads = jnp.stack([gain_grad_attn, gain_grad_mlp], axis=0)
    gain_grads = gain_grads.reshape(2, device_count, share_rows).transpose(1, 0, 2)
    gain_share = jnp.sum(exchange(gain_grads), axis=0)

    moment_qkv = momentum_decay * mom_qkv + grad_w_qkv.astype(f32)
    moment_out = momentum_decay * mom_out + grad_w_out.astype(f32)
    moment_gateup = momentum_decay * mom_gateup + grad_w_gateup.astype(f32)
    moment_down = momentum_decay * mom_down + grad_w_down.astype(f32)
    moment_gains = momentum_decay * mom_gains + gain_share
    new_qkv = (1.0 - weight_shrink) * w_qkv - matrix_rate * turn_qkv.astype(f32)
    new_out = (1.0 - weight_shrink) * w_out - output_rate * turn_out.astype(f32)
    new_gateup = (1.0 - weight_shrink) * w_gateup - matrix_rate * turn_gateup.astype(f32)
    new_down = (1.0 - weight_shrink) * w_down - matrix_rate * turn_down.astype(f32)
    new_gains = gains - gain_rate * moment_gains
    return (
        block_output,
        input_grad,
        new_qkv,
        moment_qkv,
        new_qkv.astype(jnp.bfloat16),
        new_out,
        moment_out,
        new_out.astype(jnp.bfloat16),
        new_gateup,
        moment_gateup,
        new_gateup.astype(jnp.bfloat16),
        new_down,
        moment_down,
        new_down.astype(jnp.bfloat16),
        new_gains,
        moment_gains,
        new_gains.astype(jnp.bfloat16),
    )


def solution(mesh):
    placed = (
        P(("blk", "pair"), None),
        P(("blk", "pair"), None),
        P(("blk", "pair"), None),
        P(None, ("blk", "pair")),
        P(None, ("blk", "pair"), None),
        P(None, ("blk", "pair")),
        P(None, ("blk", "pair")),
        P(("blk", "pair"), None),
        P(None, ("blk", "pair")),
        P(None, ("blk", "pair"), None),
        P(None, ("blk", "pair")),
        P(None, ("blk", "pair")),
    )
    return jax.shard_map(
        on_device,
        mesh=mesh,
        in_specs=placed,
        out_specs=(
            P(("blk", "pair"), None),
            P(("blk", "pair"), None),
            P(("blk", "pair"), None),
            P(("blk", "pair"), None),
            P(("blk", "pair"), None),
            P(None, ("blk", "pair")),
            P(None, ("blk", "pair")),
            P(None, ("blk", "pair")),
            P(None, ("blk", "pair"), None),
            P(None, ("blk", "pair"), None),
            P(None, ("blk", "pair"), None),
            P(None, ("blk", "pair")),
            P(None, ("blk", "pair")),
            P(None, ("blk", "pair")),
            P(None, ("blk", "pair")),
            P(None, ("blk", "pair")),
            P(None, ("blk", "pair")),
        ),
        check_vma=False,
    )
```

```python
import functools

import jax
import jax.numpy as jnp
from jax import lax
from jax.experimental import pallas as pl
from jax.experimental.pallas import tpu as pltpu
from jax.sharding import PartitionSpec as P

H = 10
HEAD = 256
FF = 7680
WINDOW = 2048
NS_STEPS = 5


eps_norm = 1e-06
eps_pieces = 1e-07
ns_first = 3.4445
ns_second = -4.775
ns_third = 2.0315
momentum_decay = 0.95
matrix_rate = 0.5
output_rate = 10.0
gain_rate = 0.001
weight_shrink = 0.001
masked_score = -1e30
MESH = pl.DeviceIdType.MESH


def places(planes):
    blk = lax.axis_index("blk")
    y = lax.axis_index("pair")
    core = lax.rem(blk, 2)
    x = lax.rem(lax.div(blk, 2), 2)
    z = lax.div(blk, 4)
    first = y * (1 - core) + x * core
    second = x * (1 - core) + y * core
    to_core = (blk + 1 - 2 * core, y)
    first_device = (blk + core * (2 - 4 * x), y + (1 - core) * (1 - 2 * y))
    second_device = (blk + (1 - core) * (2 - 4 * x), y + core * (1 - 2 * y))
    line = [(lax.rem(z + at, planes), at) for at in range(planes)]
    line_devices = [((blk + 4 * (spot - z)), y) for spot, at in line]
    return core, z, first, second, to_core, first_device, second_device, line, line_devices


def greet(devices):
    barrier = pltpu.get_barrier_semaphore()
    for device in devices:
        pl.semaphore_signal(barrier, inc=1, device_id=device, device_id_type=MESH)
    pl.semaphore_wait(barrier, len(devices))


def remote(source, target, send_sem, recv_sem, device):
    return pltpu.make_async_remote_copy(
        src_ref=source,
        dst_ref=target,
        send_sem=send_sem,
        recv_sem=recv_sem,
        device_id=device,
        device_id_type=MESH,
    )


def gather_kernel(planes, count, *refs):
    shards, wholes = refs[:count], refs[count : 2 * count]
    own_sem, line_send, second_send, first_send, core_send, recv, core_recv = refs[2 * count :]
    core, z, first, second, to_core, first_device, second_device, line, line_devices = places(
        planes
    )
    greet([to_core, first_device, second_device] + line_devices[1:])

    def slot(whole, spot, by_first, by_second):
        x = (1 - core) * by_second + core * by_first
        y = (1 - core) * by_first + core * by_second
        return whole.at[spot, x, core, y]

    def core_slot(whole, spot, by_first, by_second):
        x = core * by_second + (1 - core) * by_first
        y = core * by_first + (1 - core) * by_second
        return whole.at[spot, x, 1 - core, y]

    sent = []

    def send(source, target, send_sem, recv_sem, device):
        copy = remote(source, target, send_sem, recv_sem, device)
        copy.start()
        sent.append(copy)

    def arrive(target, recv_sem):
        remote(target, target, own_sem.at[0], recv_sem, to_core).wait_recv()

    own_copies = []
    for i, (shard, whole) in enumerate(zip(shards, wholes)):
        here = slot(whole, z, first, second)
        copy = pltpu.make_async_copy(shard, here, own_sem.at[i])
        copy.start()
        own_copies.append(copy)
        for spot, at in line[1:]:
            send(shard, here, line_send.at[i, at], recv.at[i, z, first, second], line_devices[at])
    for spot, at in line:
        for i, (shard, whole) in enumerate(zip(shards, wholes)):
            here = slot(whole, spot, first, second)
            source = shard
            if at:
                arrive(here, recv.at[i, spot, first, second])
                source = here
            for devices, sends in ((second_device, second_send.at[i, at]), (first_device, first_send.at[i, at, 0])):
                send(source, here, sends, recv.at[i, spot, first, second], devices)
            send(source, here, core_send.at[i, at, 0, 0], core_recv.at[i, spot, first, second], to_core)
        for i, whole in enumerate(wholes):
            here = slot(whole, spot, first, 1 - second)
            arrive(here, recv.at[i, spot, first, 1 - second])
            send(here, here, first_send.at[i, at, 1], recv.at[i, spot, first, 1 - second], first_device)
            send(here, here, core_send.at[i, at, 0, 1], core_recv.at[i, spot, first, 1 - second], to_core)
    for spot, at in line:
        for turn, by_second in enumerate((second, 1 - second)):
            for i, whole in enumerate(wholes):
                here = slot(whole, spot, 1 - first, by_second)
                arrive(here, recv.at[i, spot, 1 - first, by_second])
                send(here, here, core_send.at[i, at, 1, turn], core_recv.at[i, spot, 1 - first, by_second], to_core)
    for copy in own_copies:
        copy.wait()
    for i, whole in enumerate(wholes):
        for spot in range(planes):
            for by_first in range(2):
                for by_second in range(2):
                    arrive(
                        core_slot(whole, spot, by_first, by_second),
                        core_recv.at[i, spot, by_first, by_second],
                    )
    for copy in sent:
        copy.wait_send()


def gather_by_axes(shards, planes, collective_id):
    count = len(shards)
    any_spec = pl.BlockSpec(memory_space=pl.ANY)
    dma = pltpu.SemaphoreType.DMA
    wholes = pl.pallas_call(
        functools.partial(gather_kernel, planes, count),
        out_shape=[
            jax.ShapeDtypeStruct((planes, 2, 2, 2, *shard.shape), shard.dtype) for shard in shards
        ],
        in_specs=[any_spec] * count,
        out_specs=[any_spec] * count,
        scratch_shapes=[
            dma((count,)),
            dma((count, planes)),
            dma((count, planes)),
            dma((count, planes, 2)),
            dma((count, planes, 2, 2)),
            dma((count, planes, 2, 2)),
            dma((count, planes, 2, 2)),
        ],
        compiler_params=pltpu.CompilerParams(collective_id=collective_id, has_side_effects=True),
        name="gather_by_axes",
    )(*shards)
    return [
        whole.reshape(8 * planes * shard.shape[0], shard.shape[1])
        for whole, shard in zip(wholes, shards)
    ]


def scatter_kernel(
    planes,
    steps,
    rows,
    partial_ref,
    sum_ref,
    own,
    from_core,
    from_first,
    from_second,
    from_line,
    load_sem,
    core_sems,
    first_sems,
    second_sems,
    line_send,
    line_recv,
):
    core, z, first, second, to_core, first_device, second_device, line, line_devices = places(
        planes
    )
    greet([to_core, first_device, second_device] + line_devices[1:])

    def piece(step, by_first, by_second, plane):
        x = (1 - plane) * by_second + plane * by_first
        y = (1 - plane) * by_first + plane * by_second
        return partial_ref.at[:, x, plane, y, pl.ds(pl.multiple_of(step * rows, rows), rows)]

    def core_copy(step, half, by_second, plane):
        return remote(
            piece(step, half, by_second, plane),
            from_core.at[step, half, by_second],
            core_sems.at[0, step, half, by_second],
            core_sems.at[1, step, half, by_second],
            to_core,
        )

    def load(step, half, by_second):
        return pltpu.make_async_copy(
            piece(step, half, by_second, core),
            own.at[step, half, by_second],
            load_sem.at[step, half, by_second],
        )

    def first_copy(step, half):
        return remote(
            own.at[step, half],
            from_first.at[step],
            first_sems.at[0, step],
            first_sems.at[1, step],
            first_device,
        )

    def second_copy(step, half):
        return remote(
            own.at[step, first, half],
            from_second.at[step],
            second_sems.at[0, step],
            second_sems.at[1, step],
            second_device,
        )

    def line_copy(step, at):
        return remote(
            own.at[step, first, second, line[at][0]],
            from_line.at[step, z],
            line_send.at[step, at],
            line_recv.at[step, z],
            line_devices[at],
        )

    def start_loads(step):
        for mine, theirs in ((1 - first, 1 - second), (first, second)):
            for by_second in range(2):
                core_copy(step, theirs, by_second, 1 - core).start()
                load(step, mine, by_second).start()

    def add_core(step):
        for turn, half in enumerate((1 - first, first)):
            for by_second in range(2):
                load(step, half, by_second).wait()
                core_copy(step, half, by_second, core).wait_recv()
                own[step, half, by_second] += from_core[step, half, by_second]
            if turn == 0:
                first_copy(step, half).start()

    def add_first(step):
        first_copy(step, 1 - first).wait_recv()
        own[step, first, 1 - second] += from_first[step, 1 - second]
        second_copy(step, 1 - second).start()
        own[step, first, second] += from_first[step, second]

    def add_second(step):
        second_copy(step, 1 - second).wait_recv()
        own[step, first, second] += from_second[step]
        for at in range(1, planes):
            line_copy(step, at).start()

    def add_line(step):
        total = own[step, first, second, z].astype(jnp.float32)
        for spot, at in line[1:]:
            remote(
                own.at[step, first, second, spot],
                from_line.at[step, spot],
                line_send.at[step, at],
                line_recv.at[step, spot],
                line_devices[at],
            ).wait_recv()
            total = total + from_line[step, spot].astype(jnp.float32)
        sum_ref[pl.ds(pl.multiple_of(step * rows, rows), rows), :] = total.astype(sum_ref.dtype)

    start_loads(0)
    start_loads(1)

    @pl.loop(0, steps + 3)
    def _(turn):
        @pl.when(turn < steps - 2)
        def _():
            start_loads(turn + 2)

        @pl.when(turn < steps)
        def _():
            add_core(turn)

        @pl.when((turn >= 1) & (turn < steps + 1))
        def _():
            add_first(turn - 1)

        @pl.when((turn >= 2) & (turn < steps + 2))
        def _():
            add_second(turn - 2)

        @pl.when(turn >= 3)
        def _():
            add_line(turn - 3)

    @pl.loop(0, steps)
    def _(step):
        for half in range(2):
            for by_second in range(2):
                core_copy(step, half, by_second, 1 - core).wait_send()
        first_copy(step, 1 - first).wait_send()
        second_copy(step, 1 - second).wait_send()
        for at in range(1, planes):
            line_copy(step, at).wait_send()


def scatter_by_axes(partial, planes, collective_id):
    shard_rows = partial.shape[0] // (8 * planes)
    width = partial.shape[1]
    rows = 16
    steps = shard_rows // rows
    dtype = partial.dtype
    dma = pltpu.SemaphoreType.DMA
    return pl.pallas_call(
        functools.partial(scatter_kernel, planes, steps, rows),
        out_shape=jax.ShapeDtypeStruct((shard_rows, width), dtype),
        in_specs=[pl.BlockSpec(memory_space=pl.ANY)],
        out_specs=pl.BlockSpec(memory_space=pltpu.VMEM),
        scratch_shapes=[
            pltpu.VMEM((steps, 2, 2, planes, rows, width), dtype),
            pltpu.VMEM((steps, 2, 2, planes, rows, width), dtype),
            pltpu.VMEM((steps, 2, planes, rows, width), dtype),
            pltpu.VMEM((steps, planes, rows, width), dtype),
            pltpu.VMEM((steps, planes, rows, width), dtype),
            dma((steps, 2, 2)),
            dma((2, steps, 2, 2)),
            dma((2, steps)),
            dma((2, steps)),
            dma((steps, planes)),
            dma((steps, planes)),
        ],
        compiler_params=pltpu.CompilerParams(
            collective_id=collective_id, has_side_effects=True, vmem_limit_bytes=48 * 2**20
        ),
        name="scatter_by_axes",
    )(partial.reshape(planes, 2, 2, 2, shard_rows, width))


def rms_scale(stream, gain_row):
    mean_square = jnp.mean(stream * stream, axis=-1, keepdims=True)
    return stream * lax.rsqrt(mean_square + eps_norm) * gain_row


def gelu_product(gate_part, up_part):
    return jax.nn.gelu(gate_part, approximate=True) * up_part


def ffn_packets(part_gateup, part_down, device_count):
    row_count = part_gateup.shape[1]
    blocks = FF // HEAD
    gateup = part_gateup.reshape(2, row_count, blocks, HEAD).transpose(2, 1, 0, 3)
    down = part_down.reshape(blocks, HEAD, row_count).transpose(0, 2, 1)[:, :, None, :]
    packets = jnp.concatenate([gateup, down], axis=2).reshape(blocks, row_count, 3 * HEAD)
    return jnp.pad(packets, ((0, device_count - blocks), (0, 0), (0, 0)))


def ffn_unpack(packets):
    row_count = packets.shape[1]
    blocks = FF // HEAD
    kept = packets[:blocks].reshape(blocks, row_count, 3, HEAD)
    gateup = kept[:, :, :2].transpose(2, 1, 0, 3).reshape(2, row_count, FF)
    down = kept[:, :, 2].transpose(0, 2, 1).reshape(FF, row_count)
    return gateup, down


def column_packets(columns, device_count):
    row_count, width = columns.shape
    blocks = width // HEAD
    packets = columns.reshape(row_count, blocks, HEAD).transpose(1, 0, 2)
    return jnp.pad(packets, ((0, device_count - blocks), (0, 0), (0, 0)))


def attn_unpack(packets):
    row_count = packets.shape[1]
    part_qkv = packets[: H + 2].transpose(1, 0, 2).reshape(row_count, (H + 2) * HEAD)
    part_out = packets[H + 2 : 2 * H + 2].transpose(0, 2, 1).reshape(H * HEAD, row_count)
    return part_qkv, part_out


def orthogonalize(piece):
    values = piece.astype(jnp.float32)
    norm_size = jnp.sqrt(jnp.sum(values * values))
    current = (values / (norm_size + eps_pieces)).astype(jnp.bfloat16)
    for sweep_index in range(NS_STEPS):
        gram_matrix = jnp.einsum(
            "di,dj->ij", current, current, preferred_element_type=jnp.float32
        ).astype(jnp.bfloat16)
        square = jnp.dot(gram_matrix, gram_matrix, preferred_element_type=jnp.float32)
        mixing = (ns_second * gram_matrix.astype(jnp.float32) + ns_third * square).astype(
            jnp.bfloat16
        )
        turned = jnp.dot(current, mixing, preferred_element_type=jnp.float32)
        current = (ns_first * current.astype(jnp.float32) + turned).astype(jnp.bfloat16)
    return current


def on_device(
    tokens_in,
    cotangent,
    w_qkv,
    w_out,
    w_gateup,
    w_down,
    gains,
    mom_qkv,
    mom_out,
    mom_gateup,
    mom_down,
    mom_gains,
):
    everyone = ("blk", "pair")
    bf16 = jnp.bfloat16
    f32 = jnp.float32
    device_count = lax.axis_size("blk") * lax.axis_size("pair")
    me = lax.axis_index("blk") * lax.axis_size("pair") + lax.axis_index("pair")
    local_rows, width = tokens_in.shape
    share_rows = w_qkv.shape[0]
    score_scale = HEAD ** (-0.5)
    span = WINDOW + local_rows

    def gather(shard):
        return lax.all_gather(shard, everyone, axis=0, tiled=True)

    def scatter_sum(partial):
        return lax.psum_scatter(partial, everyone, scatter_dimension=0, tiled=True)

    def exchange(packets):
        return lax.all_to_all(packets, everyone, split_axis=0, concat_axis=0, tiled=True)

    token_count = local_rows * device_count
    large = token_count * width * 2 > 48 * 2**20

    def after(value, earlier):
        return lax.optimization_barrier((value, earlier))[0] if large else value

    planes = lax.axis_size("blk") // 4

    def gather_now(shards, collective_id):
        if large:
            return [gather(shard) for shard in shards]
        return gather_by_axes(shards, planes, collective_id)

    def scatter_now(partial, collective_id):
        if large:
            return scatter_sum(partial)
        return scatter_by_axes(partial, planes, collective_id)

    stream = tokens_in.astype(f32)
    padded_gains = jnp.pad(gains.astype(bf16), ((0, 14), (0, 128 - share_rows)))
    full_qkv, full_gains = gather_now([w_qkv.astype(bf16), padded_gains], 1)
    full_gains = full_gains.reshape(device_count, 16, 128)[:, :2, :share_rows].astype(f32)
    gain_attn = full_gains[:, 0].reshape(width)
    gain_mlp = full_gains[:, 1].reshape(width)
    normed_attn_f, norm_back_attn = jax.vjp(rms_scale, stream, gain_attn)
    normed_attn = normed_attn_f.astype(bf16)
    qkv = jnp.dot(normed_attn, full_qkv, preferred_element_type=f32).astype(bf16)
    queries = qkv[:, : H * HEAD].reshape(local_rows, H, HEAD)
    (kv_all,) = gather_now([qkv[:, H * HEAD :]], 2)
    kv_window = lax.dynamic_slice_in_dim(
        jnp.pad(kv_all, ((WINDOW, 0), (0, 0))), me * local_rows, span, 0
    )
    keys = kv_window[:, :HEAD]
    values = kv_window[:, HEAD:]
    full_out = gather(w_out.astype(bf16).T)
    ffn_weights = exchange(ffn_packets(w_gateup.astype(bf16), w_down.astype(bf16), device_count))
    ffn_weights = ffn_weights.reshape(width, 3 * HEAD)
    own_gateup = ffn_weights[:, : 2 * HEAD]
    own_down = ffn_weights[:, 2 * HEAD :]
    cotangent_all = gather(cotangent)

    key_index = jnp.arange(span, dtype=jnp.int32)[None, :]
    distance = jnp.arange(local_rows, dtype=jnp.int32)[:, None] + WINDOW - key_index
    allowed = (
        (distance >= 0) & (distance < WINDOW) & (me * local_rows - WINDOW + key_index >= 0)
    )
    raw = jnp.einsum("qhd,kd->hqk", queries, keys, preferred_element_type=f32)
    scores = jnp.where(allowed[None], raw * score_scale, masked_score)
    top_score = jnp.max(scores, axis=-1, keepdims=True)
    expo = jnp.exp(scores - top_score)
    probs = expo / jnp.sum(expo, axis=-1, keepdims=True)
    probs_low = probs.astype(bf16)
    mixed = jnp.einsum("hqk,kd->qhd", probs_low, values, preferred_element_type=f32)
    mixed = mixed.reshape(local_rows, H * HEAD).astype(bf16)
    resid = stream + jnp.einsum("tc,dc->td", mixed, full_out, preferred_element_type=f32)

    normed_mlp_f, norm_back_mlp = jax.vjp(rms_scale, resid, gain_mlp)
    (normed_mlp_all,) = gather_now([normed_mlp_f.astype(bf16)], 3)
    both_parts = jnp.dot(normed_mlp_all, own_gateup, preferred_element_type=f32)
    hidden_f, geglu_back = jax.vjp(gelu_product, both_parts[:, :HEAD], both_parts[:, HEAD:])
    hidden = hidden_f.astype(bf16)
    grad_hidden = jnp.dot(cotangent_all, own_down, preferred_element_type=f32)
    grad_gate, grad_up = geglu_back(grad_hidden)
    grad_gateup = jnp.concatenate([grad_gate.astype(bf16), grad_up.astype(bf16)], axis=1)
    grad_normed_mlp = scatter_now(
        jnp.einsum("tf,df->td", grad_gateup, own_gateup, preferred_element_type=f32).astype(bf16), 4
    ).astype(f32)
    resid_part, gain_grad_mlp = norm_back_mlp(grad_normed_mlp)
    grad_resid = cotangent.astype(f32) + resid_part
    grad_proj = grad_resid.astype(bf16)
    branch_part = jnp.einsum(
        "tf,df->td", after(hidden, grad_normed_mlp), own_down, preferred_element_type=f32
    )
    branch = scatter_now(branch_part.astype(bf16), 4).astype(f32)
    block_output = (resid + branch).astype(bf16)

    ffn_grads = jnp.concatenate(
        [
            jnp.einsum("td,tf->df", normed_mlp_all, grad_gateup, preferred_element_type=f32),
            jnp.einsum("td,tf->df", cotangent_all, hidden, preferred_element_type=f32),
        ],
        axis=1,
    )
    ffn_moms = exchange(ffn_packets(mom_gateup.astype(bf16), mom_down.astype(bf16), device_count))
    ffn_pieces = momentum_decay * ffn_moms.reshape(width, 3 * HEAD).astype(f32) + ffn_grads
    ffn_pieces = ffn_pieces.astype(bf16)
    ffn_turned = jnp.concatenate(
        [orthogonalize(ffn_pieces[:, at * HEAD : (at + 1) * HEAD]) for at in range(3)], axis=1
    )
    ffn_shape = (device_count, share_rows, 3 * HEAD)
    grad_w_gateup, grad_w_down = ffn_unpack(exchange(ffn_grads.astype(bf16).reshape(ffn_shape)))
    turn_gateup, turn_down = ffn_unpack(exchange(ffn_turned.reshape(ffn_shape)))

    grad_mixed = jnp.dot(grad_proj, full_out, preferred_element_type=f32).astype(bf16)
    grad_mixed = grad_mixed.reshape(local_rows, H, HEAD)
    grad_probs = jnp.einsum("qhd,kd->hqk", grad_mixed, values, preferred_element_type=f32)
    row_delta = jnp.sum(probs * grad_probs, axis=-1, keepdims=True)
    grad_raw = (probs * (grad_probs - row_delta) * score_scale).astype(bf16)
    grad_query = jnp.einsum("hqk,kd->qhd", grad_raw, keys, preferred_element_type=f32)
    grad_keys = jnp.einsum("hqk,qhd->kd", grad_raw, queries, preferred_element_type=f32)
    grad_values = jnp.einsum("hqk,qhd->kd", probs_low, grad_mixed, preferred_element_type=f32)
    grad_kv = jnp.concatenate([grad_keys, grad_values], axis=1).astype(bf16)
    grad_kv_all = lax.dynamic_update_slice_in_dim(
        jnp.zeros((WINDOW + token_count, 2 * HEAD), bf16), grad_kv, me * local_rows, 0
    )[WINDOW:]
    grad_qkv = jnp.concatenate(
        [grad_query.reshape(local_rows, H * HEAD).astype(bf16), scatter_now(grad_kv_all, 5)], axis=1
    )
    grad_normed_attn = jnp.einsum("tc,dc->td", grad_qkv, full_qkv, preferred_element_type=f32)
    stream_part, gain_grad_attn = norm_back_attn(grad_normed_attn)
    input_grad = grad_resid + stream_part

    attn_rights = exchange(
        column_packets(jnp.concatenate([grad_qkv, mixed], axis=1), device_count)
    ).reshape(token_count, HEAD)
    normed_attn_all = gather(after(normed_attn, (ffn_grads, block_output)))
    grad_proj_all = gather(after(grad_proj, (ffn_grads, block_output)))

    def owned_gradient(lefts):
        return jnp.einsum("td,tf->df", lefts, attn_rights, preferred_element_type=f32)

    attn_grads = lax.cond(
        me < H + 2,
        lambda: owned_gradient(normed_attn_all),
        lambda: owned_gradient(grad_proj_all),
    )
    attn_moms = exchange(
        column_packets(
            jnp.concatenate([mom_qkv.astype(bf16), mom_out.astype(bf16).T], axis=1), device_count
        )
    ).reshape(width, HEAD)
    attn_piece = (momentum_decay * attn_moms.astype(f32) + attn_grads).astype(bf16)
    attn_turned = orthogonalize(attn_piece)
    attn_shape = (device_count, share_rows, HEAD)
    grad_w_qkv, grad_w_out = attn_unpack(exchange(attn_grads.astype(bf16).reshape(attn_shape)))
    turn_qkv, turn_out = attn_unpack(exchange(attn_turned.reshape(attn_shape)))

    gain_grads = jnp.stack([gain_grad_attn, gain_grad_mlp], axis=0)
    gain_grads = gain_grads.reshape(2, device_count, share_rows).transpose(1, 0, 2)
    gain_share = jnp.sum(exchange(gain_grads), axis=0)

    moment_qkv = momentum_decay * mom_qkv + grad_w_qkv.astype(f32)
    moment_out = momentum_decay * mom_out + grad_w_out.astype(f32)
    moment_gateup = momentum_decay * mom_gateup + grad_w_gateup.astype(f32)
    moment_down = momentum_decay * mom_down + grad_w_down.astype(f32)
    moment_gains = momentum_decay * mom_gains + gain_share
    new_qkv = (1.0 - weight_shrink) * w_qkv - matrix_rate * turn_qkv.astype(f32)
    new_out = (1.0 - weight_shrink) * w_out - output_rate * turn_out.astype(f32)
    new_gateup = (1.0 - weight_shrink) * w_gateup - matrix_rate * turn_gateup.astype(f32)
    new_down = (1.0 - weight_shrink) * w_down - matrix_rate * turn_down.astype(f32)
    new_gains = gains - gain_rate * moment_gains
    return (
        block_output,
        input_grad,
        new_qkv,
        moment_qkv,
        new_qkv.astype(jnp.bfloat16),
        new_out,
        moment_out,
        new_out.astype(jnp.bfloat16),
        new_gateup,
        moment_gateup,
        new_gateup.astype(jnp.bfloat16),
        new_down,
        moment_down,
        new_down.astype(jnp.bfloat16),
        new_gains,
        moment_gains,
        new_gains.astype(jnp.bfloat16),
    )


def solution(mesh):
    placed = (
        P(("blk", "pair"), None),
        P(("blk", "pair"), None),
        P(("blk", "pair"), None),
        P(None, ("blk", "pair")),
        P(None, ("blk", "pair"), None),
        P(None, ("blk", "pair")),
        P(None, ("blk", "pair")),
        P(("blk", "pair"), None),
        P(None, ("blk", "pair")),
        P(None, ("blk", "pair"), None),
        P(None, ("blk", "pair")),
        P(None, ("blk", "pair")),
    )
    return jax.shard_map(
        on_device,
        mesh=mesh,
        in_specs=placed,
        out_specs=(
            P(("blk", "pair"), None),
            P(("blk", "pair"), None),
            P(("blk", "pair"), None),
            P(("blk", "pair"), None),
            P(("blk", "pair"), None),
            P(None, ("blk", "pair")),
            P(None, ("blk", "pair")),
            P(None, ("blk", "pair")),
            P(None, ("blk", "pair"), None),
            P(None, ("blk", "pair"), None),
            P(None, ("blk", "pair"), None),
            P(None, ("blk", "pair")),
            P(None, ("blk", "pair")),
            P(None, ("blk", "pair")),
            P(None, ("blk", "pair")),
            P(None, ("blk", "pair")),
            P(None, ("blk", "pair")),
        ),
        check_vma=False,
    )
```

```python
import functools

import jax
import jax.numpy as jnp
from jax import lax
from jax.experimental import pallas as pl
from jax.experimental.pallas import tpu as pltpu
from jax.sharding import PartitionSpec as P

H = 10
HEAD = 256
FF = 7680
WINDOW = 2048
NS_STEPS = 5


eps_norm = 1e-06
eps_pieces = 1e-07
ns_first = 3.4445
ns_second = -4.775
ns_third = 2.0315
momentum_decay = 0.95
matrix_rate = 0.5
output_rate = 10.0
gain_rate = 0.001
weight_shrink = 0.001
masked_score = -1e30
MESH = pl.DeviceIdType.MESH


def places(planes):
    blk = lax.axis_index("blk")
    y = lax.axis_index("pair")
    core = lax.rem(blk, 2)
    x = lax.rem(lax.div(blk, 2), 2)
    z = lax.div(blk, 4)
    first = y * (1 - core) + x * core
    second = x * (1 - core) + y * core
    to_core = (blk + 1 - 2 * core, y)
    first_device = (blk + core * (2 - 4 * x), y + (1 - core) * (1 - 2 * y))
    second_device = (blk + (1 - core) * (2 - 4 * x), y + core * (1 - 2 * y))
    line = [(lax.rem(z + at, planes), at) for at in range(planes)]
    line_devices = [((blk + 4 * (spot - z)), y) for spot, at in line]
    return core, z, first, second, to_core, first_device, second_device, line, line_devices


def greet(devices):
    barrier = pltpu.get_barrier_semaphore()
    for device in devices:
        pl.semaphore_signal(barrier, inc=1, device_id=device, device_id_type=MESH)
    pl.semaphore_wait(barrier, len(devices))


def remote(source, target, send_sem, recv_sem, device):
    return pltpu.make_async_remote_copy(
        src_ref=source,
        dst_ref=target,
        send_sem=send_sem,
        recv_sem=recv_sem,
        device_id=device,
        device_id_type=MESH,
    )


def gather_kernel(planes, count, *refs):
    shards, wholes = refs[:count], refs[count : 2 * count]
    own_sem, line_send, second_send, first_send, core_send, recv, core_recv = refs[2 * count :]
    core, z, first, second, to_core, first_device, second_device, line, line_devices = places(
        planes
    )
    greet([to_core, first_device, second_device] + line_devices[1:])

    def slot(whole, spot, by_first, by_second):
        x = (1 - core) * by_second + core * by_first
        y = (1 - core) * by_first + core * by_second
        return whole.at[spot, x, core, y]

    def core_slot(whole, spot, by_first, by_second):
        x = core * by_second + (1 - core) * by_first
        y = core * by_first + (1 - core) * by_second
        return whole.at[spot, x, 1 - core, y]

    sent = []

    def send(source, target, send_sem, recv_sem, device):
        copy = remote(source, target, send_sem, recv_sem, device)
        copy.start()
        sent.append(copy)

    def arrive(target, recv_sem):
        remote(target, target, own_sem.at[0], recv_sem, to_core).wait_recv()

    own_copies = []
    for i, (shard, whole) in enumerate(zip(shards, wholes)):
        here = slot(whole, z, first, second)
        copy = pltpu.make_async_copy(shard, here, own_sem.at[i])
        copy.start()
        own_copies.append(copy)
        for spot, at in line[1:]:
            send(shard, here, line_send.at[i, at], recv.at[i, z, first, second], line_devices[at])
    for spot, at in line:
        for i, (shard, whole) in enumerate(zip(shards, wholes)):
            here = slot(whole, spot, first, second)
            source = shard
            if at:
                arrive(here, recv.at[i, spot, first, second])
                source = here
            for devices, sends in ((second_device, second_send.at[i, at]), (first_device, first_send.at[i, at, 0])):
                send(source, here, sends, recv.at[i, spot, first, second], devices)
            send(source, here, core_send.at[i, at, 0, 0], core_recv.at[i, spot, first, second], to_core)
        for i, whole in enumerate(wholes):
            here = slot(whole, spot, first, 1 - second)
            arrive(here, recv.at[i, spot, first, 1 - second])
            send(here, here, first_send.at[i, at, 1], recv.at[i, spot, first, 1 - second], first_device)
            send(here, here, core_send.at[i, at, 0, 1], core_recv.at[i, spot, first, 1 - second], to_core)
    for spot, at in line:
        for turn, by_second in enumerate((second, 1 - second)):
            for i, whole in enumerate(wholes):
                here = slot(whole, spot, 1 - first, by_second)
                arrive(here, recv.at[i, spot, 1 - first, by_second])
                send(here, here, core_send.at[i, at, 1, turn], core_recv.at[i, spot, 1 - first, by_second], to_core)
    for copy in own_copies:
        copy.wait()
    for i, whole in enumerate(wholes):
        for spot in range(planes):
            for by_first in range(2):
                for by_second in range(2):
                    arrive(
                        core_slot(whole, spot, by_first, by_second),
                        core_recv.at[i, spot, by_first, by_second],
                    )
    for copy in sent:
        copy.wait_send()


def gather_by_axes(shards, planes, collective_id):
    count = len(shards)
    any_spec = pl.BlockSpec(memory_space=pl.ANY)
    dma = pltpu.SemaphoreType.DMA
    wholes = pl.pallas_call(
        functools.partial(gather_kernel, planes, count),
        out_shape=[
            jax.ShapeDtypeStruct((planes, 2, 2, 2, *shard.shape), shard.dtype) for shard in shards
        ],
        in_specs=[any_spec] * count,
        out_specs=[any_spec] * count,
        scratch_shapes=[
            dma((count,)),
            dma((count, planes)),
            dma((count, planes)),
            dma((count, planes, 2)),
            dma((count, planes, 2, 2)),
            dma((count, planes, 2, 2)),
            dma((count, planes, 2, 2)),
        ],
        compiler_params=pltpu.CompilerParams(collective_id=collective_id, has_side_effects=True),
        name="gather_by_axes",
    )(*shards)
    return [
        whole.reshape(8 * planes * shard.shape[0], shard.shape[1])
        for whole, shard in zip(wholes, shards)
    ]


def scatter_kernel(
    planes,
    steps,
    rows,
    partial_ref,
    sum_ref,
    own,
    from_core,
    from_first,
    from_second,
    from_line,
    load_sem,
    core_sems,
    first_sems,
    second_sems,
    line_send,
    line_recv,
):
    core, z, first, second, to_core, first_device, second_device, line, line_devices = places(
        planes
    )
    greet([to_core, first_device, second_device] + line_devices[1:])

    def piece(step, by_first, by_second, plane):
        x = (1 - plane) * by_second + plane * by_first
        y = (1 - plane) * by_first + plane * by_second
        return partial_ref.at[:, x, plane, y, pl.ds(pl.multiple_of(step * rows, rows), rows)]

    def core_copy(step, half, by_second, plane):
        return remote(
            piece(step, half, by_second, plane),
            from_core.at[step, half, by_second],
            core_sems.at[0, step, half, by_second],
            core_sems.at[1, step, half, by_second],
            to_core,
        )

    def load(step, half, by_second):
        return pltpu.make_async_copy(
            piece(step, half, by_second, core),
            own.at[step, half, by_second],
            load_sem.at[step, half, by_second],
        )

    def first_copy(step, half):
        return remote(
            own.at[step, half],
            from_first.at[step],
            first_sems.at[0, step],
            first_sems.at[1, step],
            first_device,
        )

    def second_copy(step, half):
        return remote(
            own.at[step, first, half],
            from_second.at[step],
            second_sems.at[0, step],
            second_sems.at[1, step],
            second_device,
        )

    def line_copy(step, at):
        return remote(
            own.at[step, first, second, line[at][0]],
            from_line.at[step, z],
            line_send.at[step, at],
            line_recv.at[step, z],
            line_devices[at],
        )

    def start_loads(step):
        for mine, theirs in ((1 - first, 1 - second), (first, second)):
            for by_second in range(2):
                core_copy(step, theirs, by_second, 1 - core).start()
                load(step, mine, by_second).start()

    def add_core(step):
        for turn, half in enumerate((1 - first, first)):
            for by_second in range(2):
                load(step, half, by_second).wait()
                core_copy(step, half, by_second, core).wait_recv()
                own[step, half, by_second] += from_core[step, half, by_second]
            if turn == 0:
                first_copy(step, half).start()

    def add_first(step):
        first_copy(step, 1 - first).wait_recv()
        own[step, first, 1 - second] += from_first[step, 1 - second]
        second_copy(step, 1 - second).start()
        own[step, first, second] += from_first[step, second]

    def add_second(step):
        second_copy(step, 1 - second).wait_recv()
        own[step, first, second] += from_second[step]
        for at in range(1, planes):
            line_copy(step, at).start()

    def add_line(step):
        total = own[step, first, second, z].astype(jnp.float32)
        for spot, at in line[1:]:
            remote(
                own.at[step, first, second, spot],
                from_line.at[step, spot],
                line_send.at[step, at],
                line_recv.at[step, spot],
                line_devices[at],
            ).wait_recv()
            total = total + from_line[step, spot].astype(jnp.float32)
        sum_ref[pl.ds(pl.multiple_of(step * rows, rows), rows), :] = total.astype(sum_ref.dtype)

    start_loads(0)
    start_loads(1)

    @pl.loop(0, steps + 3)
    def _(turn):
        @pl.when(turn < steps - 2)
        def _():
            start_loads(turn + 2)

        @pl.when(turn < steps)
        def _():
            add_core(turn)

        @pl.when((turn >= 1) & (turn < steps + 1))
        def _():
            add_first(turn - 1)

        @pl.when((turn >= 2) & (turn < steps + 2))
        def _():
            add_second(turn - 2)

        @pl.when(turn >= 3)
        def _():
            add_line(turn - 3)

    @pl.loop(0, steps)
    def _(step):
        for half in range(2):
            for by_second in range(2):
                core_copy(step, half, by_second, 1 - core).wait_send()
        first_copy(step, 1 - first).wait_send()
        second_copy(step, 1 - second).wait_send()
        for at in range(1, planes):
            line_copy(step, at).wait_send()


def scatter_by_axes(partial, planes, collective_id):
    shard_rows = partial.shape[0] // (8 * planes)
    width = partial.shape[1]
    rows = 16
    steps = shard_rows // rows
    dtype = partial.dtype
    dma = pltpu.SemaphoreType.DMA
    return pl.pallas_call(
        functools.partial(scatter_kernel, planes, steps, rows),
        out_shape=jax.ShapeDtypeStruct((shard_rows, width), dtype),
        in_specs=[pl.BlockSpec(memory_space=pl.ANY)],
        out_specs=pl.BlockSpec(memory_space=pltpu.VMEM),
        scratch_shapes=[
            pltpu.VMEM((steps, 2, 2, planes, rows, width), dtype),
            pltpu.VMEM((steps, 2, 2, planes, rows, width), dtype),
            pltpu.VMEM((steps, 2, planes, rows, width), dtype),
            pltpu.VMEM((steps, planes, rows, width), dtype),
            pltpu.VMEM((steps, planes, rows, width), dtype),
            dma((steps, 2, 2)),
            dma((2, steps, 2, 2)),
            dma((2, steps)),
            dma((2, steps)),
            dma((steps, planes)),
            dma((steps, planes)),
        ],
        compiler_params=pltpu.CompilerParams(
            collective_id=collective_id, has_side_effects=True, vmem_limit_bytes=48 * 2**20
        ),
        name="scatter_by_axes",
    )(partial.reshape(planes, 2, 2, 2, shard_rows, width))


def plane_places(planes):
    blk = lax.axis_index("blk")
    y = lax.axis_index("pair")
    core = lax.rem(blk, 2)
    x = lax.rem(lax.div(blk, 2), 2)
    z = lax.div(blk, 4)
    to_core = (blk + 1 - 2 * core, y)
    to_x = (blk + 2 - 4 * x, y)
    line = [(lax.rem(z + at, planes), at) for at in range(planes)]
    line_devices = [(blk + 4 * (spot - z), y) for spot, at in line]
    return core, x, z, to_core, to_x, line, line_devices


def plane_gather_kernel(planes, shard, whole, own_sem, line_send, x_send, core_send, recv, core_recv):
    core, x, z, to_core, to_x, line, line_devices = plane_places(planes)
    greet([to_core, to_x] + line_devices[1:])
    sent = []

    def send(source, target, send_sem, recv_sem, device):
        copy = remote(source, target, send_sem, recv_sem, device)
        copy.start()
        sent.append(copy)

    def arrive(target, recv_sem):
        remote(target, target, own_sem.at[0], recv_sem, to_core).wait_recv()

    own_copy = pltpu.make_async_copy(shard, whole.at[z, x, core], own_sem.at[0])
    own_copy.start()
    for spot, at in line[1:]:
        send(shard, whole.at[z, x, core], line_send.at[at], recv.at[z, x], line_devices[at])
    for spot, at in line:
        here = whole.at[spot, x, core]
        source = shard
        if at:
            arrive(here, recv.at[spot, x])
            source = here
        send(source, here, x_send.at[at], recv.at[spot, x], to_x)
        send(source, here, core_send.at[at, 0], core_recv.at[spot, x], to_core)
    for spot, at in line:
        there = whole.at[spot, 1 - x, core]
        arrive(there, recv.at[spot, 1 - x])
        send(there, there, core_send.at[at, 1], core_recv.at[spot, 1 - x], to_core)
    own_copy.wait()
    for spot in range(planes):
        for by_x in range(2):
            arrive(whole.at[spot, by_x, 1 - core], core_recv.at[spot, by_x])
    for copy in sent:
        copy.wait_send()


def gather_in_plane(shard, planes, collective_id):
    dma = pltpu.SemaphoreType.DMA
    whole = pl.pallas_call(
        functools.partial(plane_gather_kernel, planes),
        out_shape=jax.ShapeDtypeStruct((planes, 2, 2, *shard.shape), shard.dtype),
        in_specs=[pl.BlockSpec(memory_space=pl.ANY)],
        out_specs=pl.BlockSpec(memory_space=pl.ANY),
        scratch_shapes=[
            dma((1,)),
            dma((planes,)),
            dma((planes,)),
            dma((planes, 2)),
            dma((planes, 2)),
            dma((planes, 2)),
        ],
        compiler_params=pltpu.CompilerParams(collective_id=collective_id, has_side_effects=True),
        name="gather_in_plane",
    )(shard)
    return whole.reshape(4 * planes * shard.shape[0], shard.shape[1])


def plane_scatter_kernel(
    planes,
    steps,
    rows,
    partial_ref,
    sum_ref,
    own,
    from_core,
    from_x,
    from_line,
    load_sem,
    core_sems,
    x_sems,
    line_send,
    line_recv,
):
    core, x, z, to_core, to_x, line, line_devices = plane_places(planes)
    greet([to_core, to_x] + line_devices[1:])

    def piece(step, by_x, plane):
        return partial_ref.at[:, by_x, plane, pl.ds(pl.multiple_of(step * rows, rows), rows)]

    def core_copy(step, by_x, plane):
        return remote(
            piece(step, by_x, plane),
            from_core.at[step, by_x],
            core_sems.at[0, step, by_x],
            core_sems.at[1, step, by_x],
            to_core,
        )

    def load(step, by_x):
        return pltpu.make_async_copy(
            piece(step, by_x, core), own.at[step, by_x], load_sem.at[step, by_x]
        )

    def x_copy(step):
        return remote(
            own.at[step, 1 - x], from_x.at[step], x_sems.at[0, step], x_sems.at[1, step], to_x
        )

    def line_copy(step, at):
        return remote(
            own.at[step, x, line[at][0]],
            from_line.at[step, z],
            line_send.at[step, at],
            line_recv.at[step, z],
            line_devices[at],
        )

    def start_loads(step):
        for by_x in (1 - x, x):
            core_copy(step, by_x, 1 - core).start()
            load(step, by_x).start()

    def add_core(step):
        for turn, by_x in enumerate((1 - x, x)):
            load(step, by_x).wait()
            core_copy(step, by_x, core).wait_recv()
            own[step, by_x] += from_core[step, by_x]
            if turn == 0:
                x_copy(step).start()

    def add_x(step):
        x_copy(step).wait_recv()
        own[step, x] += from_x[step]
        for at in range(1, planes):
            line_copy(step, at).start()

    def add_line(step):
        total = own[step, x, z].astype(jnp.float32)
        for spot, at in line[1:]:
            remote(
                own.at[step, x, spot],
                from_line.at[step, spot],
                line_send.at[step, at],
                line_recv.at[step, spot],
                line_devices[at],
            ).wait_recv()
            total = total + from_line[step, spot].astype(jnp.float32)
        sum_ref[pl.ds(pl.multiple_of(step * rows, rows), rows), :] = total.astype(sum_ref.dtype)

    start_loads(0)
    start_loads(1)

    @pl.loop(0, steps + 2)
    def _(turn):
        @pl.when(turn < steps - 2)
        def _():
            start_loads(turn + 2)

        @pl.when(turn < steps)
        def _():
            add_core(turn)

        @pl.when((turn >= 1) & (turn < steps + 1))
        def _():
            add_x(turn - 1)

        @pl.when(turn >= 2)
        def _():
            add_line(turn - 2)

    @pl.loop(0, steps)
    def _(step):
        for by_x in range(2):
            core_copy(step, by_x, 1 - core).wait_send()
        x_copy(step).wait_send()
        for at in range(1, planes):
            line_copy(step, at).wait_send()


def scatter_in_plane(partial, planes, collective_id):
    shard_rows = partial.shape[0] // (4 * planes)
    width = partial.shape[1]
    rows = 16
    steps = shard_rows // rows
    dtype = partial.dtype
    dma = pltpu.SemaphoreType.DMA
    return pl.pallas_call(
        functools.partial(plane_scatter_kernel, planes, steps, rows),
        out_shape=jax.ShapeDtypeStruct((shard_rows, width), dtype),
        in_specs=[pl.BlockSpec(memory_space=pl.ANY)],
        out_specs=pl.BlockSpec(memory_space=pltpu.VMEM),
        scratch_shapes=[
            pltpu.VMEM((steps, 2, planes, rows, width), dtype),
            pltpu.VMEM((steps, 2, planes, rows, width), dtype),
            pltpu.VMEM((steps, planes, rows, width), dtype),
            pltpu.VMEM((steps, planes, rows, width), dtype),
            dma((steps, 2)),
            dma((2, steps, 2)),
            dma((2, steps)),
            dma((steps, planes)),
            dma((steps, planes)),
        ],
        compiler_params=pltpu.CompilerParams(
            collective_id=collective_id, has_side_effects=True, vmem_limit_bytes=40 * 2**20
        ),
        name="scatter_in_plane",
    )(partial.reshape(planes, 2, 2, shard_rows, width))


def flipped(block):
    return block.astype(jnp.float32).T.astype(jnp.bfloat16)


def unflipped(block):
    at = [lax.broadcasted_iota(jnp.int32, (HEAD, HEAD), axis) for axis in range(2)]
    identity = (at[0] == at[1]).astype(jnp.bfloat16)
    return lax.dot_general(
        identity, block, (((1,), (1,)), ((), ())), preferred_element_type=jnp.float32
    )


def ffn_pack_kernel(gateup_ref, down_ref, packet_ref):
    live = pl.program_id(0) < FF // HEAD

    @pl.when(live)
    def _():
        packet_ref[0, :, :HEAD] = gateup_ref[0].astype(jnp.bfloat16)
        packet_ref[0, :, HEAD : 2 * HEAD] = gateup_ref[1].astype(jnp.bfloat16)
        packet_ref[0, :, 2 * HEAD :] = flipped(down_ref[...])

    @pl.when(jnp.logical_not(live))
    def _():
        packet_ref[...] = jnp.zeros_like(packet_ref)


def ffn_packets(gateup, down, device_count):
    row_count = gateup.shape[1]
    last = FF // HEAD - 1
    return pl.pallas_call(
        ffn_pack_kernel,
        grid=(device_count,),
        in_specs=[
            pl.BlockSpec((2, row_count, HEAD), lambda j: (0, 0, jnp.minimum(j, last))),
            pl.BlockSpec((HEAD, row_count), lambda j: (jnp.minimum(j, last), 0)),
        ],
        out_specs=pl.BlockSpec((1, row_count, 3 * HEAD), lambda j: (j, 0, 0)),
        out_shape=jax.ShapeDtypeStruct((device_count, row_count, 3 * HEAD), jnp.bfloat16),
        cost_estimate=pl.CostEstimate(flops=0, bytes_accessed=14 * 2**20, transcendentals=0),
        name="ffn_packets",
    )(gateup, down)


def attn_pack_kernel(qkv_ref, out_ref, packet_ref):
    j = pl.program_id(0)

    @pl.when(j < H + 2)
    def _():
        packet_ref[0] = qkv_ref[...].astype(jnp.bfloat16)

    @pl.when((j >= H + 2) & (j < 2 * H + 2))
    def _():
        packet_ref[0] = flipped(out_ref[...])

    @pl.when(j >= 2 * H + 2)
    def _():
        packet_ref[...] = jnp.zeros_like(packet_ref)


def attn_packets(qkv, out, device_count):
    row_count = qkv.shape[0]
    return pl.pallas_call(
        attn_pack_kernel,
        grid=(device_count,),
        in_specs=[
            pl.BlockSpec((row_count, HEAD), lambda j: (0, jnp.minimum(j, H + 1))),
            pl.BlockSpec((HEAD, row_count), lambda j: (jnp.clip(j - H - 2, 0, H - 1), 0)),
        ],
        out_specs=pl.BlockSpec((1, row_count, HEAD), lambda j: (j, 0, 0)),
        out_shape=jax.ShapeDtypeStruct((device_count, row_count, HEAD), jnp.bfloat16),
        cost_estimate=pl.CostEstimate(flops=0, bytes_accessed=4 * 2**20, transcendentals=0),
        name="attn_packets",
    )(qkv, out)


def turn_kernel(grads_ref, others_ref, mom_ref, turned_ref, low_ref, current_ref):
    grads = grads_ref[...] + others_ref[...].astype(jnp.float32)
    low_ref[...] = grads.astype(jnp.bfloat16)
    moment = momentum_decay * mom_ref[...].astype(jnp.float32) + grads
    moment = moment.astype(jnp.bfloat16).astype(jnp.float32)
    norm_size = jnp.sqrt(jnp.sum(moment * moment, keepdims=True))
    current_ref[...] = (moment / (norm_size + eps_pieces)).T.astype(jnp.bfloat16)

    @pl.loop(0, NS_STEPS)
    def _(sweep_index):
        current = current_ref[...]
        gram_matrix = lax.dot_general(
            current, current, (((1,), (1,)), ((), ())), preferred_element_type=jnp.float32
        ).astype(jnp.bfloat16)
        square = jnp.dot(gram_matrix, gram_matrix, preferred_element_type=jnp.float32)
        mixing = (ns_second * gram_matrix.astype(jnp.float32) + ns_third * square).astype(
            jnp.bfloat16
        )
        turned = jnp.dot(mixing, current, preferred_element_type=jnp.float32)
        current_ref[...] = (ns_first * current.astype(jnp.float32) + turned).astype(jnp.bfloat16)

    turned_ref[...] = current_ref[...].astype(jnp.float32).T.astype(jnp.bfloat16)


def orthogonalize(grads, others, moms):
    depth, columns = grads.shape
    block = pl.BlockSpec((depth, HEAD), lambda j: (0, j))
    low = jax.ShapeDtypeStruct((depth, columns), jnp.bfloat16)
    pieces = columns // HEAD
    return pl.pallas_call(
        turn_kernel,
        grid=(pieces,),
        in_specs=[block] * 3,
        out_specs=[block] * 2,
        out_shape=[low, low],
        scratch_shapes=[pltpu.VMEM((HEAD, depth), jnp.bfloat16)],
        cost_estimate=pl.CostEstimate(
            flops=pieces * 20 * depth * HEAD * HEAD, bytes_accessed=12 * depth * columns, transcendentals=0
        ),
        compiler_params=pltpu.CompilerParams(vmem_limit_bytes=48 * 2**20),
        name="orthogonalize",
    )(grads, others, moms)


def update(rate, weight, mom, grad, turn):
    moment = momentum_decay * mom + grad
    new = (1.0 - weight_shrink) * weight - rate * turn
    return new, moment, new.astype(jnp.bfloat16)


def ffn_update_kernel(
    grad_ref, turn_ref, w_gateup_ref, mom_gateup_ref, w_down_ref, mom_down_ref, *results
):
    gateup_refs, down_refs = results[:3], results[3:]
    for part in range(2):
        columns = slice(part * HEAD, (part + 1) * HEAD)
        values = update(
            matrix_rate,
            w_gateup_ref[part],
            mom_gateup_ref[part],
            grad_ref[0, :, columns].astype(jnp.float32),
            turn_ref[0, :, columns].astype(jnp.float32),
        )
        for ref, value in zip(gateup_refs, values):
            ref[part] = value
    values = update(
        matrix_rate,
        w_down_ref[...],
        mom_down_ref[...],
        unflipped(grad_ref[0, :, 2 * HEAD :]),
        unflipped(turn_ref[0, :, 2 * HEAD :]),
    )
    for ref, value in zip(down_refs, values):
        ref[...] = value


def ffn_update(grads, turns, w_gateup, mom_gateup, w_down, mom_down):
    row_count = w_gateup.shape[1]
    packet = pl.BlockSpec((1, row_count, 3 * HEAD), lambda j: (j, 0, 0))
    gateup = pl.BlockSpec((2, row_count, HEAD), lambda j: (0, 0, j))
    down = pl.BlockSpec((HEAD, row_count), lambda j: (j, 0))
    dtypes = (jnp.float32, jnp.float32, jnp.bfloat16)
    return pl.pallas_call(
        ffn_update_kernel,
        grid=(FF // HEAD,),
        in_specs=[packet, packet, gateup, gateup, down, down],
        out_specs=[gateup] * 3 + [down] * 3,
        out_shape=[jax.ShapeDtypeStruct(w_gateup.shape, dtype) for dtype in dtypes]
        + [jax.ShapeDtypeStruct(w_down.shape, dtype) for dtype in dtypes],
        cost_estimate=pl.CostEstimate(flops=0, bytes_accessed=50 * 2**20, transcendentals=0),
        name="ffn_update",
    )(grads, turns, w_gateup, mom_gateup, w_down, mom_down)


def attn_update_kernel(rate, transposed, grad_ref, turn_ref, w_ref, mom_ref, *results):
    if transposed:
        grad, turn = unflipped(grad_ref[0]), unflipped(turn_ref[0])
    else:
        grad, turn = grad_ref[0].astype(jnp.float32), turn_ref[0].astype(jnp.float32)
    for ref, value in zip(results, update(rate, w_ref[...], mom_ref[...], grad, turn)):
        ref[...] = value


def attn_update(rate, transposed, offset, grads, turns, weight, mom):
    row_count = grads.shape[1]
    packet = pl.BlockSpec((1, row_count, HEAD), lambda j: (j + offset, 0, 0))
    if transposed:
        block = pl.BlockSpec((HEAD, row_count), lambda j: (j, 0))
        count = weight.shape[0] // HEAD
    else:
        block = pl.BlockSpec((row_count, HEAD), lambda j: (0, j))
        count = weight.shape[1] // HEAD
    return pl.pallas_call(
        functools.partial(attn_update_kernel, rate, transposed),
        grid=(count,),
        in_specs=[packet, packet, block, block],
        out_specs=[block] * 3,
        out_shape=[
            jax.ShapeDtypeStruct(weight.shape, dtype)
            for dtype in (jnp.float32, jnp.float32, jnp.bfloat16)
        ],
        cost_estimate=pl.CostEstimate(flops=0, bytes_accessed=6 * 2**20, transcendentals=0),
        name="attn_update",
    )(grads, turns, weight, mom)


def rms_scale(stream, gain_row):
    mean_square = jnp.mean(stream * stream, axis=-1, keepdims=True)
    return stream * lax.rsqrt(mean_square + eps_norm) * gain_row


def gelu_product(gate_part, up_part):
    return jax.nn.gelu(gate_part, approximate=True) * up_part


def on_device(
    tokens_in,
    cotangent,
    w_qkv,
    w_out,
    w_gateup,
    w_down,
    gains,
    mom_qkv,
    mom_out,
    mom_gateup,
    mom_down,
    mom_gains,
):
    everyone = ("blk", "pair")
    bf16 = jnp.bfloat16
    f32 = jnp.float32
    blk_count = lax.axis_size("blk")
    pair_count = lax.axis_size("pair")
    device_count = blk_count * pair_count
    block_at = lax.axis_index("blk")
    half_at = lax.axis_index("pair")
    me = block_at * pair_count + half_at
    local_rows, width = tokens_in.shape
    share_rows = w_qkv.shape[0]
    score_scale = HEAD ** (-0.5)
    span = WINDOW + local_rows
    token_count = local_rows * device_count
    large = token_count * width * 2 > 48 * 2**20
    planes = blk_count // 4

    def after(value, earlier):
        return lax.optimization_barrier((value, earlier))[0] if large else value

    def exchange(packets, axes=everyone):
        return lax.all_to_all(packets, axes, split_axis=0, concat_axis=0, tiled=True)

    def swap(shard):
        return lax.ppermute(shard, "pair", [(0, 1), (1, 0)])

    def gather_all(shards, collective_id):
        if large:
            return [lax.all_gather(shard, everyone, axis=0, tiled=True) for shard in shards]
        return gather_by_axes(shards, planes, collective_id)

    def scatter_all(partial, collective_id):
        if large:
            return lax.psum_scatter(partial, everyone, scatter_dimension=0, tiled=True)
        return scatter_by_axes(partial, planes, collective_id)

    def gather_plane(shard):
        return lax.all_gather(shard, "blk", axis=0, tiled=True)

    def scatter_plane(partial, collective_id):
        if large:
            return lax.psum_scatter(partial, "blk", scatter_dimension=0, tiled=True)
        return scatter_in_plane(partial, planes, collective_id)

    stream = tokens_in.astype(f32)
    padded_gains = jnp.pad(gains.astype(bf16), ((0, 14), (0, 128 - share_rows)))
    ffn_weights = exchange(ffn_packets(w_gateup, w_down, device_count)).reshape(width, 3 * HEAD)
    full_qkv, full_gains = gather_all([w_qkv.astype(bf16), padded_gains], 1)
    full_gains = full_gains.reshape(device_count, 16, 128)[:, :2, :share_rows].astype(f32)
    gain_attn = full_gains[:, 0].reshape(width)
    gain_mlp = full_gains[:, 1].reshape(width)
    normed_attn_f, norm_back_attn = jax.vjp(rms_scale, stream, gain_attn)
    normed_attn = normed_attn_f.astype(bf16)
    qkv = jnp.dot(normed_attn, full_qkv, preferred_element_type=f32).astype(bf16)
    queries = qkv[:, : H * HEAD].reshape(local_rows, H, HEAD)
    (kv_all,) = gather_all([qkv[:, H * HEAD :]], 2)
    kv_window = lax.dynamic_slice_in_dim(
        jnp.pad(kv_all, ((WINDOW, 0), (0, 0))), me * local_rows, span, 0
    )
    keys = kv_window[:, :HEAD]
    values = kv_window[:, HEAD:]
    full_out = lax.all_gather(w_out.astype(bf16).T, everyone, axis=0, tiled=True)
    pair_weights = lax.all_gather(ffn_weights, "pair", axis=0, tiled=False)
    own_gate, own_up, own_down = (
        [pair_weights[at, :, part * HEAD : (part + 1) * HEAD] for at in range(pair_count)]
        for part in range(3)
    )
    own_gateup = jnp.concatenate(own_gate + own_up, axis=1)
    own_down = jnp.concatenate(own_down, axis=1)
    cotangent_plane = gather_plane(cotangent)

    key_index = jnp.arange(span, dtype=jnp.int32)[None, :]
    distance = jnp.arange(local_rows, dtype=jnp.int32)[:, None] + WINDOW - key_index
    allowed = (
        (distance >= 0) & (distance < WINDOW) & (me * local_rows - WINDOW + key_index >= 0)
    )
    raw = jnp.einsum("qhd,kd->hqk", queries, keys, preferred_element_type=f32)
    scores = jnp.where(allowed[None], raw * score_scale, masked_score)
    top_score = jnp.max(scores, axis=-1, keepdims=True)
    expo = jnp.exp(scores - top_score)
    probs = expo / jnp.sum(expo, axis=-1, keepdims=True)
    probs_low = probs.astype(bf16)
    mixed = jnp.einsum("hqk,kd->qhd", probs_low, values, preferred_element_type=f32)
    mixed = mixed.reshape(local_rows, H * HEAD).astype(bf16)
    resid = stream + jnp.einsum("tc,dc->td", mixed, full_out, preferred_element_type=f32)

    normed_mlp_f, norm_back_mlp = jax.vjp(rms_scale, resid, gain_mlp)
    normed_mlp = normed_mlp_f.astype(bf16)
    if large:
        normed_mlp_plane = gather_plane(normed_mlp)
    else:
        normed_mlp_plane = gather_in_plane(normed_mlp, planes, 3)
    plane_rows = blk_count * local_rows
    both_parts = jnp.dot(normed_mlp_plane, own_gateup, preferred_element_type=f32)
    pair_width = pair_count * HEAD
    hidden_f, geglu_back = jax.vjp(
        gelu_product, both_parts[:, :pair_width], both_parts[:, pair_width:]
    )
    hidden = hidden_f.astype(bf16)
    grad_hidden = jnp.dot(cotangent_plane, own_down, preferred_element_type=f32)
    grad_gate, grad_up = geglu_back(grad_hidden)
    grad_gateup = jnp.concatenate([grad_gate.astype(bf16), grad_up.astype(bf16)], axis=1)
    grad_normed_mlp = scatter_plane(
        jnp.einsum("tf,df->td", grad_gateup, own_gateup, preferred_element_type=f32).astype(bf16), 4
    ).astype(f32)
    resid_part, gain_grad_mlp = norm_back_mlp(grad_normed_mlp)
    grad_resid = cotangent.astype(f32) + resid_part
    grad_proj = grad_resid.astype(bf16)
    branch_part = jnp.einsum(
        "tf,df->td", after(hidden, grad_normed_mlp), own_down, preferred_element_type=f32
    )
    branch = scatter_plane(branch_part.astype(bf16), 4).astype(f32)
    block_output = (resid + branch).astype(bf16)

    def ffn_gradient(owner):
        gate_right, up_right, down_right = (
            lax.dynamic_slice_in_dim(right, owner * HEAD, HEAD, 1)
            for right in (grad_gateup[:, :pair_width], grad_gateup[:, pair_width:], hidden)
        )
        gateup_right = jnp.concatenate([gate_right, up_right], axis=1)
        return jnp.concatenate(
            [
                jnp.einsum("td,tf->df", normed_mlp_plane, gateup_right, preferred_element_type=f32),
                jnp.einsum("td,tf->df", cotangent_plane, down_right, preferred_element_type=f32),
            ],
            axis=1,
        )

    ffn_others = swap(ffn_gradient(1 - half_at).astype(bf16))
    ffn_grads = ffn_gradient(half_at)
    ffn_moms = exchange(ffn_packets(mom_gateup, mom_down, device_count)).reshape(width, 3 * HEAD)
    ffn_turned, ffn_low = orthogonalize(ffn_grads, ffn_others, ffn_moms)
    ffn_shape = (device_count, share_rows, 3 * HEAD)
    ffn_low = exchange(ffn_low.reshape(ffn_shape))
    ffn_turned = exchange(ffn_turned.reshape(ffn_shape))

    grad_mixed = jnp.dot(grad_proj, full_out, preferred_element_type=f32).astype(bf16)
    grad_mixed = grad_mixed.reshape(local_rows, H, HEAD)
    grad_probs = jnp.einsum("qhd,kd->hqk", grad_mixed, values, preferred_element_type=f32)
    row_delta = jnp.sum(probs * grad_probs, axis=-1, keepdims=True)
    grad_raw = (probs * (grad_probs - row_delta) * score_scale).astype(bf16)
    grad_query = jnp.einsum("hqk,kd->qhd", grad_raw, keys, preferred_element_type=f32)
    grad_keys = jnp.einsum("hqk,qhd->kd", grad_raw, queries, preferred_element_type=f32)
    grad_values = jnp.einsum("hqk,qhd->kd", probs_low, grad_mixed, preferred_element_type=f32)
    grad_kv = jnp.concatenate([grad_keys, grad_values], axis=1).astype(bf16)
    grad_kv_all = lax.dynamic_update_slice_in_dim(
        jnp.zeros((WINDOW + token_count, 2 * HEAD), bf16), grad_kv, me * local_rows, 0
    )[WINDOW:]
    grad_qkv = jnp.concatenate(
        [grad_query.reshape(local_rows, H * HEAD).astype(bf16), scatter_all(grad_kv_all, 5)], axis=1
    )
    grad_normed_attn = jnp.einsum("tc,dc->td", grad_qkv, full_qkv, preferred_element_type=f32)
    stream_part, gain_grad_attn = norm_back_attn(grad_normed_attn)
    input_grad = grad_resid + stream_part

    attn_rights = jnp.concatenate([grad_qkv, mixed], axis=1)
    used = attn_rights.shape[1] // pair_width
    attn_rights = attn_rights.reshape(local_rows, used, pair_width).transpose(1, 0, 2)
    attn_rights = exchange(jnp.pad(attn_rights, ((0, blk_count - used), (0, 0), (0, 0))), "blk")
    attn_rights = attn_rights.reshape(plane_rows, pair_width)
    normed_attn_plane = gather_plane(after(normed_attn, (ffn_grads, block_output)))
    grad_proj_plane = gather_plane(after(grad_proj, (ffn_grads, block_output)))

    def attn_gradient(lefts):
        return jnp.einsum("td,tf->df", lefts, attn_rights, preferred_element_type=f32)

    attn_grads = lax.cond(
        block_at < (H + 2) // pair_count,
        lambda: attn_gradient(normed_attn_plane),
        lambda: attn_gradient(grad_proj_plane),
    )
    attn_others = swap(
        lax.dynamic_slice_in_dim(attn_grads, (1 - half_at) * HEAD, HEAD, 1).astype(bf16)
    )
    attn_grads = lax.dynamic_slice_in_dim(attn_grads, half_at * HEAD, HEAD, 1)
    attn_moms = exchange(attn_packets(mom_qkv, mom_out, device_count)).reshape(width, HEAD)
    attn_turned, attn_low = orthogonalize(attn_grads, attn_others, attn_moms)
    attn_shape = (device_count, share_rows, HEAD)
    attn_low = exchange(attn_low.reshape(attn_shape))
    attn_turned = exchange(attn_turned.reshape(attn_shape))

    gain_grads = jnp.stack([gain_grad_attn, gain_grad_mlp], axis=0)
    gain_grads = gain_grads.reshape(2, device_count, share_rows).transpose(1, 0, 2)
    gain_share = jnp.sum(exchange(gain_grads), axis=0)

    updated_ffn = ffn_update(ffn_low, ffn_turned, w_gateup, mom_gateup, w_down, mom_down)
    updated_qkv = attn_update(matrix_rate, False, 0, attn_low, attn_turned, w_qkv, mom_qkv)
    updated_out = attn_update(output_rate, True, H + 2, attn_low, attn_turned, w_out, mom_out)
    moment_gains = momentum_decay * mom_gains + gain_share
    new_gains = gains - gain_rate * moment_gains
    return (
        block_output,
        input_grad,
        *updated_qkv,
        *updated_out,
        *updated_ffn,
        new_gains,
        moment_gains,
        new_gains.astype(bf16),
    )


def solution(mesh):
    placed = (
        P(("blk", "pair"), None),
        P(("blk", "pair"), None),
        P(("blk", "pair"), None),
        P(None, ("blk", "pair")),
        P(None, ("blk", "pair"), None),
        P(None, ("blk", "pair")),
        P(None, ("blk", "pair")),
        P(("blk", "pair"), None),
        P(None, ("blk", "pair")),
        P(None, ("blk", "pair"), None),
        P(None, ("blk", "pair")),
        P(None, ("blk", "pair")),
    )
    return jax.shard_map(
        on_device,
        mesh=mesh,
        in_specs=placed,
        out_specs=(
            P(("blk", "pair"), None),
            P(("blk", "pair"), None),
            P(("blk", "pair"), None),
            P(("blk", "pair"), None),
            P(("blk", "pair"), None),
            P(None, ("blk", "pair")),
            P(None, ("blk", "pair")),
            P(None, ("blk", "pair")),
            P(None, ("blk", "pair"), None),
            P(None, ("blk", "pair"), None),
            P(None, ("blk", "pair"), None),
            P(None, ("blk", "pair")),
            P(None, ("blk", "pair")),
            P(None, ("blk", "pair")),
            P(None, ("blk", "pair")),
            P(None, ("blk", "pair")),
            P(None, ("blk", "pair")),
        ),
        check_vma=False,
    )
```

```python
import functools

import jax
import jax.numpy as jnp
from jax import lax
from jax.experimental import pallas as pl
from jax.experimental.pallas import tpu as pltpu
from jax.sharding import PartitionSpec as P

H = 10
HEAD = 256
FF = 7680
WINDOW = 2048
NS_STEPS = 5


eps_norm = 1e-06
eps_pieces = 1e-07
ns_first = 3.4445
ns_second = -4.775
ns_third = 2.0315
momentum_decay = 0.95
matrix_rate = 0.5
output_rate = 10.0
gain_rate = 0.001
weight_shrink = 0.001
masked_score = -1e30
MESH = pl.DeviceIdType.MESH


def places(planes):
    blk = lax.axis_index("blk")
    y = lax.axis_index("pair")
    core = lax.rem(blk, 2)
    x = lax.rem(lax.div(blk, 2), 2)
    z = lax.div(blk, 4)
    first = y * (1 - core) + x * core
    second = x * (1 - core) + y * core
    to_core = (blk + 1 - 2 * core, y)
    first_device = (blk + core * (2 - 4 * x), y + (1 - core) * (1 - 2 * y))
    second_device = (blk + (1 - core) * (2 - 4 * x), y + core * (1 - 2 * y))
    line = [(lax.rem(z + at, planes), at) for at in range(planes)]
    line_devices = [((blk + 4 * (spot - z)), y) for spot, at in line]
    return core, z, first, second, to_core, first_device, second_device, line, line_devices


def greet(devices):
    barrier = pltpu.get_barrier_semaphore()
    for device in devices:
        pl.semaphore_signal(barrier, inc=1, device_id=device, device_id_type=MESH)
    pl.semaphore_wait(barrier, len(devices))


def remote(source, target, send_sem, recv_sem, device):
    return pltpu.make_async_remote_copy(
        src_ref=source,
        dst_ref=target,
        send_sem=send_sem,
        recv_sem=recv_sem,
        device_id=device,
        device_id_type=MESH,
    )


def gather_kernel(planes, count, exchanged, *refs):
    inputs, refs = refs[: count + exchanged], refs[count + exchanged :]
    outputs, refs = refs[: count + exchanged], refs[count + exchanged :]
    shards, wholes = inputs[:count], outputs[:count]
    own_sem, line_send, second_send, first_send, core_send, recv, core_recv = refs[:7]
    core, z, first, second, to_core, first_device, second_device, line, line_devices = places(
        planes
    )
    device_count = 8 * planes
    me = lax.axis_index("blk") * 2 + lax.axis_index("pair")
    others = [lax.rem(me + at, device_count) for at in range(1, device_count)]
    others = [(other, (lax.div(other, 2), lax.rem(other, 2))) for other in others]
    if exchanged:
        greet([device for _, device in others])
    else:
        greet([to_core, first_device, second_device] + line_devices[1:])

    def slot(whole, spot, by_first, by_second):
        x = (1 - core) * by_second + core * by_first
        y = (1 - core) * by_first + core * by_second
        return whole.at[spot, x, core, y]

    def core_slot(whole, spot, by_first, by_second):
        x = core * by_second + (1 - core) * by_first
        y = core * by_first + (1 - core) * by_second
        return whole.at[spot, x, 1 - core, y]

    sent = []

    def send(source, target, send_sem, recv_sem, device):
        copy = remote(source, target, send_sem, recv_sem, device)
        copy.start()
        sent.append(copy)

    def arrive(target, recv_sem):
        remote(target, target, own_sem.at[0], recv_sem, to_core).wait_recv()

    own_copies = []
    for i, (shard, whole) in enumerate(zip(shards, wholes)):
        here = slot(whole, z, first, second)
        copy = pltpu.make_async_copy(shard, here, own_sem.at[i])
        copy.start()
        own_copies.append(copy)
        for spot, at in line[1:]:
            send(shard, here, line_send.at[i, at], recv.at[i, z, first, second], line_devices[at])
    if exchanged:
        packets, received = inputs[count], outputs[count]
        swap_own, swap_send, swap_recv = refs[7:]
        copy = pltpu.make_async_copy(packets.at[me], received.at[me], swap_own.at[0])
        copy.start()
        own_copies.append(copy)
        for at, (other, device) in enumerate(others):
            send(packets.at[other], received.at[me], swap_send.at[at], swap_recv.at[me], device)
    for spot, at in line:
        for i, (shard, whole) in enumerate(zip(shards, wholes)):
            here = slot(whole, spot, first, second)
            source = shard
            if at:
                arrive(here, recv.at[i, spot, first, second])
                source = here
            for devices, sends in ((second_device, second_send.at[i, at]), (first_device, first_send.at[i, at, 0])):
                send(source, here, sends, recv.at[i, spot, first, second], devices)
            send(source, here, core_send.at[i, at, 0, 0], core_recv.at[i, spot, first, second], to_core)
        for i, whole in enumerate(wholes):
            here = slot(whole, spot, first, 1 - second)
            arrive(here, recv.at[i, spot, first, 1 - second])
            send(here, here, first_send.at[i, at, 1], recv.at[i, spot, first, 1 - second], first_device)
            send(here, here, core_send.at[i, at, 0, 1], core_recv.at[i, spot, first, 1 - second], to_core)
    for spot, at in line:
        for turn, by_second in enumerate((second, 1 - second)):
            for i, whole in enumerate(wholes):
                here = slot(whole, spot, 1 - first, by_second)
                arrive(here, recv.at[i, spot, 1 - first, by_second])
                send(here, here, core_send.at[i, at, 1, turn], core_recv.at[i, spot, 1 - first, by_second], to_core)
    for copy in own_copies:
        copy.wait()
    for i, whole in enumerate(wholes):
        for spot in range(planes):
            for by_first in range(2):
                for by_second in range(2):
                    arrive(
                        core_slot(whole, spot, by_first, by_second),
                        core_recv.at[i, spot, by_first, by_second],
                    )
    if exchanged:
        for other, _ in others:
            arrive(received.at[other], swap_recv.at[other])
    for copy in sent:
        copy.wait_send()


def gather_by_axes(shards, planes, collective_id, packets=()):
    count = len(shards)
    exchanged = len(packets)
    operands = [*shards, *packets]
    any_spec = pl.BlockSpec(memory_space=pl.ANY)
    dma = pltpu.SemaphoreType.DMA
    wholes = pl.pallas_call(
        functools.partial(gather_kernel, planes, count, exchanged),
        out_shape=[
            jax.ShapeDtypeStruct((planes, 2, 2, 2, *shard.shape), shard.dtype) for shard in shards
        ]
        + [jax.ShapeDtypeStruct(array.shape, array.dtype) for array in packets],
        in_specs=[any_spec] * len(operands),
        out_specs=[any_spec] * len(operands),
        scratch_shapes=[
            dma((count,)),
            dma((count, planes)),
            dma((count, planes)),
            dma((count, planes, 2)),
            dma((count, planes, 2, 2)),
            dma((count, planes, 2, 2)),
            dma((count, planes, 2, 2)),
        ]
        + [dma((1,)), dma((8 * planes,)), dma((8 * planes,))] * exchanged,
        compiler_params=pltpu.CompilerParams(collective_id=collective_id, has_side_effects=True),
        name="gather_by_axes",
    )(*operands)
    return [
        whole.reshape(8 * planes * shard.shape[0], shard.shape[1])
        for whole, shard in zip(wholes, shards)
    ] + list(wholes[count:])


def scatter_kernel(
    planes,
    steps,
    rows,
    partial_ref,
    sum_ref,
    own,
    from_core,
    from_first,
    from_second,
    from_line,
    load_sem,
    core_sems,
    first_sems,
    second_sems,
    line_send,
    line_recv,
):
    core, z, first, second, to_core, first_device, second_device, line, line_devices = places(
        planes
    )
    greet([to_core, first_device, second_device] + line_devices[1:])

    def piece(step, by_first, by_second, plane):
        x = (1 - plane) * by_second + plane * by_first
        y = (1 - plane) * by_first + plane * by_second
        return partial_ref.at[:, x, plane, y, pl.ds(pl.multiple_of(step * rows, rows), rows)]

    def core_copy(step, half, by_second, plane):
        return remote(
            piece(step, half, by_second, plane),
            from_core.at[step, half, by_second],
            core_sems.at[0, step, half, by_second],
            core_sems.at[1, step, half, by_second],
            to_core,
        )

    def load(step, half, by_second):
        return pltpu.make_async_copy(
            piece(step, half, by_second, core),
            own.at[step, half, by_second],
            load_sem.at[step, half, by_second],
        )

    def first_copy(step, half):
        return remote(
            own.at[step, half],
            from_first.at[step],
            first_sems.at[0, step],
            first_sems.at[1, step],
            first_device,
        )

    def second_copy(step, half):
        return remote(
            own.at[step, first, half],
            from_second.at[step],
            second_sems.at[0, step],
            second_sems.at[1, step],
            second_device,
        )

    def line_copy(step, at):
        return remote(
            own.at[step, first, second, line[at][0]],
            from_line.at[step, z],
            line_send.at[step, at],
            line_recv.at[step, z],
            line_devices[at],
        )

    def start_loads(step):
        for mine, theirs in ((1 - first, 1 - second), (first, second)):
            for by_second in range(2):
                core_copy(step, theirs, by_second, 1 - core).start()
                load(step, mine, by_second).start()

    def add_core(step):
        for turn, half in enumerate((1 - first, first)):
            for by_second in range(2):
                load(step, half, by_second).wait()
                core_copy(step, half, by_second, core).wait_recv()
                own[step, half, by_second] += from_core[step, half, by_second]
            if turn == 0:
                first_copy(step, half).start()

    def add_first(step):
        first_copy(step, 1 - first).wait_recv()
        own[step, first, 1 - second] += from_first[step, 1 - second]
        second_copy(step, 1 - second).start()
        own[step, first, second] += from_first[step, second]

    def add_second(step):
        second_copy(step, 1 - second).wait_recv()
        own[step, first, second] += from_second[step]
        for at in range(1, planes):
            line_copy(step, at).start()

    def add_line(step):
        total = own[step, first, second, z].astype(jnp.float32)
        for spot, at in line[1:]:
            remote(
                own.at[step, first, second, spot],
                from_line.at[step, spot],
                line_send.at[step, at],
                line_recv.at[step, spot],
                line_devices[at],
            ).wait_recv()
            total = total + from_line[step, spot].astype(jnp.float32)
        sum_ref[pl.ds(pl.multiple_of(step * rows, rows), rows), :] = total.astype(sum_ref.dtype)

    start_loads(0)
    start_loads(1)

    @pl.loop(0, steps + 3)
    def _(turn):
        @pl.when(turn < steps - 2)
        def _():
            start_loads(turn + 2)

        @pl.when(turn < steps)
        def _():
            add_core(turn)

        @pl.when((turn >= 1) & (turn < steps + 1))
        def _():
            add_first(turn - 1)

        @pl.when((turn >= 2) & (turn < steps + 2))
        def _():
            add_second(turn - 2)

        @pl.when(turn >= 3)
        def _():
            add_line(turn - 3)

    @pl.loop(0, steps)
    def _(step):
        for half in range(2):
            for by_second in range(2):
                core_copy(step, half, by_second, 1 - core).wait_send()
        first_copy(step, 1 - first).wait_send()
        second_copy(step, 1 - second).wait_send()
        for at in range(1, planes):
            line_copy(step, at).wait_send()


def scatter_by_axes(partial, planes, collective_id):
    shard_rows = partial.shape[0] // (8 * planes)
    width = partial.shape[1]
    rows = 16
    steps = shard_rows // rows
    dtype = partial.dtype
    dma = pltpu.SemaphoreType.DMA
    return pl.pallas_call(
        functools.partial(scatter_kernel, planes, steps, rows),
        out_shape=jax.ShapeDtypeStruct((shard_rows, width), dtype),
        in_specs=[pl.BlockSpec(memory_space=pl.ANY)],
        out_specs=pl.BlockSpec(memory_space=pltpu.VMEM),
        scratch_shapes=[
            pltpu.VMEM((steps, 2, 2, planes, rows, width), dtype),
            pltpu.VMEM((steps, 2, 2, planes, rows, width), dtype),
            pltpu.VMEM((steps, 2, planes, rows, width), dtype),
            pltpu.VMEM((steps, planes, rows, width), dtype),
            pltpu.VMEM((steps, planes, rows, width), dtype),
            dma((steps, 2, 2)),
            dma((2, steps, 2, 2)),
            dma((2, steps)),
            dma((2, steps)),
            dma((steps, planes)),
            dma((steps, planes)),
        ],
        compiler_params=pltpu.CompilerParams(
            collective_id=collective_id, has_side_effects=True, vmem_limit_bytes=48 * 2**20
        ),
        name="scatter_by_axes",
    )(partial.reshape(planes, 2, 2, 2, shard_rows, width))


def plane_places(planes):
    blk = lax.axis_index("blk")
    y = lax.axis_index("pair")
    core = lax.rem(blk, 2)
    x = lax.rem(lax.div(blk, 2), 2)
    z = lax.div(blk, 4)
    to_core = (blk + 1 - 2 * core, y)
    to_x = (blk + 2 - 4 * x, y)
    line = [(lax.rem(z + at, planes), at) for at in range(planes)]
    line_devices = [(blk + 4 * (spot - z), y) for spot, at in line]
    return core, x, z, to_core, to_x, line, line_devices


def plane_gather_kernel(planes, shard, whole, own_sem, line_send, x_send, core_send, recv, core_recv):
    core, x, z, to_core, to_x, line, line_devices = plane_places(planes)
    greet([to_core, to_x] + line_devices[1:])
    sent = []

    def send(source, target, send_sem, recv_sem, device):
        copy = remote(source, target, send_sem, recv_sem, device)
        copy.start()
        sent.append(copy)

    def arrive(target, recv_sem):
        remote(target, target, own_sem.at[0], recv_sem, to_core).wait_recv()

    own_copy = pltpu.make_async_copy(shard, whole.at[z, x, core], own_sem.at[0])
    own_copy.start()
    for spot, at in line[1:]:
        send(shard, whole.at[z, x, core], line_send.at[at], recv.at[z, x], line_devices[at])
    for spot, at in line:
        here = whole.at[spot, x, core]
        source = shard
        if at:
            arrive(here, recv.at[spot, x])
            source = here
        send(source, here, x_send.at[at], recv.at[spot, x], to_x)
        send(source, here, core_send.at[at, 0], core_recv.at[spot, x], to_core)
    for spot, at in line:
        there = whole.at[spot, 1 - x, core]
        arrive(there, recv.at[spot, 1 - x])
        send(there, there, core_send.at[at, 1], core_recv.at[spot, 1 - x], to_core)
    own_copy.wait()
    for spot in range(planes):
        for by_x in range(2):
            arrive(whole.at[spot, by_x, 1 - core], core_recv.at[spot, by_x])
    for copy in sent:
        copy.wait_send()


def gather_in_plane(shard, planes, collective_id):
    dma = pltpu.SemaphoreType.DMA
    whole = pl.pallas_call(
        functools.partial(plane_gather_kernel, planes),
        out_shape=jax.ShapeDtypeStruct((planes, 2, 2, *shard.shape), shard.dtype),
        in_specs=[pl.BlockSpec(memory_space=pl.ANY)],
        out_specs=pl.BlockSpec(memory_space=pl.ANY),
        scratch_shapes=[
            dma((1,)),
            dma((planes,)),
            dma((planes,)),
            dma((planes, 2)),
            dma((planes, 2)),
            dma((planes, 2)),
        ],
        compiler_params=pltpu.CompilerParams(collective_id=collective_id, has_side_effects=True),
        name="gather_in_plane",
    )(shard)
    return whole.reshape(4 * planes * shard.shape[0], shard.shape[1])


def plane_scatter_kernel(
    planes,
    steps,
    rows,
    partial_ref,
    sum_ref,
    own,
    from_core,
    from_x,
    from_line,
    load_sem,
    core_sems,
    x_sems,
    line_send,
    line_recv,
):
    core, x, z, to_core, to_x, line, line_devices = plane_places(planes)
    greet([to_core, to_x] + line_devices[1:])

    def piece(step, by_x, plane):
        return partial_ref.at[:, by_x, plane, pl.ds(pl.multiple_of(step * rows, rows), rows)]

    def core_copy(step, by_x, plane):
        return remote(
            piece(step, by_x, plane),
            from_core.at[step, by_x],
            core_sems.at[0, step, by_x],
            core_sems.at[1, step, by_x],
            to_core,
        )

    def load(step, by_x):
        return pltpu.make_async_copy(
            piece(step, by_x, core), own.at[step, by_x], load_sem.at[step, by_x]
        )

    def x_copy(step):
        return remote(
            own.at[step, 1 - x], from_x.at[step], x_sems.at[0, step], x_sems.at[1, step], to_x
        )

    def line_copy(step, at):
        return remote(
            own.at[step, x, line[at][0]],
            from_line.at[step, z],
            line_send.at[step, at],
            line_recv.at[step, z],
            line_devices[at],
        )

    def start_loads(step):
        for by_x in (1 - x, x):
            core_copy(step, by_x, 1 - core).start()
            load(step, by_x).start()

    def add_core(step):
        for turn, by_x in enumerate((1 - x, x)):
            load(step, by_x).wait()
            core_copy(step, by_x, core).wait_recv()
            own[step, by_x] += from_core[step, by_x]
            if turn == 0:
                x_copy(step).start()

    def add_x(step):
        x_copy(step).wait_recv()
        own[step, x] += from_x[step]
        for at in range(1, planes):
            line_copy(step, at).start()

    def add_line(step):
        total = own[step, x, z].astype(jnp.float32)
        for spot, at in line[1:]:
            remote(
                own.at[step, x, spot],
                from_line.at[step, spot],
                line_send.at[step, at],
                line_recv.at[step, spot],
                line_devices[at],
            ).wait_recv()
            total = total + from_line[step, spot].astype(jnp.float32)
        sum_ref[pl.ds(pl.multiple_of(step * rows, rows), rows), :] = total.astype(sum_ref.dtype)

    start_loads(0)
    start_loads(1)

    @pl.loop(0, steps + 2)
    def _(turn):
        @pl.when(turn < steps - 2)
        def _():
            start_loads(turn + 2)

        @pl.when(turn < steps)
        def _():
            add_core(turn)

        @pl.when((turn >= 1) & (turn < steps + 1))
        def _():
            add_x(turn - 1)

        @pl.when(turn >= 2)
        def _():
            add_line(turn - 2)

    @pl.loop(0, steps)
    def _(step):
        for by_x in range(2):
            core_copy(step, by_x, 1 - core).wait_send()
        x_copy(step).wait_send()
        for at in range(1, planes):
            line_copy(step, at).wait_send()


def scatter_in_plane(partial, planes, collective_id):
    shard_rows = partial.shape[0] // (4 * planes)
    width = partial.shape[1]
    rows = 16
    steps = shard_rows // rows
    dtype = partial.dtype
    dma = pltpu.SemaphoreType.DMA
    return pl.pallas_call(
        functools.partial(plane_scatter_kernel, planes, steps, rows),
        out_shape=jax.ShapeDtypeStruct((shard_rows, width), dtype),
        in_specs=[pl.BlockSpec(memory_space=pl.ANY)],
        out_specs=pl.BlockSpec(memory_space=pltpu.VMEM),
        scratch_shapes=[
            pltpu.VMEM((steps, 2, planes, rows, width), dtype),
            pltpu.VMEM((steps, 2, planes, rows, width), dtype),
            pltpu.VMEM((steps, planes, rows, width), dtype),
            pltpu.VMEM((steps, planes, rows, width), dtype),
            dma((steps, 2)),
            dma((2, steps, 2)),
            dma((2, steps)),
            dma((steps, planes)),
            dma((steps, planes)),
        ],
        compiler_params=pltpu.CompilerParams(
            collective_id=collective_id, has_side_effects=True, vmem_limit_bytes=40 * 2**20
        ),
        name="scatter_in_plane",
    )(partial.reshape(planes, 2, 2, shard_rows, width))


def ffn_pack_kernel(gateup_ref, down_ref, packet_ref):
    live = pl.program_id(0) < FF // HEAD // 2

    @pl.when(live)
    def _():
        for at in range(2):
            columns = slice(at * HEAD, (at + 1) * HEAD)
            packet_ref[at, :, :HEAD] = gateup_ref[0, :, columns].astype(jnp.bfloat16)
            packet_ref[at, :, HEAD : 2 * HEAD] = gateup_ref[1, :, columns].astype(jnp.bfloat16)
            packet_ref[at, :, 2 * HEAD :] = down_ref[:, columns].astype(jnp.bfloat16)

    @pl.when(jnp.logical_not(live))
    def _():
        packet_ref[...] = jnp.zeros_like(packet_ref)


def ffn_packets(gateup, down, device_count):
    row_count = gateup.shape[1]
    last = FF // HEAD // 2 - 1
    return pl.pallas_call(
        ffn_pack_kernel,
        grid=(device_count // 2,),
        in_specs=[
            pl.BlockSpec((2, row_count, 2 * HEAD), lambda j: (0, 0, jnp.minimum(j, last))),
            pl.BlockSpec((row_count, 2 * HEAD), lambda j: (0, jnp.minimum(j, last))),
        ],
        out_specs=pl.BlockSpec((2, row_count, 3 * HEAD), lambda j: (j, 0, 0)),
        out_shape=jax.ShapeDtypeStruct((device_count, row_count, 3 * HEAD), jnp.bfloat16),
        cost_estimate=pl.CostEstimate(flops=0, bytes_accessed=14 * 2**20, transcendentals=0),
        name="ffn_packets",
    )(gateup, down)


def attn_pack_kernel(qkv_ref, out_ref, packet_ref):
    j = pl.program_id(0)

    @pl.when(j < (H + 2) // 2)
    def _():
        for at in range(2):
            packet_ref[at] = qkv_ref[:, at * HEAD : (at + 1) * HEAD].astype(jnp.bfloat16)

    @pl.when((j >= (H + 2) // 2) & (j < H + 1))
    def _():
        for at in range(2):
            packet_ref[at] = out_ref[:, at * HEAD : (at + 1) * HEAD].astype(jnp.bfloat16)

    @pl.when(j >= H + 1)
    def _():
        packet_ref[...] = jnp.zeros_like(packet_ref)


def attn_packets(qkv, out, device_count):
    row_count = qkv.shape[0]
    qkv_last, out_last = (H + 2) // 2 - 1, H // 2 - 1
    return pl.pallas_call(
        attn_pack_kernel,
        grid=(device_count // 2,),
        in_specs=[
            pl.BlockSpec((row_count, 2 * HEAD), lambda j: (0, jnp.minimum(j, qkv_last))),
            pl.BlockSpec((row_count, 2 * HEAD), lambda j: (0, jnp.clip(j - qkv_last - 1, 0, out_last))),
        ],
        out_specs=pl.BlockSpec((2, row_count, HEAD), lambda j: (j, 0, 0)),
        out_shape=jax.ShapeDtypeStruct((device_count, row_count, HEAD), jnp.bfloat16),
        cost_estimate=pl.CostEstimate(flops=0, bytes_accessed=4 * 2**20, transcendentals=0),
        name="attn_packets",
    )(qkv, out)


def turn_kernel(grads_ref, others_ref, mom_ref, turned_ref, low_ref, current_ref):
    grads = grads_ref[...] + others_ref[...].astype(jnp.float32)
    low_ref[...] = grads.astype(jnp.bfloat16)
    moment = momentum_decay * mom_ref[...].astype(jnp.float32) + grads
    moment = moment.astype(jnp.bfloat16).astype(jnp.float32)
    norm_size = jnp.sqrt(jnp.sum(moment * moment, keepdims=True))
    current_ref[...] = (moment / (norm_size + eps_pieces)).T.astype(jnp.bfloat16)

    @pl.loop(0, NS_STEPS)
    def _(sweep_index):
        current = current_ref[...]
        gram_matrix = lax.dot_general(
            current, current, (((1,), (1,)), ((), ())), preferred_element_type=jnp.float32
        ).astype(jnp.bfloat16)
        square = jnp.dot(gram_matrix, gram_matrix, preferred_element_type=jnp.float32)
        mixing = (ns_second * gram_matrix.astype(jnp.float32) + ns_third * square).astype(
            jnp.bfloat16
        )
        turned = jnp.dot(mixing, current, preferred_element_type=jnp.float32)
        current_ref[...] = (ns_first * current.astype(jnp.float32) + turned).astype(jnp.bfloat16)

    turned_ref[...] = current_ref[...].astype(jnp.float32).T.astype(jnp.bfloat16)


def orthogonalize(grads, others, moms):
    depth, columns = grads.shape
    block = pl.BlockSpec((depth, HEAD), lambda j: (0, j))
    low = jax.ShapeDtypeStruct((depth, columns), jnp.bfloat16)
    pieces = columns // HEAD
    return pl.pallas_call(
        turn_kernel,
        grid=(pieces,),
        in_specs=[block] * 3,
        out_specs=[block] * 2,
        out_shape=[low, low],
        scratch_shapes=[pltpu.VMEM((HEAD, depth), jnp.bfloat16)],
        cost_estimate=pl.CostEstimate(
            flops=pieces * 20 * depth * HEAD * HEAD, bytes_accessed=12 * depth * columns, transcendentals=0
        ),
        compiler_params=pltpu.CompilerParams(vmem_limit_bytes=48 * 2**20),
        name="orthogonalize",
    )(grads, others, moms)


def update(rate, weight, mom, grad, turn):
    moment = momentum_decay * mom + grad.astype(jnp.float32)
    new = (1.0 - weight_shrink) * weight - rate * turn.astype(jnp.float32)
    return new, moment, new.astype(jnp.bfloat16)


def ffn_update_kernel(
    grad_ref, turn_ref, w_gateup_ref, mom_gateup_ref, w_down_ref, mom_down_ref, *results
):
    for at in range(grad_ref.shape[0]):
        columns = slice(at * HEAD, (at + 1) * HEAD)
        for part in range(3):
            spot = (part, slice(None), columns) if part < 2 else (slice(None), columns)
            weight_ref, mom_ref = (
                (w_gateup_ref, mom_gateup_ref) if part < 2 else (w_down_ref, mom_down_ref)
            )
            packed = slice(part * HEAD, (part + 1) * HEAD)
            values = update(
                matrix_rate,
                weight_ref[spot],
                mom_ref[spot],
                grad_ref[at, :, packed],
                turn_ref[at, :, packed],
            )
            for ref, value in zip(results[:3] if part < 2 else results[3:], values):
                ref[spot] = value


def ffn_update(grads, turns, w_gateup, mom_gateup, w_down, mom_down):
    row_count = w_gateup.shape[1]
    wide = 3
    packet = pl.BlockSpec((wide, row_count, 3 * HEAD), lambda j: (j, 0, 0))
    gateup = pl.BlockSpec((2, row_count, wide * HEAD), lambda j: (0, 0, j))
    down = pl.BlockSpec((row_count, wide * HEAD), lambda j: (0, j))
    dtypes = (jnp.float32, jnp.float32, jnp.bfloat16)
    return pl.pallas_call(
        ffn_update_kernel,
        grid=(FF // HEAD // wide,),
        in_specs=[packet, packet, gateup, gateup, down, down],
        out_specs=[gateup] * 3 + [down] * 3,
        out_shape=[jax.ShapeDtypeStruct(w_gateup.shape, dtype) for dtype in dtypes]
        + [jax.ShapeDtypeStruct(w_down.shape, dtype) for dtype in dtypes],
        cost_estimate=pl.CostEstimate(flops=0, bytes_accessed=50 * 2**20, transcendentals=0),
        compiler_params=pltpu.CompilerParams(vmem_limit_bytes=48 * 2**20),
        name="ffn_update",
    )(grads, turns, w_gateup, mom_gateup, w_down, mom_down)


def attn_update_kernel(rate, grad_ref, turn_ref, w_ref, mom_ref, *results):
    for at in range(2):
        columns = slice(at * HEAD, (at + 1) * HEAD)
        values = update(rate, w_ref[:, columns], mom_ref[:, columns], grad_ref[at], turn_ref[at])
        for ref, value in zip(results, values):
            ref[:, columns] = value


def attn_update(rate, offset, grads, turns, weight, mom):
    row_count = grads.shape[1]
    packet = pl.BlockSpec((2, row_count, HEAD), lambda j: (j + offset // 2, 0, 0))
    block = pl.BlockSpec((row_count, 2 * HEAD), lambda j: (0, j))
    return pl.pallas_call(
        functools.partial(attn_update_kernel, rate),
        grid=(weight.shape[1] // HEAD // 2,),
        in_specs=[packet, packet, block, block],
        out_specs=[block] * 3,
        out_shape=[
            jax.ShapeDtypeStruct(weight.shape, dtype)
            for dtype in (jnp.float32, jnp.float32, jnp.bfloat16)
        ],
        cost_estimate=pl.CostEstimate(flops=0, bytes_accessed=6 * 2**20, transcendentals=0),
        name="attn_update",
    )(grads, turns, weight, mom)


def rms_scale(stream, gain_row):
    mean_square = jnp.mean(stream * stream, axis=-1, keepdims=True)
    return stream * lax.rsqrt(mean_square + eps_norm) * gain_row


def gelu_product(gate_part, up_part):
    return jax.nn.gelu(gate_part, approximate=True) * up_part


def on_device(
    tokens_in,
    cotangent,
    w_qkv,
    w_out,
    w_gateup,
    w_down,
    gains,
    mom_qkv,
    mom_out,
    mom_gateup,
    mom_down,
    mom_gains,
):
    everyone = ("blk", "pair")
    bf16 = jnp.bfloat16
    f32 = jnp.float32
    blk_count = lax.axis_size("blk")
    pair_count = lax.axis_size("pair")
    device_count = blk_count * pair_count
    block_at = lax.axis_index("blk")
    half_at = lax.axis_index("pair")
    me = block_at * pair_count + half_at
    local_rows, width = tokens_in.shape
    share_rows = w_qkv.shape[0]
    score_scale = HEAD ** (-0.5)
    span = WINDOW + local_rows
    token_count = local_rows * device_count
    large = token_count * width * 2 > 48 * 2**20
    planes = blk_count // 4

    def after(value, earlier):
        return lax.optimization_barrier((value, earlier))[0] if large else value

    def exchange(packets, axes=everyone):
        return lax.all_to_all(packets, axes, split_axis=0, concat_axis=0, tiled=True)

    def swap(shard):
        return lax.ppermute(shard, "pair", [(0, 1), (1, 0)])

    def hold(value, *earlier):
        return value if large else lax.optimization_barrier((value, earlier))[0]

    def gather_all(shards, collective_id, packets=()):
        if large:
            wholes = [lax.all_gather(shard, everyone, axis=0, tiled=True) for shard in shards]
            return wholes + [exchange(array) for array in packets]
        return gather_by_axes(shards, planes, collective_id, packets)

    def scatter_all(partial, collective_id):
        if large:
            return lax.psum_scatter(partial, everyone, scatter_dimension=0, tiled=True)
        return scatter_by_axes(partial, planes, collective_id)

    def gather_plane(shard):
        return lax.all_gather(shard, "blk", axis=0, tiled=True)

    def scatter_plane(partial, collective_id):
        if large:
            return lax.psum_scatter(partial, "blk", scatter_dimension=0, tiled=True)
        return scatter_in_plane(partial, planes, collective_id)

    stream = tokens_in.astype(f32)
    padded_gains = jnp.pad(gains.astype(bf16), ((0, 14), (0, 128 - share_rows)))
    full_qkv, full_gains, full_out, ffn_weights = gather_all(
        [w_qkv.astype(bf16), padded_gains, w_out.T.astype(bf16)],
        1,
        [ffn_packets(w_gateup, w_down.T, device_count)],
    )
    ffn_weights = ffn_weights.reshape(width, 3 * HEAD)
    full_gains = full_gains.reshape(device_count, 16, 128)[:, :2, :share_rows].astype(f32)
    gain_attn = full_gains[:, 0].reshape(width)
    gain_mlp = full_gains[:, 1].reshape(width)
    normed_attn_f, norm_back_attn = jax.vjp(rms_scale, stream, gain_attn)
    normed_attn = normed_attn_f.astype(bf16)
    qkv = jnp.dot(normed_attn, full_qkv, preferred_element_type=f32).astype(bf16)
    queries = qkv[:, : H * HEAD].reshape(local_rows, H, HEAD)
    (kv_all,) = gather_all([qkv[:, H * HEAD :]], 2)
    kv_window = lax.dynamic_slice_in_dim(
        jnp.pad(kv_all, ((WINDOW, 0), (0, 0))), me * local_rows, span, 0
    )
    keys = kv_window[:, :HEAD]
    values = kv_window[:, HEAD:]
    pair_weights = [ffn_weights, swap(ffn_weights)]
    gates, ups, downs = (
        [weights[:, part * HEAD : (part + 1) * HEAD] for weights in pair_weights]
        for part in range(3)
    )
    pair_gateup = jnp.concatenate(gates + ups, axis=1)
    pair_down = jnp.concatenate(downs, axis=1)
    cotangent_plane = gather_plane(hold(cotangent, full_gains))

    key_index = jnp.arange(span, dtype=jnp.int32)[None, :]
    distance = jnp.arange(local_rows, dtype=jnp.int32)[:, None] + WINDOW - key_index
    allowed = (
        (distance >= 0) & (distance < WINDOW) & (me * local_rows - WINDOW + key_index >= 0)
    )
    raw = jnp.einsum("qhd,kd->hqk", queries, keys, preferred_element_type=f32)
    scores = jnp.where(allowed[None], raw * score_scale, masked_score)
    top_score = jnp.max(scores, axis=-1, keepdims=True)
    expo = jnp.exp(scores - top_score)
    probs = expo / jnp.sum(expo, axis=-1, keepdims=True)
    probs_low = probs.astype(bf16)
    mixed = jnp.einsum("hqk,kd->qhd", probs_low, values, preferred_element_type=f32)
    mixed = mixed.reshape(local_rows, H * HEAD).astype(bf16)
    resid = stream + jnp.einsum("tc,dc->td", mixed, full_out, preferred_element_type=f32)

    normed_mlp_f, norm_back_mlp = jax.vjp(rms_scale, resid, gain_mlp)
    normed_mlp = normed_mlp_f.astype(bf16)
    if large:
        normed_mlp_plane = gather_plane(normed_mlp)
    else:
        normed_mlp_plane = gather_in_plane(normed_mlp, planes, 3)
    plane_rows = blk_count * local_rows
    both_parts = jnp.dot(normed_mlp_plane, pair_gateup, preferred_element_type=f32)
    pair_width = pair_count * HEAD
    hidden_f, geglu_back = jax.vjp(
        gelu_product, both_parts[:, :pair_width], both_parts[:, pair_width:]
    )
    hidden = hidden_f.astype(bf16)
    grad_hidden = jnp.dot(cotangent_plane, pair_down, preferred_element_type=f32)
    grad_gate, grad_up = geglu_back(grad_hidden)
    grad_gateup = jnp.concatenate([grad_gate.astype(bf16), grad_up.astype(bf16)], axis=1)
    grad_normed_mlp = scatter_plane(
        jnp.einsum("tf,df->td", grad_gateup, pair_gateup, preferred_element_type=f32).astype(bf16), 4
    ).astype(f32)
    def ffn_gradient(columns):
        gateup_right = jnp.concatenate(
            [grad_gate[:, columns].astype(bf16), grad_up[:, columns].astype(bf16)], axis=1
        )
        down_right = hidden[:, columns]
        return jnp.concatenate(
            [
                jnp.einsum("td,tf->df", normed_mlp_plane, gateup_right, preferred_element_type=f32),
                jnp.einsum("td,tf->df", cotangent_plane, down_right, preferred_element_type=f32),
            ],
            axis=1,
        )

    ffn_others = swap(ffn_gradient(slice(HEAD, 2 * HEAD)).astype(bf16))
    ffn_grads = ffn_gradient(slice(0, HEAD))
    ffn_moms = exchange(hold(ffn_packets(mom_gateup, mom_down.T, device_count), normed_mlp_plane))
    ffn_moms = ffn_moms.reshape(width, 3 * HEAD)
    ffn_turned_own, ffn_low = orthogonalize(ffn_grads, ffn_others, ffn_moms)
    ffn_shape = (device_count, share_rows, 3 * HEAD)
    ffn_low = exchange(ffn_low.reshape(ffn_shape))
    ffn_turned = exchange(ffn_turned_own.reshape(ffn_shape))

    resid_part, gain_grad_mlp = norm_back_mlp(hold(grad_normed_mlp, ffn_turned_own))
    grad_resid = cotangent.astype(f32) + resid_part
    grad_proj = grad_resid.astype(bf16)
    grad_mixed = jnp.dot(grad_proj, full_out, preferred_element_type=f32).astype(bf16)
    grad_mixed = grad_mixed.reshape(local_rows, H, HEAD)
    grad_probs = jnp.einsum("qhd,kd->hqk", grad_mixed, values, preferred_element_type=f32)
    row_delta = jnp.sum(probs * grad_probs, axis=-1, keepdims=True)
    grad_raw = (probs * (grad_probs - row_delta) * score_scale).astype(bf16)
    grad_query = jnp.einsum("hqk,kd->qhd", grad_raw, keys, preferred_element_type=f32)
    grad_keys = jnp.einsum("hqk,qhd->kd", grad_raw, queries, preferred_element_type=f32)
    grad_values = jnp.einsum("hqk,qhd->kd", probs_low, grad_mixed, preferred_element_type=f32)
    grad_kv = jnp.concatenate([grad_keys, grad_values], axis=1).astype(bf16)
    grad_kv_all = lax.dynamic_update_slice_in_dim(
        jnp.zeros((WINDOW + token_count, 2 * HEAD), bf16), grad_kv, me * local_rows, 0
    )[WINDOW:]
    grad_qkv = jnp.concatenate(
        [grad_query.reshape(local_rows, H * HEAD).astype(bf16), scatter_all(grad_kv_all, 5)], axis=1
    )
    grad_normed_attn = jnp.einsum("tc,dc->td", grad_qkv, full_qkv, preferred_element_type=f32)
    stream_part, gain_grad_attn = norm_back_attn(grad_normed_attn)
    input_grad = grad_resid + stream_part

    attn_rights = jnp.concatenate([grad_qkv, mixed], axis=1)
    used = attn_rights.shape[1] // pair_width
    attn_rights = attn_rights.reshape(local_rows, used, pair_width).transpose(1, 0, 2)
    attn_rights = jnp.pad(attn_rights, ((0, blk_count - used), (0, 0), (0, 0)))
    branch_part = jnp.einsum(
        "tf,df->td", after(hold(hidden, attn_rights), grad_normed_mlp), pair_down, preferred_element_type=f32
    )
    branch = scatter_plane(branch_part.astype(bf16), 4).astype(f32)
    block_output = (resid + branch).astype(bf16)
    attn_rights = exchange(attn_rights, "blk").reshape(plane_rows, pair_width)
    normed_attn_plane = gather_plane(after(hold(normed_attn, normed_mlp_plane), (ffn_grads, block_output)))
    grad_proj_plane = gather_plane(after(grad_proj, (ffn_grads, block_output)))

    def attn_gradient(lefts):
        return jnp.einsum("td,tf->df", lefts, attn_rights, preferred_element_type=f32)

    attn_grads = lax.cond(
        block_at < (H + 2) // pair_count,
        lambda: attn_gradient(normed_attn_plane),
        lambda: attn_gradient(grad_proj_plane),
    )
    attn_others = swap(
        lax.dynamic_slice_in_dim(attn_grads, (1 - half_at) * HEAD, HEAD, 1).astype(bf16)
    )
    attn_grads = lax.dynamic_slice_in_dim(attn_grads, half_at * HEAD, HEAD, 1)
    attn_moms = exchange(hold(attn_packets(mom_qkv, mom_out.T, device_count), normed_mlp_plane))
    attn_moms = attn_moms.reshape(width, HEAD)
    attn_turned, attn_low = orthogonalize(attn_grads, attn_others, attn_moms)
    attn_shape = (device_count, share_rows, HEAD)
    attn_low = exchange(attn_low.reshape(attn_shape))
    attn_turned = exchange(attn_turned.reshape(attn_shape))

    gain_grads = jnp.stack([gain_grad_attn, gain_grad_mlp], axis=0)
    gain_grads = gain_grads.reshape(2, device_count, share_rows).transpose(1, 0, 2)
    gain_share = jnp.sum(exchange(gain_grads), axis=0)

    updated_ffn = ffn_update(ffn_low, ffn_turned, w_gateup, mom_gateup, w_down.T, mom_down.T)
    updated_qkv = attn_update(matrix_rate, 0, attn_low, attn_turned, w_qkv, mom_qkv)
    updated_out = attn_update(output_rate, H + 2, attn_low, attn_turned, w_out.T, mom_out.T)
    moment_gains = momentum_decay * mom_gains + gain_share
    new_gains = gains - gain_rate * moment_gains
    return (
        block_output,
        input_grad,
        *updated_qkv,
        *(result.T for result in updated_out),
        *updated_ffn[:3],
        *(result.T for result in updated_ffn[3:]),
        new_gains,
        moment_gains,
        new_gains.astype(bf16),
    )


def solution(mesh):
    placed = (
        P(("blk", "pair"), None),
        P(("blk", "pair"), None),
        P(("blk", "pair"), None),
        P(None, ("blk", "pair")),
        P(None, ("blk", "pair"), None),
        P(None, ("blk", "pair")),
        P(None, ("blk", "pair")),
        P(("blk", "pair"), None),
        P(None, ("blk", "pair")),
        P(None, ("blk", "pair"), None),
        P(None, ("blk", "pair")),
        P(None, ("blk", "pair")),
    )
    return jax.shard_map(
        on_device,
        mesh=mesh,
        in_specs=placed,
        out_specs=(
            P(("blk", "pair"), None),
            P(("blk", "pair"), None),
            P(("blk", "pair"), None),
            P(("blk", "pair"), None),
            P(("blk", "pair"), None),
            P(None, ("blk", "pair")),
            P(None, ("blk", "pair")),
            P(None, ("blk", "pair")),
            P(None, ("blk", "pair"), None),
            P(None, ("blk", "pair"), None),
            P(None, ("blk", "pair"), None),
            P(None, ("blk", "pair")),
            P(None, ("blk", "pair")),
            P(None, ("blk", "pair")),
            P(None, ("blk", "pair")),
            P(None, ("blk", "pair")),
            P(None, ("blk", "pair")),
        ),
        check_vma=False,
    )
```

```python
import functools

import jax
import jax.numpy as jnp
from jax import lax
from jax.experimental import pallas as pl
from jax.experimental.pallas import tpu as pltpu
from jax.sharding import PartitionSpec as P

H = 10
HEAD = 256
FF = 7680
WINDOW = 2048
NS_STEPS = 5


eps_norm = 1e-06
eps_pieces = 1e-07
ns_first = 3.4445
ns_second = -4.775
ns_third = 2.0315
momentum_decay = 0.95
matrix_rate = 0.5
output_rate = 10.0
gain_rate = 0.001
weight_shrink = 0.001
masked_score = -1e30
MESH = pl.DeviceIdType.MESH


def places(planes):
    blk = lax.axis_index("blk")
    y = lax.axis_index("pair")
    core = lax.rem(blk, 2)
    x = lax.rem(lax.div(blk, 2), 2)
    z = lax.div(blk, 4)
    first = y * (1 - core) + x * core
    second = x * (1 - core) + y * core
    to_core = (blk + 1 - 2 * core, y)
    first_device = (blk + core * (2 - 4 * x), y + (1 - core) * (1 - 2 * y))
    second_device = (blk + (1 - core) * (2 - 4 * x), y + core * (1 - 2 * y))
    line = [(lax.rem(z + at, planes), at) for at in range(planes)]
    line_devices = [((blk + 4 * (spot - z)), y) for spot, at in line]
    return core, z, first, second, to_core, first_device, second_device, line, line_devices


def greet(devices):
    barrier = pltpu.get_barrier_semaphore()
    for device in devices:
        pl.semaphore_signal(barrier, inc=1, device_id=device, device_id_type=MESH)
    pl.semaphore_wait(barrier, len(devices))


def remote(source, target, send_sem, recv_sem, device):
    return pltpu.make_async_remote_copy(
        src_ref=source,
        dst_ref=target,
        send_sem=send_sem,
        recv_sem=recv_sem,
        device_id=device,
        device_id_type=MESH,
    )


def gather_kernel(planes, count, exchanged, *refs):
    inputs, refs = refs[: count + exchanged], refs[count + exchanged :]
    outputs, refs = refs[: count + exchanged], refs[count + exchanged :]
    shards, wholes = inputs[:count], outputs[:count]
    own_sem, line_send, second_send, first_send, core_send, recv, core_recv = refs[:7]
    core, z, first, second, to_core, first_device, second_device, line, line_devices = places(
        planes
    )
    device_count = 8 * planes
    me = lax.axis_index("blk") * 2 + lax.axis_index("pair")
    others = [lax.rem(me + at, device_count) for at in range(1, device_count)]
    others = [(other, (lax.div(other, 2), lax.rem(other, 2))) for other in others]
    if exchanged:
        greet([device for _, device in others])
    else:
        greet([to_core, first_device, second_device] + line_devices[1:])

    def slot(whole, spot, by_first, by_second):
        x = (1 - core) * by_second + core * by_first
        y = (1 - core) * by_first + core * by_second
        return whole.at[spot, x, core, y]

    def core_slot(whole, spot, by_first, by_second):
        x = core * by_second + (1 - core) * by_first
        y = core * by_first + (1 - core) * by_second
        return whole.at[spot, x, 1 - core, y]

    sent = []

    def send(source, target, send_sem, recv_sem, device):
        copy = remote(source, target, send_sem, recv_sem, device)
        copy.start()
        sent.append(copy)

    def arrive(target, recv_sem):
        remote(target, target, own_sem.at[0], recv_sem, to_core).wait_recv()

    own_copies = []
    for i, (shard, whole) in enumerate(zip(shards, wholes)):
        here = slot(whole, z, first, second)
        copy = pltpu.make_async_copy(shard, here, own_sem.at[i])
        copy.start()
        own_copies.append(copy)
        for spot, at in line[1:]:
            send(shard, here, line_send.at[i, at], recv.at[i, z, first, second], line_devices[at])
    if exchanged:
        packets, received = inputs[count], outputs[count]
        swap_own, swap_send, swap_recv = refs[7:]
        copy = pltpu.make_async_copy(packets.at[me], received.at[me], swap_own.at[0])
        copy.start()
        own_copies.append(copy)
        for at, (other, device) in enumerate(others):
            send(packets.at[other], received.at[me], swap_send.at[at], swap_recv.at[me], device)
    for spot, at in line:
        for i, (shard, whole) in enumerate(zip(shards, wholes)):
            here = slot(whole, spot, first, second)
            source = shard
            if at:
                arrive(here, recv.at[i, spot, first, second])
                source = here
            for devices, sends in ((second_device, second_send.at[i, at]), (first_device, first_send.at[i, at, 0])):
                send(source, here, sends, recv.at[i, spot, first, second], devices)
            send(source, here, core_send.at[i, at, 0, 0], core_recv.at[i, spot, first, second], to_core)
        for i, whole in enumerate(wholes):
            here = slot(whole, spot, first, 1 - second)
            arrive(here, recv.at[i, spot, first, 1 - second])
            send(here, here, first_send.at[i, at, 1], recv.at[i, spot, first, 1 - second], first_device)
            send(here, here, core_send.at[i, at, 0, 1], core_recv.at[i, spot, first, 1 - second], to_core)
    for spot, at in line:
        for turn, by_second in enumerate((second, 1 - second)):
            for i, whole in enumerate(wholes):
                here = slot(whole, spot, 1 - first, by_second)
                arrive(here, recv.at[i, spot, 1 - first, by_second])
                send(here, here, core_send.at[i, at, 1, turn], core_recv.at[i, spot, 1 - first, by_second], to_core)
    for copy in own_copies:
        copy.wait()
    for i, whole in enumerate(wholes):
        for spot in range(planes):
            for by_first in range(2):
                for by_second in range(2):
                    arrive(
                        core_slot(whole, spot, by_first, by_second),
                        core_recv.at[i, spot, by_first, by_second],
                    )
    if exchanged:
        for other, _ in others:
            arrive(received.at[other], swap_recv.at[other])
    for copy in sent:
        copy.wait_send()


def gather_by_axes(shards, planes, collective_id, packets=()):
    count = len(shards)
    exchanged = len(packets)
    operands = [*shards, *packets]
    any_spec = pl.BlockSpec(memory_space=pl.ANY)
    dma = pltpu.SemaphoreType.DMA
    wholes = pl.pallas_call(
        functools.partial(gather_kernel, planes, count, exchanged),
        out_shape=[
            jax.ShapeDtypeStruct((planes, 2, 2, 2, *shard.shape), shard.dtype) for shard in shards
        ]
        + [jax.ShapeDtypeStruct(array.shape, array.dtype) for array in packets],
        in_specs=[any_spec] * len(operands),
        out_specs=[any_spec] * len(operands),
        scratch_shapes=[
            dma((count,)),
            dma((count, planes)),
            dma((count, planes)),
            dma((count, planes, 2)),
            dma((count, planes, 2, 2)),
            dma((count, planes, 2, 2)),
            dma((count, planes, 2, 2)),
        ]
        + [dma((1,)), dma((8 * planes,)), dma((8 * planes,))] * exchanged,
        compiler_params=pltpu.CompilerParams(collective_id=collective_id, has_side_effects=True),
        cost_estimate=pl.CostEstimate(flops=0, bytes_accessed=200 * 2**20, transcendentals=0),
        name="gather_by_axes",
    )(*operands)
    return [
        whole.reshape(8 * planes * shard.shape[0], shard.shape[1])
        for whole, shard in zip(wholes, shards)
    ] + list(wholes[count:])


def scatter_kernel(
    planes,
    steps,
    rows,
    partial_ref,
    sum_ref,
    own,
    from_core,
    from_first,
    from_second,
    from_line,
    load_sem,
    core_sems,
    first_sems,
    second_sems,
    line_send,
    line_recv,
):
    core, z, first, second, to_core, first_device, second_device, line, line_devices = places(
        planes
    )
    greet([to_core, first_device, second_device] + line_devices[1:])

    def piece(step, by_first, by_second, plane):
        x = (1 - plane) * by_second + plane * by_first
        y = (1 - plane) * by_first + plane * by_second
        return partial_ref.at[:, x, plane, y, pl.ds(pl.multiple_of(step * rows, rows), rows)]

    def core_copy(step, half, by_second, plane):
        return remote(
            piece(step, half, by_second, plane),
            from_core.at[step, half, by_second],
            core_sems.at[0, step, half, by_second],
            core_sems.at[1, step, half, by_second],
            to_core,
        )

    def load(step, half, by_second):
        return pltpu.make_async_copy(
            piece(step, half, by_second, core),
            own.at[step, half, by_second],
            load_sem.at[step, half, by_second],
        )

    def first_copy(step, half):
        return remote(
            own.at[step, half],
            from_first.at[step],
            first_sems.at[0, step],
            first_sems.at[1, step],
            first_device,
        )

    def second_copy(step, half):
        return remote(
            own.at[step, first, half],
            from_second.at[step],
            second_sems.at[0, step],
            second_sems.at[1, step],
            second_device,
        )

    def line_copy(step, at):
        return remote(
            own.at[step, first, second, line[at][0]],
            from_line.at[step, z],
            line_send.at[step, at],
            line_recv.at[step, z],
            line_devices[at],
        )

    def start_loads(step):
        for mine, theirs in ((1 - first, 1 - second), (first, second)):
            for by_second in range(2):
                core_copy(step, theirs, by_second, 1 - core).start()
                load(step, mine, by_second).start()

    def add_core(step):
        for turn, half in enumerate((1 - first, first)):
            for by_second in range(2):
                load(step, half, by_second).wait()
                core_copy(step, half, by_second, core).wait_recv()
                own[step, half, by_second] += from_core[step, half, by_second]
            if turn == 0:
                first_copy(step, half).start()

    def add_first(step):
        first_copy(step, 1 - first).wait_recv()
        own[step, first, 1 - second] += from_first[step, 1 - second]
        second_copy(step, 1 - second).start()
        own[step, first, second] += from_first[step, second]

    def add_second(step):
        second_copy(step, 1 - second).wait_recv()
        own[step, first, second] += from_second[step]
        for at in range(1, planes):
            line_copy(step, at).start()

    def add_line(step):
        total = own[step, first, second, z].astype(jnp.float32)
        for spot, at in line[1:]:
            remote(
                own.at[step, first, second, spot],
                from_line.at[step, spot],
                line_send.at[step, at],
                line_recv.at[step, spot],
                line_devices[at],
            ).wait_recv()
            total = total + from_line[step, spot].astype(jnp.float32)
        sum_ref[pl.ds(pl.multiple_of(step * rows, rows), rows), :] = total.astype(sum_ref.dtype)

    start_loads(0)
    start_loads(1)

    @pl.loop(0, steps + 3)
    def _(turn):
        @pl.when(turn < steps - 2)
        def _():
            start_loads(turn + 2)

        @pl.when(turn < steps)
        def _():
            add_core(turn)

        @pl.when((turn >= 1) & (turn < steps + 1))
        def _():
            add_first(turn - 1)

        @pl.when((turn >= 2) & (turn < steps + 2))
        def _():
            add_second(turn - 2)

        @pl.when(turn >= 3)
        def _():
            add_line(turn - 3)

    @pl.loop(0, steps)
    def _(step):
        for half in range(2):
            for by_second in range(2):
                core_copy(step, half, by_second, 1 - core).wait_send()
        first_copy(step, 1 - first).wait_send()
        second_copy(step, 1 - second).wait_send()
        for at in range(1, planes):
            line_copy(step, at).wait_send()


def scatter_by_axes(partial, planes, collective_id):
    shard_rows = partial.shape[0] // (8 * planes)
    width = partial.shape[1]
    rows = 16
    steps = shard_rows // rows
    dtype = partial.dtype
    dma = pltpu.SemaphoreType.DMA
    return pl.pallas_call(
        functools.partial(scatter_kernel, planes, steps, rows),
        out_shape=jax.ShapeDtypeStruct((shard_rows, width), dtype),
        in_specs=[pl.BlockSpec(memory_space=pl.ANY)],
        out_specs=pl.BlockSpec(memory_space=pltpu.VMEM),
        scratch_shapes=[
            pltpu.VMEM((steps, 2, 2, planes, rows, width), dtype),
            pltpu.VMEM((steps, 2, 2, planes, rows, width), dtype),
            pltpu.VMEM((steps, 2, planes, rows, width), dtype),
            pltpu.VMEM((steps, planes, rows, width), dtype),
            pltpu.VMEM((steps, planes, rows, width), dtype),
            dma((steps, 2, 2)),
            dma((2, steps, 2, 2)),
            dma((2, steps)),
            dma((2, steps)),
            dma((steps, planes)),
            dma((steps, planes)),
        ],
        compiler_params=pltpu.CompilerParams(
            collective_id=collective_id, has_side_effects=True, vmem_limit_bytes=48 * 2**20
        ),
        cost_estimate=pl.CostEstimate(flops=0, bytes_accessed=100 * 2**20, transcendentals=0),
        name="scatter_by_axes",
    )(partial.reshape(planes, 2, 2, 2, shard_rows, width))


def plane_places(planes):
    blk = lax.axis_index("blk")
    y = lax.axis_index("pair")
    core = lax.rem(blk, 2)
    x = lax.rem(lax.div(blk, 2), 2)
    z = lax.div(blk, 4)
    to_core = (blk + 1 - 2 * core, y)
    to_x = (blk + 2 - 4 * x, y)
    line = [(lax.rem(z + at, planes), at) for at in range(planes)]
    line_devices = [(blk + 4 * (spot - z), y) for spot, at in line]
    return core, x, z, to_core, to_x, line, line_devices


def plane_gather_kernel(planes, shard, whole, own_sem, line_send, x_send, core_send, recv, core_recv):
    core, x, z, to_core, to_x, line, line_devices = plane_places(planes)
    greet([to_core, to_x] + line_devices[1:])
    sent = []

    def send(source, target, send_sem, recv_sem, device):
        copy = remote(source, target, send_sem, recv_sem, device)
        copy.start()
        sent.append(copy)

    def arrive(target, recv_sem):
        remote(target, target, own_sem.at[0], recv_sem, to_core).wait_recv()

    own_copy = pltpu.make_async_copy(shard, whole.at[z, x, core], own_sem.at[0])
    own_copy.start()
    for spot, at in line[1:]:
        send(shard, whole.at[z, x, core], line_send.at[at], recv.at[z, x], line_devices[at])
    for spot, at in line:
        here = whole.at[spot, x, core]
        source = shard
        if at:
            arrive(here, recv.at[spot, x])
            source = here
        send(source, here, x_send.at[at], recv.at[spot, x], to_x)
        send(source, here, core_send.at[at, 0], core_recv.at[spot, x], to_core)
    for spot, at in line:
        there = whole.at[spot, 1 - x, core]
        arrive(there, recv.at[spot, 1 - x])
        send(there, there, core_send.at[at, 1], core_recv.at[spot, 1 - x], to_core)
    own_copy.wait()
    for spot in range(planes):
        for by_x in range(2):
            arrive(whole.at[spot, by_x, 1 - core], core_recv.at[spot, by_x])
    for copy in sent:
        copy.wait_send()


def gather_in_plane(shard, planes, collective_id):
    dma = pltpu.SemaphoreType.DMA
    whole = pl.pallas_call(
        functools.partial(plane_gather_kernel, planes),
        out_shape=jax.ShapeDtypeStruct((planes, 2, 2, *shard.shape), shard.dtype),
        in_specs=[pl.BlockSpec(memory_space=pl.ANY)],
        out_specs=pl.BlockSpec(memory_space=pl.ANY),
        scratch_shapes=[
            dma((1,)),
            dma((planes,)),
            dma((planes,)),
            dma((planes, 2)),
            dma((planes, 2)),
            dma((planes, 2)),
        ],
        compiler_params=pltpu.CompilerParams(collective_id=collective_id, has_side_effects=True),
        cost_estimate=pl.CostEstimate(flops=0, bytes_accessed=200 * 2**20, transcendentals=0),
        name="gather_in_plane",
    )(shard)
    return whole.reshape(4 * planes * shard.shape[0], shard.shape[1])


def plane_scatter_kernel(planes, steps, rows, exchanged, partial_ref, *refs):
    packets, (sum_ref, *refs) = refs[:exchanged], refs[exchanged:]
    received, refs = refs[:exchanged], refs[exchanged:]
    own, from_core, from_x, from_line, load_sem, core_sems, x_sems, line_send, line_recv = refs[:9]
    core, x, z, to_core, to_x, line, line_devices = plane_places(planes)
    blk, y = lax.axis_index("blk"), lax.axis_index("pair")
    others = [lax.rem(blk + at, 4 * planes) for at in range(1, 4 * planes)]
    if exchanged:
        greet([(other, y) for other in others])
    else:
        greet([to_core, to_x] + line_devices[1:])

    def piece(step, by_x, plane):
        return partial_ref.at[:, by_x, plane, pl.ds(pl.multiple_of(step * rows, rows), rows)]

    def core_copy(step, by_x, plane):
        return remote(
            piece(step, by_x, plane),
            from_core.at[step, by_x],
            core_sems.at[0, step, by_x],
            core_sems.at[1, step, by_x],
            to_core,
        )

    def load(step, by_x):
        return pltpu.make_async_copy(
            piece(step, by_x, core), own.at[step, by_x], load_sem.at[step, by_x]
        )

    def x_copy(step):
        return remote(
            own.at[step, 1 - x], from_x.at[step], x_sems.at[0, step], x_sems.at[1, step], to_x
        )

    def line_copy(step, at):
        return remote(
            own.at[step, x, line[at][0]],
            from_line.at[step, z],
            line_send.at[step, at],
            line_recv.at[step, z],
            line_devices[at],
        )

    def start_loads(step):
        for by_x in (1 - x, x):
            core_copy(step, by_x, 1 - core).start()
            load(step, by_x).start()

    def add_core(step):
        for turn, by_x in enumerate((1 - x, x)):
            load(step, by_x).wait()
            core_copy(step, by_x, core).wait_recv()
            own[step, by_x] += from_core[step, by_x]
            if turn == 0:
                x_copy(step).start()

    def add_x(step):
        x_copy(step).wait_recv()
        own[step, x] += from_x[step]
        for at in range(1, planes):
            line_copy(step, at).start()

    def add_line(step):
        total = own[step, x, z].astype(jnp.float32)
        for spot, at in line[1:]:
            remote(
                own.at[step, x, spot],
                from_line.at[step, spot],
                line_send.at[step, at],
                line_recv.at[step, spot],
                line_devices[at],
            ).wait_recv()
            total = total + from_line[step, spot].astype(jnp.float32)
        sum_ref[pl.ds(pl.multiple_of(step * rows, rows), rows), :] = total.astype(sum_ref.dtype)

    start_loads(0)
    start_loads(1)
    swaps = []
    if exchanged:
        swap_own, swap_send, swap_recv = refs[9:]
        own_packet = pltpu.make_async_copy(packets[0].at[blk], received[0].at[blk], swap_own.at[0])
        own_packet.start()
        for at, other in enumerate(others):
            copy = remote(
                packets[0].at[other],
                received[0].at[blk],
                swap_send.at[at],
                swap_recv.at[blk],
                (other, y),
            )
            copy.start()
            swaps.append(copy)

    @pl.loop(0, steps + 2)
    def _(turn):
        @pl.when(turn < steps - 2)
        def _():
            start_loads(turn + 2)

        @pl.when(turn < steps)
        def _():
            add_core(turn)

        @pl.when((turn >= 1) & (turn < steps + 1))
        def _():
            add_x(turn - 1)

        @pl.when(turn >= 2)
        def _():
            add_line(turn - 2)

    @pl.loop(0, steps)
    def _(step):
        for by_x in range(2):
            core_copy(step, by_x, 1 - core).wait_send()
        x_copy(step).wait_send()
        for at in range(1, planes):
            line_copy(step, at).wait_send()

    if exchanged:
        own_packet.wait()
        for other in others:
            place = received[0].at[other]
            remote(place, place, swap_own.at[0], swap_recv.at[other], to_core).wait_recv()
        for copy in swaps:
            copy.wait_send()


def scatter_in_plane(partial, planes, collective_id, packets=()):
    exchanged = len(packets)
    shard_rows = partial.shape[0] // (4 * planes)
    width = partial.shape[1]
    rows = 16
    steps = shard_rows // rows
    dtype = partial.dtype
    dma = pltpu.SemaphoreType.DMA
    return pl.pallas_call(
        functools.partial(plane_scatter_kernel, planes, steps, rows, exchanged),
        out_shape=[jax.ShapeDtypeStruct((shard_rows, width), dtype)]
        + [jax.ShapeDtypeStruct(array.shape, array.dtype) for array in packets],
        in_specs=[pl.BlockSpec(memory_space=pl.ANY)] * (1 + exchanged),
        out_specs=[pl.BlockSpec(memory_space=pltpu.VMEM)]
        + [pl.BlockSpec(memory_space=pl.ANY)] * exchanged,
        scratch_shapes=[
            pltpu.VMEM((steps, 2, planes, rows, width), dtype),
            pltpu.VMEM((steps, 2, planes, rows, width), dtype),
            pltpu.VMEM((steps, planes, rows, width), dtype),
            pltpu.VMEM((steps, planes, rows, width), dtype),
            dma((steps, 2)),
            dma((2, steps, 2)),
            dma((2, steps)),
            dma((steps, planes)),
            dma((steps, planes)),
        ]
        + [dma((1,)), dma((4 * planes,)), dma((4 * planes,))] * exchanged,
        compiler_params=pltpu.CompilerParams(
            collective_id=collective_id, has_side_effects=True, vmem_limit_bytes=40 * 2**20
        ),
        cost_estimate=pl.CostEstimate(flops=0, bytes_accessed=200 * 2**20, transcendentals=0),
        name="scatter_in_plane",
    )(partial.reshape(planes, 2, 2, shard_rows, width), *packets)


def ffn_pack_kernel(gateup_ref, down_ref, packet_ref):
    live = pl.program_id(0) < FF // HEAD // 2

    @pl.when(live)
    def _():
        for at in range(2):
            columns = slice(at * HEAD, (at + 1) * HEAD)
            packet_ref[at, :, :HEAD] = gateup_ref[0, :, columns].astype(jnp.bfloat16)
            packet_ref[at, :, HEAD : 2 * HEAD] = gateup_ref[1, :, columns].astype(jnp.bfloat16)
            packet_ref[at, :, 2 * HEAD :] = down_ref[:, columns].astype(jnp.bfloat16)

    @pl.when(jnp.logical_not(live))
    def _():
        packet_ref[...] = jnp.zeros_like(packet_ref)


def ffn_packets(gateup, down, device_count):
    row_count = gateup.shape[1]
    last = FF // HEAD // 2 - 1
    return pl.pallas_call(
        ffn_pack_kernel,
        grid=(device_count // 2,),
        in_specs=[
            pl.BlockSpec((2, row_count, 2 * HEAD), lambda j: (0, 0, jnp.minimum(j, last))),
            pl.BlockSpec((row_count, 2 * HEAD), lambda j: (0, jnp.minimum(j, last))),
        ],
        out_specs=pl.BlockSpec((2, row_count, 3 * HEAD), lambda j: (j, 0, 0)),
        out_shape=jax.ShapeDtypeStruct((device_count, row_count, 3 * HEAD), jnp.bfloat16),
        cost_estimate=pl.CostEstimate(flops=0, bytes_accessed=14 * 2**20, transcendentals=0),
        name="ffn_packets",
    )(gateup, down)


def attn_pack_kernel(qkv_ref, out_ref, packet_ref):
    j = pl.program_id(0)

    @pl.when(j < (H + 2) // 2)
    def _():
        for at in range(2):
            packet_ref[at] = qkv_ref[:, at * HEAD : (at + 1) * HEAD].astype(jnp.bfloat16)

    @pl.when((j >= (H + 2) // 2) & (j < H + 1))
    def _():
        for at in range(2):
            packet_ref[at] = out_ref[:, at * HEAD : (at + 1) * HEAD].astype(jnp.bfloat16)

    @pl.when(j >= H + 1)
    def _():
        packet_ref[...] = jnp.zeros_like(packet_ref)


def attn_packets(qkv, out, device_count):
    row_count = qkv.shape[0]
    qkv_last, out_last = (H + 2) // 2 - 1, H // 2 - 1
    return pl.pallas_call(
        attn_pack_kernel,
        grid=(device_count // 2,),
        in_specs=[
            pl.BlockSpec((row_count, 2 * HEAD), lambda j: (0, jnp.minimum(j, qkv_last))),
            pl.BlockSpec((row_count, 2 * HEAD), lambda j: (0, jnp.clip(j - qkv_last - 1, 0, out_last))),
        ],
        out_specs=pl.BlockSpec((2, row_count, HEAD), lambda j: (j, 0, 0)),
        out_shape=jax.ShapeDtypeStruct((device_count, row_count, HEAD), jnp.bfloat16),
        cost_estimate=pl.CostEstimate(flops=0, bytes_accessed=4 * 2**20, transcendentals=0),
        name="attn_packets",
    )(qkv, out)


def turn_kernel(grads_ref, others_ref, mom_ref, result_ref, current_ref):
    grads = grads_ref[...] + others_ref[...].astype(jnp.float32)
    result_ref[:, :HEAD] = grads.astype(jnp.bfloat16)
    moment = momentum_decay * mom_ref[...].astype(jnp.float32) + grads
    moment = moment.astype(jnp.bfloat16).astype(jnp.float32)
    norm_size = jnp.sqrt(jnp.sum(moment * moment, keepdims=True))
    current_ref[...] = (moment / (norm_size + eps_pieces)).T.astype(jnp.bfloat16)

    @pl.loop(0, NS_STEPS)
    def _(sweep_index):
        current = current_ref[...]
        gram_matrix = lax.dot_general(
            current, current, (((1,), (1,)), ((), ())), preferred_element_type=jnp.float32
        ).astype(jnp.bfloat16)
        square = jnp.dot(gram_matrix, gram_matrix, preferred_element_type=jnp.float32)
        mixing = (ns_second * gram_matrix.astype(jnp.float32) + ns_third * square).astype(
            jnp.bfloat16
        )
        turned = jnp.dot(mixing, current, preferred_element_type=jnp.float32)
        current_ref[...] = (ns_first * current.astype(jnp.float32) + turned).astype(jnp.bfloat16)

    result_ref[:, HEAD:] = current_ref[...].astype(jnp.float32).T.astype(jnp.bfloat16)


def orthogonalize(grads, others, moms):
    depth, columns = grads.shape
    block = pl.BlockSpec((depth, HEAD), lambda j: (0, j))
    pieces = columns // HEAD
    return pl.pallas_call(
        turn_kernel,
        grid=(pieces,),
        in_specs=[block] * 3,
        out_specs=pl.BlockSpec((depth, 2 * HEAD), lambda j: (0, j)),
        out_shape=jax.ShapeDtypeStruct((depth, 2 * columns), jnp.bfloat16),
        scratch_shapes=[pltpu.VMEM((HEAD, depth), jnp.bfloat16)],
        cost_estimate=pl.CostEstimate(
            flops=pieces * 20 * depth * HEAD * HEAD, bytes_accessed=12 * depth * columns, transcendentals=0
        ),
        compiler_params=pltpu.CompilerParams(vmem_limit_bytes=48 * 2**20),
        name="orthogonalize",
    )(grads, others, moms)


def update(rate, weight, mom, grad, turn):
    moment = momentum_decay * mom + grad.astype(jnp.float32)
    new = (1.0 - weight_shrink) * weight - rate * turn.astype(jnp.float32)
    return new, moment, new.astype(jnp.bfloat16)


def ffn_update_kernel(
    packet_ref, w_gateup_ref, mom_gateup_ref, w_down_ref, mom_down_ref, *results
):
    for at in range(packet_ref.shape[0]):
        columns = slice(at * HEAD, (at + 1) * HEAD)
        for part in range(3):
            spot = (part, slice(None), columns) if part < 2 else (slice(None), columns)
            weight_ref, mom_ref = (
                (w_gateup_ref, mom_gateup_ref) if part < 2 else (w_down_ref, mom_down_ref)
            )
            start = 2 * part * HEAD
            values = update(
                matrix_rate,
                weight_ref[spot],
                mom_ref[spot],
                packet_ref[at, :, start : start + HEAD],
                packet_ref[at, :, start + HEAD : start + 2 * HEAD],
            )
            for ref, value in zip(results[:3] if part < 2 else results[3:], values):
                ref[spot] = value


def ffn_update(packets, w_gateup, mom_gateup, w_down, mom_down):
    row_count = w_gateup.shape[1]
    wide = 3
    packet = pl.BlockSpec((wide, row_count, 6 * HEAD), lambda j: (j, 0, 0))
    gateup = pl.BlockSpec((2, row_count, wide * HEAD), lambda j: (0, 0, j))
    down = pl.BlockSpec((row_count, wide * HEAD), lambda j: (0, j))
    dtypes = (jnp.float32, jnp.float32, jnp.bfloat16)
    return pl.pallas_call(
        ffn_update_kernel,
        grid=(FF // HEAD // wide,),
        in_specs=[packet, gateup, gateup, down, down],
        out_specs=[gateup] * 3 + [down] * 3,
        out_shape=[jax.ShapeDtypeStruct(w_gateup.shape, dtype) for dtype in dtypes]
        + [jax.ShapeDtypeStruct(w_down.shape, dtype) for dtype in dtypes],
        cost_estimate=pl.CostEstimate(flops=0, bytes_accessed=50 * 2**20, transcendentals=0),
        compiler_params=pltpu.CompilerParams(vmem_limit_bytes=48 * 2**20),
        name="ffn_update",
    )(packets, w_gateup, mom_gateup, w_down, mom_down)


def attn_update_kernel(rate, packet_ref, w_ref, mom_ref, *results):
    for at in range(2):
        columns = slice(at * HEAD, (at + 1) * HEAD)
        values = update(
            rate,
            w_ref[:, columns],
            mom_ref[:, columns],
            packet_ref[at, :, :HEAD],
            packet_ref[at, :, HEAD:],
        )
        for ref, value in zip(results, values):
            ref[:, columns] = value


def attn_update(rate, offset, packets, weight, mom):
    row_count = packets.shape[1]
    packet = pl.BlockSpec((2, row_count, 2 * HEAD), lambda j: (j + offset // 2, 0, 0))
    block = pl.BlockSpec((row_count, 2 * HEAD), lambda j: (0, j))
    return pl.pallas_call(
        functools.partial(attn_update_kernel, rate),
        grid=(weight.shape[1] // HEAD // 2,),
        in_specs=[packet, block, block],
        out_specs=[block] * 3,
        out_shape=[
            jax.ShapeDtypeStruct(weight.shape, dtype)
            for dtype in (jnp.float32, jnp.float32, jnp.bfloat16)
        ],
        cost_estimate=pl.CostEstimate(flops=0, bytes_accessed=6 * 2**20, transcendentals=0),
        name="attn_update",
    )(packets, weight, mom)


def two_heads(ref):
    return jnp.concatenate([ref[:, :HEAD], ref[:, HEAD:]], axis=0)


def visible(tokens, first_token, shape, query_axis):
    query = lax.rem(lax.broadcasted_iota(jnp.int32, shape, query_axis), tokens)
    key = lax.broadcasted_iota(jnp.int32, shape, 1 - query_axis)
    distance = query + WINDOW - key
    return (distance >= 0) & (distance < WINDOW) & (first_token - WINDOW + key >= 0)


def attend_kernel(first_ref, queries_ref, kv_ref, mixed_ref, log_total_ref):
    tokens = queries_ref.shape[0]
    raw = lax.dot_general(
        two_heads(queries_ref),
        kv_ref[:, :HEAD],
        (((1,), (1,)), ((), ())),
        preferred_element_type=jnp.float32,
    )
    allowed = visible(tokens, first_ref[0], raw.shape, 0)
    scores = jnp.where(allowed, raw * HEAD ** (-0.5), masked_score)
    top_score = jnp.max(scores, axis=-1, keepdims=True)
    expo = jnp.exp(scores - top_score)
    total = jnp.sum(expo, axis=-1, keepdims=True)
    probs = (expo / total).astype(jnp.bfloat16)
    mixed = jnp.dot(probs, kv_ref[:, HEAD:], preferred_element_type=jnp.float32)
    mixed_ref[:, :HEAD] = mixed[:tokens].astype(jnp.bfloat16)
    mixed_ref[:, HEAD:] = mixed[tokens:].astype(jnp.bfloat16)
    log_total_ref[0] = jnp.broadcast_to(top_score + jnp.log(total), log_total_ref.shape[1:])


def attend(first_token, qkv, kv_window):
    tokens = qkv.shape[0]
    span = kv_window.shape[0]
    pairs = H // 2
    return pl.pallas_call(
        attend_kernel,
        grid=(pairs,),
        in_specs=[
            pl.BlockSpec(memory_space=pltpu.SMEM),
            pl.BlockSpec((tokens, 2 * HEAD), lambda j: (0, j)),
            pl.BlockSpec((span, 2 * HEAD), lambda j: (0, 0)),
        ],
        out_specs=[
            pl.BlockSpec((tokens, 2 * HEAD), lambda j: (0, j)),
            pl.BlockSpec((1, 2 * tokens, 128), lambda j: (j, 0, 0)),
        ],
        out_shape=[
            jax.ShapeDtypeStruct((tokens, H * HEAD), jnp.bfloat16),
            jax.ShapeDtypeStruct((pairs, 2 * tokens, 128), jnp.float32),
        ],
        cost_estimate=pl.CostEstimate(
            flops=4 * H * tokens * span * HEAD,
            bytes_accessed=4 * 2**20,
            transcendentals=H * tokens * span,
        ),
        compiler_params=pltpu.CompilerParams(vmem_limit_bytes=48 * 2**20),
        name="attend",
    )(first_token, qkv, kv_window)


def attend_back_kernel(
    first_ref, queries_ref, grads_ref, log_total_ref, kv_ref, grad_query_ref, grad_kv_ref, sums_ref
):
    tokens = queries_ref.shape[0]
    score_scale = HEAD ** (-0.5)
    keys, values = kv_ref[:, :HEAD], kv_ref[:, HEAD:]
    queries, grads = two_heads(queries_ref), two_heads(grads_ref)

    def against(left, right):
        return lax.dot_general(
            left, right, (((1,), (1,)), ((), ())), preferred_element_type=jnp.float32
        )

    raw = against(keys, queries)
    allowed = visible(tokens, first_ref[0], raw.shape, 1)
    scores = jnp.where(allowed, raw * score_scale, masked_score)
    log_total = log_total_ref[0].T[:1]
    probs = jnp.exp(scores - log_total)
    grad_probs = against(values, grads)
    row_delta = jnp.sum(probs * grad_probs, axis=0, keepdims=True)
    grad_raw = (probs * (grad_probs - row_delta) * score_scale).astype(jnp.bfloat16)
    grad_query = lax.dot_general(
        grad_raw, keys, (((0,), (0,)), ((), ())), preferred_element_type=jnp.float32
    )
    grad_query_ref[:, :HEAD] = grad_query[:tokens].astype(jnp.bfloat16)
    grad_query_ref[:, HEAD:] = grad_query[tokens:].astype(jnp.bfloat16)

    @pl.when(pl.program_id(0) == 0)
    def _():
        sums_ref[...] = jnp.zeros_like(sums_ref)

    sums_ref[:, :HEAD] += jnp.dot(grad_raw, queries, preferred_element_type=jnp.float32)
    sums_ref[:, HEAD:] += jnp.dot(
        probs.astype(jnp.bfloat16), grads, preferred_element_type=jnp.float32
    )

    @pl.when(pl.program_id(0) == pl.num_programs(0) - 1)
    def _():
        grad_kv_ref[...] = sums_ref[...].astype(jnp.bfloat16)


def attend_back(first_token, qkv, grads, log_total, kv_window):
    tokens = qkv.shape[0]
    span = kv_window.shape[0]
    heads = pl.BlockSpec((tokens, 2 * HEAD), lambda j: (0, j))
    window = pl.BlockSpec((span, 2 * HEAD), lambda j: (0, 0))
    return pl.pallas_call(
        attend_back_kernel,
        grid=(H // 2,),
        in_specs=[
            pl.BlockSpec(memory_space=pltpu.SMEM),
            heads,
            heads,
            pl.BlockSpec((1, 2 * tokens, 128), lambda j: (j, 0, 0)),
            window,
        ],
        out_specs=[heads, window],
        out_shape=[
            jax.ShapeDtypeStruct((tokens, H * HEAD), jnp.bfloat16),
            jax.ShapeDtypeStruct((span, 2 * HEAD), jnp.bfloat16),
        ],
        scratch_shapes=[pltpu.VMEM((span, 2 * HEAD), jnp.float32)],
        cost_estimate=pl.CostEstimate(
            flops=10 * H * tokens * span * HEAD,
            bytes_accessed=8 * 2**20,
            transcendentals=H * tokens * span,
        ),
        compiler_params=pltpu.CompilerParams(vmem_limit_bytes=48 * 2**20),
        name="attend_back",
    )(first_token, qkv, grads, log_total, kv_window)


def rms_scale(stream, gain_row):
    mean_square = jnp.mean(stream * stream, axis=-1, keepdims=True)
    return stream * lax.rsqrt(mean_square + eps_norm) * gain_row


def gelu_product(gate_part, up_part):
    return jax.nn.gelu(gate_part, approximate=True) * up_part


def on_device(
    tokens_in,
    cotangent,
    w_qkv,
    w_out,
    w_gateup,
    w_down,
    gains,
    mom_qkv,
    mom_out,
    mom_gateup,
    mom_down,
    mom_gains,
):
    everyone = ("blk", "pair")
    bf16 = jnp.bfloat16
    f32 = jnp.float32
    blk_count = lax.axis_size("blk")
    pair_count = lax.axis_size("pair")
    device_count = blk_count * pair_count
    block_at = lax.axis_index("blk")
    half_at = lax.axis_index("pair")
    me = block_at * pair_count + half_at
    local_rows, width = tokens_in.shape
    share_rows = w_qkv.shape[0]
    span = WINDOW + local_rows
    token_count = local_rows * device_count
    large = token_count * width * 2 > 48 * 2**20
    planes = blk_count // 4

    def after(value, earlier):
        return lax.optimization_barrier((value, earlier))[0] if large else value

    def exchange(packets, axes=everyone):
        return lax.all_to_all(packets, axes, split_axis=0, concat_axis=0, tiled=True)

    def swap(shard):
        return lax.ppermute(shard, "pair", [(0, 1), (1, 0)])

    def hold(value, *earlier):
        return value if large else lax.optimization_barrier((value, earlier))[0]

    def gather_all(shards, collective_id, packets=()):
        if large:
            wholes = [lax.all_gather(shard, everyone, axis=0, tiled=True) for shard in shards]
            return wholes + [exchange(array) for array in packets]
        return gather_by_axes(shards, planes, collective_id, packets)

    def scatter_all(partial, collective_id):
        if large:
            return lax.psum_scatter(partial, everyone, scatter_dimension=0, tiled=True)
        return scatter_by_axes(partial, planes, collective_id)

    def gather_plane(shard):
        return lax.all_gather(shard, "blk", axis=0, tiled=True)

    def scatter_plane(partial, collective_id, packets=()):
        if large:
            part = lax.psum_scatter(partial, "blk", scatter_dimension=0, tiled=True)
            return [part] + [exchange(array, "blk") for array in packets]
        return scatter_in_plane(partial, planes, collective_id, packets)

    stream = tokens_in.astype(f32)
    padded_gains = jnp.pad(gains.astype(bf16), ((0, 14), (0, 128 - share_rows)))
    full_qkv, full_gains, full_out, ffn_weights = gather_all(
        [w_qkv.astype(bf16), padded_gains, w_out.T.astype(bf16)],
        1,
        [ffn_packets(w_gateup, w_down.T, device_count)],
    )
    ffn_weights = ffn_weights.reshape(width, 3 * HEAD)
    full_gains = full_gains.reshape(device_count, 16, 128)[:, :2, :share_rows].astype(f32)
    gain_attn = full_gains[:, 0].reshape(width)
    gain_mlp = full_gains[:, 1].reshape(width)
    normed_attn_f, norm_back_attn = jax.vjp(rms_scale, stream, gain_attn)
    normed_attn = normed_attn_f.astype(bf16)
    qkv = jnp.dot(normed_attn, full_qkv, preferred_element_type=f32).astype(bf16)
    (kv_all,) = gather_all([qkv[:, H * HEAD :]], 2)
    kv_window = lax.dynamic_slice_in_dim(
        jnp.pad(kv_all, ((WINDOW, 0), (0, 0))), me * local_rows, span, 0
    )
    first_token = (me * local_rows).astype(jnp.int32).reshape(1)
    pair_weights = [ffn_weights, swap(hold(ffn_weights, kv_all))]
    gates, ups, downs = (
        [weights[:, part * HEAD : (part + 1) * HEAD] for weights in pair_weights]
        for part in range(3)
    )
    pair_gateup = jnp.concatenate(gates + ups, axis=1)
    pair_down = jnp.concatenate(downs, axis=1)
    cotangent_plane = gather_plane(hold(cotangent, kv_all))

    mixed, log_total = attend(first_token, qkv, kv_window)
    resid = stream + jnp.einsum("tc,dc->td", mixed, full_out, preferred_element_type=f32)

    normed_mlp_f, norm_back_mlp = jax.vjp(rms_scale, resid, gain_mlp)
    normed_mlp = normed_mlp_f.astype(bf16)
    if large:
        normed_mlp_plane = gather_plane(normed_mlp)
    else:
        normed_mlp_plane = gather_in_plane(normed_mlp, planes, 3)
    plane_rows = blk_count * local_rows
    both_parts = jnp.dot(normed_mlp_plane, pair_gateup, preferred_element_type=f32)
    pair_width = pair_count * HEAD
    hidden_f, geglu_back = jax.vjp(
        gelu_product, both_parts[:, :pair_width], both_parts[:, pair_width:]
    )
    hidden = hidden_f.astype(bf16)
    grad_hidden = jnp.dot(cotangent_plane, pair_down, preferred_element_type=f32)
    grad_gate, grad_up = geglu_back(grad_hidden)
    grad_gateup = jnp.concatenate([grad_gate.astype(bf16), grad_up.astype(bf16)], axis=1)
    grad_normed_part = jnp.einsum("tf,df->td", grad_gateup, pair_gateup, preferred_element_type=f32)
    (grad_normed_mlp,) = scatter_plane(grad_normed_part.astype(bf16), 4)
    grad_normed_mlp = grad_normed_mlp.astype(f32)

    def ffn_gradient(columns):
        gateup_right = jnp.concatenate(
            [grad_gate[:, columns].astype(bf16), grad_up[:, columns].astype(bf16)], axis=1
        )
        down_right = hidden[:, columns]
        return jnp.concatenate(
            [
                jnp.einsum("td,tf->df", normed_mlp_plane, gateup_right, preferred_element_type=f32),
                jnp.einsum("td,tf->df", cotangent_plane, down_right, preferred_element_type=f32),
            ],
            axis=1,
        )

    ffn_others = swap(ffn_gradient(slice(HEAD, 2 * HEAD)).astype(bf16))
    ffn_grads = ffn_gradient(slice(0, HEAD))
    ffn_moms = exchange(hold(ffn_packets(mom_gateup, mom_down.T, device_count), normed_mlp_plane))
    ffn_moms = ffn_moms.reshape(width, 3 * HEAD)
    ffn_results = orthogonalize(ffn_grads, ffn_others, ffn_moms)
    ffn_results_back = exchange(ffn_results.reshape(device_count, share_rows, 6 * HEAD))

    resid_part, gain_grad_mlp = norm_back_mlp(hold(grad_normed_mlp, ffn_results))
    grad_resid = cotangent.astype(f32) + resid_part
    grad_proj = grad_resid.astype(bf16)
    grad_mixed = jnp.dot(grad_proj, full_out, preferred_element_type=f32).astype(bf16)
    grad_query, grad_kv = attend_back(first_token, qkv, grad_mixed, log_total, kv_window)
    grad_kv_all = lax.dynamic_update_slice_in_dim(
        jnp.zeros((WINDOW + token_count, 2 * HEAD), bf16), grad_kv, me * local_rows, 0
    )[WINDOW:]
    grad_qkv = jnp.concatenate(
        [grad_query, scatter_all(grad_kv_all, 5)], axis=1
    )
    grad_normed_attn = jnp.einsum("tc,dc->td", grad_qkv, full_qkv, preferred_element_type=f32)
    stream_part, gain_grad_attn = norm_back_attn(grad_normed_attn)
    input_grad = grad_resid + stream_part

    attn_rights = jnp.concatenate([grad_qkv, mixed], axis=1)
    used = attn_rights.shape[1] // pair_width
    attn_rights = attn_rights.reshape(local_rows, used, pair_width).transpose(1, 0, 2)
    attn_rights = jnp.pad(attn_rights, ((0, blk_count - used), (0, 0), (0, 0)))
    attn_rights = hold(attn_rights, ffn_results_back)
    branch_part = jnp.einsum(
        "tf,df->td", after(hidden, grad_normed_mlp), pair_down, preferred_element_type=f32
    )
    branch, attn_rights = scatter_plane(branch_part.astype(bf16), 6, [attn_rights])
    attn_rights = attn_rights.reshape(plane_rows, pair_width)
    block_output = (resid + branch.astype(f32)).astype(bf16)
    normed_attn_plane = gather_plane(after(hold(normed_attn, normed_mlp_plane), (ffn_grads, block_output)))
    grad_proj_plane = gather_plane(after(grad_proj, (ffn_grads, block_output)))

    def attn_gradient(lefts):
        return jnp.einsum("td,tf->df", lefts, attn_rights, preferred_element_type=f32)

    attn_grads = lax.cond(
        block_at < (H + 2) // pair_count,
        lambda: attn_gradient(normed_attn_plane),
        lambda: attn_gradient(grad_proj_plane),
    )
    attn_others = swap(
        lax.dynamic_slice_in_dim(attn_grads, (1 - half_at) * HEAD, HEAD, 1).astype(bf16)
    )
    attn_grads = lax.dynamic_slice_in_dim(attn_grads, half_at * HEAD, HEAD, 1)
    attn_moms = exchange(hold(attn_packets(mom_qkv, mom_out.T, device_count), normed_mlp_plane))
    attn_moms = attn_moms.reshape(width, HEAD)
    updated_ffn = ffn_update(ffn_results_back, w_gateup, mom_gateup, w_down.T, mom_down.T)
    attn_results = orthogonalize(attn_grads, hold(attn_others, updated_ffn[0]), attn_moms)
    attn_results_back = exchange(attn_results.reshape(device_count, share_rows, 2 * HEAD))

    gain_grads = lax.psum(jnp.stack([gain_grad_attn, gain_grad_mlp], axis=0), everyone)
    gain_share = lax.dynamic_slice_in_dim(gain_grads, me * share_rows, share_rows, 1)

    updated_qkv = attn_update(matrix_rate, 0, attn_results_back, w_qkv, mom_qkv)
    updated_out = attn_update(output_rate, H + 2, attn_results_back, w_out.T, mom_out.T)
    moment_gains = momentum_decay * mom_gains + gain_share
    new_gains = gains - gain_rate * moment_gains
    return (
        block_output,
        input_grad,
        *updated_qkv,
        *(result.T for result in updated_out),
        *updated_ffn[:3],
        *(result.T for result in updated_ffn[3:]),
        new_gains,
        moment_gains,
        new_gains.astype(bf16),
    )


def solution(mesh):
    placed = (
        P(("blk", "pair"), None),
        P(("blk", "pair"), None),
        P(("blk", "pair"), None),
        P(None, ("blk", "pair")),
        P(None, ("blk", "pair"), None),
        P(None, ("blk", "pair")),
        P(None, ("blk", "pair")),
        P(("blk", "pair"), None),
        P(None, ("blk", "pair")),
        P(None, ("blk", "pair"), None),
        P(None, ("blk", "pair")),
        P(None, ("blk", "pair")),
    )
    return jax.shard_map(
        on_device,
        mesh=mesh,
        in_specs=placed,
        out_specs=(
            P(("blk", "pair"), None),
            P(("blk", "pair"), None),
            P(("blk", "pair"), None),
            P(("blk", "pair"), None),
            P(("blk", "pair"), None),
            P(None, ("blk", "pair")),
            P(None, ("blk", "pair")),
            P(None, ("blk", "pair")),
            P(None, ("blk", "pair"), None),
            P(None, ("blk", "pair"), None),
            P(None, ("blk", "pair"), None),
            P(None, ("blk", "pair")),
            P(None, ("blk", "pair")),
            P(None, ("blk", "pair")),
            P(None, ("blk", "pair")),
            P(None, ("blk", "pair")),
            P(None, ("blk", "pair")),
        ),
        check_vma=False,
    )
```

```python
import functools
from typing import NamedTuple

import jax
import jax.numpy as jnp
from jax import lax
from jax.experimental import pallas as pl
from jax.experimental.pallas import tpu as pltpu
from jax.sharding import PartitionSpec as P

H = 10
HEAD = 256
FF = 7680
WINDOW = 2048
NS_STEPS = 5


eps_norm = 1e-06
eps_pieces = 1e-07
ns_first = 3.4445
ns_second = -4.775
ns_third = 2.0315
momentum_decay = 0.95
matrix_rate = 0.5
output_rate = 10.0
gain_rate = 0.001
weight_shrink = 0.001
masked_score = -1e30
MESH = pl.DeviceIdType.MESH


def position():
    blk, y = lax.axis_index("blk"), lax.axis_index("pair")
    return blk, lax.div(blk, 4), lax.rem(lax.div(blk, 2), 2), lax.rem(blk, 2), y


def greet(devices):
    barrier = pltpu.get_barrier_semaphore()
    for device in devices:
        pl.semaphore_signal(barrier, inc=1, device_id=device, device_id_type=MESH)
    pl.semaphore_wait(barrier, len(devices))


def remote(source, target, send_sem, recv_sem, device):
    return pltpu.make_async_remote_copy(
        src_ref=source,
        dst_ref=target,
        send_sem=send_sem,
        recv_sem=recv_sem,
        device_id=device,
        device_id_type=MESH,
    )


class Exchange(NamedTuple):
    packets: jax.Array
    in_plane: bool
    sources: int
    targets: int


def others_of(planes, in_plane):
    blk, _, _, _, y = position()
    if in_plane:
        count, here = 4 * planes, blk
    else:
        count, here = 8 * planes, 2 * blk + y
    places = [lax.rem(here + at, count) for at in range(1, count)]
    if in_plane:
        return here, [(place, (place, y)) for place in places]
    return here, [(place, (lax.div(place, 2), lax.rem(place, 2))) for place in places]


def greeted(planes, specs, nearby):
    if any(not in_plane for in_plane, _, _ in specs):
        return [device for _, device in others_of(planes, False)[1]]
    return nearby


def start_exchange(planes, spec, packets, received, sems):
    in_plane, sources, targets = spec
    own_sem, send_sems, recv_sems = sems
    here, others = others_of(planes, in_plane)

    def copy(at, place, device):
        return remote(
            packets.at[place], received.at[here], send_sems.at[at], recv_sems.at[here], device
        )

    def arrival(place, device):
        spot = received.at[place]
        return remote(spot, spot, own_sem.at[0], recv_sems.at[place], device)

    def own():
        return pltpu.make_async_copy(packets.at[here], received.at[here], own_sem.at[0])

    @pl.when((here < sources) & (here < targets))
    def _():
        own().start()

    for at, (place, device) in enumerate(others):

        @pl.when((here < sources) & (place < targets))
        def _():
            copy(at, place, device).start()

    def finish():
        @pl.when((here < sources) & (here < targets))
        def _():
            own().wait()

        for at, (place, device) in enumerate(others):

            @pl.when((place < sources) & (here < targets))
            def _():
                arrival(place, device).wait_recv()

            @pl.when((here < sources) & (place < targets))
            def _():
                copy(at, place, device).wait_send()

    return finish


def exchange_sems(exchanges):
    dma = pltpu.SemaphoreType.DMA
    return [
        dma((count,))
        for exchange in exchanges
        for count in (1, exchange.packets.shape[0], exchange.packets.shape[0])
    ]


def exchange_specs(exchanges):
    return tuple((each.in_plane, each.sources, each.targets) for each in exchanges)


def same_shape(arrays):
    return [jax.ShapeDtypeStruct(array.shape, array.dtype) for array in arrays]


def communicate(kernel, operands, exchanges, outputs, scratch, collective_id, cost, name, out_spec=pl.ANY, **options):
    packets = [each.packets for each in exchanges]
    any_spec = pl.BlockSpec(memory_space=pl.ANY)
    return pl.pallas_call(
        kernel,
        out_shape=outputs + same_shape(packets),
        in_specs=[any_spec] * (len(operands) + len(packets)),
        out_specs=[pl.BlockSpec(memory_space=out_spec)] * len(outputs) + [any_spec] * len(packets),
        scratch_shapes=scratch + exchange_sems(exchanges),
        compiler_params=pltpu.CompilerParams(
            collective_id=collective_id, has_side_effects=True, **options
        ),
        cost_estimate=pl.CostEstimate(flops=0, bytes_accessed=cost * 2**20, transcendentals=0),
        name=name,
    )(*operands, *packets)


def split_refs(refs, inputs, outputs, specs):
    riders = len(specs)
    ins, refs = refs[: inputs + riders], refs[inputs + riders :]
    outs, refs = refs[: outputs + riders], refs[outputs + riders :]
    scratch = refs[: len(refs) - 3 * riders]
    sems = refs[len(refs) - 3 * riders :]
    rides = [
        (spec, ins[inputs + i], outs[outputs + i], sems[3 * i : 3 * i + 3])
        for i, spec in enumerate(specs)
    ]
    return ins[:inputs], outs[:outputs], scratch, rides


def start_rides(planes, rides):
    return [start_exchange(planes, *ride) for ride in rides]


def exchange_kernel(planes, specs, *refs):
    _, _, _, rides = split_refs(refs, 0, 0, specs)
    greet(greeted(planes, specs, []))
    for finish in start_rides(planes, rides):
        finish()


def exchange_now(exchanges, planes, collective_id):
    specs = exchange_specs(exchanges)
    kernel = functools.partial(exchange_kernel, planes, specs)
    return communicate(kernel, [], exchanges, [], [], collective_id, 100, "exchange_now")


def gather_kernel(planes, count, whole_slice, specs, *refs):
    shards, wholes, scratch, rides = split_refs(refs, count, count, specs)
    own_sem, line_send, second_send, first_send, core_send, recv, core_recv = scratch
    blk, z, x, core, y = position()
    firsts = 2 if whole_slice else 1
    to_core = (blk + 1 - 2 * core, y)
    if whole_slice:
        first = y * (1 - core) + x * core
        second = x * (1 - core) + y * core
        first_device = (blk + core * (2 - 4 * x), y + (1 - core) * (1 - 2 * y))
        second_device = (blk + (1 - core) * (2 - 4 * x), y + core * (1 - 2 * y))
    else:
        first, second = 0, x
        first_device, second_device = None, (blk + 2 - 4 * x, y)
    line = [(blk + 4 * (lax.rem(z + at, planes) - z), y) for at in range(1, planes)]
    nearby = [to_core, second_device] + [first_device] * whole_slice + line
    greet(greeted(planes, specs, nearby))

    def slot(whole, spot, by_first, by_second, plane):
        if whole_slice:
            by_x = (1 - plane) * by_second + plane * by_first
            by_y = (1 - plane) * by_first + plane * by_second
            return whole.at[spot, by_x, plane, by_y]
        return whole.at[spot, by_second, plane]

    def arrive(i, spot, by_first, by_second):
        here = slot(wholes[i], spot, by_first, by_second, core)
        remote(here, here, own_sem.at[0], recv.at[i, spot, by_first, by_second], to_core).wait_recv()

    def up(i, source, spot):
        target = slot(wholes[i], spot, first, second, core)
        device = (blk + 4, y)
        return remote(source, target, line_send.at[0, i, spot], recv.at[i, spot, first, second], device)

    def down(i, source, spot):
        target = slot(wholes[i], spot, first, second, core)
        device = (blk - 4, y)
        return remote(source, target, line_send.at[1, i, spot], recv.at[i, spot, first, second], device)

    def onward(i, source, spot):
        target = slot(wholes[i], spot, first, second, core)
        arrived = recv.at[i, spot, first, second]
        yield remote(source, target, second_send.at[i, spot], arrived, second_device)
        if whole_slice:
            yield remote(source, target, first_send.at[i, spot, 0], arrived, first_device)
        yield remote(
            source, target, core_send.at[i, spot, 0, 0], core_recv.at[i, spot, first, second], to_core
        )

    def after_second(i, spot):
        here = slot(wholes[i], spot, first, 1 - second, core)
        if whole_slice:
            yield remote(
                here, here, first_send.at[i, spot, 1], recv.at[i, spot, first, 1 - second], first_device
            )
        yield remote(
            here, here, core_send.at[i, spot, 0, 1], core_recv.at[i, spot, first, 1 - second], to_core
        )

    def after_first(i, spot, turn):
        by_second = second if turn == 0 else 1 - second
        here = slot(wholes[i], spot, 1 - first, by_second, core)
        return remote(
            here, here, core_send.at[i, spot, 1, turn], core_recv.at[i, spot, 1 - first, by_second], to_core
        )

    def line_steps():
        for far in range(1, planes):
            yield z - far, z >= far, up, z < planes - 1
            yield z + far, z < planes - far, down, z > 0

    own_copies = []
    for i in range(count):
        copy = pltpu.make_async_copy(
            shards[i], slot(wholes[i], z, first, second, core), own_sem.at[1 + i]
        )
        copy.start()
        own_copies.append(copy)

        @pl.when(z < planes - 1)
        def _():
            up(i, shards[i], z).start()

        @pl.when(z > 0)
        def _():
            down(i, shards[i], z).start()

        for copy in onward(i, shards[i], z):
            copy.start()
    finishes = start_rides(planes, rides)
    for i in range(count):
        arrive(i, z, first, 1 - second)
        for copy in after_second(i, z):
            copy.start()
    for spot, there, direction, further in line_steps():

        @pl.when(there)
        def _():
            for i in range(count):
                here = slot(wholes[i], spot, first, second, core)
                arrive(i, spot, first, second)

                @pl.when(further)
                def _():
                    direction(i, here, spot).start()

                for copy in onward(i, here, spot):
                    copy.start()
            for i in range(count):
                arrive(i, spot, first, 1 - second)
                for copy in after_second(i, spot):
                    copy.start()

    spots = [lax.rem(z + at, planes) for at in range(planes)]
    if whole_slice:
        for spot in spots:
            for turn in range(2):
                for i in range(count):
                    arrive(i, spot, 1 - first, second if turn == 0 else 1 - second)
                    after_first(i, spot, turn).start()
    for copy in own_copies:
        copy.wait()
    for i in range(count):
        for spot in range(planes):
            for by_first in range(firsts):
                for by_second in range(2):
                    there = slot(wholes[i], spot, by_first, by_second, 1 - core)
                    arrived = core_recv.at[i, spot, by_first, by_second]
                    remote(there, there, own_sem.at[0], arrived, to_core).wait_recv()
    for finish in finishes:
        finish()
    for i in range(count):

        @pl.when(z < planes - 1)
        def _():
            up(i, shards[i], z).wait_send()

        @pl.when(z > 0)
        def _():
            down(i, shards[i], z).wait_send()

        for spot, there, direction, further in line_steps():

            @pl.when(there & further)
            def _():
                direction(i, shards[i], spot).wait_send()

        for spot in spots:
            for copy in onward(i, shards[i], spot):
                copy.wait_send()
            for copy in after_second(i, spot):
                copy.wait_send()
            for turn in range(2 * (firsts - 1)):
                after_first(i, spot, turn).wait_send()


def gather_now(shards, planes, whole_slice, collective_id, exchanges=()):
    count = len(shards)
    firsts = 2 if whole_slice else 1
    specs = exchange_specs(exchanges)
    dma = pltpu.SemaphoreType.DMA
    grid = (planes, 2, 2, 2) if whole_slice else (planes, 2, 2)
    results = communicate(
        functools.partial(gather_kernel, planes, count, whole_slice, specs),
        list(shards),
        exchanges,
        [jax.ShapeDtypeStruct((*grid, *shard.shape), shard.dtype) for shard in shards],
        [
            dma((count + 1,)),
            dma((2, count, planes)),
            dma((count, planes)),
            dma((count, planes, 2)),
            dma((count, planes, 2, 2)),
            dma((count, planes, firsts, 2)),
            dma((count, planes, firsts, 2)),
        ],
        collective_id,
        200,
        "gather_now",
    )
    places = 4 * planes * firsts
    wholes = [
        whole.reshape(places * shard.shape[0], shard.shape[1])
        for whole, shard in zip(results, shards)
    ]
    return wholes + list(results[count:])


def scatter_kernel(planes, steps, rows, whole_slice, specs, *refs):
    (partial_ref,), (sum_ref,), scratch, rides = split_refs(refs, 1, 1, specs)
    own, from_core, from_first, from_second, from_below, from_above = scratch[:6]
    load_sem, core_sems, first_sems, second_sems, up_sems, down_sems = scratch[6:]
    blk, z, x, core, y = position()
    firsts = 2 if whole_slice else 1
    to_core = (blk + 1 - 2 * core, y)
    if whole_slice:
        first = y * (1 - core) + x * core
        second = x * (1 - core) + y * core
        core_second = second
        first_device = (blk + core * (2 - 4 * x), y + (1 - core) * (1 - 2 * y))
        second_device = (blk + (1 - core) * (2 - 4 * x), y + core * (1 - 2 * y))
    else:
        first, second = 0, x
        first_device, second_device = None, (blk + 2 - 4 * x, y)
    line = [(blk + 4 * (lax.rem(z + at, planes) - z), y) for at in range(1, planes)]
    nearby = [to_core, second_device] + [first_device] * whole_slice + line
    greet(greeted(planes, specs, nearby))

    def piece(step, by_first, by_second, plane):
        some = pl.ds(pl.multiple_of(step * rows, rows), rows)
        if whole_slice:
            by_x = (1 - plane) * by_second + plane * by_first
            by_y = (1 - plane) * by_first + plane * by_second
            return partial_ref.at[:, by_x, plane, by_y, some]
        return partial_ref.at[:, by_second, plane, some]

    def core_copy(step, by_first, by_second, plane):
        return remote(
            piece(step, by_first, by_second, plane),
            from_core.at[step, by_first, by_second],
            core_sems.at[0, step, by_first, by_second],
            core_sems.at[1, step, by_first, by_second],
            to_core,
        )

    def load(step, by_first, by_second):
        return pltpu.make_async_copy(
            piece(step, by_first, by_second, core),
            own.at[step, by_first, by_second],
            load_sem.at[step, by_first, by_second],
        )

    def first_copy(step):
        return remote(
            own.at[step, 1 - first],
            from_first.at[step],
            first_sems.at[0, step],
            first_sems.at[1, step],
            first_device,
        )

    def second_copy(step):
        return remote(
            own.at[step, first, 1 - second],
            from_second.at[step],
            second_sems.at[0, step],
            second_sems.at[1, step],
            second_device,
        )

    def up_copy(step, target):
        return remote(
            own.at[step, first, second, target],
            from_below.at[step, target],
            up_sems.at[0, step, target],
            up_sems.at[1, step, target],
            (blk + 4, y),
        )

    def down_copy(step, target):
        return remote(
            own.at[step, first, second, target],
            from_above.at[step, target],
            down_sems.at[0, step, target],
            down_sems.at[1, step, target],
            (blk - 4, y),
        )

    def halves():
        if not whole_slice:
            return [(0, 1 - second), (0, second)]
        return [(1 - first, 0), (1 - first, 1), (first, 0), (first, 1)]

    def core_halves():
        if not whole_slice:
            return [(0, 1 - second), (0, second)]
        return [(1 - core_second, 0), (1 - core_second, 1), (core_second, 0), (core_second, 1)]

    def start_loads(step):
        for mine, theirs in zip(halves(), core_halves()):
            core_copy(step, *theirs, 1 - core).start()
            load(step, *mine).start()

    def add_core(step):
        for turn, mine in enumerate(halves()):
            load(step, *mine).wait()
            core_copy(step, *mine, core).wait_recv()
            own[step, *mine] += from_core[step, *mine]
            if whole_slice and turn == 1:
                first_copy(step).start()
            if not whole_slice and turn == 0:
                second_copy(step).start()

    def add_first(step):
        first_copy(step).wait_recv()
        own[step, first, 1 - second] += from_first[step, 1 - second]
        second_copy(step).start()
        own[step, first, second] += from_first[step, second]

    def add_second(step):
        second_copy(step).wait_recv()
        own[step, first, second] += from_second[step]

    def pass_up(step):
        for target in range(planes):

            @pl.when((z > 0) & (z <= target))
            def _():
                up_copy(step, target).wait_recv()

            @pl.when((z > 0) & (z < target))
            def _():
                own[step, first, second, target] += from_below[step, target]

            @pl.when(z < target)
            def _():
                up_copy(step, target).start()

    def pass_down(step):
        for target in range(planes):

            @pl.when((z < planes - 1) & (z >= target))
            def _():
                down_copy(step, target).wait_recv()

            @pl.when((z < planes - 1) & (z > target))
            def _():
                own[step, first, second, target] += from_above[step, target]

            @pl.when(z > target)
            def _():
                down_copy(step, target).start()

    def add_line(step):
        some = pl.ds(pl.multiple_of(step * rows, rows), rows)
        sum_ref[some, :] = own[step, first, second, z]

        @pl.when(z > 0)
        def _():
            sum_ref[some, :] += from_below[step, z]

        @pl.when(z < planes - 1)
        def _():
            sum_ref[some, :] += from_above[step, z]

    start_loads(0)
    start_loads(1)
    finishes = start_rides(planes, rides)
    early = firsts + 1

    @pl.loop(0, steps + early + planes)
    def _(turn):
        def stage(step, work):
            @pl.when((step >= 0) & (step < steps))
            def _():
                work(step)

        @pl.when(turn < steps - 2)
        def _():
            start_loads(turn + 2)

        stage(turn, add_core)
        if whole_slice:
            stage(turn - 1, add_first)
        stage(turn - early + 1, add_second)
        stage(turn - early - z, pass_up)
        stage(turn - early - (planes - 1 - z), pass_down)
        stage(turn - early - planes + 1, add_line)

    @pl.loop(0, steps)
    def _(step):
        for theirs in core_halves():
            core_copy(step, *theirs, 1 - core).wait_send()
        if whole_slice:
            first_copy(step).wait_send()
        second_copy(step).wait_send()
        for target in range(planes):

            @pl.when(z < target)
            def _():
                up_copy(step, target).wait_send()

            @pl.when(z > target)
            def _():
                down_copy(step, target).wait_send()

    for finish in finishes:
        finish()


def scatter_now(partial, planes, whole_slice, collective_id, exchanges=()):
    firsts = 2 if whole_slice else 1
    shard_rows = partial.shape[0] // (4 * planes * firsts)
    width = partial.shape[1]
    rows = 16
    steps = shard_rows // rows
    dtype = partial.dtype
    specs = exchange_specs(exchanges)
    dma = pltpu.SemaphoreType.DMA
    grid = (planes, 2, 2, 2) if whole_slice else (planes, 2, 2)
    return communicate(
        functools.partial(scatter_kernel, planes, steps, rows, whole_slice, specs),
        [partial.reshape(*grid, shard_rows, width)],
        exchanges,
        [jax.ShapeDtypeStruct((shard_rows, width), dtype)],
        [
            pltpu.VMEM((steps, firsts, 2, planes, rows, width), dtype),
            pltpu.VMEM((steps, firsts, 2, planes, rows, width), dtype),
            pltpu.VMEM((steps if whole_slice else 1, 2, planes, rows, width), dtype),
            pltpu.VMEM((steps, planes, rows, width), dtype),
            pltpu.VMEM((steps, planes, rows, width), dtype),
            pltpu.VMEM((steps, planes, rows, width), dtype),
            dma((steps, firsts, 2)),
            dma((2, steps, firsts, 2)),
            dma((2, steps)),
            dma((2, steps)),
            dma((2, steps, planes)),
            dma((2, steps, planes)),
        ],
        collective_id,
        200,
        "scatter_now",
        out_spec=pltpu.VMEM,
        vmem_limit_bytes=48 * 2**20,
    )


def ffn_pack_kernel(gateup_ref, down_ref, packet_ref):
    live = pl.program_id(0) < FF // HEAD // 2

    @pl.when(live)
    def _():
        for at in range(2):
            columns = slice(at * HEAD, (at + 1) * HEAD)
            packet_ref[at, :, :HEAD] = gateup_ref[0, :, columns].astype(jnp.bfloat16)
            packet_ref[at, :, HEAD : 2 * HEAD] = gateup_ref[1, :, columns].astype(jnp.bfloat16)
            packet_ref[at, :, 2 * HEAD :] = down_ref[:, columns].astype(jnp.bfloat16)

    @pl.when(jnp.logical_not(live))
    def _():
        packet_ref[...] = jnp.zeros_like(packet_ref)


def ffn_packets(gateup, down, device_count):
    row_count = gateup.shape[1]
    last = FF // HEAD // 2 - 1
    return pl.pallas_call(
        ffn_pack_kernel,
        grid=(device_count // 2,),
        in_specs=[
            pl.BlockSpec((2, row_count, 2 * HEAD), lambda j: (0, 0, jnp.minimum(j, last))),
            pl.BlockSpec((row_count, 2 * HEAD), lambda j: (0, jnp.minimum(j, last))),
        ],
        out_specs=pl.BlockSpec((2, row_count, 3 * HEAD), lambda j: (j, 0, 0)),
        out_shape=jax.ShapeDtypeStruct((device_count, row_count, 3 * HEAD), jnp.bfloat16),
        cost_estimate=pl.CostEstimate(flops=0, bytes_accessed=14 * 2**20, transcendentals=0),
        name="ffn_packets",
    )(gateup, down)


def attn_pack_kernel(qkv_ref, out_ref, packet_ref):
    j = pl.program_id(0)

    @pl.when(j < (H + 2) // 2)
    def _():
        for at in range(2):
            packet_ref[at] = qkv_ref[:, at * HEAD : (at + 1) * HEAD].astype(jnp.bfloat16)

    @pl.when((j >= (H + 2) // 2) & (j < H + 1))
    def _():
        for at in range(2):
            packet_ref[at] = out_ref[:, at * HEAD : (at + 1) * HEAD].astype(jnp.bfloat16)

    @pl.when(j >= H + 1)
    def _():
        packet_ref[...] = jnp.zeros_like(packet_ref)


def attn_packets(qkv, out, device_count):
    row_count = qkv.shape[0]
    qkv_last, out_last = (H + 2) // 2 - 1, H // 2 - 1
    return pl.pallas_call(
        attn_pack_kernel,
        grid=(device_count // 2,),
        in_specs=[
            pl.BlockSpec((row_count, 2 * HEAD), lambda j: (0, jnp.minimum(j, qkv_last))),
            pl.BlockSpec((row_count, 2 * HEAD), lambda j: (0, jnp.clip(j - qkv_last - 1, 0, out_last))),
        ],
        out_specs=pl.BlockSpec((2, row_count, HEAD), lambda j: (j, 0, 0)),
        out_shape=jax.ShapeDtypeStruct((device_count, row_count, HEAD), jnp.bfloat16),
        cost_estimate=pl.CostEstimate(flops=0, bytes_accessed=4 * 2**20, transcendentals=0),
        name="attn_packets",
    )(qkv, out)


def turn_kernel(grads_ref, others_ref, mom_ref, *refs):
    *results, current_ref = refs
    if len(results) == 1:
        low_ref, turned_ref = results[0].at[:, :HEAD], results[0].at[:, HEAD:]
    else:
        low_ref, turned_ref = results
    grads = grads_ref[...] + others_ref[...].astype(jnp.float32)
    low_ref[...] = grads.astype(jnp.bfloat16)
    moment = momentum_decay * mom_ref[...].astype(jnp.float32) + grads
    moment = moment.astype(jnp.bfloat16).astype(jnp.float32)
    norm_size = jnp.sqrt(jnp.sum(moment * moment, keepdims=True))
    current_ref[...] = (moment / (norm_size + eps_pieces)).T.astype(jnp.bfloat16)

    @pl.loop(0, NS_STEPS)
    def _(sweep_index):
        current = current_ref[...]
        gram_matrix = lax.dot_general(
            current, current, (((1,), (1,)), ((), ())), preferred_element_type=jnp.float32
        ).astype(jnp.bfloat16)
        square = jnp.dot(gram_matrix, gram_matrix, preferred_element_type=jnp.float32)
        mixing = (ns_second * gram_matrix.astype(jnp.float32) + ns_third * square).astype(
            jnp.bfloat16
        )
        turned = jnp.dot(mixing, current, preferred_element_type=jnp.float32)
        current_ref[...] = (ns_first * current.astype(jnp.float32) + turned).astype(jnp.bfloat16)

    turned_ref[...] = current_ref[...].astype(jnp.float32).T.astype(jnp.bfloat16)


def orthogonalize(grads, others, moms, results):
    depth, columns = grads.shape
    block = pl.BlockSpec((depth, HEAD), lambda j: (0, j))
    pieces = columns // HEAD
    return pl.pallas_call(
        turn_kernel,
        grid=(pieces,),
        in_specs=[block] * 3,
        out_specs=[pl.BlockSpec((depth, 2 // results * HEAD), lambda j: (0, j))] * results,
        out_shape=[jax.ShapeDtypeStruct((depth, 2 // results * columns), jnp.bfloat16)] * results,
        scratch_shapes=[pltpu.VMEM((HEAD, depth), jnp.bfloat16)],
        cost_estimate=pl.CostEstimate(
            flops=pieces * 20 * depth * HEAD * HEAD, bytes_accessed=12 * depth * columns, transcendentals=0
        ),
        compiler_params=pltpu.CompilerParams(vmem_limit_bytes=48 * 2**20),
        name="orthogonalize",
    )(grads, others, moms)


def update(rate, weight, mom, grad, turn):
    moment = momentum_decay * mom + grad.astype(jnp.float32)
    new = (1.0 - weight_shrink) * weight - rate * turn.astype(jnp.float32)
    return new, moment, new.astype(jnp.bfloat16)


def ffn_update_kernel(
    grad_ref, turn_ref, w_gateup_ref, mom_gateup_ref, w_down_ref, mom_down_ref, *results
):
    for at in range(grad_ref.shape[0]):
        columns = slice(at * HEAD, (at + 1) * HEAD)
        for part in range(3):
            spot = (part, slice(None), columns) if part < 2 else (slice(None), columns)
            weight_ref, mom_ref = (
                (w_gateup_ref, mom_gateup_ref) if part < 2 else (w_down_ref, mom_down_ref)
            )
            packed = slice(part * HEAD, (part + 1) * HEAD)
            values = update(
                matrix_rate,
                weight_ref[spot],
                mom_ref[spot],
                grad_ref[at, :, packed],
                turn_ref[at, :, packed],
            )
            for ref, value in zip(results[:3] if part < 2 else results[3:], values):
                ref[spot] = value


def ffn_update(grads, turns, w_gateup, mom_gateup, w_down, mom_down):
    row_count = w_gateup.shape[1]
    wide = 3
    packet = pl.BlockSpec((wide, row_count, 3 * HEAD), lambda j: (j, 0, 0))
    gateup = pl.BlockSpec((2, row_count, wide * HEAD), lambda j: (0, 0, j))
    down = pl.BlockSpec((row_count, wide * HEAD), lambda j: (0, j))
    dtypes = (jnp.float32, jnp.float32, jnp.bfloat16)
    return pl.pallas_call(
        ffn_update_kernel,
        grid=(FF // HEAD // wide,),
        in_specs=[packet, packet, gateup, gateup, down, down],
        out_specs=[gateup] * 3 + [down] * 3,
        out_shape=[jax.ShapeDtypeStruct(w_gateup.shape, dtype) for dtype in dtypes]
        + [jax.ShapeDtypeStruct(w_down.shape, dtype) for dtype in dtypes],
        cost_estimate=pl.CostEstimate(flops=0, bytes_accessed=50 * 2**20, transcendentals=0),
        compiler_params=pltpu.CompilerParams(vmem_limit_bytes=48 * 2**20),
        name="ffn_update",
    )(grads, turns, w_gateup, mom_gateup, w_down, mom_down)


def attn_update_kernel(rate, packet_ref, w_ref, mom_ref, *results):
    for at in range(2):
        columns = slice(at * HEAD, (at + 1) * HEAD)
        values = update(
            rate,
            w_ref[:, columns],
            mom_ref[:, columns],
            packet_ref[at, :, :HEAD],
            packet_ref[at, :, HEAD:],
        )
        for ref, value in zip(results, values):
            ref[:, columns] = value


def attn_update(rate, offset, packets, weight, mom):
    row_count = packets.shape[1]
    packet = pl.BlockSpec((2, row_count, 2 * HEAD), lambda j: (j + offset // 2, 0, 0))
    block = pl.BlockSpec((row_count, 2 * HEAD), lambda j: (0, j))
    return pl.pallas_call(
        functools.partial(attn_update_kernel, rate),
        grid=(weight.shape[1] // HEAD // 2,),
        in_specs=[packet, block, block],
        out_specs=[block] * 3,
        out_shape=[
            jax.ShapeDtypeStruct(weight.shape, dtype)
            for dtype in (jnp.float32, jnp.float32, jnp.bfloat16)
        ],
        cost_estimate=pl.CostEstimate(flops=0, bytes_accessed=6 * 2**20, transcendentals=0),
        name="attn_update",
    )(packets, weight, mom)


def two_heads(ref):
    return jnp.concatenate([ref[:, :HEAD], ref[:, HEAD:]], axis=0)


def visible(tokens, first_token, shape, query_axis):
    query = lax.rem(lax.broadcasted_iota(jnp.int32, shape, query_axis), tokens)
    key = lax.broadcasted_iota(jnp.int32, shape, 1 - query_axis)
    distance = query + WINDOW - key
    return (distance >= 0) & (distance < WINDOW) & (first_token - WINDOW + key >= 0)


def attend_kernel(first_ref, queries_ref, kv_ref, mixed_ref, log_total_ref):
    tokens = queries_ref.shape[0]
    raw = lax.dot_general(
        two_heads(queries_ref),
        kv_ref[:, :HEAD],
        (((1,), (1,)), ((), ())),
        preferred_element_type=jnp.float32,
    )
    allowed = visible(tokens, first_ref[0], raw.shape, 0)
    scores = jnp.where(allowed, raw * HEAD ** (-0.5), masked_score)
    top_score = jnp.max(scores, axis=-1, keepdims=True)
    expo = jnp.exp(scores - top_score)
    total = jnp.sum(expo, axis=-1, keepdims=True)
    probs = (expo / total).astype(jnp.bfloat16)
    mixed = jnp.dot(probs, kv_ref[:, HEAD:], preferred_element_type=jnp.float32)
    mixed_ref[:, :HEAD] = mixed[:tokens].astype(jnp.bfloat16)
    mixed_ref[:, HEAD:] = mixed[tokens:].astype(jnp.bfloat16)
    log_total_ref[0] = jnp.broadcast_to(top_score + jnp.log(total), log_total_ref.shape[1:])


def attend(first_token, qkv, kv_window):
    tokens = qkv.shape[0]
    span = kv_window.shape[0]
    pairs = H // 2
    return pl.pallas_call(
        attend_kernel,
        grid=(pairs,),
        in_specs=[
            pl.BlockSpec(memory_space=pltpu.SMEM),
            pl.BlockSpec((tokens, 2 * HEAD), lambda j: (0, j)),
            pl.BlockSpec((span, 2 * HEAD), lambda j: (0, 0)),
        ],
        out_specs=[
            pl.BlockSpec((tokens, 2 * HEAD), lambda j: (0, j)),
            pl.BlockSpec((1, 2 * tokens, 128), lambda j: (j, 0, 0)),
        ],
        out_shape=[
            jax.ShapeDtypeStruct((tokens, H * HEAD), jnp.bfloat16),
            jax.ShapeDtypeStruct((pairs, 2 * tokens, 128), jnp.float32),
        ],
        cost_estimate=pl.CostEstimate(
            flops=4 * H * tokens * span * HEAD,
            bytes_accessed=4 * 2**20,
            transcendentals=H * tokens * span,
        ),
        compiler_params=pltpu.CompilerParams(vmem_limit_bytes=48 * 2**20),
        name="attend",
    )(first_token, qkv, kv_window)


def attend_back_kernel(
    first_ref, queries_ref, grads_ref, log_total_ref, kv_ref, grad_query_ref, grad_kv_ref, sums_ref
):
    tokens = queries_ref.shape[0]
    score_scale = HEAD ** (-0.5)
    keys, values = kv_ref[:, :HEAD], kv_ref[:, HEAD:]
    queries, grads = two_heads(queries_ref), two_heads(grads_ref)

    def against(left, right):
        return lax.dot_general(
            left, right, (((1,), (1,)), ((), ())), preferred_element_type=jnp.float32
        )

    raw = against(keys, queries)
    allowed = visible(tokens, first_ref[0], raw.shape, 1)
    scores = jnp.where(allowed, raw * score_scale, masked_score)
    log_total = log_total_ref[0].T[:1]
    probs = jnp.exp(scores - log_total)
    grad_probs = against(values, grads)
    row_delta = jnp.sum(probs * grad_probs, axis=0, keepdims=True)
    grad_raw = (probs * (grad_probs - row_delta) * score_scale).astype(jnp.bfloat16)
    grad_query = lax.dot_general(
        grad_raw, keys, (((0,), (0,)), ((), ())), preferred_element_type=jnp.float32
    )
    grad_query_ref[:, :HEAD] = grad_query[:tokens].astype(jnp.bfloat16)
    grad_query_ref[:, HEAD:] = grad_query[tokens:].astype(jnp.bfloat16)

    @pl.when(pl.program_id(0) == 0)
    def _():
        sums_ref[...] = jnp.zeros_like(sums_ref)

    sums_ref[:, :HEAD] += jnp.dot(grad_raw, queries, preferred_element_type=jnp.float32)
    sums_ref[:, HEAD:] += jnp.dot(
        probs.astype(jnp.bfloat16), grads, preferred_element_type=jnp.float32
    )

    @pl.when(pl.program_id(0) == pl.num_programs(0) - 1)
    def _():
        grad_kv_ref[...] = sums_ref[...].astype(jnp.bfloat16)


def attend_back(first_token, qkv, grads, log_total, kv_window):
    tokens = qkv.shape[0]
    span = kv_window.shape[0]
    heads = pl.BlockSpec((tokens, 2 * HEAD), lambda j: (0, j))
    window = pl.BlockSpec((span, 2 * HEAD), lambda j: (0, 0))
    return pl.pallas_call(
        attend_back_kernel,
        grid=(H // 2,),
        in_specs=[
            pl.BlockSpec(memory_space=pltpu.SMEM),
            heads,
            heads,
            pl.BlockSpec((1, 2 * tokens, 128), lambda j: (j, 0, 0)),
            window,
        ],
        out_specs=[heads, window],
        out_shape=[
            jax.ShapeDtypeStruct((tokens, H * HEAD), jnp.bfloat16),
            jax.ShapeDtypeStruct((span, 2 * HEAD), jnp.bfloat16),
        ],
        scratch_shapes=[pltpu.VMEM((span, 2 * HEAD), jnp.float32)],
        cost_estimate=pl.CostEstimate(
            flops=10 * H * tokens * span * HEAD,
            bytes_accessed=8 * 2**20,
            transcendentals=H * tokens * span,
        ),
        compiler_params=pltpu.CompilerParams(vmem_limit_bytes=48 * 2**20),
        name="attend_back",
    )(first_token, qkv, grads, log_total, kv_window)


def rms_scale(stream, gain_row):
    mean_square = jnp.mean(stream * stream, axis=-1, keepdims=True)
    return stream * lax.rsqrt(mean_square + eps_norm) * gain_row


def gelu_product(gate_part, up_part):
    return jax.nn.gelu(gate_part, approximate=True) * up_part


def on_device(
    tokens_in,
    cotangent,
    w_qkv,
    w_out,
    w_gateup,
    w_down,
    gains,
    mom_qkv,
    mom_out,
    mom_gateup,
    mom_down,
    mom_gains,
):
    everyone = ("blk", "pair")
    bf16 = jnp.bfloat16
    f32 = jnp.float32
    blk_count = lax.axis_size("blk")
    pair_count = lax.axis_size("pair")
    device_count = blk_count * pair_count
    block_at = lax.axis_index("blk")
    half_at = lax.axis_index("pair")
    me = block_at * pair_count + half_at
    local_rows, width = tokens_in.shape
    share_rows = w_qkv.shape[0]
    span = WINDOW + local_rows
    token_count = local_rows * device_count
    large = token_count * width * 2 > 48 * 2**20
    planes = blk_count // 4

    def after(value, earlier):
        return lax.optimization_barrier((value, earlier))[0] if large else value

    def exchange(packets, axes=everyone):
        return lax.all_to_all(packets, axes, split_axis=0, concat_axis=0, tiled=True)

    def swap(shard):
        return lax.ppermute(shard, "pair", [(0, 1), (1, 0)])

    def hold(value, *earlier):
        return value if large else lax.optimization_barrier((value, earlier))[0]

    def ride(packets, in_plane=False, sources=None, targets=None):
        places = packets.shape[0]
        return Exchange(packets, in_plane, sources or places, targets or places)

    def exchanged(rides):
        return [exchange(each.packets, "blk" if each.in_plane else everyone) for each in rides]

    def gather(shards, whole_slice, collective_id, rides=()):
        if large:
            axes = everyone if whole_slice else "blk"
            wholes = [lax.all_gather(shard, axes, axis=0, tiled=True) for shard in shards]
            return wholes + exchanged(rides)
        return gather_now(shards, planes, whole_slice, collective_id, rides)

    def scatter(partial, whole_slice, collective_id, rides=()):
        if large:
            axes = everyone if whole_slice else "blk"
            part = lax.psum_scatter(partial, axes, scatter_dimension=0, tiled=True)
            return [part] + exchanged(rides)
        return scatter_now(partial, planes, whole_slice, collective_id, rides)

    def gather_plane(shard):
        return lax.all_gather(shard, "blk", axis=0, tiled=True)

    stream = tokens_in.astype(f32)
    padded_gains = jnp.pad(gains.astype(bf16), ((0, 14), (0, 128 - share_rows)))
    full_qkv, full_gains, full_out, ffn_weights = gather(
        [w_qkv.astype(bf16), padded_gains, w_out.T.astype(bf16)],
        True,
        1,
        [ride(ffn_packets(w_gateup, w_down.T, device_count))],
    )
    ffn_weights = ffn_weights.reshape(width, 3 * HEAD)
    full_gains = full_gains.reshape(device_count, 16, 128)[:, :2, :share_rows].astype(f32)
    gain_attn = full_gains[:, 0].reshape(width)
    gain_mlp = full_gains[:, 1].reshape(width)
    normed_attn_f, norm_back_attn = jax.vjp(rms_scale, stream, gain_attn)
    normed_attn = normed_attn_f.astype(bf16)
    qkv = jnp.dot(normed_attn, full_qkv, preferred_element_type=f32).astype(bf16)
    (kv_all,) = gather([qkv[:, H * HEAD :]], True, 2)
    kv_window = lax.dynamic_slice_in_dim(
        jnp.pad(kv_all, ((WINDOW, 0), (0, 0))), me * local_rows, span, 0
    )
    first_token = (me * local_rows).astype(jnp.int32).reshape(1)
    pair_weights = [ffn_weights, swap(hold(ffn_weights, kv_all))]
    gates, ups, downs = (
        [weights[:, part * HEAD : (part + 1) * HEAD] for weights in pair_weights]
        for part in range(3)
    )
    pair_gateup = jnp.concatenate(gates + ups, axis=1)
    pair_down = jnp.concatenate(downs, axis=1)

    mixed, log_total = attend(first_token, qkv, kv_window)
    resid = stream + jnp.einsum("tc,dc->td", mixed, full_out, preferred_element_type=f32)

    normed_mlp_f, norm_back_mlp = jax.vjp(rms_scale, resid, gain_mlp)
    normed_mlp = normed_mlp_f.astype(bf16)
    normed_mlp_plane, cotangent_plane = gather([normed_mlp, cotangent], False, 3)
    plane_rows = blk_count * local_rows
    both_parts = jnp.dot(normed_mlp_plane, pair_gateup, preferred_element_type=f32)
    pair_width = pair_count * HEAD
    hidden_f, geglu_back = jax.vjp(
        gelu_product, both_parts[:, :pair_width], both_parts[:, pair_width:]
    )
    hidden = hidden_f.astype(bf16)
    grad_hidden = jnp.dot(cotangent_plane, pair_down, preferred_element_type=f32)
    grad_gate, grad_up = geglu_back(grad_hidden)
    grad_gateup = jnp.concatenate([grad_gate.astype(bf16), grad_up.astype(bf16)], axis=1)
    def ffn_gradient(columns):
        gateup_right = jnp.concatenate(
            [grad_gate[:, columns].astype(bf16), grad_up[:, columns].astype(bf16)], axis=1
        )
        down_right = hidden[:, columns]
        return jnp.concatenate(
            [
                jnp.einsum("td,tf->df", normed_mlp_plane, gateup_right, preferred_element_type=f32),
                jnp.einsum("td,tf->df", cotangent_plane, down_right, preferred_element_type=f32),
            ],
            axis=1,
        )

    ffn_theirs = ffn_gradient(slice(HEAD, 2 * HEAD)).astype(bf16)
    ffn_others = swap(ffn_theirs)
    grad_normed_part = jnp.einsum("tf,df->td", grad_gateup, pair_gateup, preferred_element_type=f32)
    grad_normed_mlp, ffn_moms, attn_moms = scatter(
        hold(grad_normed_part.astype(bf16), ffn_theirs),
        False,
        4,
        [
            ride(ffn_packets(mom_gateup, mom_down.T, device_count), targets=FF // HEAD),
            ride(attn_packets(mom_qkv, mom_out.T, device_count), targets=2 * H + 2),
        ],
    )
    grad_normed_mlp = grad_normed_mlp.astype(f32)

    ffn_grads = ffn_gradient(slice(0, HEAD))
    ffn_low, ffn_turned = orthogonalize(
        ffn_grads, ffn_others, ffn_moms.reshape(width, 3 * HEAD), 2
    )
    ffn_shape = (device_count, share_rows, 3 * HEAD)

    resid_part, gain_grad_mlp = norm_back_mlp(grad_normed_mlp)
    grad_resid = cotangent.astype(f32) + resid_part
    grad_proj = grad_resid.astype(bf16)
    grad_mixed = jnp.dot(grad_proj, full_out, preferred_element_type=f32).astype(bf16)
    grad_query, grad_kv = attend_back(first_token, qkv, grad_mixed, log_total, kv_window)
    grad_kv_all = lax.dynamic_update_slice_in_dim(
        jnp.zeros((WINDOW + token_count, 2 * HEAD), bf16), grad_kv, me * local_rows, 0
    )[WINDOW:]
    grad_kv, ffn_low = scatter(
        grad_kv_all, True, 5, [ride(ffn_low.reshape(ffn_shape), sources=FF // HEAD)]
    )
    grad_qkv = jnp.concatenate([grad_query, grad_kv], axis=1)
    grad_normed_attn = jnp.einsum("tc,dc->td", grad_qkv, full_qkv, preferred_element_type=f32)
    stream_part, gain_grad_attn = norm_back_attn(grad_normed_attn)
    input_grad = grad_resid + stream_part

    attn_rights = jnp.concatenate([grad_qkv, mixed], axis=1)
    used = attn_rights.shape[1] // pair_width
    attn_rights = attn_rights.reshape(local_rows, used, pair_width).transpose(1, 0, 2)
    attn_rights = jnp.pad(attn_rights, ((0, blk_count - used), (0, 0), (0, 0)))
    branch_part = jnp.einsum(
        "tf,df->td", after(hidden, grad_normed_mlp), pair_down, preferred_element_type=f32
    )
    branch, ffn_turned, attn_rights = scatter(
        branch_part.astype(bf16),
        False,
        6,
        [
            ride(ffn_turned.reshape(ffn_shape), sources=FF // HEAD),
            ride(attn_rights, in_plane=True, targets=used),
        ],
    )
    attn_rights = attn_rights.reshape(plane_rows, pair_width)
    block_output = (resid + branch.astype(f32)).astype(bf16)
    normed_attn_plane = gather_plane(after(hold(normed_attn, normed_mlp_plane), (ffn_grads, block_output)))
    grad_proj_plane = gather_plane(after(grad_proj, (ffn_grads, block_output)))

    def attn_gradient(lefts):
        return jnp.einsum("td,tf->df", lefts, attn_rights, preferred_element_type=f32)

    attn_grads = lax.cond(
        block_at < (H + 2) // pair_count,
        lambda: attn_gradient(normed_attn_plane),
        lambda: attn_gradient(grad_proj_plane),
    )
    attn_others = swap(
        lax.dynamic_slice_in_dim(attn_grads, (1 - half_at) * HEAD, HEAD, 1).astype(bf16)
    )
    attn_grads = lax.dynamic_slice_in_dim(attn_grads, half_at * HEAD, HEAD, 1)
    updated_ffn = ffn_update(ffn_low, ffn_turned, w_gateup, mom_gateup, w_down.T, mom_down.T)
    (attn_results,) = orthogonalize(
        attn_grads, hold(attn_others, updated_ffn[0]), attn_moms.reshape(width, HEAD), 1
    )
    gain_grads = jnp.stack([gain_grad_attn, gain_grad_mlp], axis=0)
    gain_grads = gain_grads.reshape(2, device_count, share_rows).transpose(1, 0, 2)
    last_rides = [
        ride(attn_results.reshape(device_count, share_rows, 2 * HEAD), sources=2 * H + 2),
        ride(jnp.pad(gain_grads, ((0, 0), (0, 6), (0, 128 - share_rows)))),
    ]
    if large:
        attn_results, gain_grads = exchanged(last_rides)
    else:
        attn_results, gain_grads = exchange_now(last_rides, planes, 7)
    gain_share = jnp.sum(gain_grads, axis=0)[:2, :share_rows]

    updated_qkv = attn_update(matrix_rate, 0, attn_results, w_qkv, mom_qkv)
    updated_out = attn_update(output_rate, H + 2, attn_results, w_out.T, mom_out.T)
    moment_gains = momentum_decay * mom_gains + gain_share
    new_gains = gains - gain_rate * moment_gains
    return (
        block_output,
        input_grad,
        *updated_qkv,
        *(result.T for result in updated_out),
        *updated_ffn[:3],
        *(result.T for result in updated_ffn[3:]),
        new_gains,
        moment_gains,
        new_gains.astype(bf16),
    )


def solution(mesh):
    placed = (
        P(("blk", "pair"), None),
        P(("blk", "pair"), None),
        P(("blk", "pair"), None),
        P(None, ("blk", "pair")),
        P(None, ("blk", "pair"), None),
        P(None, ("blk", "pair")),
        P(None, ("blk", "pair")),
        P(("blk", "pair"), None),
        P(None, ("blk", "pair")),
        P(None, ("blk", "pair"), None),
        P(None, ("blk", "pair")),
        P(None, ("blk", "pair")),
    )
    return jax.shard_map(
        on_device,
        mesh=mesh,
        in_specs=placed,
        out_specs=(
            P(("blk", "pair"), None),
            P(("blk", "pair"), None),
            P(("blk", "pair"), None),
            P(("blk", "pair"), None),
            P(("blk", "pair"), None),
            P(None, ("blk", "pair")),
            P(None, ("blk", "pair")),
            P(None, ("blk", "pair")),
            P(None, ("blk", "pair"), None),
            P(None, ("blk", "pair"), None),
            P(None, ("blk", "pair"), None),
            P(None, ("blk", "pair")),
            P(None, ("blk", "pair")),
            P(None, ("blk", "pair")),
            P(None, ("blk", "pair")),
            P(None, ("blk", "pair")),
            P(None, ("blk", "pair")),
        ),
        check_vma=False,
    )
```

```python
import functools
from typing import NamedTuple

import jax
import jax.numpy as jnp
from jax import lax
from jax.experimental import pallas as pl
from jax.experimental.pallas import tpu as pltpu
from jax.sharding import PartitionSpec as P

H = 10
HEAD = 256
FF = 7680
WINDOW = 2048
NS_STEPS = 5


eps_norm = 1e-06
eps_pieces = 1e-07
ns_first = 3.4445
ns_second = -4.775
ns_third = 2.0315
momentum_decay = 0.95
matrix_rate = 0.5
output_rate = 10.0
gain_rate = 0.001
weight_shrink = 0.001
masked_score = -1e30
MESH = pl.DeviceIdType.MESH


def position():
    blk, y = lax.axis_index("blk"), lax.axis_index("pair")
    return blk, lax.div(blk, 4), lax.rem(lax.div(blk, 2), 2), lax.rem(blk, 2), y


def greet(devices):
    barrier = pltpu.get_barrier_semaphore()
    for device in devices:
        pl.semaphore_signal(barrier, inc=1, device_id=device, device_id_type=MESH)
    pl.semaphore_wait(barrier, len(devices))


def remote(source, target, send_sem, recv_sem, device):
    return pltpu.make_async_remote_copy(
        src_ref=source,
        dst_ref=target,
        send_sem=send_sem,
        recv_sem=recv_sem,
        device_id=device,
        device_id_type=MESH,
    )


class Exchange(NamedTuple):
    packets: jax.Array
    among: str
    sources: int
    targets: int


def all_devices():
    blk, _, _, _, y = position()
    count = 2 * lax.axis_size("blk")
    here = 2 * blk + y
    places = [lax.rem(here + at, count) for at in range(1, count)]
    return [(lax.div(place, 2), lax.rem(place, 2)) for place in places]


def plane_devices():
    blk, _, _, _, y = position()
    count = lax.axis_size("blk")
    return [(lax.rem(blk + at, count), y) for at in range(1, count)]


def greeted(specs, nearby):
    if any(among == "all" for among, _, _ in specs):
        return all_devices()
    blk, _, _, _, y = position()
    pair = [(blk, 1 - y)] * any(among == "pair" for among, _, _ in specs)
    if any(among == "plane" for among, _, _ in specs):
        return plane_devices() + pair
    return nearby + pair


PAIR_PARTS = 4


def exchange_count(planes, among):
    return {"all": 8 * planes, "plane": 4 * planes, "pair": PAIR_PARTS}[among]


class Ride:
    def __init__(self, planes, spec, packets, received, sems):
        self.planes, self.packets, self.received = planes, packets, received
        self.among, self.sources, self.targets = spec
        self.own_sem, self.send_sems, self.recv_sems = sems
        self.count = exchange_count(planes, self.among)
        self.issued = 0
        blk, self.z, _, _, self.y = position()
        self.blk = blk
        self.here = blk if self.among == "plane" else 2 * blk + self.y

    def place(self, q):
        near = self.count // self.planes
        spot = lax.rem(self.z + 1 + lax.rem(q, self.planes), self.planes)
        return spot * near + lax.rem(self.here + lax.div(q, self.planes), near)

    def copy(self, q):
        if self.among == "pair":
            rows = self.packets.shape[0] // PAIR_PARTS
            some = pl.ds(pl.multiple_of(q * rows, rows), rows)
            return remote(
                self.packets.at[some],
                self.received.at[some],
                self.send_sems.at[q],
                self.recv_sems.at[q],
                (self.blk, 1 - self.y),
            )
        place = self.place(q)
        device = (place, self.y)
        if self.among == "all":
            device = (lax.div(place, 2), lax.rem(place, 2))
        return remote(
            self.packets.at[place],
            self.received.at[self.here],
            self.send_sems.at[q],
            self.recv_sems.at[self.here],
            device,
        )

    def own(self):
        return pltpu.make_async_copy(
            self.packets.at[self.here], self.received.at[self.here], self.own_sem.at[0]
        )

    def sends(self, q):
        if self.among == "pair":
            return q < self.count
        away = (q < self.count) & (q != self.planes - 1)
        return away & (self.here < self.sources) & (self.place(q) < self.targets)

    def keeps(self):
        return (self.here < self.sources) & (self.here < self.targets)

    def start_own(self):
        if self.among != "pair":

            @pl.when(self.keeps())
            def _():
                self.own().start()

    def issue(self, q):
        @pl.when(self.sends(q))
        def _():
            self.copy(q).start()

    def issue_more(self, number):
        first, self.issued = self.issued, min(self.issued + number, self.count)

        @pl.loop(first, self.issued)
        def _(q):
            self.issue(q)

    def finish(self):
        @pl.loop(0, self.count)
        def _(q):
            @pl.when(self.sends(q))
            def _():
                self.copy(q).wait_send()

            if self.among == "pair":
                self.copy(q).wait_recv()
            else:

                @pl.when((q != self.here) & (q < self.sources) & (self.here < self.targets))
                def _():
                    spot = self.received.at[q]
                    remote(
                        spot, spot, self.own_sem.at[0], self.recv_sems.at[q], (self.blk, self.y)
                    ).wait_recv()

        if self.among != "pair":

            @pl.when(self.keeps())
            def _():
                self.own().wait()


def rides_of(planes, rides):
    rides = [Ride(planes, *ride) for ride in rides]
    for ride in rides:
        ride.start_own()
    return rides


def exchange_sems(exchanges, planes):
    dma = pltpu.SemaphoreType.DMA
    return [
        dma((count,))
        for exchange in exchanges
        for count in (1,) + (exchange_count(planes, exchange.among),) * 2
    ]


def exchange_specs(exchanges):
    return tuple((each.among, each.sources, each.targets) for each in exchanges)


def same_shape(arrays):
    return [jax.ShapeDtypeStruct(array.shape, array.dtype) for array in arrays]


def communicate(
    kernel,
    operands,
    exchanges,
    outputs,
    scratch,
    planes,
    collective_id,
    cost,
    name,
    out_spec=pl.ANY,
    **options,
):
    packets = [each.packets for each in exchanges]
    any_spec = pl.BlockSpec(memory_space=pl.ANY)
    return pl.pallas_call(
        kernel,
        out_shape=outputs + same_shape(packets),
        in_specs=[any_spec] * (len(operands) + len(packets)),
        out_specs=[pl.BlockSpec(memory_space=out_spec)] * len(outputs) + [any_spec] * len(packets),
        scratch_shapes=scratch + exchange_sems(exchanges, planes),
        compiler_params=pltpu.CompilerParams(
            collective_id=collective_id, has_side_effects=True, **options
        ),
        cost_estimate=pl.CostEstimate(flops=0, bytes_accessed=cost * 2**20, transcendentals=0),
        name=name,
    )(*operands, *packets)


def split_refs(refs, inputs, outputs, specs):
    riders = len(specs)
    ins, refs = refs[: inputs + riders], refs[inputs + riders :]
    outs, refs = refs[: outputs + riders], refs[outputs + riders :]
    scratch = refs[: len(refs) - 3 * riders]
    sems = refs[len(refs) - 3 * riders :]
    rides = [
        (spec, ins[inputs + i], outs[outputs + i], sems[3 * i : 3 * i + 3])
        for i, spec in enumerate(specs)
    ]
    return ins[:inputs], outs[:outputs], scratch, rides


def exchange_kernel(planes, specs, *refs):
    _, _, _, rides = split_refs(refs, 0, 0, specs)
    greet(greeted(specs, []))
    rides = rides_of(planes, rides)
    for ride in rides:
        ride.issue_more(ride.count)
    for ride in rides:
        ride.finish()


def exchange_now(exchanges, planes, collective_id):
    specs = exchange_specs(exchanges)
    kernel = functools.partial(exchange_kernel, planes, specs)
    return communicate(kernel, [], exchanges, [], [], planes, collective_id, 100, "exchange_now")


def gather_kernel(planes, parts, whole_slice, specs, *refs):
    arrays = 1 + max(array for array, _, _ in parts)
    shard_refs, whole_refs, scratch, rides = split_refs(refs, arrays, arrays, specs)
    count = len(parts)
    shards = [shard_refs[array].at[pl.ds(start, size)] for array, start, size in parts]
    own_sem, line_send, second_send, first_send, core_send, recv, core_recv = scratch
    blk, z, x, core, y = position()
    firsts = 2 if whole_slice else 1
    to_core = (blk + 1 - 2 * core, y)
    if whole_slice:
        first = y * (1 - core) + x * core
        second = x * (1 - core) + y * core
        first_device = (blk + core * (2 - 4 * x), y + (1 - core) * (1 - 2 * y))
        second_device = (blk + (1 - core) * (2 - 4 * x), y + core * (1 - 2 * y))
    else:
        first, second = 0, x
        first_device, second_device = None, (blk + 2 - 4 * x, y)
    line = [(blk + 4 * (lax.rem(z + at, planes) - z), y) for at in range(1, planes)]
    nearby = [to_core, second_device] + [first_device] * whole_slice + line
    greet(greeted(specs, nearby))

    def slot(i, spot, by_first, by_second, plane):
        array, start, size = parts[i]
        whole, some = whole_refs[array], pl.ds(start, size)
        if whole_slice:
            by_x = (1 - plane) * by_second + plane * by_first
            by_y = (1 - plane) * by_first + plane * by_second
            return whole.at[spot, by_x, plane, by_y, some]
        return whole.at[spot, by_second, plane, some]

    def arrive(i, spot, by_first, by_second):
        here = slot(i, spot, by_first, by_second, core)
        remote(here, here, own_sem.at[0], recv.at[i, spot, by_first, by_second], to_core).wait_recv()

    def up(i, source, spot):
        target = slot(i, spot, first, second, core)
        device = (blk + 4, y)
        return remote(source, target, line_send.at[0, i, spot], recv.at[i, spot, first, second], device)

    def down(i, source, spot):
        target = slot(i, spot, first, second, core)
        device = (blk - 4, y)
        return remote(source, target, line_send.at[1, i, spot], recv.at[i, spot, first, second], device)

    def onward(i, source, spot):
        target = slot(i, spot, first, second, core)
        arrived = recv.at[i, spot, first, second]
        yield remote(source, target, second_send.at[i, spot], arrived, second_device)
        if whole_slice:
            yield remote(source, target, first_send.at[i, spot, 0], arrived, first_device)
        yield remote(
            source, target, core_send.at[i, spot, 0, 0], core_recv.at[i, spot, first, second], to_core
        )

    def after_second(i, spot):
        here = slot(i, spot, first, 1 - second, core)
        if whole_slice:
            yield remote(
                here, here, first_send.at[i, spot, 1], recv.at[i, spot, first, 1 - second], first_device
            )
        yield remote(
            here, here, core_send.at[i, spot, 0, 1], core_recv.at[i, spot, first, 1 - second], to_core
        )

    def after_first(i, spot, turn):
        by_second = second if turn == 0 else 1 - second
        here = slot(i, spot, 1 - first, by_second, core)
        return remote(
            here, here, core_send.at[i, spot, 1, turn], core_recv.at[i, spot, 1 - first, by_second], to_core
        )

    def line_steps():
        for far in range(1, planes):
            yield z - far, z >= far, up, z < planes - 1
            yield z + far, z < planes - far, down, z > 0

    own_copies = []
    for i in range(count):
        copy = pltpu.make_async_copy(
            shards[i], slot(i, z, first, second, core), own_sem.at[1 + i]
        )
        copy.start()
        own_copies.append(copy)

        @pl.when(z < planes - 1)
        def _():
            up(i, shards[i], z).start()

        @pl.when(z > 0)
        def _():
            down(i, shards[i], z).start()

        for copy in onward(i, shards[i], z):
            copy.start()
    rides = rides_of(planes, rides)

    def issue(number):
        for ride in rides:
            ride.issue_more(number)

    issue(6)
    for i in range(count):
        arrive(i, z, first, 1 - second)
        for copy in after_second(i, z):
            copy.start()
    issue(4)
    for spot, there, direction, further in line_steps():

        @pl.when(there)
        def _():
            for i in range(count):
                here = slot(i, spot, first, second, core)
                arrive(i, spot, first, second)

                @pl.when(further)
                def _():
                    direction(i, here, spot).start()

                for copy in onward(i, here, spot):
                    copy.start()
            for i in range(count):
                arrive(i, spot, first, 1 - second)
                for copy in after_second(i, spot):
                    copy.start()

        issue(4)

    issue(8 * planes)
    spots = [lax.rem(z + at, planes) for at in range(planes)]
    if whole_slice:
        for spot in spots:
            for turn in range(2):
                for i in range(count):
                    arrive(i, spot, 1 - first, second if turn == 0 else 1 - second)
                    after_first(i, spot, turn).start()
    for copy in own_copies:
        copy.wait()
    for i in range(count):
        for spot in range(planes):
            for by_first in range(firsts):
                for by_second in range(2):
                    there = slot(i, spot, by_first, by_second, 1 - core)
                    arrived = core_recv.at[i, spot, by_first, by_second]
                    remote(there, there, own_sem.at[0], arrived, to_core).wait_recv()
    for ride in rides:
        ride.finish()
    for i in range(count):

        @pl.when(z < planes - 1)
        def _():
            up(i, shards[i], z).wait_send()

        @pl.when(z > 0)
        def _():
            down(i, shards[i], z).wait_send()

        for spot, there, direction, further in line_steps():

            @pl.when(there & further)
            def _():
                direction(i, shards[i], spot).wait_send()

        for spot in spots:
            for copy in onward(i, shards[i], spot):
                copy.wait_send()
            for copy in after_second(i, spot):
                copy.wait_send()
            for turn in range(2 * (firsts - 1)):
                after_first(i, spot, turn).wait_send()


def gather_now(shards, planes, whole_slice, collective_id, exchanges=(), part_rows=128):
    parts = [
        (array, start, min(part_rows, shard.shape[0] - start))
        for array, shard in enumerate(shards)
        for start in range(0, shard.shape[0], part_rows)
    ]
    count = len(parts)
    firsts = 2 if whole_slice else 1
    specs = exchange_specs(exchanges)
    dma = pltpu.SemaphoreType.DMA
    grid = (planes, 2, 2, 2) if whole_slice else (planes, 2, 2)
    results = communicate(
        functools.partial(gather_kernel, planes, parts, whole_slice, specs),
        list(shards),
        exchanges,
        [jax.ShapeDtypeStruct((*grid, *shard.shape), shard.dtype) for shard in shards],
        [
            dma((count + 1,)),
            dma((2, count, planes)),
            dma((count, planes)),
            dma((count, planes, 2)),
            dma((count, planes, 2, 2)),
            dma((count, planes, firsts, 2)),
            dma((count, planes, firsts, 2)),
        ],
        planes,
        collective_id,
        200,
        "gather_now",
    )
    places = 4 * planes * firsts
    wholes = [
        whole.reshape(places * shard.shape[0], shard.shape[1])
        for whole, shard in zip(results, shards)
    ]
    return wholes + list(results[len(shards) :])


def scatter_kernel(planes, steps, rows, whole_slice, specs, *refs):
    (partial_ref,), (sum_ref,), scratch, rides = split_refs(refs, 1, 1, specs)
    own, from_core, from_first, from_second, from_below, from_above = scratch[:6]
    load_sem, core_sems, first_sems, second_sems, up_sems, down_sems = scratch[6:]
    blk, z, x, core, y = position()
    firsts = 2 if whole_slice else 1
    to_core = (blk + 1 - 2 * core, y)
    if whole_slice:
        first = y * (1 - core) + x * core
        second = x * (1 - core) + y * core
        core_second = second
        first_device = (blk + core * (2 - 4 * x), y + (1 - core) * (1 - 2 * y))
        second_device = (blk + (1 - core) * (2 - 4 * x), y + core * (1 - 2 * y))
    else:
        first, second = 0, x
        first_device, second_device = None, (blk + 2 - 4 * x, y)
    line = [(blk + 4 * (lax.rem(z + at, planes) - z), y) for at in range(1, planes)]
    nearby = [to_core, second_device] + [first_device] * whole_slice + line
    greet(greeted(specs, nearby))

    def piece(step, by_first, by_second, plane):
        some = pl.ds(pl.multiple_of(step * rows, rows), rows)
        if whole_slice:
            by_x = (1 - plane) * by_second + plane * by_first
            by_y = (1 - plane) * by_first + plane * by_second
            return partial_ref.at[:, by_x, plane, by_y, some]
        return partial_ref.at[:, by_second, plane, some]

    def core_copy(step, by_first, by_second, plane):
        return remote(
            piece(step, by_first, by_second, plane),
            from_core.at[step, by_first, by_second],
            core_sems.at[0, step, by_first, by_second],
            core_sems.at[1, step, by_first, by_second],
            to_core,
        )

    def load(step, by_first, by_second):
        return pltpu.make_async_copy(
            piece(step, by_first, by_second, core),
            own.at[step, by_first, by_second],
            load_sem.at[step, by_first, by_second],
        )

    def first_copy(step):
        return remote(
            own.at[step, 1 - first],
            from_first.at[step],
            first_sems.at[0, step],
            first_sems.at[1, step],
            first_device,
        )

    def second_copy(step):
        return remote(
            own.at[step, first, 1 - second],
            from_second.at[step],
            second_sems.at[0, step],
            second_sems.at[1, step],
            second_device,
        )

    def up_copy(step, target):
        return remote(
            own.at[step, first, second, target],
            from_below.at[step, target],
            up_sems.at[0, step, target],
            up_sems.at[1, step, target],
            (blk + 4, y),
        )

    def down_copy(step, target):
        return remote(
            own.at[step, first, second, target],
            from_above.at[step, target],
            down_sems.at[0, step, target],
            down_sems.at[1, step, target],
            (blk - 4, y),
        )

    def halves():
        if not whole_slice:
            return [(0, 1 - second), (0, second)]
        return [(1 - first, 0), (1 - first, 1), (first, 0), (first, 1)]

    def core_halves():
        if not whole_slice:
            return [(0, 1 - second), (0, second)]
        return [(1 - core_second, 0), (1 - core_second, 1), (core_second, 0), (core_second, 1)]

    def start_loads(step):
        for mine, theirs in zip(halves(), core_halves()):
            core_copy(step, *theirs, 1 - core).start()
            load(step, *mine).start()

    def add_core(step):
        for turn, mine in enumerate(halves()):
            load(step, *mine).wait()
            core_copy(step, *mine, core).wait_recv()
            own[step, *mine] += from_core[step, *mine]
            if whole_slice and turn == 1:
                first_copy(step).start()
            if not whole_slice and turn == 0:
                second_copy(step).start()

    def add_first(step):
        first_copy(step).wait_recv()
        own[step, first, 1 - second] += from_first[step, 1 - second]
        second_copy(step).start()
        own[step, first, second] += from_first[step, second]

    def add_second(step):
        second_copy(step).wait_recv()
        own[step, first, second] += from_second[step]

    def pass_up(step):
        for target in range(planes):

            @pl.when((z > 0) & (z <= target))
            def _():
                up_copy(step, target).wait_recv()

            @pl.when((z > 0) & (z < target))
            def _():
                own[step, first, second, target] += from_below[step, target]

            @pl.when(z < target)
            def _():
                up_copy(step, target).start()

    def pass_down(step):
        for target in range(planes):

            @pl.when((z < planes - 1) & (z >= target))
            def _():
                down_copy(step, target).wait_recv()

            @pl.when((z < planes - 1) & (z > target))
            def _():
                own[step, first, second, target] += from_above[step, target]

            @pl.when(z > target)
            def _():
                down_copy(step, target).start()

    def add_line(step):
        some = pl.ds(pl.multiple_of(step * rows, rows), rows)
        sum_ref[some, :] = own[step, first, second, z]

        @pl.when(z > 0)
        def _():
            sum_ref[some, :] += from_below[step, z]

        @pl.when(z < planes - 1)
        def _():
            sum_ref[some, :] += from_above[step, z]

    start_loads(0)
    start_loads(1)
    rides = rides_of(planes, rides)
    early = firsts + 1
    hurry = [-(-ride.count // steps) for ride in rides]

    @pl.loop(0, steps + early + planes)
    def _(turn):
        def stage(step, work):
            @pl.when((step >= 0) & (step < steps))
            def _():
                work(step)

        @pl.when(turn < steps - 2)
        def _():
            start_loads(turn + 2)

        stage(turn, add_core)
        for ride, number in zip(rides, hurry):
            for at in range(number):
                ride.issue(turn * number + at)
        if whole_slice:
            stage(turn - 1, add_first)
        stage(turn - early + 1, add_second)
        stage(turn - early - z, pass_up)
        stage(turn - early - (planes - 1 - z), pass_down)
        stage(turn - early - planes + 1, add_line)

    @pl.loop(0, steps)
    def _(step):
        for theirs in core_halves():
            core_copy(step, *theirs, 1 - core).wait_send()
        if whole_slice:
            first_copy(step).wait_send()
        second_copy(step).wait_send()
        for target in range(planes):

            @pl.when(z < target)
            def _():
                up_copy(step, target).wait_send()

            @pl.when(z > target)
            def _():
                down_copy(step, target).wait_send()

    for ride in rides:
        ride.finish()


def scatter_now(partial, planes, whole_slice, collective_id, exchanges=()):
    firsts = 2 if whole_slice else 1
    shard_rows = partial.shape[0] // (4 * planes * firsts)
    width = partial.shape[1]
    rows = 16
    steps = shard_rows // rows
    dtype = partial.dtype
    specs = exchange_specs(exchanges)
    dma = pltpu.SemaphoreType.DMA
    grid = (planes, 2, 2, 2) if whole_slice else (planes, 2, 2)
    return communicate(
        functools.partial(scatter_kernel, planes, steps, rows, whole_slice, specs),
        [partial.reshape(*grid, shard_rows, width)],
        exchanges,
        [jax.ShapeDtypeStruct((shard_rows, width), dtype)],
        [
            pltpu.VMEM((steps, firsts, 2, planes, rows, width), dtype),
            pltpu.VMEM((steps, firsts, 2, planes, rows, width), dtype),
            pltpu.VMEM((steps if whole_slice else 1, 2, planes, rows, width), dtype),
            pltpu.VMEM((steps, planes, rows, width), dtype),
            pltpu.VMEM((steps, planes, rows, width), dtype),
            pltpu.VMEM((steps, planes, rows, width), dtype),
            dma((steps, firsts, 2)),
            dma((2, steps, firsts, 2)),
            dma((2, steps)),
            dma((2, steps)),
            dma((2, steps, planes)),
            dma((2, steps, planes)),
        ],
        planes,
        collective_id,
        200,
        "scatter_now",
        out_spec=pltpu.VMEM,
        vmem_limit_bytes=48 * 2**20,
    )


def ffn_pack_kernel(gateup_ref, down_ref, packet_ref):
    live = pl.program_id(0) < FF // HEAD // 2

    @pl.when(live)
    def _():
        for at in range(2):
            columns = slice(at * HEAD, (at + 1) * HEAD)
            packet_ref[at, :, :HEAD] = gateup_ref[0, :, columns].astype(jnp.bfloat16)
            packet_ref[at, :, HEAD : 2 * HEAD] = gateup_ref[1, :, columns].astype(jnp.bfloat16)
            packet_ref[at, :, 2 * HEAD :] = down_ref[:, columns].astype(jnp.bfloat16)

    @pl.when(jnp.logical_not(live))
    def _():
        packet_ref[...] = jnp.zeros_like(packet_ref)


def ffn_packets(gateup, down, device_count):
    row_count = gateup.shape[1]
    last = FF // HEAD // 2 - 1
    return pl.pallas_call(
        ffn_pack_kernel,
        grid=(device_count // 2,),
        in_specs=[
            pl.BlockSpec((2, row_count, 2 * HEAD), lambda j: (0, 0, jnp.minimum(j, last))),
            pl.BlockSpec((row_count, 2 * HEAD), lambda j: (0, jnp.minimum(j, last))),
        ],
        out_specs=pl.BlockSpec((2, row_count, 3 * HEAD), lambda j: (j, 0, 0)),
        out_shape=jax.ShapeDtypeStruct((device_count, row_count, 3 * HEAD), jnp.bfloat16),
        cost_estimate=pl.CostEstimate(flops=0, bytes_accessed=14 * 2**20, transcendentals=0),
        name="ffn_packets",
    )(gateup, down)


def attn_pack_kernel(qkv_ref, out_ref, packet_ref):
    j = pl.program_id(0)

    @pl.when(j < (H + 2) // 2)
    def _():
        for at in range(2):
            packet_ref[at] = qkv_ref[:, at * HEAD : (at + 1) * HEAD].astype(jnp.bfloat16)

    @pl.when((j >= (H + 2) // 2) & (j < H + 1))
    def _():
        for at in range(2):
            packet_ref[at] = out_ref[:, at * HEAD : (at + 1) * HEAD].astype(jnp.bfloat16)

    @pl.when(j >= H + 1)
    def _():
        packet_ref[...] = jnp.zeros_like(packet_ref)


def attn_packets(qkv, out, device_count):
    row_count = qkv.shape[0]
    qkv_last, out_last = (H + 2) // 2 - 1, H // 2 - 1
    return pl.pallas_call(
        attn_pack_kernel,
        grid=(device_count // 2,),
        in_specs=[
            pl.BlockSpec((row_count, 2 * HEAD), lambda j: (0, jnp.minimum(j, qkv_last))),
            pl.BlockSpec((row_count, 2 * HEAD), lambda j: (0, jnp.clip(j - qkv_last - 1, 0, out_last))),
        ],
        out_specs=pl.BlockSpec((2, row_count, HEAD), lambda j: (j, 0, 0)),
        out_shape=jax.ShapeDtypeStruct((device_count, row_count, HEAD), jnp.bfloat16),
        cost_estimate=pl.CostEstimate(flops=0, bytes_accessed=4 * 2**20, transcendentals=0),
        name="attn_packets",
    )(qkv, out)


def turn_kernel(grads_ref, others_ref, mom_ref, *refs):
    *results, current_ref = refs
    if len(results) == 1:
        low_ref, turned_ref = results[0].at[:, :HEAD], results[0].at[:, HEAD:]
    else:
        low_ref, turned_ref = results
    grads = grads_ref[...] + others_ref[...].astype(jnp.float32)
    low_ref[...] = grads.astype(jnp.bfloat16)
    moment = momentum_decay * mom_ref[...].astype(jnp.float32) + grads
    moment = moment.astype(jnp.bfloat16).astype(jnp.float32)
    norm_size = jnp.sqrt(jnp.sum(moment * moment, keepdims=True))
    current_ref[...] = (moment / (norm_size + eps_pieces)).T.astype(jnp.bfloat16)

    @pl.loop(0, NS_STEPS)
    def _(sweep_index):
        current = current_ref[...]
        gram_matrix = lax.dot_general(
            current, current, (((1,), (1,)), ((), ())), preferred_element_type=jnp.float32
        ).astype(jnp.bfloat16)
        square = jnp.dot(gram_matrix, gram_matrix, preferred_element_type=jnp.float32)
        mixing = (ns_second * gram_matrix.astype(jnp.float32) + ns_third * square).astype(
            jnp.bfloat16
        )
        turned = jnp.dot(mixing, current, preferred_element_type=jnp.float32)
        current_ref[...] = (ns_first * current.astype(jnp.float32) + turned).astype(jnp.bfloat16)

    turned_ref[...] = current_ref[...].astype(jnp.float32).T.astype(jnp.bfloat16)


def orthogonalize(grads, others, moms, results):
    depth, columns = grads.shape
    block = pl.BlockSpec((depth, HEAD), lambda j: (0, j))
    pieces = columns // HEAD
    return pl.pallas_call(
        turn_kernel,
        grid=(pieces,),
        in_specs=[block] * 3,
        out_specs=[pl.BlockSpec((depth, 2 // results * HEAD), lambda j: (0, j))] * results,
        out_shape=[jax.ShapeDtypeStruct((depth, 2 // results * columns), jnp.bfloat16)] * results,
        scratch_shapes=[pltpu.VMEM((HEAD, depth), jnp.bfloat16)],
        cost_estimate=pl.CostEstimate(
            flops=pieces * 20 * depth * HEAD * HEAD, bytes_accessed=12 * depth * columns, transcendentals=0
        ),
        compiler_params=pltpu.CompilerParams(vmem_limit_bytes=48 * 2**20),
        name="orthogonalize",
    )(grads, others, moms)


def update(rate, weight, mom, grad, turn):
    moment = momentum_decay * mom + grad.astype(jnp.float32)
    new = (1.0 - weight_shrink) * weight - rate * turn.astype(jnp.float32)
    return new, moment, new.astype(jnp.bfloat16)


def ffn_update_kernel(
    grad_ref, turn_ref, w_gateup_ref, mom_gateup_ref, w_down_ref, mom_down_ref, *results
):
    for at in range(grad_ref.shape[0]):
        columns = slice(at * HEAD, (at + 1) * HEAD)
        for part in range(3):
            spot = (part, slice(None), columns) if part < 2 else (slice(None), columns)
            weight_ref, mom_ref = (
                (w_gateup_ref, mom_gateup_ref) if part < 2 else (w_down_ref, mom_down_ref)
            )
            packed = slice(part * HEAD, (part + 1) * HEAD)
            values = update(
                matrix_rate,
                weight_ref[spot],
                mom_ref[spot],
                grad_ref[at, :, packed],
                turn_ref[at, :, packed],
            )
            for ref, value in zip(results[:3] if part < 2 else results[3:], values):
                ref[spot] = value


def ffn_update(grads, turns, w_gateup, mom_gateup, w_down, mom_down):
    row_count = w_gateup.shape[1]
    wide = 3
    packet = pl.BlockSpec((wide, row_count, 3 * HEAD), lambda j: (j, 0, 0))
    gateup = pl.BlockSpec((2, row_count, wide * HEAD), lambda j: (0, 0, j))
    down = pl.BlockSpec((row_count, wide * HEAD), lambda j: (0, j))
    dtypes = (jnp.float32, jnp.float32, jnp.bfloat16)
    return pl.pallas_call(
        ffn_update_kernel,
        grid=(FF // HEAD // wide,),
        in_specs=[packet, packet, gateup, gateup, down, down],
        out_specs=[gateup] * 3 + [down] * 3,
        out_shape=[jax.ShapeDtypeStruct(w_gateup.shape, dtype) for dtype in dtypes]
        + [jax.ShapeDtypeStruct(w_down.shape, dtype) for dtype in dtypes],
        cost_estimate=pl.CostEstimate(flops=0, bytes_accessed=50 * 2**20, transcendentals=0),
        compiler_params=pltpu.CompilerParams(vmem_limit_bytes=48 * 2**20),
        name="ffn_update",
    )(grads, turns, w_gateup, mom_gateup, w_down, mom_down)


def attn_update_kernel(rate, packet_ref, w_ref, mom_ref, *results):
    for at in range(2):
        columns = slice(at * HEAD, (at + 1) * HEAD)
        values = update(
            rate,
            w_ref[:, columns],
            mom_ref[:, columns],
            packet_ref[at, :, :HEAD],
            packet_ref[at, :, HEAD:],
        )
        for ref, value in zip(results, values):
            ref[:, columns] = value


def attn_update(rate, offset, packets, weight, mom):
    row_count = packets.shape[1]
    packet = pl.BlockSpec((2, row_count, 2 * HEAD), lambda j: (j + offset // 2, 0, 0))
    block = pl.BlockSpec((row_count, 2 * HEAD), lambda j: (0, j))
    return pl.pallas_call(
        functools.partial(attn_update_kernel, rate),
        grid=(weight.shape[1] // HEAD // 2,),
        in_specs=[packet, block, block],
        out_specs=[block] * 3,
        out_shape=[
            jax.ShapeDtypeStruct(weight.shape, dtype)
            for dtype in (jnp.float32, jnp.float32, jnp.bfloat16)
        ],
        cost_estimate=pl.CostEstimate(flops=0, bytes_accessed=6 * 2**20, transcendentals=0),
        name="attn_update",
    )(packets, weight, mom)


def two_heads(ref):
    return jnp.concatenate([ref[:, :HEAD], ref[:, HEAD:]], axis=0)


def visible(tokens, first_token, shape, query_axis):
    query = lax.rem(lax.broadcasted_iota(jnp.int32, shape, query_axis), tokens)
    key = lax.broadcasted_iota(jnp.int32, shape, 1 - query_axis)
    distance = query + WINDOW - key
    return (distance >= 0) & (distance < WINDOW) & (first_token - WINDOW + key >= 0)


def attend_kernel(first_ref, queries_ref, kv_ref, mixed_ref, log_total_ref):
    tokens = queries_ref.shape[0]
    raw = lax.dot_general(
        two_heads(queries_ref),
        kv_ref[:, :HEAD],
        (((1,), (1,)), ((), ())),
        preferred_element_type=jnp.float32,
    )
    allowed = visible(tokens, first_ref[0], raw.shape, 0)
    scores = jnp.where(allowed, raw * HEAD ** (-0.5), masked_score)
    top_score = jnp.max(scores, axis=-1, keepdims=True)
    expo = jnp.exp(scores - top_score)
    total = jnp.sum(expo, axis=-1, keepdims=True)
    probs = (expo / total).astype(jnp.bfloat16)
    mixed = jnp.dot(probs, kv_ref[:, HEAD:], preferred_element_type=jnp.float32)
    mixed_ref[:, :HEAD] = mixed[:tokens].astype(jnp.bfloat16)
    mixed_ref[:, HEAD:] = mixed[tokens:].astype(jnp.bfloat16)
    log_total_ref[0] = jnp.broadcast_to(top_score + jnp.log(total), log_total_ref.shape[1:])


def attend(first_token, qkv, kv_window):
    tokens = qkv.shape[0]
    span = kv_window.shape[0]
    pairs = H // 2
    return pl.pallas_call(
        attend_kernel,
        grid=(pairs,),
        in_specs=[
            pl.BlockSpec(memory_space=pltpu.SMEM),
            pl.BlockSpec((tokens, 2 * HEAD), lambda j: (0, j)),
            pl.BlockSpec((span, 2 * HEAD), lambda j: (0, 0)),
        ],
        out_specs=[
            pl.BlockSpec((tokens, 2 * HEAD), lambda j: (0, j)),
            pl.BlockSpec((1, 2 * tokens, 128), lambda j: (j, 0, 0)),
        ],
        out_shape=[
            jax.ShapeDtypeStruct((tokens, H * HEAD), jnp.bfloat16),
            jax.ShapeDtypeStruct((pairs, 2 * tokens, 128), jnp.float32),
        ],
        cost_estimate=pl.CostEstimate(
            flops=4 * H * tokens * span * HEAD,
            bytes_accessed=4 * 2**20,
            transcendentals=H * tokens * span,
        ),
        compiler_params=pltpu.CompilerParams(vmem_limit_bytes=48 * 2**20),
        name="attend",
    )(first_token, qkv, kv_window)


def attend_back_kernel(
    first_ref, queries_ref, grads_ref, log_total_ref, kv_ref, grad_query_ref, grad_kv_ref, sums_ref
):
    tokens = queries_ref.shape[0]
    score_scale = HEAD ** (-0.5)
    keys, values = kv_ref[:, :HEAD], kv_ref[:, HEAD:]
    queries, grads = two_heads(queries_ref), two_heads(grads_ref)

    def against(left, right):
        return lax.dot_general(
            left, right, (((1,), (1,)), ((), ())), preferred_element_type=jnp.float32
        )

    raw = against(keys, queries)
    allowed = visible(tokens, first_ref[0], raw.shape, 1)
    scores = jnp.where(allowed, raw * score_scale, masked_score)
    log_total = log_total_ref[0].T[:1]
    probs = jnp.exp(scores - log_total)
    grad_probs = against(values, grads)
    row_delta = jnp.sum(probs * grad_probs, axis=0, keepdims=True)
    grad_raw = (probs * (grad_probs - row_delta) * score_scale).astype(jnp.bfloat16)
    grad_query = lax.dot_general(
        grad_raw, keys, (((0,), (0,)), ((), ())), preferred_element_type=jnp.float32
    )
    grad_query_ref[:, :HEAD] = grad_query[:tokens].astype(jnp.bfloat16)
    grad_query_ref[:, HEAD:] = grad_query[tokens:].astype(jnp.bfloat16)

    @pl.when(pl.program_id(0) == 0)
    def _():
        sums_ref[...] = jnp.zeros_like(sums_ref)

    sums_ref[:, :HEAD] += jnp.dot(grad_raw, queries, preferred_element_type=jnp.float32)
    sums_ref[:, HEAD:] += jnp.dot(
        probs.astype(jnp.bfloat16), grads, preferred_element_type=jnp.float32
    )

    @pl.when(pl.program_id(0) == pl.num_programs(0) - 1)
    def _():
        grad_kv_ref[...] = sums_ref[...].astype(jnp.bfloat16)


def attend_back(first_token, qkv, grads, log_total, kv_window):
    tokens = qkv.shape[0]
    span = kv_window.shape[0]
    heads = pl.BlockSpec((tokens, 2 * HEAD), lambda j: (0, j))
    window = pl.BlockSpec((span, 2 * HEAD), lambda j: (0, 0))
    return pl.pallas_call(
        attend_back_kernel,
        grid=(H // 2,),
        in_specs=[
            pl.BlockSpec(memory_space=pltpu.SMEM),
            heads,
            heads,
            pl.BlockSpec((1, 2 * tokens, 128), lambda j: (j, 0, 0)),
            window,
        ],
        out_specs=[heads, window],
        out_shape=[
            jax.ShapeDtypeStruct((tokens, H * HEAD), jnp.bfloat16),
            jax.ShapeDtypeStruct((span, 2 * HEAD), jnp.bfloat16),
        ],
        scratch_shapes=[pltpu.VMEM((span, 2 * HEAD), jnp.float32)],
        cost_estimate=pl.CostEstimate(
            flops=10 * H * tokens * span * HEAD,
            bytes_accessed=8 * 2**20,
            transcendentals=H * tokens * span,
        ),
        compiler_params=pltpu.CompilerParams(vmem_limit_bytes=48 * 2**20),
        name="attend_back",
    )(first_token, qkv, grads, log_total, kv_window)


def rms_scale(stream, gain_row):
    mean_square = jnp.mean(stream * stream, axis=-1, keepdims=True)
    return stream * lax.rsqrt(mean_square + eps_norm) * gain_row


def gelu_product(gate_part, up_part):
    return jax.nn.gelu(gate_part, approximate=True) * up_part


def on_device(
    tokens_in,
    cotangent,
    w_qkv,
    w_out,
    w_gateup,
    w_down,
    gains,
    mom_qkv,
    mom_out,
    mom_gateup,
    mom_down,
    mom_gains,
):
    everyone = ("blk", "pair")
    bf16 = jnp.bfloat16
    f32 = jnp.float32
    blk_count = lax.axis_size("blk")
    pair_count = lax.axis_size("pair")
    device_count = blk_count * pair_count
    block_at = lax.axis_index("blk")
    half_at = lax.axis_index("pair")
    me = block_at * pair_count + half_at
    local_rows, width = tokens_in.shape
    share_rows = w_qkv.shape[0]
    span = WINDOW + local_rows
    token_count = local_rows * device_count
    large = token_count * width * 2 > 48 * 2**20
    planes = blk_count // 4

    def after(value, earlier):
        return lax.optimization_barrier((value, earlier))[0] if large else value

    def exchange(packets, axes=everyone):
        return lax.all_to_all(packets, axes, split_axis=0, concat_axis=0, tiled=True)

    def swap(shard):
        return lax.ppermute(shard, "pair", [(0, 1), (1, 0)])

    def hold(value, *earlier):
        return value if large else lax.optimization_barrier((value, earlier))[0]

    def ride(packets, among="all", sources=None, targets=None):
        places = packets.shape[0]
        return Exchange(packets, among, sources or places, targets or places)

    def exchanged(rides):
        axes = {"all": everyone, "plane": "blk"}
        return [
            swap(each.packets) if each.among == "pair" else exchange(each.packets, axes[each.among])
            for each in rides
        ]

    def gather(shards, whole_slice, collective_id, rides=(), **options):
        if large:
            axes = everyone if whole_slice else "blk"
            wholes = [lax.all_gather(shard, axes, axis=0, tiled=True) for shard in shards]
            return wholes + exchanged(rides)
        return gather_now(shards, planes, whole_slice, collective_id, rides, **options)

    def scatter(partial, whole_slice, collective_id, rides=()):
        if large:
            axes = everyone if whole_slice else "blk"
            part = lax.psum_scatter(partial, axes, scatter_dimension=0, tiled=True)
            return [part] + exchanged(rides)
        return scatter_now(partial, planes, whole_slice, collective_id, rides)

    def gather_plane(shard):
        return lax.all_gather(shard, "blk", axis=0, tiled=True)

    stream = tokens_in.astype(f32)
    padded_gains = jnp.pad(gains.astype(bf16), ((0, 14), (0, 128 - share_rows)))
    full_qkv, full_gains, full_out, ffn_weights = gather(
        [w_qkv.astype(bf16), padded_gains, w_out.T.astype(bf16)],
        True,
        1,
        [ride(ffn_packets(w_gateup, w_down.T, device_count))],
    )
    ffn_weights = ffn_weights.reshape(width, 3 * HEAD)
    full_gains = full_gains.reshape(device_count, 16, 128)[:, :2, :share_rows].astype(f32)
    gain_attn = full_gains[:, 0].reshape(width)
    gain_mlp = full_gains[:, 1].reshape(width)
    normed_attn_f, norm_back_attn = jax.vjp(rms_scale, stream, gain_attn)
    normed_attn = normed_attn_f.astype(bf16)
    qkv = jnp.dot(normed_attn, full_qkv, preferred_element_type=f32).astype(bf16)
    (kv_all,) = gather([qkv[:, H * HEAD :]], True, 2)
    kv_window = lax.dynamic_slice_in_dim(
        jnp.pad(kv_all, ((WINDOW, 0), (0, 0))), me * local_rows, span, 0
    )
    first_token = (me * local_rows).astype(jnp.int32).reshape(1)
    mixed, log_total = attend(first_token, qkv, kv_window)
    resid = stream + jnp.einsum("tc,dc->td", mixed, full_out, preferred_element_type=f32)

    normed_mlp_f, norm_back_mlp = jax.vjp(rms_scale, resid, gain_mlp)
    normed_mlp = normed_mlp_f.astype(bf16)
    normed_mlp_plane, cotangent_plane, other_weights = gather(
        [normed_mlp, cotangent], False, 3, [ride(ffn_weights, "pair")], part_rows=64
    )
    pair_weights = [ffn_weights, other_weights]
    gates, ups, downs = (
        [weights[:, part * HEAD : (part + 1) * HEAD] for weights in pair_weights]
        for part in range(3)
    )
    pair_gateup = jnp.concatenate(gates + ups, axis=1)
    pair_down = jnp.concatenate(downs, axis=1)
    plane_rows = blk_count * local_rows
    both_parts = jnp.dot(normed_mlp_plane, pair_gateup, preferred_element_type=f32)
    pair_width = pair_count * HEAD
    hidden_f, geglu_back = jax.vjp(
        gelu_product, both_parts[:, :pair_width], both_parts[:, pair_width:]
    )
    hidden = hidden_f.astype(bf16)
    grad_hidden = jnp.dot(cotangent_plane, pair_down, preferred_element_type=f32)
    grad_gate, grad_up = geglu_back(grad_hidden)
    grad_gateup = jnp.concatenate([grad_gate.astype(bf16), grad_up.astype(bf16)], axis=1)
    def ffn_gradient(columns):
        gateup_right = jnp.concatenate(
            [grad_gate[:, columns].astype(bf16), grad_up[:, columns].astype(bf16)], axis=1
        )
        down_right = hidden[:, columns]
        return jnp.concatenate(
            [
                jnp.einsum("td,tf->df", normed_mlp_plane, gateup_right, preferred_element_type=f32),
                jnp.einsum("td,tf->df", cotangent_plane, down_right, preferred_element_type=f32),
            ],
            axis=1,
        )

    ffn_theirs = ffn_gradient(slice(HEAD, 2 * HEAD)).astype(bf16)
    grad_normed_part = jnp.einsum("tf,df->td", grad_gateup, pair_gateup, preferred_element_type=f32)
    grad_normed_mlp, ffn_others, ffn_moms, attn_moms = scatter(
        grad_normed_part.astype(bf16),
        False,
        4,
        [
            ride(ffn_theirs, "pair"),
            ride(ffn_packets(mom_gateup, mom_down.T, device_count), targets=FF // HEAD),
            ride(attn_packets(mom_qkv, mom_out.T, device_count), targets=2 * H + 2),
        ],
    )
    grad_normed_mlp = grad_normed_mlp.astype(f32)

    ffn_grads = ffn_gradient(slice(0, HEAD))
    ffn_low, ffn_turned = orthogonalize(
        ffn_grads, ffn_others, ffn_moms.reshape(width, 3 * HEAD), 2
    )
    ffn_shape = (device_count, share_rows, 3 * HEAD)

    resid_part, gain_grad_mlp = norm_back_mlp(grad_normed_mlp)
    grad_resid = cotangent.astype(f32) + resid_part
    grad_proj = grad_resid.astype(bf16)
    grad_mixed = jnp.dot(grad_proj, full_out, preferred_element_type=f32).astype(bf16)
    grad_query, grad_kv = attend_back(first_token, qkv, grad_mixed, log_total, kv_window)
    grad_kv_all = lax.dynamic_update_slice_in_dim(
        jnp.zeros((WINDOW + token_count, 2 * HEAD), bf16), grad_kv, me * local_rows, 0
    )[WINDOW:]
    grad_kv, ffn_low = scatter(
        grad_kv_all, True, 5, [ride(ffn_low.reshape(ffn_shape), sources=FF // HEAD)]
    )
    grad_qkv = jnp.concatenate([grad_query, grad_kv], axis=1)
    grad_normed_attn = jnp.einsum("tc,dc->td", grad_qkv, full_qkv, preferred_element_type=f32)
    stream_part, gain_grad_attn = norm_back_attn(grad_normed_attn)
    input_grad = grad_resid + stream_part

    attn_rights = jnp.concatenate([grad_qkv, mixed], axis=1)
    used = attn_rights.shape[1] // pair_width
    attn_rights = attn_rights.reshape(local_rows, used, pair_width).transpose(1, 0, 2)
    attn_rights = jnp.pad(attn_rights, ((0, blk_count - used), (0, 0), (0, 0)))
    branch_part = jnp.einsum(
        "tf,df->td", after(hidden, grad_normed_mlp), pair_down, preferred_element_type=f32
    )
    branch, ffn_turned, attn_rights = scatter(
        branch_part.astype(bf16),
        False,
        6,
        [
            ride(ffn_turned.reshape(ffn_shape), sources=FF // HEAD),
            ride(attn_rights, "plane", targets=used),
        ],
    )
    attn_rights = attn_rights.reshape(plane_rows, pair_width)
    block_output = (resid + branch.astype(f32)).astype(bf16)
    normed_attn_plane = gather_plane(after(hold(normed_attn, normed_mlp_plane), (ffn_grads, block_output)))
    grad_proj_plane = gather_plane(after(grad_proj, (ffn_grads, block_output)))

    def attn_gradient(lefts):
        return jnp.einsum("td,tf->df", lefts, attn_rights, preferred_element_type=f32)

    attn_grads = lax.cond(
        block_at < (H + 2) // pair_count,
        lambda: attn_gradient(normed_attn_plane),
        lambda: attn_gradient(grad_proj_plane),
    )
    attn_others = swap(
        lax.dynamic_slice_in_dim(attn_grads, (1 - half_at) * HEAD, HEAD, 1).astype(bf16)
    )
    attn_grads = lax.dynamic_slice_in_dim(attn_grads, half_at * HEAD, HEAD, 1)
    updated_ffn = ffn_update(ffn_low, ffn_turned, w_gateup, mom_gateup, w_down.T, mom_down.T)
    (attn_results,) = orthogonalize(
        attn_grads, hold(attn_others, updated_ffn[0]), attn_moms.reshape(width, HEAD), 1
    )
    gain_grads = jnp.stack([gain_grad_attn, gain_grad_mlp], axis=0)
    gain_grads = gain_grads.reshape(2, device_count, share_rows).transpose(1, 0, 2)
    last_rides = [
        ride(attn_results.reshape(device_count, share_rows, 2 * HEAD), sources=2 * H + 2),
        ride(jnp.pad(gain_grads, ((0, 0), (0, 6), (0, 128 - share_rows)))),
    ]
    if large:
        attn_results, gain_grads = exchanged(last_rides)
    else:
        attn_results, gain_grads = exchange_now(last_rides, planes, 7)
    gain_share = jnp.sum(gain_grads, axis=0)[:2, :share_rows]

    updated_qkv = attn_update(matrix_rate, 0, attn_results, w_qkv, mom_qkv)
    updated_out = attn_update(output_rate, H + 2, attn_results, w_out.T, mom_out.T)
    moment_gains = momentum_decay * mom_gains + gain_share
    new_gains = gains - gain_rate * moment_gains
    return (
        block_output,
        input_grad,
        *updated_qkv,
        *(result.T for result in updated_out),
        *updated_ffn[:3],
        *(result.T for result in updated_ffn[3:]),
        new_gains,
        moment_gains,
        new_gains.astype(bf16),
    )


def solution(mesh):
    placed = (
        P(("blk", "pair"), None),
        P(("blk", "pair"), None),
        P(("blk", "pair"), None),
        P(None, ("blk", "pair")),
        P(None, ("blk", "pair"), None),
        P(None, ("blk", "pair")),
        P(None, ("blk", "pair")),
        P(("blk", "pair"), None),
        P(None, ("blk", "pair")),
        P(None, ("blk", "pair"), None),
        P(None, ("blk", "pair")),
        P(None, ("blk", "pair")),
    )
    return jax.shard_map(
        on_device,
        mesh=mesh,
        in_specs=placed,
        out_specs=(
            P(("blk", "pair"), None),
            P(("blk", "pair"), None),
            P(("blk", "pair"), None),
            P(("blk", "pair"), None),
            P(("blk", "pair"), None),
            P(None, ("blk", "pair")),
            P(None, ("blk", "pair")),
            P(None, ("blk", "pair")),
            P(None, ("blk", "pair"), None),
            P(None, ("blk", "pair"), None),
            P(None, ("blk", "pair"), None),
            P(None, ("blk", "pair")),
            P(None, ("blk", "pair")),
            P(None, ("blk", "pair")),
            P(None, ("blk", "pair")),
            P(None, ("blk", "pair")),
            P(None, ("blk", "pair")),
        ),
        check_vma=False,
    )
```

```python
import functools
from typing import NamedTuple

import jax
import jax.numpy as jnp
from jax import lax
from jax.experimental import pallas as pl
from jax.experimental.pallas import tpu as pltpu
from jax.sharding import PartitionSpec as P

H = 10
HEAD = 256
FF = 7680
WINDOW = 2048
NS_STEPS = 5


eps_norm = 1e-06
eps_pieces = 1e-07
ns_first = 3.4445
ns_second = -4.775
ns_third = 2.0315
momentum_decay = 0.95
matrix_rate = 0.5
output_rate = 10.0
gain_rate = 0.001
weight_shrink = 0.001
masked_score = -1e30
MESH = pl.DeviceIdType.MESH


def position():
    blk, y = lax.axis_index("blk"), lax.axis_index("pair")
    return blk, lax.div(blk, 4), lax.rem(lax.div(blk, 2), 2), lax.rem(blk, 2), y


def greet(devices):
    barrier = pltpu.get_barrier_semaphore()
    for device in devices:
        pl.semaphore_signal(barrier, inc=1, device_id=device, device_id_type=MESH)
    pl.semaphore_wait(barrier, len(devices))


def remote(source, target, send_sem, recv_sem, device):
    return pltpu.make_async_remote_copy(
        src_ref=source,
        dst_ref=target,
        send_sem=send_sem,
        recv_sem=recv_sem,
        device_id=device,
        device_id_type=MESH,
    )


class Exchange(NamedTuple):
    packets: jax.Array
    among: str
    sources: int
    first_target: int = 0
    spread_sources: bool = False
    spread_targets: bool = False


def spread_place(planes, blk):
    return lax.rem(blk, 4) * planes + lax.div(blk, 4)


def all_devices():
    blk, _, _, _, y = position()
    count = 2 * lax.axis_size("blk")
    here = 2 * blk + y
    places = [lax.rem(here + at, count) for at in range(1, count)]
    return [(lax.div(place, 2), lax.rem(place, 2)) for place in places]


def plane_devices():
    blk, _, _, _, y = position()
    count = lax.axis_size("blk")
    return [(lax.rem(blk + at, count), y) for at in range(1, count)]


def greeted(specs, nearby):
    if any(among == "all" for among, *_ in specs):
        return all_devices()
    blk, _, _, _, y = position()
    pair = [(blk, 1 - y)] * any(among == "pair" for among, *_ in specs)
    if any(among == "plane" for among, *_ in specs):
        return plane_devices() + pair
    return nearby + pair


PAIR_PARTS = 4


def exchange_count(planes, among):
    return {"all": 8 * planes, "plane": 4 * planes, "pair": PAIR_PARTS}[among]


class Ride:
    def __init__(self, planes, spec, packets, received, sems):
        self.planes, self.packets, self.received = planes, packets, received
        self.among, self.sources, self.first_target, self.from_spread, self.to_spread = spec
        self.own_sem, self.send_sems, self.recv_sems = sems
        self.count = exchange_count(planes, self.among)
        self.issued = 0
        blk, self.z, _, _, self.y = position()
        self.blk = blk
        self.here = blk if self.among == "plane" else 2 * blk + self.y

    def place(self, q):
        near = self.count // self.planes
        spot = lax.rem(self.z + 1 + lax.rem(q, self.planes), self.planes)
        return spot * near + lax.rem(self.here + lax.div(q, self.planes), near)

    def counted(self, place, spread):
        if not spread:
            return place
        if self.among == "plane":
            return spread_place(self.planes, place)
        return 2 * spread_place(self.planes, lax.div(place, 2)) + lax.rem(place, 2)

    def source(self, place):
        return self.counted(place, self.from_spread)

    def target(self, place):
        return self.counted(place, self.to_spread) - self.first_target

    def sending(self, place):
        return self.source(place) < self.sources

    def receiving(self, place):
        target = self.target(place)
        return (target >= 0) & (target < self.packets.shape[0])

    def copy(self, q):
        if self.among == "pair":
            rows = self.packets.shape[0] // PAIR_PARTS
            some = pl.ds(pl.multiple_of(q * rows, rows), rows)
            return remote(
                self.packets.at[some],
                self.received.at[some],
                self.send_sems.at[q],
                self.recv_sems.at[q],
                (self.blk, 1 - self.y),
            )
        place = self.place(q)
        device = (place, self.y)
        if self.among == "all":
            device = (lax.div(place, 2), lax.rem(place, 2))
        source = self.source(self.here)
        return remote(
            self.packets.at[self.target(place)],
            self.received.at[source],
            self.send_sems.at[q],
            self.recv_sems.at[source],
            device,
        )

    def own(self):
        return pltpu.make_async_copy(
            self.packets.at[self.target(self.here)],
            self.received.at[self.source(self.here)],
            self.own_sem.at[0],
        )

    def sends(self, q):
        away = (q < self.count) & (q != self.planes - 1)
        return away & self.sending(self.here) & self.receiving(self.place(q))

    def keeps(self):
        return self.sending(self.here) & self.receiving(self.here)

    def start_own(self):
        if self.among == "pair":
            for q in range(self.count):
                self.copy(q).start()
        else:

            @pl.when(self.keeps())
            def _():
                self.own().start()

    def issue(self, q):
        if self.among != "pair":

            @pl.when(self.sends(q))
            def _():
                self.copy(q).start()

    def issue_more(self, number):
        first, self.issued = self.issued, min(self.issued + number, self.count)

        @pl.loop(first, self.issued)
        def _(q):
            self.issue(q)

    def finish(self):
        if self.among == "pair":
            for q in range(self.count):
                self.copy(q).wait()
            return

        @pl.loop(0, self.count)
        def _(q):
            @pl.when(self.sends(q))
            def _():
                self.copy(q).wait_send()

            @pl.when((q != self.here) & self.sending(q) & self.receiving(self.here))
            def _():
                source = self.source(q)
                spot = self.received.at[source]
                remote(
                    spot, spot, self.own_sem.at[0], self.recv_sems.at[source], (self.blk, self.y)
                ).wait_recv()

        @pl.when(self.keeps())
        def _():
            self.own().wait()


def rides_of(planes, rides):
    rides = [Ride(planes, *ride) for ride in rides]
    for ride in rides:
        ride.start_own()
    return rides


def exchange_sems(exchanges, planes):
    dma = pltpu.SemaphoreType.DMA
    return [
        dma((count,))
        for exchange in exchanges
        for count in (1,) + (exchange_count(planes, exchange.among),) * 2
    ]


def exchange_specs(exchanges):
    return tuple((each.among, *each[2:]) for each in exchanges)


def communicate(
    kernel,
    operands,
    exchanges,
    outputs,
    scratch,
    planes,
    collective_id,
    cost,
    name,
    out_spec=pl.ANY,
    **options,
):
    packets = [each.packets for each in exchanges]
    received = [
        jax.ShapeDtypeStruct(
            array.shape
            if each.among == "pair"
            else (exchange_count(planes, each.among), *array.shape[1:]),
            array.dtype,
        )
        for each, array in zip(exchanges, packets)
    ]
    any_spec = pl.BlockSpec(memory_space=pl.ANY)
    return pl.pallas_call(
        kernel,
        out_shape=outputs + received,
        in_specs=[any_spec] * (len(operands) + len(packets)),
        out_specs=[pl.BlockSpec(memory_space=out_spec)] * len(outputs) + [any_spec] * len(packets),
        scratch_shapes=scratch + exchange_sems(exchanges, planes),
        compiler_params=pltpu.CompilerParams(
            collective_id=collective_id, has_side_effects=True, **options
        ),
        cost_estimate=pl.CostEstimate(flops=0, bytes_accessed=cost * 2**20, transcendentals=0),
        name=name,
    )(*operands, *packets)


def split_refs(refs, inputs, outputs, specs):
    riders = len(specs)
    ins, refs = refs[: inputs + riders], refs[inputs + riders :]
    outs, refs = refs[: outputs + riders], refs[outputs + riders :]
    scratch = refs[: len(refs) - 3 * riders]
    sems = refs[len(refs) - 3 * riders :]
    rides = [
        (spec, ins[inputs + i], outs[outputs + i], sems[3 * i : 3 * i + 3])
        for i, spec in enumerate(specs)
    ]
    return ins[:inputs], outs[:outputs], scratch, rides


def exchange_kernel(planes, specs, *refs):
    _, _, _, rides = split_refs(refs, 0, 0, specs)
    greet(greeted(specs, []))
    rides = rides_of(planes, rides)
    for ride in rides:
        ride.issue_more(ride.count)
    for ride in rides:
        ride.finish()


def exchange_now(exchanges, planes, collective_id):
    specs = exchange_specs(exchanges)
    kernel = functools.partial(exchange_kernel, planes, specs)
    return communicate(kernel, [], exchanges, [], [], planes, collective_id, 100, "exchange_now")


def gather_kernel(planes, parts, whole_slice, specs, *refs):
    arrays = 1 + max(array for array, _, _ in parts)
    shard_refs, whole_refs, scratch, rides = split_refs(refs, arrays, arrays, specs)
    count = len(parts)
    shards = [shard_refs[array].at[pl.ds(start, size)] for array, start, size in parts]
    own_sem, line_send, second_send, first_send, core_send, recv, core_recv = scratch
    blk, z, x, core, y = position()
    firsts = 2 if whole_slice else 1
    to_core = (blk + 1 - 2 * core, y)
    if whole_slice:
        first = y * (1 - core) + x * core
        second = x * (1 - core) + y * core
        first_device = (blk + core * (2 - 4 * x), y + (1 - core) * (1 - 2 * y))
        second_device = (blk + (1 - core) * (2 - 4 * x), y + core * (1 - 2 * y))
    else:
        first, second = 0, x
        first_device, second_device = None, (blk + 2 - 4 * x, y)
    line = [(blk + 4 * (lax.rem(z + at, planes) - z), y) for at in range(1, planes)]
    nearby = [to_core, second_device] + [first_device] * whole_slice + line
    greet(greeted(specs, nearby))

    def slot(i, spot, by_first, by_second, plane):
        array, start, size = parts[i]
        whole, some = whole_refs[array], pl.ds(start, size)
        if whole_slice:
            by_x = (1 - plane) * by_second + plane * by_first
            by_y = (1 - plane) * by_first + plane * by_second
            return whole.at[spot, by_x, plane, by_y, some]
        return whole.at[spot, by_second, plane, some]

    def arrive(i, spot, by_first, by_second):
        here = slot(i, spot, by_first, by_second, core)
        remote(here, here, own_sem.at[0], recv.at[i, spot, by_first, by_second], to_core).wait_recv()

    def up(i, source, spot):
        target = slot(i, spot, first, second, core)
        device = (blk + 4, y)
        return remote(source, target, line_send.at[0, i, spot], recv.at[i, spot, first, second], device)

    def down(i, source, spot):
        target = slot(i, spot, first, second, core)
        device = (blk - 4, y)
        return remote(source, target, line_send.at[1, i, spot], recv.at[i, spot, first, second], device)

    def onward(i, source, spot):
        target = slot(i, spot, first, second, core)
        arrived = recv.at[i, spot, first, second]
        yield remote(source, target, second_send.at[i, spot], arrived, second_device)
        if whole_slice:
            yield remote(source, target, first_send.at[i, spot, 0], arrived, first_device)
        yield remote(
            source, target, core_send.at[i, spot, 0, 0], core_recv.at[i, spot, first, second], to_core
        )

    def after_second(i, spot):
        here = slot(i, spot, first, 1 - second, core)
        if whole_slice:
            yield remote(
                here, here, first_send.at[i, spot, 1], recv.at[i, spot, first, 1 - second], first_device
            )
        yield remote(
            here, here, core_send.at[i, spot, 0, 1], core_recv.at[i, spot, first, 1 - second], to_core
        )

    def after_first(i, spot, turn):
        by_second = second if turn == 0 else 1 - second
        here = slot(i, spot, 1 - first, by_second, core)
        return remote(
            here, here, core_send.at[i, spot, 1, turn], core_recv.at[i, spot, 1 - first, by_second], to_core
        )

    def line_steps():
        for far in range(1, planes):
            yield z - far, z >= far, up, z < planes - 1
            yield z + far, z < planes - far, down, z > 0

    own_copies = []
    for i in range(count):
        copy = pltpu.make_async_copy(
            shards[i], slot(i, z, first, second, core), own_sem.at[1 + i]
        )
        copy.start()
        own_copies.append(copy)

        @pl.when(z < planes - 1)
        def _():
            up(i, shards[i], z).start()

        @pl.when(z > 0)
        def _():
            down(i, shards[i], z).start()

        for copy in onward(i, shards[i], z):
            copy.start()
    rides = rides_of(planes, rides)

    def issue(number):
        for ride in rides:
            ride.issue_more(number)

    issue(6)
    for i in range(count):
        arrive(i, z, first, 1 - second)
        for copy in after_second(i, z):
            copy.start()
    issue(4)
    for spot, there, direction, further in line_steps():

        @pl.when(there)
        def _():
            for i in range(count):
                here = slot(i, spot, first, second, core)
                arrive(i, spot, first, second)

                @pl.when(further)
                def _():
                    direction(i, here, spot).start()

                for copy in onward(i, here, spot):
                    copy.start()
            for i in range(count):
                arrive(i, spot, first, 1 - second)
                for copy in after_second(i, spot):
                    copy.start()

        issue(4)

    issue(8 * planes)
    spots = [lax.rem(z + at, planes) for at in range(planes)]
    if whole_slice:
        for spot in spots:
            for turn in range(2):
                for i in range(count):
                    arrive(i, spot, 1 - first, second if turn == 0 else 1 - second)
                    after_first(i, spot, turn).start()
    for copy in own_copies:
        copy.wait()
    for i in range(count):
        for spot in range(planes):
            for by_first in range(firsts):
                for by_second in range(2):
                    there = slot(i, spot, by_first, by_second, 1 - core)
                    arrived = core_recv.at[i, spot, by_first, by_second]
                    remote(there, there, own_sem.at[0], arrived, to_core).wait_recv()
    for ride in rides:
        ride.finish()
    for i in range(count):

        @pl.when(z < planes - 1)
        def _():
            up(i, shards[i], z).wait_send()

        @pl.when(z > 0)
        def _():
            down(i, shards[i], z).wait_send()

        for spot, there, direction, further in line_steps():

            @pl.when(there & further)
            def _():
                direction(i, shards[i], spot).wait_send()

        for spot in spots:
            for copy in onward(i, shards[i], spot):
                copy.wait_send()
            for copy in after_second(i, spot):
                copy.wait_send()
            for turn in range(2 * (firsts - 1)):
                after_first(i, spot, turn).wait_send()


def gather_now(shards, planes, whole_slice, collective_id, exchanges=(), part_rows=128):
    parts = [
        (array, start, min(part_rows, shard.shape[0] - start))
        for array, shard in enumerate(shards)
        for start in range(0, shard.shape[0], part_rows)
    ]
    count = len(parts)
    firsts = 2 if whole_slice else 1
    specs = exchange_specs(exchanges)
    dma = pltpu.SemaphoreType.DMA
    grid = (planes, 2, 2, 2) if whole_slice else (planes, 2, 2)
    results = communicate(
        functools.partial(gather_kernel, planes, parts, whole_slice, specs),
        list(shards),
        exchanges,
        [jax.ShapeDtypeStruct((*grid, *shard.shape), shard.dtype) for shard in shards],
        [
            dma((count + 1,)),
            dma((2, count, planes)),
            dma((count, planes)),
            dma((count, planes, 2)),
            dma((count, planes, 2, 2)),
            dma((count, planes, firsts, 2)),
            dma((count, planes, firsts, 2)),
        ],
        planes,
        collective_id,
        200,
        "gather_now",
    )
    places = 4 * planes * firsts
    wholes = [
        whole.reshape(places * shard.shape[0], shard.shape[1])
        for whole, shard in zip(results, shards)
    ]
    return wholes + list(results[len(shards) :])


def scatter_kernel(planes, steps, rows, whole_slice, specs, *refs):
    (partial_ref,), (sum_ref,), scratch, rides = split_refs(refs, 1, 1, specs)
    own, from_core, from_first, from_second, from_below, from_above = scratch[:6]
    load_sem, core_sems, first_sems, second_sems, up_sems, down_sems = scratch[6:]
    blk, z, x, core, y = position()
    firsts = 2 if whole_slice else 1
    to_core = (blk + 1 - 2 * core, y)
    if whole_slice:
        first = y * (1 - core) + x * core
        second = x * (1 - core) + y * core
        core_second = second
        first_device = (blk + core * (2 - 4 * x), y + (1 - core) * (1 - 2 * y))
        second_device = (blk + (1 - core) * (2 - 4 * x), y + core * (1 - 2 * y))
    else:
        first, second = 0, x
        first_device, second_device = None, (blk + 2 - 4 * x, y)
    line = [(blk + 4 * (lax.rem(z + at, planes) - z), y) for at in range(1, planes)]
    nearby = [to_core, second_device] + [first_device] * whole_slice + line
    greet(greeted(specs, nearby))

    def piece(step, by_first, by_second, plane):
        some = pl.ds(pl.multiple_of(step * rows, rows), rows)
        if whole_slice:
            by_x = (1 - plane) * by_second + plane * by_first
            by_y = (1 - plane) * by_first + plane * by_second
            return partial_ref.at[:, by_x, plane, by_y, some]
        return partial_ref.at[:, by_second, plane, some]

    def core_copy(step, by_first, by_second, plane):
        return remote(
            piece(step, by_first, by_second, plane),
            from_core.at[step, by_first, by_second],
            core_sems.at[0, step, by_first, by_second],
            core_sems.at[1, step, by_first, by_second],
            to_core,
        )

    def load(step, by_first, by_second):
        return pltpu.make_async_copy(
            piece(step, by_first, by_second, core),
            own.at[step, by_first, by_second],
            load_sem.at[step, by_first, by_second],
        )

    def first_copy(step):
        return remote(
            own.at[step, 1 - first],
            from_first.at[step],
            first_sems.at[0, step],
            first_sems.at[1, step],
            first_device,
        )

    def second_copy(step):
        return remote(
            own.at[step, first, 1 - second],
            from_second.at[step],
            second_sems.at[0, step],
            second_sems.at[1, step],
            second_device,
        )

    def up_copy(step, target):
        return remote(
            own.at[step, first, second, target],
            from_below.at[step, target],
            up_sems.at[0, step, target],
            up_sems.at[1, step, target],
            (blk + 4, y),
        )

    def down_copy(step, target):
        return remote(
            own.at[step, first, second, target],
            from_above.at[step, target],
            down_sems.at[0, step, target],
            down_sems.at[1, step, target],
            (blk - 4, y),
        )

    def halves():
        if not whole_slice:
            return [(0, 1 - second), (0, second)]
        return [(1 - first, 0), (1 - first, 1), (first, 0), (first, 1)]

    def core_halves():
        if not whole_slice:
            return [(0, 1 - second), (0, second)]
        return [(1 - core_second, 0), (1 - core_second, 1), (core_second, 0), (core_second, 1)]

    def start_loads(step):
        for mine, theirs in zip(halves(), core_halves()):
            core_copy(step, *theirs, 1 - core).start()
            load(step, *mine).start()

    def add_core(step):
        for turn, mine in enumerate(halves()):
            load(step, *mine).wait()
            core_copy(step, *mine, core).wait_recv()
            own[step, *mine] += from_core[step, *mine]
            if whole_slice and turn == 1:
                first_copy(step).start()
            if not whole_slice and turn == 0:
                second_copy(step).start()

    def add_first(step):
        first_copy(step).wait_recv()
        own[step, first, 1 - second] += from_first[step, 1 - second]
        second_copy(step).start()
        own[step, first, second] += from_first[step, second]

    def add_second(step):
        second_copy(step).wait_recv()
        own[step, first, second] += from_second[step]

    def pass_up(step):
        for target in range(planes):

            @pl.when((z > 0) & (z <= target))
            def _():
                up_copy(step, target).wait_recv()

            @pl.when((z > 0) & (z < target))
            def _():
                own[step, first, second, target] += from_below[step, target]

            @pl.when(z < target)
            def _():
                up_copy(step, target).start()

    def pass_down(step):
        for target in range(planes):

            @pl.when((z < planes - 1) & (z >= target))
            def _():
                down_copy(step, target).wait_recv()

            @pl.when((z < planes - 1) & (z > target))
            def _():
                own[step, first, second, target] += from_above[step, target]

            @pl.when(z > target)
            def _():
                down_copy(step, target).start()

    def add_line(step):
        some = pl.ds(pl.multiple_of(step * rows, rows), rows)
        sum_ref[some, :] = own[step, first, second, z]

        @pl.when(z > 0)
        def _():
            sum_ref[some, :] += from_below[step, z]

        @pl.when(z < planes - 1)
        def _():
            sum_ref[some, :] += from_above[step, z]

    start_loads(0)
    start_loads(1)
    rides = rides_of(planes, rides)
    early = firsts + 1
    hurry = [-(-ride.count // steps) for ride in rides]

    @pl.loop(0, steps + early + planes)
    def _(turn):
        def stage(step, work):
            @pl.when((step >= 0) & (step < steps))
            def _():
                work(step)

        @pl.when(turn < steps - 2)
        def _():
            start_loads(turn + 2)

        stage(turn, add_core)
        for ride, number in zip(rides, hurry):
            for at in range(number):
                ride.issue(turn * number + at)
        if whole_slice:
            stage(turn - 1, add_first)
        stage(turn - early + 1, add_second)
        stage(turn - early - z, pass_up)
        stage(turn - early - (planes - 1 - z), pass_down)
        stage(turn - early - planes + 1, add_line)

    @pl.loop(0, steps)
    def _(step):
        for theirs in core_halves():
            core_copy(step, *theirs, 1 - core).wait_send()
        if whole_slice:
            first_copy(step).wait_send()
        second_copy(step).wait_send()
        for target in range(planes):

            @pl.when(z < target)
            def _():
                up_copy(step, target).wait_send()

            @pl.when(z > target)
            def _():
                down_copy(step, target).wait_send()

    for ride in rides:
        ride.finish()


def scatter_now(partial, planes, whole_slice, collective_id, exchanges=()):
    firsts = 2 if whole_slice else 1
    shard_rows = partial.shape[0] // (4 * planes * firsts)
    width = partial.shape[1]
    rows = 16
    steps = shard_rows // rows
    dtype = partial.dtype
    specs = exchange_specs(exchanges)
    dma = pltpu.SemaphoreType.DMA
    grid = (planes, 2, 2, 2) if whole_slice else (planes, 2, 2)
    return communicate(
        functools.partial(scatter_kernel, planes, steps, rows, whole_slice, specs),
        [partial.reshape(*grid, shard_rows, width)],
        exchanges,
        [jax.ShapeDtypeStruct((shard_rows, width), dtype)],
        [
            pltpu.VMEM((steps, firsts, 2, planes, rows, width), dtype),
            pltpu.VMEM((steps, firsts, 2, planes, rows, width), dtype),
            pltpu.VMEM((steps if whole_slice else 1, 2, planes, rows, width), dtype),
            pltpu.VMEM((steps, planes, rows, width), dtype),
            pltpu.VMEM((steps, planes, rows, width), dtype),
            pltpu.VMEM((steps, planes, rows, width), dtype),
            dma((steps, firsts, 2)),
            dma((2, steps, firsts, 2)),
            dma((2, steps)),
            dma((2, steps)),
            dma((2, steps, planes)),
            dma((2, steps, planes)),
        ],
        planes,
        collective_id,
        200,
        "scatter_now",
        out_spec=pltpu.VMEM,
        vmem_limit_bytes=48 * 2**20,
    )


def ffn_pack_kernel(gateup_ref, down_ref, packet_ref):
    live = pl.program_id(0) < FF // HEAD // 2

    @pl.when(live)
    def _():
        for at in range(2):
            columns = slice(at * HEAD, (at + 1) * HEAD)
            packet_ref[at, :, :HEAD] = gateup_ref[0, :, columns].astype(jnp.bfloat16)
            packet_ref[at, :, HEAD : 2 * HEAD] = gateup_ref[1, :, columns].astype(jnp.bfloat16)
            packet_ref[at, :, 2 * HEAD :] = down_ref[:, columns].astype(jnp.bfloat16)

    @pl.when(jnp.logical_not(live))
    def _():
        packet_ref[...] = jnp.zeros_like(packet_ref)


def ffn_packets(gateup, down, count):
    row_count = gateup.shape[1]
    last = FF // HEAD // 2 - 1
    return pl.pallas_call(
        ffn_pack_kernel,
        grid=(count // 2,),
        in_specs=[
            pl.BlockSpec((2, row_count, 2 * HEAD), lambda j: (0, 0, jnp.minimum(j, last))),
            pl.BlockSpec((row_count, 2 * HEAD), lambda j: (0, jnp.minimum(j, last))),
        ],
        out_specs=pl.BlockSpec((2, row_count, 3 * HEAD), lambda j: (j, 0, 0)),
        out_shape=jax.ShapeDtypeStruct((count, row_count, 3 * HEAD), jnp.bfloat16),
        cost_estimate=pl.CostEstimate(flops=0, bytes_accessed=14 * 2**20, transcendentals=0),
        name="ffn_packets",
    )(gateup, down)


def attn_pack_kernel(qkv_ref, out_ref, packet_ref):
    j = pl.program_id(0)

    @pl.when(j < (H + 2) // 2)
    def _():
        for at in range(2):
            packet_ref[at] = qkv_ref[:, at * HEAD : (at + 1) * HEAD].astype(jnp.bfloat16)

    @pl.when(j >= (H + 2) // 2)
    def _():
        for at in range(2):
            packet_ref[at] = out_ref[:, at * HEAD : (at + 1) * HEAD].astype(jnp.bfloat16)


def attn_packets(qkv, out):
    row_count = qkv.shape[0]
    qkv_last, out_last = (H + 2) // 2 - 1, H // 2 - 1
    return pl.pallas_call(
        attn_pack_kernel,
        grid=(H + 1,),
        in_specs=[
            pl.BlockSpec((row_count, 2 * HEAD), lambda j: (0, jnp.minimum(j, qkv_last))),
            pl.BlockSpec((row_count, 2 * HEAD), lambda j: (0, jnp.clip(j - qkv_last - 1, 0, out_last))),
        ],
        out_specs=pl.BlockSpec((2, row_count, HEAD), lambda j: (j, 0, 0)),
        out_shape=jax.ShapeDtypeStruct((2 * H + 2, row_count, HEAD), jnp.bfloat16),
        cost_estimate=pl.CostEstimate(flops=0, bytes_accessed=4 * 2**20, transcendentals=0),
        name="attn_packets",
    )(qkv, out)


def turn_kernel(grads_ref, others_ref, mom_ref, *refs):
    *results, current_ref = refs
    if len(results) == 1:
        low_ref, turned_ref = results[0].at[:, :HEAD], results[0].at[:, HEAD:]
    else:
        low_ref, turned_ref = results
    grads = grads_ref[...] + others_ref[...].astype(jnp.float32)
    low_ref[...] = grads.astype(jnp.bfloat16)
    moment = momentum_decay * mom_ref[...].astype(jnp.float32) + grads
    moment = moment.astype(jnp.bfloat16).astype(jnp.float32)
    norm_size = jnp.sqrt(jnp.sum(moment * moment, keepdims=True))
    current_ref[...] = (moment / (norm_size + eps_pieces)).T.astype(jnp.bfloat16)

    @pl.loop(0, NS_STEPS)
    def _(sweep_index):
        current = current_ref[...]
        gram_matrix = lax.dot_general(
            current, current, (((1,), (1,)), ((), ())), preferred_element_type=jnp.float32
        ).astype(jnp.bfloat16)
        square = jnp.dot(gram_matrix, gram_matrix, preferred_element_type=jnp.float32)
        mixing = (ns_second * gram_matrix.astype(jnp.float32) + ns_third * square).astype(
            jnp.bfloat16
        )
        turned = jnp.dot(mixing, current, preferred_element_type=jnp.float32)
        current_ref[...] = (ns_first * current.astype(jnp.float32) + turned).astype(jnp.bfloat16)

    turned_ref[...] = current_ref[...].astype(jnp.float32).T.astype(jnp.bfloat16)


def orthogonalize(grads, others, moms, results):
    depth, columns = grads.shape
    block = pl.BlockSpec((depth, HEAD), lambda j: (0, j))
    pieces = columns // HEAD
    return pl.pallas_call(
        turn_kernel,
        grid=(pieces,),
        in_specs=[block] * 3,
        out_specs=[pl.BlockSpec((depth, 2 // results * HEAD), lambda j: (0, j))] * results,
        out_shape=[jax.ShapeDtypeStruct((depth, 2 // results * columns), jnp.bfloat16)] * results,
        scratch_shapes=[pltpu.VMEM((HEAD, depth), jnp.bfloat16)],
        cost_estimate=pl.CostEstimate(
            flops=pieces * 20 * depth * HEAD * HEAD, bytes_accessed=12 * depth * columns, transcendentals=0
        ),
        compiler_params=pltpu.CompilerParams(vmem_limit_bytes=48 * 2**20),
        name="orthogonalize",
    )(grads, others, moms)


def update(rate, weight, mom, grad, turn):
    moment = momentum_decay * mom + grad.astype(jnp.float32)
    new = (1.0 - weight_shrink) * weight - rate * turn.astype(jnp.float32)
    return new, moment, new.astype(jnp.bfloat16)


def ffn_update_kernel(
    grad_ref, turn_ref, w_gateup_ref, mom_gateup_ref, w_down_ref, mom_down_ref, *results
):
    for at in range(grad_ref.shape[0]):
        columns = slice(at * HEAD, (at + 1) * HEAD)
        for part in range(3):
            spot = (part, slice(None), columns) if part < 2 else (slice(None), columns)
            weight_ref, mom_ref = (
                (w_gateup_ref, mom_gateup_ref) if part < 2 else (w_down_ref, mom_down_ref)
            )
            packed = slice(part * HEAD, (part + 1) * HEAD)
            values = update(
                matrix_rate,
                weight_ref[spot],
                mom_ref[spot],
                grad_ref[at, :, packed],
                turn_ref[at, :, packed],
            )
            for ref, value in zip(results[:3] if part < 2 else results[3:], values):
                ref[spot] = value


def ffn_update(grads, turns, w_gateup, mom_gateup, w_down, mom_down):
    row_count = w_gateup.shape[1]
    wide = 3
    packet = pl.BlockSpec((wide, row_count, 3 * HEAD), lambda j: (j, 0, 0))
    gateup = pl.BlockSpec((2, row_count, wide * HEAD), lambda j: (0, 0, j))
    down = pl.BlockSpec((row_count, wide * HEAD), lambda j: (0, j))
    dtypes = (jnp.float32, jnp.float32, jnp.bfloat16)
    return pl.pallas_call(
        ffn_update_kernel,
        grid=(FF // HEAD // wide,),
        in_specs=[packet, packet, gateup, gateup, down, down],
        out_specs=[gateup] * 3 + [down] * 3,
        out_shape=[jax.ShapeDtypeStruct(w_gateup.shape, dtype) for dtype in dtypes]
        + [jax.ShapeDtypeStruct(w_down.shape, dtype) for dtype in dtypes],
        cost_estimate=pl.CostEstimate(flops=0, bytes_accessed=50 * 2**20, transcendentals=0),
        compiler_params=pltpu.CompilerParams(vmem_limit_bytes=48 * 2**20),
        name="ffn_update",
    )(grads, turns, w_gateup, mom_gateup, w_down, mom_down)


def attn_update_kernel(rate, packet_ref, w_ref, mom_ref, *results):
    for at in range(2):
        columns = slice(at * HEAD, (at + 1) * HEAD)
        values = update(
            rate,
            w_ref[:, columns],
            mom_ref[:, columns],
            packet_ref[at, :, :HEAD],
            packet_ref[at, :, HEAD:],
        )
        for ref, value in zip(results, values):
            ref[:, columns] = value


def attn_update(rate, offset, packets, weight, mom):
    row_count = packets.shape[1]
    packet = pl.BlockSpec((2, row_count, 2 * HEAD), lambda j: (j + offset // 2, 0, 0))
    block = pl.BlockSpec((row_count, 2 * HEAD), lambda j: (0, j))
    return pl.pallas_call(
        functools.partial(attn_update_kernel, rate),
        grid=(weight.shape[1] // HEAD // 2,),
        in_specs=[packet, block, block],
        out_specs=[block] * 3,
        out_shape=[
            jax.ShapeDtypeStruct(weight.shape, dtype)
            for dtype in (jnp.float32, jnp.float32, jnp.bfloat16)
        ],
        cost_estimate=pl.CostEstimate(flops=0, bytes_accessed=6 * 2**20, transcendentals=0),
        name="attn_update",
    )(packets, weight, mom)


def two_heads(ref):
    return jnp.concatenate([ref[:, :HEAD], ref[:, HEAD:]], axis=0)


def visible(tokens, first_token, shape, query_axis):
    query = lax.rem(lax.broadcasted_iota(jnp.int32, shape, query_axis), tokens)
    key = lax.broadcasted_iota(jnp.int32, shape, 1 - query_axis)
    distance = query + WINDOW - key
    return (distance >= 0) & (distance < WINDOW) & (first_token - WINDOW + key >= 0)


def attend_kernel(first_ref, queries_ref, kv_ref, mixed_ref, log_total_ref):
    tokens = queries_ref.shape[0]
    raw = lax.dot_general(
        two_heads(queries_ref),
        kv_ref[:, :HEAD],
        (((1,), (1,)), ((), ())),
        preferred_element_type=jnp.float32,
    )
    allowed = visible(tokens, first_ref[0], raw.shape, 0)
    scores = jnp.where(allowed, raw * HEAD ** (-0.5), masked_score)
    top_score = jnp.max(scores, axis=-1, keepdims=True)
    expo = jnp.exp(scores - top_score)
    total = jnp.sum(expo, axis=-1, keepdims=True)
    probs = (expo / total).astype(jnp.bfloat16)
    mixed = jnp.dot(probs, kv_ref[:, HEAD:], preferred_element_type=jnp.float32)
    mixed_ref[:, :HEAD] = mixed[:tokens].astype(jnp.bfloat16)
    mixed_ref[:, HEAD:] = mixed[tokens:].astype(jnp.bfloat16)
    log_total_ref[0] = jnp.broadcast_to(top_score + jnp.log(total), log_total_ref.shape[1:])


def attend(first_token, qkv, kv_window):
    tokens = qkv.shape[0]
    span = kv_window.shape[0]
    pairs = H // 2
    return pl.pallas_call(
        attend_kernel,
        grid=(pairs,),
        in_specs=[
            pl.BlockSpec(memory_space=pltpu.SMEM),
            pl.BlockSpec((tokens, 2 * HEAD), lambda j: (0, j)),
            pl.BlockSpec((span, 2 * HEAD), lambda j: (0, 0)),
        ],
        out_specs=[
            pl.BlockSpec((tokens, 2 * HEAD), lambda j: (0, j)),
            pl.BlockSpec((1, 2 * tokens, 128), lambda j: (j, 0, 0)),
        ],
        out_shape=[
            jax.ShapeDtypeStruct((tokens, H * HEAD), jnp.bfloat16),
            jax.ShapeDtypeStruct((pairs, 2 * tokens, 128), jnp.float32),
        ],
        cost_estimate=pl.CostEstimate(
            flops=4 * H * tokens * span * HEAD,
            bytes_accessed=4 * 2**20,
            transcendentals=H * tokens * span,
        ),
        compiler_params=pltpu.CompilerParams(vmem_limit_bytes=48 * 2**20),
        name="attend",
    )(first_token, qkv, kv_window)


def attend_back_kernel(
    first_ref, queries_ref, grads_ref, log_total_ref, kv_ref, grad_query_ref, grad_kv_ref, sums_ref
):
    tokens = queries_ref.shape[0]
    score_scale = HEAD ** (-0.5)
    keys, values = kv_ref[:, :HEAD], kv_ref[:, HEAD:]
    queries, grads = two_heads(queries_ref), two_heads(grads_ref)

    def against(left, right):
        return lax.dot_general(
            left, right, (((1,), (1,)), ((), ())), preferred_element_type=jnp.float32
        )

    raw = against(keys, queries)
    allowed = visible(tokens, first_ref[0], raw.shape, 1)
    scores = jnp.where(allowed, raw * score_scale, masked_score)
    log_total = log_total_ref[0].T[:1]
    probs = jnp.exp(scores - log_total)
    grad_probs = against(values, grads)
    row_delta = jnp.sum(probs * grad_probs, axis=0, keepdims=True)
    grad_raw = (probs * (grad_probs - row_delta) * score_scale).astype(jnp.bfloat16)
    grad_query = lax.dot_general(
        grad_raw, keys, (((0,), (0,)), ((), ())), preferred_element_type=jnp.float32
    )
    grad_query_ref[:, :HEAD] = grad_query[:tokens].astype(jnp.bfloat16)
    grad_query_ref[:, HEAD:] = grad_query[tokens:].astype(jnp.bfloat16)

    @pl.when(pl.program_id(0) == 0)
    def _():
        sums_ref[...] = jnp.zeros_like(sums_ref)

    sums_ref[:, :HEAD] += jnp.dot(grad_raw, queries, preferred_element_type=jnp.float32)
    sums_ref[:, HEAD:] += jnp.dot(
        probs.astype(jnp.bfloat16), grads, preferred_element_type=jnp.float32
    )

    @pl.when(pl.program_id(0) == pl.num_programs(0) - 1)
    def _():
        grad_kv_ref[...] = sums_ref[...].astype(jnp.bfloat16)


def attend_back(first_token, qkv, grads, log_total, kv_window):
    tokens = qkv.shape[0]
    span = kv_window.shape[0]
    heads = pl.BlockSpec((tokens, 2 * HEAD), lambda j: (0, j))
    window = pl.BlockSpec((span, 2 * HEAD), lambda j: (0, 0))
    return pl.pallas_call(
        attend_back_kernel,
        grid=(H // 2,),
        in_specs=[
            pl.BlockSpec(memory_space=pltpu.SMEM),
            heads,
            heads,
            pl.BlockSpec((1, 2 * tokens, 128), lambda j: (j, 0, 0)),
            window,
        ],
        out_specs=[heads, window],
        out_shape=[
            jax.ShapeDtypeStruct((tokens, H * HEAD), jnp.bfloat16),
            jax.ShapeDtypeStruct((span, 2 * HEAD), jnp.bfloat16),
        ],
        scratch_shapes=[pltpu.VMEM((span, 2 * HEAD), jnp.float32)],
        cost_estimate=pl.CostEstimate(
            flops=10 * H * tokens * span * HEAD,
            bytes_accessed=8 * 2**20,
            transcendentals=H * tokens * span,
        ),
        compiler_params=pltpu.CompilerParams(vmem_limit_bytes=48 * 2**20),
        name="attend_back",
    )(first_token, qkv, grads, log_total, kv_window)


def rms_scale(stream, gain_row):
    mean_square = jnp.mean(stream * stream, axis=-1, keepdims=True)
    return stream * lax.rsqrt(mean_square + eps_norm) * gain_row


def gelu_product(gate_part, up_part):
    return jax.nn.gelu(gate_part, approximate=True) * up_part


def on_device(
    tokens_in,
    cotangent,
    w_qkv,
    w_out,
    w_gateup,
    w_down,
    gains,
    mom_qkv,
    mom_out,
    mom_gateup,
    mom_down,
    mom_gains,
):
    everyone = ("blk", "pair")
    bf16 = jnp.bfloat16
    f32 = jnp.float32
    blk_count = lax.axis_size("blk")
    pair_count = lax.axis_size("pair")
    device_count = blk_count * pair_count
    block_at = lax.axis_index("blk")
    half_at = lax.axis_index("pair")
    me = block_at * pair_count + half_at
    local_rows, width = tokens_in.shape
    share_rows = w_qkv.shape[0]
    span = WINDOW + local_rows
    token_count = local_rows * device_count
    large = token_count * width * 2 > 48 * 2**20
    planes = blk_count // 4
    spread = not large

    def after(value, earlier):
        return lax.optimization_barrier((value, earlier))[0] if large else value

    def exchange(packets, axes=everyone):
        return lax.all_to_all(packets, axes, split_axis=0, concat_axis=0, tiled=True)

    def swap(shard):
        return lax.ppermute(shard, "pair", [(0, 1), (1, 0)])

    def hold(value, *earlier):
        return value if large else lax.optimization_barrier((value, earlier))[0]

    def ride(packets, among="all", **options):
        sources = {"all": device_count, "plane": blk_count, "pair": pair_count}[among]
        return Exchange(packets, among, **(dict(sources=sources) | options))

    def exchanged(rides):
        results = []
        for packets, among, _, before, _, _ in rides:
            if among == "pair":
                results.append(swap(packets))
                continue
            axes, places = (everyone, device_count) if among == "all" else ("blk", blk_count)
            after_last = places - before - packets.shape[0]
            packets = jnp.pad(packets, ((before, after_last),) + ((0, 0),) * (packets.ndim - 1))
            results.append(exchange(packets, axes))
        return results

    def gather(shards, whole_slice, collective_id, rides=(), **options):
        if large:
            axes = everyone if whole_slice else "blk"
            wholes = [lax.all_gather(shard, axes, axis=0, tiled=True) for shard in shards]
            return wholes + exchanged(rides)
        return gather_now(shards, planes, whole_slice, collective_id, rides, **options)

    def scatter(partial, whole_slice, collective_id, rides=()):
        if large:
            axes = everyone if whole_slice else "blk"
            part = lax.psum_scatter(partial, axes, scatter_dimension=0, tiled=True)
            return [part] + exchanged(rides)
        return scatter_now(partial, planes, whole_slice, collective_id, rides)

    def gather_plane(shard):
        return lax.all_gather(shard, "blk", axis=0, tiled=True)

    stream = tokens_in.astype(f32)
    padded_gains = jnp.pad(gains.astype(bf16), ((0, 14), (0, 128 - share_rows)))
    full_qkv, full_gains, full_out, ffn_weights = gather(
        [w_qkv.astype(bf16), padded_gains, w_out.T.astype(bf16)],
        True,
        1,
        [ride(ffn_packets(w_gateup, w_down.T, device_count))],
        part_rows=48,
    )
    ffn_weights = ffn_weights.reshape(width, 3 * HEAD)
    full_gains = full_gains.reshape(device_count, 16, 128)[:, :2, :share_rows].astype(f32)
    gain_attn = full_gains[:, 0].reshape(width)
    gain_mlp = full_gains[:, 1].reshape(width)
    normed_attn_f, norm_back_attn = jax.vjp(rms_scale, stream, gain_attn)
    normed_attn = normed_attn_f.astype(bf16)
    qkv = jnp.dot(normed_attn, full_qkv, preferred_element_type=f32).astype(bf16)
    (kv_all,) = gather([qkv[:, H * HEAD :]], True, 2)
    kv_window = lax.dynamic_slice_in_dim(
        jnp.pad(kv_all, ((WINDOW, 0), (0, 0))), me * local_rows, span, 0
    )
    first_token = (me * local_rows).astype(jnp.int32).reshape(1)
    mixed, log_total = attend(first_token, qkv, kv_window)
    resid = stream + jnp.einsum("tc,dc->td", mixed, full_out, preferred_element_type=f32)

    normed_mlp_f, norm_back_mlp = jax.vjp(rms_scale, resid, gain_mlp)
    normed_mlp = normed_mlp_f.astype(bf16)
    normed_mlp_plane, cotangent_plane, other_weights = gather(
        [normed_mlp, cotangent], False, 3, [ride(ffn_weights, "pair")], part_rows=64
    )
    pair_weights = [ffn_weights, other_weights]
    gates, ups, downs = (
        [weights[:, part * HEAD : (part + 1) * HEAD] for weights in pair_weights]
        for part in range(3)
    )
    pair_gateup = jnp.concatenate(gates + ups, axis=1)
    pair_down = jnp.concatenate(downs, axis=1)
    plane_rows = blk_count * local_rows
    both_parts = jnp.dot(normed_mlp_plane, pair_gateup, preferred_element_type=f32)
    pair_width = pair_count * HEAD
    hidden_f, geglu_back = jax.vjp(
        gelu_product, both_parts[:, :pair_width], both_parts[:, pair_width:]
    )
    hidden = hidden_f.astype(bf16)
    grad_hidden = jnp.dot(cotangent_plane, pair_down, preferred_element_type=f32)
    grad_gate, grad_up = geglu_back(grad_hidden)
    grad_gateup = jnp.concatenate([grad_gate.astype(bf16), grad_up.astype(bf16)], axis=1)
    def ffn_gradient(columns):
        gateup_right = jnp.concatenate(
            [grad_gate[:, columns].astype(bf16), grad_up[:, columns].astype(bf16)], axis=1
        )
        down_right = hidden[:, columns]
        return jnp.concatenate(
            [
                jnp.einsum("td,tf->df", normed_mlp_plane, gateup_right, preferred_element_type=f32),
                jnp.einsum("td,tf->df", cotangent_plane, down_right, preferred_element_type=f32),
            ],
            axis=1,
        )

    def pair_columns(columns):
        return columns.reshape(local_rows, -1, pair_width).transpose(1, 0, 2)

    ffn_theirs = ffn_gradient(slice(HEAD, 2 * HEAD)).astype(bf16)
    grad_normed_part = jnp.einsum("tf,df->td", grad_gateup, pair_gateup, preferred_element_type=f32)
    grad_normed_mlp, ffn_others, ffn_moms, attn_moms, out_rights = scatter(
        grad_normed_part.astype(bf16),
        False,
        4,
        [
            ride(ffn_theirs, "pair"),
            ride(ffn_packets(mom_gateup, mom_down.T, FF // HEAD)),
            ride(attn_packets(mom_qkv, mom_out.T), spread_targets=spread),
            ride(
                pair_columns(mixed), "plane", first_target=(H + 2) // 2, spread_targets=spread
            ),
        ],
    )
    grad_normed_mlp = grad_normed_mlp.astype(f32)

    ffn_grads = ffn_gradient(slice(0, HEAD))
    ffn_low, ffn_turned = orthogonalize(
        ffn_grads, ffn_others, ffn_moms.reshape(width, 3 * HEAD), 2
    )
    ffn_shape = (device_count, share_rows, 3 * HEAD)

    resid_part, gain_grad_mlp = norm_back_mlp(grad_normed_mlp)
    grad_resid = cotangent.astype(f32) + resid_part
    grad_proj = grad_resid.astype(bf16)
    grad_mixed = jnp.dot(grad_proj, full_out, preferred_element_type=f32).astype(bf16)
    grad_query, grad_kv = attend_back(first_token, qkv, grad_mixed, log_total, kv_window)
    grad_kv_all = lax.dynamic_update_slice_in_dim(
        jnp.zeros((WINDOW + token_count, 2 * HEAD), bf16), grad_kv, me * local_rows, 0
    )[WINDOW:]
    grad_kv, ffn_low = scatter(
        grad_kv_all, True, 5, [ride(ffn_low.reshape(ffn_shape), sources=FF // HEAD)]
    )
    grad_qkv = jnp.concatenate([grad_query, grad_kv], axis=1)
    grad_normed_attn = jnp.einsum("tc,dc->td", grad_qkv, full_qkv, preferred_element_type=f32)
    stream_part, gain_grad_attn = norm_back_attn(grad_normed_attn)
    input_grad = grad_resid + stream_part

    branch_part = jnp.einsum(
        "tf,df->td", after(hidden, grad_normed_mlp), pair_down, preferred_element_type=f32
    )
    branch, ffn_turned, qkv_rights = scatter(
        branch_part.astype(bf16),
        False,
        6,
        [
            ride(ffn_turned.reshape(ffn_shape), sources=FF // HEAD),
            ride(pair_columns(grad_qkv), "plane", spread_targets=spread),
        ],
    )
    block_output = (resid + branch.astype(f32)).astype(bf16)
    normed_attn_plane = gather_plane(after(hold(normed_attn, normed_mlp_plane), (ffn_grads, block_output)))
    grad_proj_plane = gather_plane(after(grad_proj, (ffn_grads, block_output)))

    def attn_gradient(lefts, rights):
        rights = rights.reshape(plane_rows, pair_width)
        return jnp.einsum("td,tf->df", lefts, rights, preferred_element_type=f32)

    pair_at = spread_place(planes, block_at) if spread else block_at
    attn_grads = lax.cond(
        pair_at < (H + 2) // pair_count,
        lambda: attn_gradient(normed_attn_plane, qkv_rights),
        lambda: attn_gradient(grad_proj_plane, out_rights),
    )
    attn_others = swap(
        lax.dynamic_slice_in_dim(attn_grads, (1 - half_at) * HEAD, HEAD, 1).astype(bf16)
    )
    attn_grads = lax.dynamic_slice_in_dim(attn_grads, half_at * HEAD, HEAD, 1)
    updated_ffn = ffn_update(ffn_low, ffn_turned, w_gateup, mom_gateup, w_down.T, mom_down.T)
    (attn_results,) = orthogonalize(
        attn_grads, hold(attn_others, updated_ffn[0]), attn_moms.reshape(width, HEAD), 1
    )
    gain_grads = jnp.stack([gain_grad_attn, gain_grad_mlp], axis=0)
    gain_grads = gain_grads.reshape(2, device_count, share_rows).transpose(1, 0, 2)
    last_rides = [
        ride(
            attn_results.reshape(device_count, share_rows, 2 * HEAD),
            sources=2 * H + 2,
            spread_sources=spread,
        ),
        ride(jnp.pad(gain_grads, ((0, 0), (0, 6), (0, 128 - share_rows)))),
    ]
    if large:
        attn_results, gain_grads = exchanged(last_rides)
    else:
        attn_results, gain_grads = exchange_now(last_rides, planes, 7)
    gain_share = jnp.sum(gain_grads, axis=0)[:2, :share_rows]

    updated_qkv = attn_update(matrix_rate, 0, attn_results, w_qkv, mom_qkv)
    updated_out = attn_update(output_rate, H + 2, attn_results, w_out.T, mom_out.T)
    moment_gains = momentum_decay * mom_gains + gain_share
    new_gains = gains - gain_rate * moment_gains
    return (
        block_output,
        input_grad,
        *updated_qkv,
        *(result.T for result in updated_out),
        *updated_ffn[:3],
        *(result.T for result in updated_ffn[3:]),
        new_gains,
        moment_gains,
        new_gains.astype(bf16),
    )


def solution(mesh):
    placed = (
        P(("blk", "pair"), None),
        P(("blk", "pair"), None),
        P(("blk", "pair"), None),
        P(None, ("blk", "pair")),
        P(None, ("blk", "pair"), None),
        P(None, ("blk", "pair")),
        P(None, ("blk", "pair")),
        P(("blk", "pair"), None),
        P(None, ("blk", "pair")),
        P(None, ("blk", "pair"), None),
        P(None, ("blk", "pair")),
        P(None, ("blk", "pair")),
    )
    return jax.shard_map(
        on_device,
        mesh=mesh,
        in_specs=placed,
        out_specs=(
            P(("blk", "pair"), None),
            P(("blk", "pair"), None),
            P(("blk", "pair"), None),
            P(("blk", "pair"), None),
            P(("blk", "pair"), None),
            P(None, ("blk", "pair")),
            P(None, ("blk", "pair")),
            P(None, ("blk", "pair")),
            P(None, ("blk", "pair"), None),
            P(None, ("blk", "pair"), None),
            P(None, ("blk", "pair"), None),
            P(None, ("blk", "pair")),
            P(None, ("blk", "pair")),
            P(None, ("blk", "pair")),
            P(None, ("blk", "pair")),
            P(None, ("blk", "pair")),
            P(None, ("blk", "pair")),
        ),
        check_vma=False,
    )
```

```python
import functools
from typing import NamedTuple

import jax
import jax.numpy as jnp
from jax import lax
from jax.experimental import pallas as pl
from jax.experimental.pallas import tpu as pltpu
from jax.sharding import PartitionSpec as P

H = 10
HEAD = 256
FF = 7680
WINDOW = 2048
NS_STEPS = 5


eps_norm = 1e-06
eps_pieces = 1e-07
ns_first = 3.4445
ns_second = -4.775
ns_third = 2.0315
momentum_decay = 0.95
matrix_rate = 0.5
output_rate = 10.0
gain_rate = 0.001
weight_shrink = 0.001
masked_score = -1e30
MESH = pl.DeviceIdType.MESH


def position():
    blk, y = lax.axis_index("blk"), lax.axis_index("pair")
    return blk, lax.div(blk, 4), lax.rem(lax.div(blk, 2), 2), lax.rem(blk, 2), y


def greet(devices):
    barrier = pltpu.get_barrier_semaphore()
    for device in devices:
        pl.semaphore_signal(barrier, inc=1, device_id=device, device_id_type=MESH)
    pl.semaphore_wait(barrier, len(devices))


def remote(source, target, send_sem, recv_sem, device):
    return pltpu.make_async_remote_copy(
        src_ref=source,
        dst_ref=target,
        send_sem=send_sem,
        recv_sem=recv_sem,
        device_id=device,
        device_id_type=MESH,
    )


class Exchange(NamedTuple):
    packets: jax.Array
    among: str
    sources: int
    first_target: int = 0
    spread_sources: bool = False
    spread_targets: bool = False


def spread_place(planes, blk):
    z, x, core = lax.div(blk, 4), lax.rem(lax.div(blk, 2), 2), lax.rem(blk, 2)
    return (2 * core + lax.rem(x + z, 2)) * planes + z


def all_devices():
    blk, _, _, _, y = position()
    count = 2 * lax.axis_size("blk")
    here = 2 * blk + y
    places = [lax.rem(here + at, count) for at in range(1, count)]
    return [(lax.div(place, 2), lax.rem(place, 2)) for place in places]


def plane_devices():
    blk, _, _, _, y = position()
    count = lax.axis_size("blk")
    return [(lax.rem(blk + at, count), y) for at in range(1, count)]


def greeted(specs, nearby):
    if any(among == "all" for among, *_ in specs):
        return all_devices()
    blk, _, _, _, y = position()
    pair = [(blk, 1 - y)] * any(among == "pair" for among, *_ in specs)
    if any(among == "plane" for among, *_ in specs):
        return plane_devices() + pair
    return nearby + pair


PAIR_PARTS = 4


def exchange_count(planes, among):
    return {"all": 8 * planes, "plane": 4 * planes, "pair": PAIR_PARTS}[among]


class Ride:
    def __init__(self, planes, spec, packets, received, sems):
        self.planes, self.packets, self.received = planes, packets, received
        self.among, self.sources, self.first_target, self.from_spread, self.to_spread = spec
        self.own_sem, self.send_sems, self.recv_sems = sems
        self.count = exchange_count(planes, self.among)
        self.issued = 0
        blk, self.z, _, _, self.y = position()
        self.blk = blk
        self.here = blk if self.among == "plane" else 2 * blk + self.y

    def place(self, q):
        near = self.count // self.planes
        spot = lax.rem(self.z + 1 + lax.rem(q, self.planes), self.planes)
        return spot * near + lax.rem(self.here + lax.div(q, self.planes), near)

    def counted(self, place, spread):
        if not spread:
            return place
        if self.among == "plane":
            return spread_place(self.planes, place)
        return 2 * spread_place(self.planes, lax.div(place, 2)) + lax.rem(place, 2)

    def source(self, place):
        return self.counted(place, self.from_spread)

    def target(self, place):
        return self.counted(place, self.to_spread) - self.first_target

    def sending(self, place):
        return self.source(place) < self.sources

    def receiving(self, place):
        target = self.target(place)
        return (target >= 0) & (target < self.packets.shape[0])

    def copy(self, q):
        if self.among == "pair":
            rows = self.packets.shape[0] // PAIR_PARTS
            some = pl.ds(pl.multiple_of(q * rows, rows), rows)
            return remote(
                self.packets.at[some],
                self.received.at[some],
                self.send_sems.at[q],
                self.recv_sems.at[q],
                (self.blk, 1 - self.y),
            )
        place = self.place(q)
        device = (place, self.y)
        if self.among == "all":
            device = (lax.div(place, 2), lax.rem(place, 2))
        source = self.source(self.here)
        return remote(
            self.packets.at[self.target(place)],
            self.received.at[source],
            self.send_sems.at[q],
            self.recv_sems.at[source],
            device,
        )

    def own(self):
        return pltpu.make_async_copy(
            self.packets.at[self.target(self.here)],
            self.received.at[self.source(self.here)],
            self.own_sem.at[0],
        )

    def sends(self, q):
        away = (q < self.count) & (q != self.planes - 1)
        return away & self.sending(self.here) & self.receiving(self.place(q))

    def keeps(self):
        return self.sending(self.here) & self.receiving(self.here)

    def start_own(self):
        if self.among == "pair":
            for q in range(self.count):
                self.copy(q).start()
        else:

            @pl.when(self.keeps())
            def _():
                self.own().start()

    def issue(self, q):
        if self.among != "pair":

            @pl.when(self.sends(q))
            def _():
                self.copy(q).start()

    def issue_more(self, number):
        first, self.issued = self.issued, min(self.issued + number, self.count)

        @pl.loop(first, self.issued)
        def _(q):
            self.issue(q)

    def finish(self):
        if self.among == "pair":
            for q in range(self.count):
                self.copy(q).wait()
            return

        @pl.loop(0, self.count)
        def _(q):
            @pl.when(self.sends(q))
            def _():
                self.copy(q).wait_send()

            @pl.when((q != self.here) & self.sending(q) & self.receiving(self.here))
            def _():
                source = self.source(q)
                spot = self.received.at[source]
                remote(
                    spot, spot, self.own_sem.at[0], self.recv_sems.at[source], (self.blk, self.y)
                ).wait_recv()

        @pl.when(self.keeps())
        def _():
            self.own().wait()


def rides_of(planes, rides):
    rides = [Ride(planes, *ride) for ride in rides]
    for ride in rides:
        ride.start_own()
    return rides


def exchange_sems(exchanges, planes):
    dma = pltpu.SemaphoreType.DMA
    return [
        dma((count,))
        for exchange in exchanges
        for count in (1,) + (exchange_count(planes, exchange.among),) * 2
    ]


def exchange_specs(exchanges):
    return tuple((each.among, *each[2:]) for each in exchanges)


def communicate(
    kernel,
    operands,
    exchanges,
    outputs,
    scratch,
    planes,
    collective_id,
    cost,
    name,
    out_spec=pl.ANY,
    **options,
):
    packets = [each.packets for each in exchanges]
    received = [
        jax.ShapeDtypeStruct(
            array.shape
            if each.among == "pair"
            else (exchange_count(planes, each.among), *array.shape[1:]),
            array.dtype,
        )
        for each, array in zip(exchanges, packets)
    ]
    any_spec = pl.BlockSpec(memory_space=pl.ANY)
    return pl.pallas_call(
        kernel,
        out_shape=outputs + received,
        in_specs=[any_spec] * (len(operands) + len(packets)),
        out_specs=[pl.BlockSpec(memory_space=out_spec)] * len(outputs) + [any_spec] * len(packets),
        scratch_shapes=scratch + exchange_sems(exchanges, planes),
        compiler_params=pltpu.CompilerParams(
            collective_id=collective_id, has_side_effects=True, **options
        ),
        cost_estimate=pl.CostEstimate(flops=0, bytes_accessed=cost * 2**20, transcendentals=0),
        name=name,
    )(*operands, *packets)


def split_refs(refs, inputs, outputs, specs):
    riders = len(specs)
    ins, refs = refs[: inputs + riders], refs[inputs + riders :]
    outs, refs = refs[: outputs + riders], refs[outputs + riders :]
    scratch = refs[: len(refs) - 3 * riders]
    sems = refs[len(refs) - 3 * riders :]
    rides = [
        (spec, ins[inputs + i], outs[outputs + i], sems[3 * i : 3 * i + 3])
        for i, spec in enumerate(specs)
    ]
    return ins[:inputs], outs[:outputs], scratch, rides


def exchange_kernel(planes, specs, *refs):
    _, _, _, rides = split_refs(refs, 0, 0, specs)
    greet(greeted(specs, []))
    rides = rides_of(planes, rides)
    for ride in rides:
        ride.issue_more(ride.count)
    for ride in rides:
        ride.finish()


def exchange_now(exchanges, planes, collective_id):
    specs = exchange_specs(exchanges)
    kernel = functools.partial(exchange_kernel, planes, specs)
    return communicate(kernel, [], exchanges, [], [], planes, collective_id, 100, "exchange_now")


def gather_kernel(planes, parts, whole_slice, specs, *refs):
    arrays = 1 + max(array for array, _, _ in parts)
    shard_refs, whole_refs, scratch, rides = split_refs(refs, arrays, arrays, specs)
    count = len(parts)
    shards = [shard_refs[array].at[pl.ds(start, size)] for array, start, size in parts]
    own_sem, line_send, second_send, first_send, core_send, recv, core_recv = scratch
    blk, z, x, core, y = position()
    firsts = 2 if whole_slice else 1
    to_core = (blk + 1 - 2 * core, y)
    if whole_slice:
        first = y * (1 - core) + x * core
        second = x * (1 - core) + y * core
        first_device = (blk + core * (2 - 4 * x), y + (1 - core) * (1 - 2 * y))
        second_device = (blk + (1 - core) * (2 - 4 * x), y + core * (1 - 2 * y))
    else:
        first, second = 0, x
        first_device, second_device = None, (blk + 2 - 4 * x, y)
    line = [(blk + 4 * (lax.rem(z + at, planes) - z), y) for at in range(1, planes)]
    nearby = [to_core, second_device] + [first_device] * whole_slice + line
    greet(greeted(specs, nearby))

    def slot(i, spot, by_first, by_second, plane):
        array, start, size = parts[i]
        whole, some = whole_refs[array], pl.ds(start, size)
        if whole_slice:
            by_x = (1 - plane) * by_second + plane * by_first
            by_y = (1 - plane) * by_first + plane * by_second
            return whole.at[spot, by_x, plane, by_y, some]
        return whole.at[spot, by_second, plane, some]

    def arrive(i, spot, by_first, by_second):
        here = slot(i, spot, by_first, by_second, core)
        remote(here, here, own_sem.at[0], recv.at[i, spot, by_first, by_second], to_core).wait_recv()

    def up(i, source, spot):
        target = slot(i, spot, first, second, core)
        device = (blk + 4, y)
        return remote(source, target, line_send.at[0, i, spot], recv.at[i, spot, first, second], device)

    def down(i, source, spot):
        target = slot(i, spot, first, second, core)
        device = (blk - 4, y)
        return remote(source, target, line_send.at[1, i, spot], recv.at[i, spot, first, second], device)

    def onward(i, source, spot):
        target = slot(i, spot, first, second, core)
        arrived = recv.at[i, spot, first, second]
        yield remote(source, target, second_send.at[i, spot], arrived, second_device)
        if whole_slice:
            yield remote(source, target, first_send.at[i, spot, 0], arrived, first_device)
        yield remote(
            source, target, core_send.at[i, spot, 0, 0], core_recv.at[i, spot, first, second], to_core
        )

    def after_second(i, spot):
        here = slot(i, spot, first, 1 - second, core)
        if whole_slice:
            yield remote(
                here, here, first_send.at[i, spot, 1], recv.at[i, spot, first, 1 - second], first_device
            )
        yield remote(
            here, here, core_send.at[i, spot, 0, 1], core_recv.at[i, spot, first, 1 - second], to_core
        )

    def after_first(i, spot, turn):
        by_second = second if turn == 0 else 1 - second
        here = slot(i, spot, 1 - first, by_second, core)
        return remote(
            here, here, core_send.at[i, spot, 1, turn], core_recv.at[i, spot, 1 - first, by_second], to_core
        )

    def line_steps():
        for far in range(1, planes):
            yield z - far, z >= far, up, z < planes - 1
            yield z + far, z < planes - far, down, z > 0

    own_copies = []
    for i in range(count):
        copy = pltpu.make_async_copy(
            shards[i], slot(i, z, first, second, core), own_sem.at[1 + i]
        )
        copy.start()
        own_copies.append(copy)

        @pl.when(z < planes - 1)
        def _():
            up(i, shards[i], z).start()

        @pl.when(z > 0)
        def _():
            down(i, shards[i], z).start()

        for copy in onward(i, shards[i], z):
            copy.start()
    rides = rides_of(planes, rides)

    def issue(number):
        for ride in rides:
            ride.issue_more(number)

    issue(6)
    for i in range(count):
        arrive(i, z, first, 1 - second)
        for copy in after_second(i, z):
            copy.start()
    issue(4)
    for spot, there, direction, further in line_steps():

        @pl.when(there)
        def _():
            for i in range(count):
                here = slot(i, spot, first, second, core)
                arrive(i, spot, first, second)

                @pl.when(further)
                def _():
                    direction(i, here, spot).start()

                for copy in onward(i, here, spot):
                    copy.start()
            for i in range(count):
                arrive(i, spot, first, 1 - second)
                for copy in after_second(i, spot):
                    copy.start()

        issue(4)

    issue(8 * planes)
    spots = [lax.rem(z + at, planes) for at in range(planes)]
    if whole_slice:
        for spot in spots:
            for turn in range(2):
                for i in range(count):
                    arrive(i, spot, 1 - first, second if turn == 0 else 1 - second)
                    after_first(i, spot, turn).start()
    for copy in own_copies:
        copy.wait()
    for i in range(count):
        for spot in range(planes):
            for by_first in range(firsts):
                for by_second in range(2):
                    there = slot(i, spot, by_first, by_second, 1 - core)
                    arrived = core_recv.at[i, spot, by_first, by_second]
                    remote(there, there, own_sem.at[0], arrived, to_core).wait_recv()
    for ride in rides:
        ride.finish()
    for i in range(count):

        @pl.when(z < planes - 1)
        def _():
            up(i, shards[i], z).wait_send()

        @pl.when(z > 0)
        def _():
            down(i, shards[i], z).wait_send()

        for spot, there, direction, further in line_steps():

            @pl.when(there & further)
            def _():
                direction(i, shards[i], spot).wait_send()

        for spot in spots:
            for copy in onward(i, shards[i], spot):
                copy.wait_send()
            for copy in after_second(i, spot):
                copy.wait_send()
            for turn in range(2 * (firsts - 1)):
                after_first(i, spot, turn).wait_send()


def gather_now(shards, planes, whole_slice, collective_id, exchanges=(), part_rows=128):
    parts = [
        (array, start, min(part_rows, shard.shape[0] - start))
        for array, shard in enumerate(shards)
        for start in range(0, shard.shape[0], part_rows)
    ]
    count = len(parts)
    firsts = 2 if whole_slice else 1
    specs = exchange_specs(exchanges)
    dma = pltpu.SemaphoreType.DMA
    grid = (planes, 2, 2, 2) if whole_slice else (planes, 2, 2)
    results = communicate(
        functools.partial(gather_kernel, planes, parts, whole_slice, specs),
        list(shards),
        exchanges,
        [jax.ShapeDtypeStruct((*grid, *shard.shape), shard.dtype) for shard in shards],
        [
            dma((count + 1,)),
            dma((2, count, planes)),
            dma((count, planes)),
            dma((count, planes, 2)),
            dma((count, planes, 2, 2)),
            dma((count, planes, firsts, 2)),
            dma((count, planes, firsts, 2)),
        ],
        planes,
        collective_id,
        200,
        "gather_now",
    )
    places = 4 * planes * firsts
    wholes = [
        whole.reshape(places * shard.shape[0], shard.shape[1])
        for whole, shard in zip(results, shards)
    ]
    return wholes + list(results[len(shards) :])


def scatter_kernel(planes, steps, rows, whole_slice, specs, *refs):
    (partial_ref,), (sum_ref,), scratch, rides = split_refs(refs, 1, 1, specs)
    own, from_core, from_first, from_second, from_below, from_above = scratch[:6]
    load_sem, core_sems, first_sems, second_sems, up_sems, down_sems = scratch[6:]
    blk, z, x, core, y = position()
    firsts = 2 if whole_slice else 1
    to_core = (blk + 1 - 2 * core, y)
    if whole_slice:
        first = y * (1 - core) + x * core
        second = x * (1 - core) + y * core
        core_second = second
        first_device = (blk + core * (2 - 4 * x), y + (1 - core) * (1 - 2 * y))
        second_device = (blk + (1 - core) * (2 - 4 * x), y + core * (1 - 2 * y))
    else:
        first, second = 0, x
        first_device, second_device = None, (blk + 2 - 4 * x, y)
    line = [(blk + 4 * (lax.rem(z + at, planes) - z), y) for at in range(1, planes)]
    nearby = [to_core, second_device] + [first_device] * whole_slice + line
    greet(greeted(specs, nearby))

    def piece(step, by_first, by_second, plane):
        some = pl.ds(pl.multiple_of(step * rows, rows), rows)
        if whole_slice:
            by_x = (1 - plane) * by_second + plane * by_first
            by_y = (1 - plane) * by_first + plane * by_second
            return partial_ref.at[:, by_x, plane, by_y, some]
        return partial_ref.at[:, by_second, plane, some]

    def core_copy(step, by_first, by_second, plane):
        return remote(
            piece(step, by_first, by_second, plane),
            from_core.at[step, by_first, by_second],
            core_sems.at[0, step, by_first, by_second],
            core_sems.at[1, step, by_first, by_second],
            to_core,
        )

    def load(step, by_first, by_second):
        return pltpu.make_async_copy(
            piece(step, by_first, by_second, core),
            own.at[step, by_first, by_second],
            load_sem.at[step, by_first, by_second],
        )

    def first_copy(step):
        return remote(
            own.at[step, 1 - first],
            from_first.at[step],
            first_sems.at[0, step],
            first_sems.at[1, step],
            first_device,
        )

    def second_copy(step):
        return remote(
            own.at[step, first, 1 - second],
            from_second.at[step],
            second_sems.at[0, step],
            second_sems.at[1, step],
            second_device,
        )

    def up_copy(step, target):
        return remote(
            own.at[step, first, second, target],
            from_below.at[step, target],
            up_sems.at[0, step, target],
            up_sems.at[1, step, target],
            (blk + 4, y),
        )

    def down_copy(step, target):
        return remote(
            own.at[step, first, second, target],
            from_above.at[step, target],
            down_sems.at[0, step, target],
            down_sems.at[1, step, target],
            (blk - 4, y),
        )

    def halves():
        if not whole_slice:
            return [(0, 1 - second), (0, second)]
        return [(1 - first, 0), (1 - first, 1), (first, 0), (first, 1)]

    def core_halves():
        if not whole_slice:
            return [(0, 1 - second), (0, second)]
        return [(1 - core_second, 0), (1 - core_second, 1), (core_second, 0), (core_second, 1)]

    def start_loads(step):
        for mine, theirs in zip(halves(), core_halves()):
            core_copy(step, *theirs, 1 - core).start()
            load(step, *mine).start()

    def add_core(step):
        for turn, mine in enumerate(halves()):
            load(step, *mine).wait()
            core_copy(step, *mine, core).wait_recv()
            own[step, *mine] += from_core[step, *mine]
            if whole_slice and turn == 1:
                first_copy(step).start()
            if not whole_slice and turn == 0:
                second_copy(step).start()

    def add_first(step):
        first_copy(step).wait_recv()
        own[step, first, 1 - second] += from_first[step, 1 - second]
        second_copy(step).start()
        own[step, first, second] += from_first[step, second]

    def add_second(step):
        second_copy(step).wait_recv()
        own[step, first, second] += from_second[step]

    def pass_up(step):
        for target in range(planes):

            @pl.when((z > 0) & (z <= target))
            def _():
                up_copy(step, target).wait_recv()

            @pl.when((z > 0) & (z < target))
            def _():
                own[step, first, second, target] += from_below[step, target]

            @pl.when(z < target)
            def _():
                up_copy(step, target).start()

    def pass_down(step):
        for target in range(planes):

            @pl.when((z < planes - 1) & (z >= target))
            def _():
                down_copy(step, target).wait_recv()

            @pl.when((z < planes - 1) & (z > target))
            def _():
                own[step, first, second, target] += from_above[step, target]

            @pl.when(z > target)
            def _():
                down_copy(step, target).start()

    def add_line(step):
        some = pl.ds(pl.multiple_of(step * rows, rows), rows)
        sum_ref[some, :] = own[step, first, second, z]

        @pl.when(z > 0)
        def _():
            sum_ref[some, :] += from_below[step, z]

        @pl.when(z < planes - 1)
        def _():
            sum_ref[some, :] += from_above[step, z]

    start_loads(0)
    start_loads(1)
    rides = rides_of(planes, rides)
    early = firsts + 1
    hurry = [-(-ride.count // steps) for ride in rides]

    @pl.loop(0, steps + early + planes)
    def _(turn):
        def stage(step, work):
            @pl.when((step >= 0) & (step < steps))
            def _():
                work(step)

        @pl.when(turn < steps - 2)
        def _():
            start_loads(turn + 2)

        stage(turn, add_core)
        for ride, number in zip(rides, hurry):
            for at in range(number):
                ride.issue(turn * number + at)
        if whole_slice:
            stage(turn - 1, add_first)
        stage(turn - early + 1, add_second)
        stage(turn - early - z, pass_up)
        stage(turn - early - (planes - 1 - z), pass_down)
        stage(turn - early - planes + 1, add_line)

    @pl.loop(0, steps)
    def _(step):
        for theirs in core_halves():
            core_copy(step, *theirs, 1 - core).wait_send()
        if whole_slice:
            first_copy(step).wait_send()
        second_copy(step).wait_send()
        for target in range(planes):

            @pl.when(z < target)
            def _():
                up_copy(step, target).wait_send()

            @pl.when(z > target)
            def _():
                down_copy(step, target).wait_send()

    for ride in rides:
        ride.finish()


def scatter_now(partial, planes, whole_slice, collective_id, exchanges=()):
    firsts = 2 if whole_slice else 1
    shard_rows = partial.shape[0] // (4 * planes * firsts)
    width = partial.shape[1]
    rows = 16
    steps = shard_rows // rows
    dtype = partial.dtype
    specs = exchange_specs(exchanges)
    dma = pltpu.SemaphoreType.DMA
    grid = (planes, 2, 2, 2) if whole_slice else (planes, 2, 2)
    return communicate(
        functools.partial(scatter_kernel, planes, steps, rows, whole_slice, specs),
        [partial.reshape(*grid, shard_rows, width)],
        exchanges,
        [jax.ShapeDtypeStruct((shard_rows, width), dtype)],
        [
            pltpu.VMEM((steps, firsts, 2, planes, rows, width), dtype),
            pltpu.VMEM((steps, firsts, 2, planes, rows, width), dtype),
            pltpu.VMEM((steps if whole_slice else 1, 2, planes, rows, width), dtype),
            pltpu.VMEM((steps, planes, rows, width), dtype),
            pltpu.VMEM((steps, planes, rows, width), dtype),
            pltpu.VMEM((steps, planes, rows, width), dtype),
            dma((steps, firsts, 2)),
            dma((2, steps, firsts, 2)),
            dma((2, steps)),
            dma((2, steps)),
            dma((2, steps, planes)),
            dma((2, steps, planes)),
        ],
        planes,
        collective_id,
        200,
        "scatter_now",
        out_spec=pltpu.VMEM,
        vmem_limit_bytes=48 * 2**20,
    )


def ffn_pack_kernel(gateup_ref, down_ref, packet_ref):
    for at in range(packet_ref.shape[0]):
        columns = slice(at * HEAD, (at + 1) * HEAD)
        packet_ref[at, :, :HEAD] = gateup_ref[0, :, columns].astype(jnp.bfloat16)
        packet_ref[at, :, HEAD : 2 * HEAD] = gateup_ref[1, :, columns].astype(jnp.bfloat16)
        packet_ref[at, :, 2 * HEAD :] = down_ref[:, columns].astype(jnp.bfloat16)


def ffn_packets(gateup, down):
    row_count = gateup.shape[1]
    blocks, wide = FF // HEAD, 5
    return pl.pallas_call(
        ffn_pack_kernel,
        grid=(blocks // wide,),
        in_specs=[
            pl.BlockSpec((2, row_count, wide * HEAD), lambda j: (0, 0, j)),
            pl.BlockSpec((row_count, wide * HEAD), lambda j: (0, j)),
        ],
        out_specs=pl.BlockSpec((wide, row_count, 3 * HEAD), lambda j: (j, 0, 0)),
        out_shape=jax.ShapeDtypeStruct((blocks, row_count, 3 * HEAD), jnp.bfloat16),
        cost_estimate=pl.CostEstimate(flops=0, bytes_accessed=12 * 2**20, transcendentals=0),
        compiler_params=pltpu.CompilerParams(vmem_limit_bytes=32 * 2**20),
        name="ffn_packets",
    )(gateup, down)


def attn_pack_kernel(qkv_ref, out_ref, packet_ref):
    j = pl.program_id(0)

    @pl.when(j < (H + 2) // 2)
    def _():
        for at in range(2):
            packet_ref[at] = qkv_ref[:, at * HEAD : (at + 1) * HEAD].astype(jnp.bfloat16)

    @pl.when(j >= (H + 2) // 2)
    def _():
        for at in range(2):
            packet_ref[at] = out_ref[:, at * HEAD : (at + 1) * HEAD].astype(jnp.bfloat16)


def attn_packets(qkv, out):
    row_count = qkv.shape[0]
    qkv_last, out_last = (H + 2) // 2 - 1, H // 2 - 1
    return pl.pallas_call(
        attn_pack_kernel,
        grid=(H + 1,),
        in_specs=[
            pl.BlockSpec((row_count, 2 * HEAD), lambda j: (0, jnp.minimum(j, qkv_last))),
            pl.BlockSpec((row_count, 2 * HEAD), lambda j: (0, jnp.clip(j - qkv_last - 1, 0, out_last))),
        ],
        out_specs=pl.BlockSpec((2, row_count, HEAD), lambda j: (j, 0, 0)),
        out_shape=jax.ShapeDtypeStruct((2 * H + 2, row_count, HEAD), jnp.bfloat16),
        cost_estimate=pl.CostEstimate(flops=0, bytes_accessed=4 * 2**20, transcendentals=0),
        name="attn_packets",
    )(qkv, out)


def turn_kernel(grads_ref, others_ref, mom_ref, *refs):
    *results, current_ref = refs
    if len(results) == 1:
        low_ref, turned_ref = results[0].at[:, :HEAD], results[0].at[:, HEAD:]
    else:
        low_ref, turned_ref = results
    grads = grads_ref[...] + others_ref[...].astype(jnp.float32)
    low_ref[...] = grads.astype(jnp.bfloat16)
    moment = momentum_decay * mom_ref[...].astype(jnp.float32) + grads
    moment = moment.astype(jnp.bfloat16).astype(jnp.float32)
    norm_size = jnp.sqrt(jnp.sum(moment * moment, keepdims=True))
    current_ref[...] = (moment / (norm_size + eps_pieces)).T.astype(jnp.bfloat16)

    @pl.loop(0, NS_STEPS)
    def _(sweep_index):
        current = current_ref[...]
        gram_matrix = lax.dot_general(
            current, current, (((1,), (1,)), ((), ())), preferred_element_type=jnp.float32
        ).astype(jnp.bfloat16)
        square = jnp.dot(gram_matrix, gram_matrix, preferred_element_type=jnp.float32)
        mixing = (ns_second * gram_matrix.astype(jnp.float32) + ns_third * square).astype(
            jnp.bfloat16
        )
        turned = jnp.dot(mixing, current, preferred_element_type=jnp.float32)
        current_ref[...] = (ns_first * current.astype(jnp.float32) + turned).astype(jnp.bfloat16)

    turned_ref[...] = current_ref[...].astype(jnp.float32).T.astype(jnp.bfloat16)


def orthogonalize(grads, others, moms, results):
    depth, columns = grads.shape
    block = pl.BlockSpec((depth, HEAD), lambda j: (0, j))
    pieces = columns // HEAD
    return pl.pallas_call(
        turn_kernel,
        grid=(pieces,),
        in_specs=[block] * 3,
        out_specs=[pl.BlockSpec((depth, 2 // results * HEAD), lambda j: (0, j))] * results,
        out_shape=[jax.ShapeDtypeStruct((depth, 2 // results * columns), jnp.bfloat16)] * results,
        scratch_shapes=[pltpu.VMEM((HEAD, depth), jnp.bfloat16)],
        cost_estimate=pl.CostEstimate(
            flops=pieces * 20 * depth * HEAD * HEAD, bytes_accessed=12 * depth * columns, transcendentals=0
        ),
        compiler_params=pltpu.CompilerParams(vmem_limit_bytes=48 * 2**20),
        name="orthogonalize",
    )(grads, others, moms)


def update(rate, weight, mom, grad, turn):
    moment = momentum_decay * mom + grad.astype(jnp.float32)
    new = (1.0 - weight_shrink) * weight - rate * turn.astype(jnp.float32)
    return new, moment, new.astype(jnp.bfloat16)


def ffn_update_kernel(
    grad_ref, turn_ref, w_gateup_ref, mom_gateup_ref, w_down_ref, mom_down_ref, *results
):
    for at in range(grad_ref.shape[0]):
        columns = slice(at * HEAD, (at + 1) * HEAD)
        for part in range(3):
            spot = (part, slice(None), columns) if part < 2 else (slice(None), columns)
            weight_ref, mom_ref = (
                (w_gateup_ref, mom_gateup_ref) if part < 2 else (w_down_ref, mom_down_ref)
            )
            packed = slice(part * HEAD, (part + 1) * HEAD)
            values = update(
                matrix_rate,
                weight_ref[spot],
                mom_ref[spot],
                grad_ref[at, :, packed],
                turn_ref[at, :, packed],
            )
            for ref, value in zip(results[:3] if part < 2 else results[3:], values):
                ref[spot] = value


def ffn_update(grads, turns, w_gateup, mom_gateup, w_down, mom_down):
    row_count = w_gateup.shape[1]
    wide = 3
    packet = pl.BlockSpec((wide, row_count, 3 * HEAD), lambda j: (j, 0, 0))
    gateup = pl.BlockSpec((2, row_count, wide * HEAD), lambda j: (0, 0, j))
    down = pl.BlockSpec((row_count, wide * HEAD), lambda j: (0, j))
    dtypes = (jnp.float32, jnp.float32, jnp.bfloat16)
    return pl.pallas_call(
        ffn_update_kernel,
        grid=(FF // HEAD // wide,),
        in_specs=[packet, packet, gateup, gateup, down, down],
        out_specs=[gateup] * 3 + [down] * 3,
        out_shape=[jax.ShapeDtypeStruct(w_gateup.shape, dtype) for dtype in dtypes]
        + [jax.ShapeDtypeStruct(w_down.shape, dtype) for dtype in dtypes],
        cost_estimate=pl.CostEstimate(flops=0, bytes_accessed=50 * 2**20, transcendentals=0),
        compiler_params=pltpu.CompilerParams(vmem_limit_bytes=48 * 2**20),
        name="ffn_update",
    )(grads, turns, w_gateup, mom_gateup, w_down, mom_down)


def attn_update_kernel(rate, packet_ref, w_ref, mom_ref, *results):
    for at in range(2):
        columns = slice(at * HEAD, (at + 1) * HEAD)
        values = update(
            rate,
            w_ref[:, columns],
            mom_ref[:, columns],
            packet_ref[at, :, :HEAD],
            packet_ref[at, :, HEAD:],
        )
        for ref, value in zip(results, values):
            ref[:, columns] = value


def attn_update(rate, offset, packets, weight, mom):
    row_count = packets.shape[1]
    packet = pl.BlockSpec((2, row_count, 2 * HEAD), lambda j: (j + offset // 2, 0, 0))
    block = pl.BlockSpec((row_count, 2 * HEAD), lambda j: (0, j))
    return pl.pallas_call(
        functools.partial(attn_update_kernel, rate),
        grid=(weight.shape[1] // HEAD // 2,),
        in_specs=[packet, block, block],
        out_specs=[block] * 3,
        out_shape=[
            jax.ShapeDtypeStruct(weight.shape, dtype)
            for dtype in (jnp.float32, jnp.float32, jnp.bfloat16)
        ],
        cost_estimate=pl.CostEstimate(flops=0, bytes_accessed=6 * 2**20, transcendentals=0),
        name="attn_update",
    )(packets, weight, mom)


def two_heads(ref):
    return jnp.concatenate([ref[:, :HEAD], ref[:, HEAD:]], axis=0)


def visible(tokens, first_token, shape, query_axis):
    query = lax.rem(lax.broadcasted_iota(jnp.int32, shape, query_axis), tokens)
    key = lax.broadcasted_iota(jnp.int32, shape, 1 - query_axis)
    distance = query + WINDOW - key
    return (distance >= 0) & (distance < WINDOW) & (first_token - WINDOW + key >= 0)


def attend_kernel(first_ref, queries_ref, kv_ref, mixed_ref, log_total_ref):
    tokens = queries_ref.shape[0]
    raw = lax.dot_general(
        two_heads(queries_ref),
        kv_ref[:, :HEAD],
        (((1,), (1,)), ((), ())),
        preferred_element_type=jnp.float32,
    )
    allowed = visible(tokens, first_ref[0], raw.shape, 0)
    scores = jnp.where(allowed, raw * HEAD ** (-0.5), masked_score)
    top_score = jnp.max(scores, axis=-1, keepdims=True)
    expo = jnp.exp(scores - top_score)
    total = jnp.sum(expo, axis=-1, keepdims=True)
    probs = (expo / total).astype(jnp.bfloat16)
    mixed = jnp.dot(probs, kv_ref[:, HEAD:], preferred_element_type=jnp.float32)
    mixed_ref[:, :HEAD] = mixed[:tokens].astype(jnp.bfloat16)
    mixed_ref[:, HEAD:] = mixed[tokens:].astype(jnp.bfloat16)
    log_total_ref[0] = jnp.broadcast_to(top_score + jnp.log(total), log_total_ref.shape[1:])


def attend(first_token, qkv, kv_window):
    tokens = qkv.shape[0]
    span = kv_window.shape[0]
    pairs = H // 2
    return pl.pallas_call(
        attend_kernel,
        grid=(pairs,),
        in_specs=[
            pl.BlockSpec(memory_space=pltpu.SMEM),
            pl.BlockSpec((tokens, 2 * HEAD), lambda j: (0, j)),
            pl.BlockSpec((span, 2 * HEAD), lambda j: (0, 0)),
        ],
        out_specs=[
            pl.BlockSpec((tokens, 2 * HEAD), lambda j: (0, j)),
            pl.BlockSpec((1, 2 * tokens, 128), lambda j: (j, 0, 0)),
        ],
        out_shape=[
            jax.ShapeDtypeStruct((tokens, H * HEAD), jnp.bfloat16),
            jax.ShapeDtypeStruct((pairs, 2 * tokens, 128), jnp.float32),
        ],
        cost_estimate=pl.CostEstimate(
            flops=4 * H * tokens * span * HEAD,
            bytes_accessed=4 * 2**20,
            transcendentals=H * tokens * span,
        ),
        compiler_params=pltpu.CompilerParams(vmem_limit_bytes=48 * 2**20),
        name="attend",
    )(first_token, qkv, kv_window)


def attend_back_kernel(
    first_ref, queries_ref, grads_ref, log_total_ref, kv_ref, grad_query_ref, grad_kv_ref, sums_ref
):
    tokens = queries_ref.shape[0]
    score_scale = HEAD ** (-0.5)
    keys, values = kv_ref[:, :HEAD], kv_ref[:, HEAD:]
    queries, grads = two_heads(queries_ref), two_heads(grads_ref)

    def against(left, right):
        return lax.dot_general(
            left, right, (((1,), (1,)), ((), ())), preferred_element_type=jnp.float32
        )

    raw = against(keys, queries)
    allowed = visible(tokens, first_ref[0], raw.shape, 1)
    scores = jnp.where(allowed, raw * score_scale, masked_score)
    log_total = log_total_ref[0].T[:1]
    probs = jnp.exp(scores - log_total)
    grad_probs = against(values, grads)
    row_delta = jnp.sum(probs * grad_probs, axis=0, keepdims=True)
    grad_raw = (probs * (grad_probs - row_delta) * score_scale).astype(jnp.bfloat16)
    grad_query = lax.dot_general(
        grad_raw, keys, (((0,), (0,)), ((), ())), preferred_element_type=jnp.float32
    )
    grad_query_ref[:, :HEAD] = grad_query[:tokens].astype(jnp.bfloat16)
    grad_query_ref[:, HEAD:] = grad_query[tokens:].astype(jnp.bfloat16)

    @pl.when(pl.program_id(0) == 0)
    def _():
        sums_ref[...] = jnp.zeros_like(sums_ref)

    sums_ref[:, :HEAD] += jnp.dot(grad_raw, queries, preferred_element_type=jnp.float32)
    sums_ref[:, HEAD:] += jnp.dot(
        probs.astype(jnp.bfloat16), grads, preferred_element_type=jnp.float32
    )

    @pl.when(pl.program_id(0) == pl.num_programs(0) - 1)
    def _():
        grad_kv_ref[...] = sums_ref[...].astype(jnp.bfloat16)


def attend_back(first_token, qkv, grads, log_total, kv_window):
    tokens = qkv.shape[0]
    span = kv_window.shape[0]
    heads = pl.BlockSpec((tokens, 2 * HEAD), lambda j: (0, j))
    window = pl.BlockSpec((span, 2 * HEAD), lambda j: (0, 0))
    return pl.pallas_call(
        attend_back_kernel,
        grid=(H // 2,),
        in_specs=[
            pl.BlockSpec(memory_space=pltpu.SMEM),
            heads,
            heads,
            pl.BlockSpec((1, 2 * tokens, 128), lambda j: (j, 0, 0)),
            window,
        ],
        out_specs=[heads, window],
        out_shape=[
            jax.ShapeDtypeStruct((tokens, H * HEAD), jnp.bfloat16),
            jax.ShapeDtypeStruct((span, 2 * HEAD), jnp.bfloat16),
        ],
        scratch_shapes=[pltpu.VMEM((span, 2 * HEAD), jnp.float32)],
        cost_estimate=pl.CostEstimate(
            flops=10 * H * tokens * span * HEAD,
            bytes_accessed=8 * 2**20,
            transcendentals=H * tokens * span,
        ),
        compiler_params=pltpu.CompilerParams(vmem_limit_bytes=48 * 2**20),
        name="attend_back",
    )(first_token, qkv, grads, log_total, kv_window)


def rms_scale(stream, gain_row):
    mean_square = jnp.mean(stream * stream, axis=-1, keepdims=True)
    return stream * lax.rsqrt(mean_square + eps_norm) * gain_row


def gelu_product(gate_part, up_part):
    return jax.nn.gelu(gate_part, approximate=True) * up_part


def on_device(
    tokens_in,
    cotangent,
    w_qkv,
    w_out,
    w_gateup,
    w_down,
    gains,
    mom_qkv,
    mom_out,
    mom_gateup,
    mom_down,
    mom_gains,
):
    everyone = ("blk", "pair")
    bf16 = jnp.bfloat16
    f32 = jnp.float32
    blk_count = lax.axis_size("blk")
    pair_count = lax.axis_size("pair")
    device_count = blk_count * pair_count
    block_at = lax.axis_index("blk")
    half_at = lax.axis_index("pair")
    me = block_at * pair_count + half_at
    local_rows, width = tokens_in.shape
    share_rows = w_qkv.shape[0]
    span = WINDOW + local_rows
    token_count = local_rows * device_count
    large = token_count * width * 2 > 48 * 2**20
    planes = blk_count // 4
    spread = not large

    def after(value, earlier):
        return lax.optimization_barrier((value, earlier))[0] if large else value

    def exchange(packets, axes=everyone):
        return lax.all_to_all(packets, axes, split_axis=0, concat_axis=0, tiled=True)

    def swap(shard):
        return lax.ppermute(shard, "pair", [(0, 1), (1, 0)])

    def hold(value, *earlier):
        return value if large else lax.optimization_barrier((value, earlier))[0]

    def ride(packets, among="all", **options):
        sources = {"all": device_count, "plane": blk_count, "pair": pair_count}[among]
        return Exchange(packets, among, **(dict(sources=sources) | options))

    def exchanged(rides):
        results = []
        for packets, among, _, before, _, _ in rides:
            if among == "pair":
                results.append(swap(packets))
                continue
            axes, places = (everyone, device_count) if among == "all" else ("blk", blk_count)
            after_last = places - before - packets.shape[0]
            packets = jnp.pad(packets, ((before, after_last),) + ((0, 0),) * (packets.ndim - 1))
            results.append(exchange(packets, axes))
        return results

    def gather(shards, whole_slice, collective_id, rides=(), **options):
        if large:
            axes = everyone if whole_slice else "blk"
            wholes = [lax.all_gather(shard, axes, axis=0, tiled=True) for shard in shards]
            return wholes + exchanged(rides)
        return gather_now(shards, planes, whole_slice, collective_id, rides, **options)

    def scatter(partial, whole_slice, collective_id, rides=()):
        if large:
            axes = everyone if whole_slice else "blk"
            part = lax.psum_scatter(partial, axes, scatter_dimension=0, tiled=True)
            return [part] + exchanged(rides)
        return scatter_now(partial, planes, whole_slice, collective_id, rides)

    def gather_plane(shard):
        return lax.all_gather(shard, "blk", axis=0, tiled=True)

    stream = tokens_in.astype(f32)
    padded_gains = jnp.pad(gains.astype(bf16), ((0, 14), (0, 128 - share_rows)))
    full_qkv, full_gains, ffn_weights = gather(
        [w_qkv.astype(bf16), padded_gains],
        True,
        1,
        [ride(ffn_packets(w_gateup, w_down.T))],
    )
    ffn_weights = ffn_weights.reshape(width, 3 * HEAD)
    full_gains = full_gains.reshape(device_count, 16, 128)[:, :2, :share_rows].astype(f32)
    gain_attn = full_gains[:, 0].reshape(width)
    gain_mlp = full_gains[:, 1].reshape(width)
    normed_attn_f, norm_back_attn = jax.vjp(rms_scale, stream, gain_attn)
    normed_attn = normed_attn_f.astype(bf16)
    qkv = jnp.dot(normed_attn, full_qkv, preferred_element_type=f32).astype(bf16)
    kv_all, full_out = gather([qkv[:, H * HEAD :], w_out.T.astype(bf16)], True, 2)
    kv_window = lax.dynamic_slice_in_dim(
        jnp.pad(kv_all, ((WINDOW, 0), (0, 0))), me * local_rows, span, 0
    )
    first_token = (me * local_rows).astype(jnp.int32).reshape(1)
    mixed, log_total = attend(first_token, qkv, kv_window)
    resid = stream + jnp.einsum("tc,dc->td", mixed, full_out, preferred_element_type=f32)

    normed_mlp_f, norm_back_mlp = jax.vjp(rms_scale, resid, gain_mlp)
    normed_mlp = normed_mlp_f.astype(bf16)
    normed_mlp_plane, cotangent_plane, other_weights = gather(
        [normed_mlp, cotangent], False, 3, [ride(ffn_weights, "pair")], part_rows=64
    )
    pair_weights = [ffn_weights, other_weights]
    gates, ups, downs = (
        [weights[:, part * HEAD : (part + 1) * HEAD] for weights in pair_weights]
        for part in range(3)
    )
    owns_block = me < FF // HEAD
    pair_gateup = jnp.where(owns_block, jnp.concatenate(gates + ups, axis=1), 0)
    pair_down = jnp.where(owns_block, jnp.concatenate(downs, axis=1), 0)
    plane_rows = blk_count * local_rows
    both_parts = jnp.dot(normed_mlp_plane, pair_gateup, preferred_element_type=f32)
    pair_width = pair_count * HEAD
    hidden_f, geglu_back = jax.vjp(
        gelu_product, both_parts[:, :pair_width], both_parts[:, pair_width:]
    )
    hidden = hidden_f.astype(bf16)
    grad_hidden = jnp.dot(cotangent_plane, pair_down, preferred_element_type=f32)
    grad_gate, grad_up = geglu_back(grad_hidden)
    grad_gateup = jnp.concatenate([grad_gate.astype(bf16), grad_up.astype(bf16)], axis=1)
    def ffn_gradient(columns):
        gateup_right = jnp.concatenate(
            [grad_gate[:, columns].astype(bf16), grad_up[:, columns].astype(bf16)], axis=1
        )
        down_right = hidden[:, columns]
        return jnp.concatenate(
            [
                jnp.einsum("td,tf->df", normed_mlp_plane, gateup_right, preferred_element_type=f32),
                jnp.einsum("td,tf->df", cotangent_plane, down_right, preferred_element_type=f32),
            ],
            axis=1,
        )

    def pair_columns(columns):
        return columns.reshape(local_rows, -1, pair_width).transpose(1, 0, 2)

    ffn_theirs = ffn_gradient(slice(HEAD, 2 * HEAD)).astype(bf16)
    grad_normed_part = jnp.einsum("tf,df->td", grad_gateup, pair_gateup, preferred_element_type=f32)
    grad_normed_mlp, ffn_others, ffn_moms, attn_moms, out_rights = scatter(
        grad_normed_part.astype(bf16),
        False,
        4,
        [
            ride(ffn_theirs, "pair"),
            ride(ffn_packets(mom_gateup, mom_down.T)),
            ride(attn_packets(mom_qkv, mom_out.T), spread_targets=spread),
            ride(
                pair_columns(mixed), "plane", first_target=(H + 2) // 2, spread_targets=spread
            ),
        ],
    )
    grad_normed_mlp = grad_normed_mlp.astype(f32)

    ffn_grads = ffn_gradient(slice(0, HEAD))
    ffn_low, ffn_turned = orthogonalize(
        ffn_grads, ffn_others, ffn_moms.reshape(width, 3 * HEAD), 2
    )
    ffn_shape = (device_count, share_rows, 3 * HEAD)

    resid_part, gain_grad_mlp = norm_back_mlp(grad_normed_mlp)
    grad_resid = cotangent.astype(f32) + resid_part
    grad_proj = grad_resid.astype(bf16)
    grad_mixed = jnp.dot(grad_proj, full_out, preferred_element_type=f32).astype(bf16)
    grad_query, grad_kv = attend_back(first_token, qkv, grad_mixed, log_total, kv_window)
    grad_kv_all = lax.dynamic_update_slice_in_dim(
        jnp.zeros((WINDOW + token_count, 2 * HEAD), bf16), grad_kv, me * local_rows, 0
    )[WINDOW:]
    grad_kv, ffn_low = scatter(
        grad_kv_all, True, 5, [ride(ffn_low.reshape(ffn_shape), sources=FF // HEAD)]
    )
    grad_qkv = jnp.concatenate([grad_query, grad_kv], axis=1)
    grad_normed_attn = jnp.einsum("tc,dc->td", grad_qkv, full_qkv, preferred_element_type=f32)
    stream_part, gain_grad_attn = norm_back_attn(grad_normed_attn)
    input_grad = grad_resid + stream_part

    branch_part = jnp.einsum(
        "tf,df->td", after(hidden, grad_normed_mlp), pair_down, preferred_element_type=f32
    )
    branch, ffn_turned, qkv_rights = scatter(
        branch_part.astype(bf16),
        False,
        6,
        [
            ride(ffn_turned.reshape(ffn_shape), sources=FF // HEAD),
            ride(pair_columns(grad_qkv), "plane", spread_targets=spread),
        ],
    )
    block_output = (resid + branch.astype(f32)).astype(bf16)
    normed_attn_plane = gather_plane(after(hold(normed_attn, normed_mlp_plane), (ffn_grads, block_output)))
    grad_proj_plane = gather_plane(after(grad_proj, (ffn_grads, block_output)))

    pair_at = spread_place(planes, block_at) if spread else block_at

    def attn_gradient(half, qkv_rights, out_rights):
        def product(lefts, rights):
            rights = rights.reshape(plane_rows, pair_width)
            rights = lax.dynamic_slice_in_dim(rights, half * HEAD, HEAD, 1)
            return jnp.einsum("td,tf->df", lefts, rights, preferred_element_type=f32)

        return lax.cond(
            pair_at < (H + 2) // pair_count,
            lambda: product(normed_attn_plane, qkv_rights),
            lambda: product(grad_proj_plane, out_rights),
        )

    attn_theirs = attn_gradient(1 - half_at, qkv_rights, out_rights).astype(bf16)
    attn_others = swap(attn_theirs)
    attn_grads = attn_gradient(half_at, *hold((qkv_rights, out_rights), attn_theirs))
    updated_ffn = ffn_update(ffn_low, ffn_turned, w_gateup, mom_gateup, w_down.T, mom_down.T)
    (attn_results,) = orthogonalize(
        attn_grads, hold(attn_others, updated_ffn[0]), attn_moms.reshape(width, HEAD), 1
    )
    gain_grads = jnp.stack([gain_grad_attn, gain_grad_mlp], axis=0)
    gain_grads = gain_grads.reshape(2, device_count, share_rows).transpose(1, 0, 2)
    last_rides = [
        ride(
            attn_results.reshape(device_count, share_rows, 2 * HEAD),
            sources=2 * H + 2,
            spread_sources=spread,
        ),
        ride(jnp.pad(gain_grads, ((0, 0), (0, 6), (0, 128 - share_rows)))),
    ]
    if large:
        attn_results, gain_grads = exchanged(last_rides)
    else:
        attn_results, gain_grads = exchange_now(last_rides, planes, 7)
    gain_share = jnp.sum(gain_grads, axis=0)[:2, :share_rows]

    updated_qkv = attn_update(matrix_rate, 0, attn_results, w_qkv, mom_qkv)
    updated_out = attn_update(output_rate, H + 2, attn_results, w_out.T, mom_out.T)
    moment_gains = momentum_decay * mom_gains + gain_share
    new_gains = gains - gain_rate * moment_gains
    return (
        block_output,
        input_grad,
        *updated_qkv,
        *(result.T for result in updated_out),
        *updated_ffn[:3],
        *(result.T for result in updated_ffn[3:]),
        new_gains,
        moment_gains,
        new_gains.astype(bf16),
    )


def solution(mesh):
    placed = (
        P(("blk", "pair"), None),
        P(("blk", "pair"), None),
        P(("blk", "pair"), None),
        P(None, ("blk", "pair")),
        P(None, ("blk", "pair"), None),
        P(None, ("blk", "pair")),
        P(None, ("blk", "pair")),
        P(("blk", "pair"), None),
        P(None, ("blk", "pair")),
        P(None, ("blk", "pair"), None),
        P(None, ("blk", "pair")),
        P(None, ("blk", "pair")),
    )
    return jax.shard_map(
        on_device,
        mesh=mesh,
        in_specs=placed,
        out_specs=(
            P(("blk", "pair"), None),
            P(("blk", "pair"), None),
            P(("blk", "pair"), None),
            P(("blk", "pair"), None),
            P(("blk", "pair"), None),
            P(None, ("blk", "pair")),
            P(None, ("blk", "pair")),
            P(None, ("blk", "pair")),
            P(None, ("blk", "pair"), None),
            P(None, ("blk", "pair"), None),
            P(None, ("blk", "pair"), None),
            P(None, ("blk", "pair")),
            P(None, ("blk", "pair")),
            P(None, ("blk", "pair")),
            P(None, ("blk", "pair")),
            P(None, ("blk", "pair")),
            P(None, ("blk", "pair")),
        ),
        check_vma=False,
    )
```

```python
import functools
from typing import NamedTuple

import jax
import jax.numpy as jnp
from jax import lax
from jax.experimental import pallas as pl
from jax.experimental.pallas import tpu as pltpu
from jax.sharding import PartitionSpec as P

H = 10
HEAD = 256
FF = 7680
WINDOW = 2048
NS_STEPS = 5


eps_norm = 1e-06
eps_pieces = 1e-07
ns_first = 3.4445
ns_second = -4.775
ns_third = 2.0315
momentum_decay = 0.95
matrix_rate = 0.5
output_rate = 10.0
gain_rate = 0.001
weight_shrink = 0.001
masked_score = -1e30
MESH = pl.DeviceIdType.MESH


def position():
    blk, y = lax.axis_index("blk"), lax.axis_index("pair")
    return blk, lax.div(blk, 4), lax.rem(lax.div(blk, 2), 2), lax.rem(blk, 2), y


def greet(devices):
    barrier = pltpu.get_barrier_semaphore()
    for device in devices:
        pl.semaphore_signal(barrier, inc=1, device_id=device, device_id_type=MESH)
    pl.semaphore_wait(barrier, len(devices))


def remote(source, target, send_sem, recv_sem, device):
    return pltpu.make_async_remote_copy(
        src_ref=source,
        dst_ref=target,
        send_sem=send_sem,
        recv_sem=recv_sem,
        device_id=device,
        device_id_type=MESH,
    )


class Exchange(NamedTuple):
    packets: jax.Array
    among: str
    sources: int
    first_target: int = 0
    spread_sources: bool = False
    spread_targets: bool = False


def spread_place(planes, blk):
    z, x, core = lax.div(blk, 4), lax.rem(lax.div(blk, 2), 2), lax.rem(blk, 2)
    return (2 * core + lax.rem(x + z, 2)) * planes + z


def all_devices():
    blk, _, _, _, y = position()
    count = 2 * lax.axis_size("blk")
    here = 2 * blk + y
    places = [lax.rem(here + at, count) for at in range(1, count)]
    return [(lax.div(place, 2), lax.rem(place, 2)) for place in places]


def plane_devices():
    blk, _, _, _, y = position()
    count = lax.axis_size("blk")
    return [(lax.rem(blk + at, count), y) for at in range(1, count)]


def greeted(specs, nearby):
    if any(among == "all" for among, *_ in specs):
        return all_devices()
    blk, _, _, _, y = position()
    pair = [(blk, 1 - y)] * any(among == "pair" for among, *_ in specs)
    if any(among == "plane" for among, *_ in specs):
        return plane_devices() + pair
    return nearby + pair


PAIR_PARTS = 4


def exchange_count(planes, among):
    return {"all": 8 * planes, "plane": 4 * planes, "pair": PAIR_PARTS}[among]


class Ride:
    def __init__(self, planes, spec, packets, received, sems):
        self.planes, self.packets, self.received = planes, packets, received
        self.among, self.sources, self.first_target, self.from_spread, self.to_spread = spec
        self.own_sem, self.send_sems, self.recv_sems = sems
        self.count = exchange_count(planes, self.among)
        self.issued = 0
        blk, self.z, _, _, self.y = position()
        self.blk = blk
        self.here = blk if self.among == "plane" else 2 * blk + self.y

    def place(self, q):
        near = self.count // self.planes
        spot = lax.rem(self.z + 1 + lax.rem(q, self.planes), self.planes)
        return spot * near + lax.rem(self.here + lax.div(q, self.planes), near)

    def counted(self, place, spread):
        if not spread:
            return place
        if self.among == "plane":
            return spread_place(self.planes, place)
        return 2 * spread_place(self.planes, lax.div(place, 2)) + lax.rem(place, 2)

    def source(self, place):
        return self.counted(place, self.from_spread)

    def target(self, place):
        return self.counted(place, self.to_spread) - self.first_target

    def sending(self, place):
        return self.source(place) < self.sources

    def receiving(self, place):
        target = self.target(place)
        return (target >= 0) & (target < self.packets.shape[0])

    def copy(self, q):
        if self.among == "pair":
            rows = self.packets.shape[0] // PAIR_PARTS
            some = pl.ds(pl.multiple_of(q * rows, rows), rows)
            return remote(
                self.packets.at[some],
                self.received.at[some],
                self.send_sems.at[q],
                self.recv_sems.at[q],
                (self.blk, 1 - self.y),
            )
        place = self.place(q)
        device = (place, self.y)
        if self.among == "all":
            device = (lax.div(place, 2), lax.rem(place, 2))
        source = self.source(self.here)
        return remote(
            self.packets.at[self.target(place)],
            self.received.at[source],
            self.send_sems.at[q],
            self.recv_sems.at[source],
            device,
        )

    def own(self):
        return pltpu.make_async_copy(
            self.packets.at[self.target(self.here)],
            self.received.at[self.source(self.here)],
            self.own_sem.at[0],
        )

    def sends(self, q):
        away = (q < self.count) & (q != self.planes - 1)
        return away & self.sending(self.here) & self.receiving(self.place(q))

    def keeps(self):
        return self.sending(self.here) & self.receiving(self.here)

    def start_own(self):
        if self.among == "pair":
            for q in range(self.count):
                self.copy(q).start()
        else:

            @pl.when(self.keeps())
            def _():
                self.own().start()

    def issue(self, q):
        if self.among != "pair":

            @pl.when(self.sends(q))
            def _():
                self.copy(q).start()

    def issue_more(self, number):
        first, self.issued = self.issued, min(self.issued + number, self.count)

        @pl.loop(first, self.issued)
        def _(q):
            self.issue(q)

    def finish(self):
        if self.among == "pair":
            for q in range(self.count):
                self.copy(q).wait()
            return

        @pl.loop(0, self.count)
        def _(q):
            @pl.when(self.sends(q))
            def _():
                self.copy(q).wait_send()

            @pl.when((q != self.here) & self.sending(q) & self.receiving(self.here))
            def _():
                source = self.source(q)
                spot = self.received.at[source]
                remote(
                    spot, spot, self.own_sem.at[0], self.recv_sems.at[source], (self.blk, self.y)
                ).wait_recv()

        @pl.when(self.keeps())
        def _():
            self.own().wait()


def rides_of(planes, rides):
    rides = [Ride(planes, *ride) for ride in rides]
    for ride in rides:
        ride.start_own()
    return rides


def exchange_sems(exchanges, planes):
    dma = pltpu.SemaphoreType.DMA
    return [
        dma((count,))
        for exchange in exchanges
        for count in (1,) + (exchange_count(planes, exchange.among),) * 2
    ]


def exchange_specs(exchanges):
    return tuple((each.among, *each[2:]) for each in exchanges)


def communicate(
    kernel,
    operands,
    exchanges,
    outputs,
    scratch,
    planes,
    collective_id,
    cost,
    name,
    out_spec=pl.ANY,
    **options,
):
    packets = [each.packets for each in exchanges]
    received = [
        jax.ShapeDtypeStruct(
            array.shape
            if each.among == "pair"
            else (exchange_count(planes, each.among), *array.shape[1:]),
            array.dtype,
        )
        for each, array in zip(exchanges, packets)
    ]
    any_spec = pl.BlockSpec(memory_space=pl.ANY)
    return pl.pallas_call(
        kernel,
        out_shape=outputs + received,
        in_specs=[any_spec] * (len(operands) + len(packets)),
        out_specs=[pl.BlockSpec(memory_space=out_spec)] * len(outputs) + [any_spec] * len(packets),
        scratch_shapes=scratch + exchange_sems(exchanges, planes),
        compiler_params=pltpu.CompilerParams(
            collective_id=collective_id, has_side_effects=True, **options
        ),
        cost_estimate=pl.CostEstimate(flops=0, bytes_accessed=cost * 2**20, transcendentals=0),
        name=name,
    )(*operands, *packets)


def split_refs(refs, inputs, outputs, specs):
    riders = len(specs)
    ins, refs = refs[: inputs + riders], refs[inputs + riders :]
    outs, refs = refs[: outputs + riders], refs[outputs + riders :]
    scratch = refs[: len(refs) - 3 * riders]
    sems = refs[len(refs) - 3 * riders :]
    rides = [
        (spec, ins[inputs + i], outs[outputs + i], sems[3 * i : 3 * i + 3])
        for i, spec in enumerate(specs)
    ]
    return ins[:inputs], outs[:outputs], scratch, rides


def exchange_kernel(planes, specs, *refs):
    _, _, _, rides = split_refs(refs, 0, 0, specs)
    greet(greeted(specs, []))
    rides = rides_of(planes, rides)
    for ride in rides:
        ride.issue_more(ride.count)
    for ride in rides:
        ride.finish()


def exchange_now(exchanges, planes, collective_id):
    specs = exchange_specs(exchanges)
    kernel = functools.partial(exchange_kernel, planes, specs)
    return communicate(kernel, [], exchanges, [], [], planes, collective_id, 100, "exchange_now")


def gather_kernel(planes, parts, whole_slice, specs, *refs):
    arrays = 1 + max(array for array, *_ in parts)
    shard_refs, whole_refs, scratch, rides = split_refs(refs, arrays, arrays, specs)
    count = len(parts)
    shards = [shard_refs[array].at[pl.ds(start, size)] for array, start, size, _ in parts]
    late = [is_late for *_, is_late in parts]
    own_sem, line_send, second_send, first_send, core_send, recv, core_recv = scratch
    blk, z, x, core, y = position()
    firsts = 2 if whole_slice else 1
    to_core = (blk + 1 - 2 * core, y)
    if whole_slice:
        first = y * (1 - core) + x * core
        second = x * (1 - core) + y * core
        first_device = (blk + core * (2 - 4 * x), y + (1 - core) * (1 - 2 * y))
        second_device = (blk + (1 - core) * (2 - 4 * x), y + core * (1 - 2 * y))
    else:
        first, second = 0, x
        first_device, second_device = None, (blk + 2 - 4 * x, y)
    line = [(blk + 4 * (lax.rem(z + at, planes) - z), y) for at in range(1, planes)]
    nearby = [to_core, second_device] + [first_device] * whole_slice + line
    greet(greeted(specs, nearby))

    def slot(i, spot, by_first, by_second, plane):
        array, start, size, _ = parts[i]
        whole, some = whole_refs[array], pl.ds(start, size)
        if whole_slice:
            by_x = (1 - plane) * by_second + plane * by_first
            by_y = (1 - plane) * by_first + plane * by_second
            return whole.at[spot, by_x, plane, by_y, some]
        return whole.at[spot, by_second, plane, some]

    def arrive(i, spot, by_first, by_second):
        here = slot(i, spot, by_first, by_second, core)
        remote(here, here, own_sem.at[0], recv.at[i, spot, by_first, by_second], to_core).wait_recv()

    def along(i, source, spot, turn, way):
        by_second = second if turn == 0 else 1 - second
        target = slot(i, spot, first, by_second, core)
        sems = line_send.at[way, i, spot, turn], recv.at[i, spot, first, by_second]
        return remote(source, target, *sems, (blk + 4 - 8 * way, y))

    def onward(i, source, spot, own):
        target = slot(i, spot, first, second, core)
        arrived = recv.at[i, spot, first, second]
        if own or not late[i]:
            yield remote(source, target, second_send.at[i, spot], arrived, second_device)
        if whole_slice:
            yield remote(source, target, first_send.at[i, spot, 0], arrived, first_device)
        yield remote(
            source, target, core_send.at[i, spot, 0, 0], core_recv.at[i, spot, first, second], to_core
        )

    def after_second(i, spot):
        here = slot(i, spot, first, 1 - second, core)
        if whole_slice:
            yield remote(
                here, here, first_send.at[i, spot, 1], recv.at[i, spot, first, 1 - second], first_device
            )
        yield remote(
            here, here, core_send.at[i, spot, 0, 1], core_recv.at[i, spot, first, 1 - second], to_core
        )

    def after_first(i, spot, turn):
        by_second = second if turn == 0 else 1 - second
        here = slot(i, spot, 1 - first, by_second, core)
        return remote(
            here, here, core_send.at[i, spot, 1, turn], core_recv.at[i, spot, 1 - first, by_second], to_core
        )

    def line_steps():
        for far in range(1, planes):
            yield z - far, z >= far, 0, z < planes - 1
            yield z + far, z < planes - far, 1, z > 0

    ends = [(0, z < planes - 1), (1, z > 0)]
    own_copies = []
    for i in range(count):
        copy = pltpu.make_async_copy(
            shards[i], slot(i, z, first, second, core), own_sem.at[1 + i]
        )
        copy.start()
        own_copies.append(copy)

        for way, further in ends:

            @pl.when(further)
            def _():
                along(i, shards[i], z, 0, way).start()

        for copy in onward(i, shards[i], z, True):
            copy.start()
    rides = rides_of(planes, rides)

    def issue(number):
        for ride in rides:
            ride.issue_more(number)

    issue(6)
    for i in range(count):
        arrive(i, z, first, 1 - second)
        for way, further in ends * late[i]:

            @pl.when(further)
            def _():
                along(i, slot(i, z, first, 1 - second, core), z, 1, way).start()

        for copy in after_second(i, z):
            copy.start()
    issue(4)
    for spot, there, way, further in line_steps():

        @pl.when(there)
        def _():
            for i in range(count):
                here = slot(i, spot, first, second, core)
                arrive(i, spot, first, second)

                @pl.when(further)
                def _():
                    along(i, here, spot, 0, way).start()

                for copy in onward(i, here, spot, False):
                    copy.start()
            for i in range(count):
                arrive(i, spot, first, 1 - second)
                if late[i]:

                    @pl.when(further)
                    def _():
                        along(i, slot(i, spot, first, 1 - second, core), spot, 1, way).start()

                for copy in after_second(i, spot):
                    copy.start()

        issue(4)

    issue(8 * planes)
    spots = [lax.rem(z + at, planes) for at in range(planes)]
    if whole_slice:
        for spot in spots:
            for turn in range(2):
                for i in range(count):
                    arrive(i, spot, 1 - first, second if turn == 0 else 1 - second)
                    after_first(i, spot, turn).start()
    for copy in own_copies:
        copy.wait()
    for i in range(count):
        for spot in range(planes):
            for by_first in range(firsts):
                for by_second in range(2):
                    there = slot(i, spot, by_first, by_second, 1 - core)
                    arrived = core_recv.at[i, spot, by_first, by_second]
                    remote(there, there, own_sem.at[0], arrived, to_core).wait_recv()
    for ride in rides:
        ride.finish()
    for i in range(count):
        for turn in range(1 + late[i]):
            for way, further in ends:

                @pl.when(further)
                def _():
                    along(i, shards[i], z, turn, way).wait_send()

            for spot, there, way, further in line_steps():

                @pl.when(there & further)
                def _():
                    along(i, shards[i], spot, turn, way).wait_send()

        for at, spot in enumerate(spots):
            for copy in onward(i, shards[i], spot, at == 0):
                copy.wait_send()
            for copy in after_second(i, spot):
                copy.wait_send()
            for turn in range(2 * (firsts - 1)):
                after_first(i, spot, turn).wait_send()


def gather_now(shards, planes, whole_slice, collective_id, exchanges=(), late_rows=None):
    parts = []
    for array, shard in enumerate(shards):
        rows = shard.shape[0]
        early = rows - (late_rows[array] if late_rows else 0)
        parts += [(array, 0, early, False)] * (early > 0)
        parts += [(array, early, rows - early, True)] * (early < rows)
    count = len(parts)
    firsts = 2 if whole_slice else 1
    specs = exchange_specs(exchanges)
    dma = pltpu.SemaphoreType.DMA
    grid = (planes, 2, 2, 2) if whole_slice else (planes, 2, 2)
    results = communicate(
        functools.partial(gather_kernel, planes, parts, whole_slice, specs),
        list(shards),
        exchanges,
        [jax.ShapeDtypeStruct((*grid, *shard.shape), shard.dtype) for shard in shards],
        [
            dma((count + 1,)),
            dma((2, count, planes, 2)),
            dma((count, planes)),
            dma((count, planes, 2)),
            dma((count, planes, 2, 2)),
            dma((count, planes, firsts, 2)),
            dma((count, planes, firsts, 2)),
        ],
        planes,
        collective_id,
        200,
        "gather_now",
    )
    places = 4 * planes * firsts
    wholes = [
        whole.reshape(places * shard.shape[0], shard.shape[1])
        for whole, shard in zip(results, shards)
    ]
    return wholes + list(results[len(shards) :])


def scatter_kernel(planes, steps, rows, whole_slice, specs, *refs):
    (partial_ref,), (sum_ref,), scratch, rides = split_refs(refs, 1, 1, specs)
    own, from_core, from_first, from_second, from_below, from_above = scratch[:6]
    load_sem, core_sems, first_sems, second_sems, up_sems, down_sems = scratch[6:]
    blk, z, x, core, y = position()
    firsts = 2 if whole_slice else 1
    to_core = (blk + 1 - 2 * core, y)
    if whole_slice:
        first = y * (1 - core) + x * core
        second = x * (1 - core) + y * core
        core_second = second
        first_device = (blk + core * (2 - 4 * x), y + (1 - core) * (1 - 2 * y))
        second_device = (blk + (1 - core) * (2 - 4 * x), y + core * (1 - 2 * y))
    else:
        first, second = 0, x
        first_device, second_device = None, (blk + 2 - 4 * x, y)
    line = [(blk + 4 * (lax.rem(z + at, planes) - z), y) for at in range(1, planes)]
    nearby = [to_core, second_device] + [first_device] * whole_slice + line
    greet(greeted(specs, nearby))

    def piece(step, by_first, by_second, plane):
        some = pl.ds(pl.multiple_of(step * rows, rows), rows)
        if whole_slice:
            by_x = (1 - plane) * by_second + plane * by_first
            by_y = (1 - plane) * by_first + plane * by_second
            return partial_ref.at[:, by_x, plane, by_y, some]
        return partial_ref.at[:, by_second, plane, some]

    def core_copy(step, by_first, by_second, plane):
        return remote(
            piece(step, by_first, by_second, plane),
            from_core.at[step, by_first, by_second],
            core_sems.at[0, step, by_first, by_second],
            core_sems.at[1, step, by_first, by_second],
            to_core,
        )

    def load(step, by_first, by_second):
        return pltpu.make_async_copy(
            piece(step, by_first, by_second, core),
            own.at[step, by_first, by_second],
            load_sem.at[step, by_first, by_second],
        )

    def first_copy(step):
        return remote(
            own.at[step, 1 - first],
            from_first.at[step],
            first_sems.at[0, step],
            first_sems.at[1, step],
            first_device,
        )

    def second_copy(step):
        return remote(
            own.at[step, first, 1 - second],
            from_second.at[step],
            second_sems.at[0, step],
            second_sems.at[1, step],
            second_device,
        )

    def up_copy(step, target):
        return remote(
            own.at[step, first, second, target],
            from_below.at[step, target],
            up_sems.at[0, step, target],
            up_sems.at[1, step, target],
            (blk + 4, y),
        )

    def down_copy(step, target):
        return remote(
            own.at[step, first, second, target],
            from_above.at[step, target],
            down_sems.at[0, step, target],
            down_sems.at[1, step, target],
            (blk - 4, y),
        )

    def halves():
        if not whole_slice:
            return [(0, 1 - second), (0, second)]
        return [(1 - first, 0), (1 - first, 1), (first, 0), (first, 1)]

    def core_halves():
        if not whole_slice:
            return [(0, 1 - second), (0, second)]
        return [(1 - core_second, 0), (1 - core_second, 1), (core_second, 0), (core_second, 1)]

    def start_loads(step):
        for mine, theirs in zip(halves(), core_halves()):
            core_copy(step, *theirs, 1 - core).start()
            load(step, *mine).start()

    def add_core(step):
        for turn, mine in enumerate(halves()):
            load(step, *mine).wait()
            core_copy(step, *mine, core).wait_recv()
            own[step, *mine] += from_core[step, *mine]
            if whole_slice and turn == 1:
                first_copy(step).start()
            if not whole_slice and turn == 0:
                second_copy(step).start()

    def add_first(step):
        first_copy(step).wait_recv()
        own[step, first, 1 - second] += from_first[step, 1 - second]
        second_copy(step).start()
        own[step, first, second] += from_first[step, second]

    def add_second(step):
        second_copy(step).wait_recv()
        own[step, first, second] += from_second[step]

    def pass_up(step):
        for target in range(planes):

            @pl.when((z > 0) & (z <= target))
            def _():
                up_copy(step, target).wait_recv()

            @pl.when((z > 0) & (z < target))
            def _():
                own[step, first, second, target] += from_below[step, target]

            @pl.when(z < target)
            def _():
                up_copy(step, target).start()

    def pass_down(step):
        for target in range(planes):

            @pl.when((z < planes - 1) & (z >= target))
            def _():
                down_copy(step, target).wait_recv()

            @pl.when((z < planes - 1) & (z > target))
            def _():
                own[step, first, second, target] += from_above[step, target]

            @pl.when(z > target)
            def _():
                down_copy(step, target).start()

    def add_line(step):
        some = pl.ds(pl.multiple_of(step * rows, rows), rows)
        sum_ref[some, :] = own[step, first, second, z]

        @pl.when(z > 0)
        def _():
            sum_ref[some, :] += from_below[step, z]

        @pl.when(z < planes - 1)
        def _():
            sum_ref[some, :] += from_above[step, z]

    start_loads(0)
    start_loads(1)
    rides = rides_of(planes, rides)
    early = firsts + 1
    hurry = [-(-ride.count // steps) for ride in rides]

    @pl.loop(0, steps + early + planes)
    def _(turn):
        def stage(step, work):
            @pl.when((step >= 0) & (step < steps))
            def _():
                work(step)

        @pl.when(turn < steps - 2)
        def _():
            start_loads(turn + 2)

        stage(turn, add_core)
        for ride, number in zip(rides, hurry):
            for at in range(number):
                ride.issue(turn * number + at)
        if whole_slice:
            stage(turn - 1, add_first)
        stage(turn - early + 1, add_second)
        stage(turn - early - z, pass_up)
        stage(turn - early - (planes - 1 - z), pass_down)
        stage(turn - early - planes + 1, add_line)

    @pl.loop(0, steps)
    def _(step):
        for theirs in core_halves():
            core_copy(step, *theirs, 1 - core).wait_send()
        if whole_slice:
            first_copy(step).wait_send()
        second_copy(step).wait_send()
        for target in range(planes):

            @pl.when(z < target)
            def _():
                up_copy(step, target).wait_send()

            @pl.when(z > target)
            def _():
                down_copy(step, target).wait_send()

    for ride in rides:
        ride.finish()


def scatter_now(partial, planes, whole_slice, collective_id, exchanges=()):
    firsts = 2 if whole_slice else 1
    shard_rows = partial.shape[0] // (4 * planes * firsts)
    width = partial.shape[1]
    rows = 16
    steps = shard_rows // rows
    dtype = partial.dtype
    specs = exchange_specs(exchanges)
    dma = pltpu.SemaphoreType.DMA
    grid = (planes, 2, 2, 2) if whole_slice else (planes, 2, 2)
    return communicate(
        functools.partial(scatter_kernel, planes, steps, rows, whole_slice, specs),
        [partial.reshape(*grid, shard_rows, width)],
        exchanges,
        [jax.ShapeDtypeStruct((shard_rows, width), dtype)],
        [
            pltpu.VMEM((steps, firsts, 2, planes, rows, width), dtype),
            pltpu.VMEM((steps, firsts, 2, planes, rows, width), dtype),
            pltpu.VMEM((steps if whole_slice else 1, 2, planes, rows, width), dtype),
            pltpu.VMEM((steps, planes, rows, width), dtype),
            pltpu.VMEM((steps, planes, rows, width), dtype),
            pltpu.VMEM((steps, planes, rows, width), dtype),
            dma((steps, firsts, 2)),
            dma((2, steps, firsts, 2)),
            dma((2, steps)),
            dma((2, steps)),
            dma((2, steps, planes)),
            dma((2, steps, planes)),
        ],
        planes,
        collective_id,
        200,
        "scatter_now",
        out_spec=pltpu.VMEM,
        vmem_limit_bytes=48 * 2**20,
    )


def ffn_pack_kernel(gateup_ref, down_ref, packet_ref):
    for at in range(packet_ref.shape[0]):
        columns = slice(at * HEAD, (at + 1) * HEAD)
        packet_ref[at, :, :HEAD] = gateup_ref[0, :, columns].astype(jnp.bfloat16)
        packet_ref[at, :, HEAD : 2 * HEAD] = gateup_ref[1, :, columns].astype(jnp.bfloat16)
        packet_ref[at, :, 2 * HEAD :] = down_ref[:, columns].astype(jnp.bfloat16)


def ffn_packets(gateup, down):
    row_count = gateup.shape[1]
    blocks, wide = FF // HEAD, 5
    return pl.pallas_call(
        ffn_pack_kernel,
        grid=(blocks // wide,),
        in_specs=[
            pl.BlockSpec((2, row_count, wide * HEAD), lambda j: (0, 0, j)),
            pl.BlockSpec((row_count, wide * HEAD), lambda j: (0, j)),
        ],
        out_specs=pl.BlockSpec((wide, row_count, 3 * HEAD), lambda j: (j, 0, 0)),
        out_shape=jax.ShapeDtypeStruct((blocks, row_count, 3 * HEAD), jnp.bfloat16),
        cost_estimate=pl.CostEstimate(flops=0, bytes_accessed=12 * 2**20, transcendentals=0),
        compiler_params=pltpu.CompilerParams(vmem_limit_bytes=32 * 2**20),
        name="ffn_packets",
    )(gateup, down)


def attn_pack_kernel(qkv_ref, out_ref, packet_ref):
    j = pl.program_id(0)

    @pl.when(j < (H + 2) // 2)
    def _():
        for at in range(2):
            packet_ref[at] = qkv_ref[:, at * HEAD : (at + 1) * HEAD].astype(jnp.bfloat16)

    @pl.when(j >= (H + 2) // 2)
    def _():
        for at in range(2):
            packet_ref[at] = out_ref[:, at * HEAD : (at + 1) * HEAD].astype(jnp.bfloat16)


def attn_packets(qkv, out):
    row_count = qkv.shape[0]
    qkv_last, out_last = (H + 2) // 2 - 1, H // 2 - 1
    return pl.pallas_call(
        attn_pack_kernel,
        grid=(H + 1,),
        in_specs=[
            pl.BlockSpec((row_count, 2 * HEAD), lambda j: (0, jnp.minimum(j, qkv_last))),
            pl.BlockSpec((row_count, 2 * HEAD), lambda j: (0, jnp.clip(j - qkv_last - 1, 0, out_last))),
        ],
        out_specs=pl.BlockSpec((2, row_count, HEAD), lambda j: (j, 0, 0)),
        out_shape=jax.ShapeDtypeStruct((2 * H + 2, row_count, HEAD), jnp.bfloat16),
        cost_estimate=pl.CostEstimate(flops=0, bytes_accessed=4 * 2**20, transcendentals=0),
        name="attn_packets",
    )(qkv, out)


def turn_kernel(grads_ref, others_ref, mom_ref, *refs):
    *results, current_ref = refs
    if len(results) == 1:
        low_ref, turned_ref = results[0].at[:, :HEAD], results[0].at[:, HEAD:]
    else:
        low_ref, turned_ref = results
    grads = grads_ref[...] + others_ref[...].astype(jnp.float32)
    low_ref[...] = grads.astype(jnp.bfloat16)
    moment = momentum_decay * mom_ref[...].astype(jnp.float32) + grads
    moment = moment.astype(jnp.bfloat16).astype(jnp.float32)
    norm_size = jnp.sqrt(jnp.sum(moment * moment, keepdims=True))
    current_ref[...] = (moment / (norm_size + eps_pieces)).T.astype(jnp.bfloat16)

    @pl.loop(0, NS_STEPS)
    def _(sweep_index):
        current = current_ref[...]
        gram_matrix = lax.dot_general(
            current, current, (((1,), (1,)), ((), ())), preferred_element_type=jnp.float32
        ).astype(jnp.bfloat16)
        square = jnp.dot(gram_matrix, gram_matrix, preferred_element_type=jnp.float32)
        mixing = (ns_second * gram_matrix.astype(jnp.float32) + ns_third * square).astype(
            jnp.bfloat16
        )
        turned = jnp.dot(mixing, current, preferred_element_type=jnp.float32)
        current_ref[...] = (ns_first * current.astype(jnp.float32) + turned).astype(jnp.bfloat16)

    turned_ref[...] = current_ref[...].astype(jnp.float32).T.astype(jnp.bfloat16)


def orthogonalize(grads, others, moms, results):
    depth, columns = grads.shape
    block = pl.BlockSpec((depth, HEAD), lambda j: (0, j))
    pieces = columns // HEAD
    return pl.pallas_call(
        turn_kernel,
        grid=(pieces,),
        in_specs=[block] * 3,
        out_specs=[pl.BlockSpec((depth, 2 // results * HEAD), lambda j: (0, j))] * results,
        out_shape=[jax.ShapeDtypeStruct((depth, 2 // results * columns), jnp.bfloat16)] * results,
        scratch_shapes=[pltpu.VMEM((HEAD, depth), jnp.bfloat16)],
        cost_estimate=pl.CostEstimate(
            flops=pieces * 20 * depth * HEAD * HEAD, bytes_accessed=12 * depth * columns, transcendentals=0
        ),
        compiler_params=pltpu.CompilerParams(vmem_limit_bytes=48 * 2**20),
        name="orthogonalize",
    )(grads, others, moms)


def update(rate, weight, mom, grad, turn):
    moment = momentum_decay * mom + grad.astype(jnp.float32)
    new = (1.0 - weight_shrink) * weight - rate * turn.astype(jnp.float32)
    return new, moment, new.astype(jnp.bfloat16)


def ffn_update_kernel(
    grad_ref, turn_ref, w_gateup_ref, mom_gateup_ref, w_down_ref, mom_down_ref, *results
):
    for at in range(grad_ref.shape[0]):
        columns = slice(at * HEAD, (at + 1) * HEAD)
        for part in range(3):
            spot = (part, slice(None), columns) if part < 2 else (slice(None), columns)
            weight_ref, mom_ref = (
                (w_gateup_ref, mom_gateup_ref) if part < 2 else (w_down_ref, mom_down_ref)
            )
            packed = slice(part * HEAD, (part + 1) * HEAD)
            values = update(
                matrix_rate,
                weight_ref[spot],
                mom_ref[spot],
                grad_ref[at, :, packed],
                turn_ref[at, :, packed],
            )
            for ref, value in zip(results[:3] if part < 2 else results[3:], values):
                ref[spot] = value


def ffn_update(grads, turns, w_gateup, mom_gateup, w_down, mom_down):
    row_count = w_gateup.shape[1]
    wide = 3
    packet = pl.BlockSpec((wide, row_count, 3 * HEAD), lambda j: (j, 0, 0))
    gateup = pl.BlockSpec((2, row_count, wide * HEAD), lambda j: (0, 0, j))
    down = pl.BlockSpec((row_count, wide * HEAD), lambda j: (0, j))
    dtypes = (jnp.float32, jnp.float32, jnp.bfloat16)
    return pl.pallas_call(
        ffn_update_kernel,
        grid=(FF // HEAD // wide,),
        in_specs=[packet, packet, gateup, gateup, down, down],
        out_specs=[gateup] * 3 + [down] * 3,
        out_shape=[jax.ShapeDtypeStruct(w_gateup.shape, dtype) for dtype in dtypes]
        + [jax.ShapeDtypeStruct(w_down.shape, dtype) for dtype in dtypes],
        cost_estimate=pl.CostEstimate(flops=0, bytes_accessed=50 * 2**20, transcendentals=0),
        compiler_params=pltpu.CompilerParams(vmem_limit_bytes=48 * 2**20),
        name="ffn_update",
    )(grads, turns, w_gateup, mom_gateup, w_down, mom_down)


def attn_update_kernel(rate, packet_ref, w_ref, mom_ref, *results):
    for at in range(2):
        columns = slice(at * HEAD, (at + 1) * HEAD)
        values = update(
            rate,
            w_ref[:, columns],
            mom_ref[:, columns],
            packet_ref[at, :, :HEAD],
            packet_ref[at, :, HEAD:],
        )
        for ref, value in zip(results, values):
            ref[:, columns] = value


def attn_update(rate, offset, packets, weight, mom):
    row_count = packets.shape[1]
    packet = pl.BlockSpec((2, row_count, 2 * HEAD), lambda j: (j + offset // 2, 0, 0))
    block = pl.BlockSpec((row_count, 2 * HEAD), lambda j: (0, j))
    return pl.pallas_call(
        functools.partial(attn_update_kernel, rate),
        grid=(weight.shape[1] // HEAD // 2,),
        in_specs=[packet, block, block],
        out_specs=[block] * 3,
        out_shape=[
            jax.ShapeDtypeStruct(weight.shape, dtype)
            for dtype in (jnp.float32, jnp.float32, jnp.bfloat16)
        ],
        cost_estimate=pl.CostEstimate(flops=0, bytes_accessed=6 * 2**20, transcendentals=0),
        name="attn_update",
    )(packets, weight, mom)


def two_heads(ref):
    return jnp.concatenate([ref[:, :HEAD], ref[:, HEAD:]], axis=0)


def visible(tokens, first_token, shape, query_axis):
    query = lax.rem(lax.broadcasted_iota(jnp.int32, shape, query_axis), tokens)
    key = lax.broadcasted_iota(jnp.int32, shape, 1 - query_axis)
    distance = query + WINDOW - key
    return (distance >= 0) & (distance < WINDOW) & (first_token - WINDOW + key >= 0)


def attend_kernel(first_ref, queries_ref, kv_ref, mixed_ref, log_total_ref):
    tokens = queries_ref.shape[0]
    raw = lax.dot_general(
        two_heads(queries_ref),
        kv_ref[:, :HEAD],
        (((1,), (1,)), ((), ())),
        preferred_element_type=jnp.float32,
    )
    allowed = visible(tokens, first_ref[0], raw.shape, 0)
    scores = jnp.where(allowed, raw * HEAD ** (-0.5), masked_score)
    top_score = jnp.max(scores, axis=-1, keepdims=True)
    expo = jnp.exp(scores - top_score)
    total = jnp.sum(expo, axis=-1, keepdims=True)
    probs = (expo / total).astype(jnp.bfloat16)
    mixed = jnp.dot(probs, kv_ref[:, HEAD:], preferred_element_type=jnp.float32)
    mixed_ref[:, :HEAD] = mixed[:tokens].astype(jnp.bfloat16)
    mixed_ref[:, HEAD:] = mixed[tokens:].astype(jnp.bfloat16)
    log_total_ref[0] = jnp.broadcast_to(top_score + jnp.log(total), log_total_ref.shape[1:])


def attend(first_token, qkv, kv_window):
    tokens = qkv.shape[0]
    span = kv_window.shape[0]
    pairs = H // 2
    return pl.pallas_call(
        attend_kernel,
        grid=(pairs,),
        in_specs=[
            pl.BlockSpec(memory_space=pltpu.SMEM),
            pl.BlockSpec((tokens, 2 * HEAD), lambda j: (0, j)),
            pl.BlockSpec((span, 2 * HEAD), lambda j: (0, 0)),
        ],
        out_specs=[
            pl.BlockSpec((tokens, 2 * HEAD), lambda j: (0, j)),
            pl.BlockSpec((1, 2 * tokens, 128), lambda j: (j, 0, 0)),
        ],
        out_shape=[
            jax.ShapeDtypeStruct((tokens, H * HEAD), jnp.bfloat16),
            jax.ShapeDtypeStruct((pairs, 2 * tokens, 128), jnp.float32),
        ],
        cost_estimate=pl.CostEstimate(
            flops=4 * H * tokens * span * HEAD,
            bytes_accessed=4 * 2**20,
            transcendentals=H * tokens * span,
        ),
        compiler_params=pltpu.CompilerParams(vmem_limit_bytes=48 * 2**20),
        name="attend",
    )(first_token, qkv, kv_window)


def attend_back_kernel(
    first_ref, queries_ref, grads_ref, log_total_ref, kv_ref, grad_query_ref, grad_kv_ref, sums_ref
):
    tokens = queries_ref.shape[0]
    score_scale = HEAD ** (-0.5)
    keys, values = kv_ref[:, :HEAD], kv_ref[:, HEAD:]
    queries, grads = two_heads(queries_ref), two_heads(grads_ref)

    def against(left, right):
        return lax.dot_general(
            left, right, (((1,), (1,)), ((), ())), preferred_element_type=jnp.float32
        )

    raw = against(keys, queries)
    allowed = visible(tokens, first_ref[0], raw.shape, 1)
    scores = jnp.where(allowed, raw * score_scale, masked_score)
    log_total = log_total_ref[0].T[:1]
    probs = jnp.exp(scores - log_total)
    grad_probs = against(values, grads)
    row_delta = jnp.sum(probs * grad_probs, axis=0, keepdims=True)
    grad_raw = (probs * (grad_probs - row_delta) * score_scale).astype(jnp.bfloat16)
    grad_query = lax.dot_general(
        grad_raw, keys, (((0,), (0,)), ((), ())), preferred_element_type=jnp.float32
    )
    grad_query_ref[:, :HEAD] = grad_query[:tokens].astype(jnp.bfloat16)
    grad_query_ref[:, HEAD:] = grad_query[tokens:].astype(jnp.bfloat16)

    @pl.when(pl.program_id(0) == 0)
    def _():
        sums_ref[...] = jnp.zeros_like(sums_ref)

    sums_ref[:, :HEAD] += jnp.dot(grad_raw, queries, preferred_element_type=jnp.float32)
    sums_ref[:, HEAD:] += jnp.dot(
        probs.astype(jnp.bfloat16), grads, preferred_element_type=jnp.float32
    )

    @pl.when(pl.program_id(0) == pl.num_programs(0) - 1)
    def _():
        grad_kv_ref[...] = sums_ref[...].astype(jnp.bfloat16)


def attend_back(first_token, qkv, grads, log_total, kv_window):
    tokens = qkv.shape[0]
    span = kv_window.shape[0]
    heads = pl.BlockSpec((tokens, 2 * HEAD), lambda j: (0, j))
    window = pl.BlockSpec((span, 2 * HEAD), lambda j: (0, 0))
    return pl.pallas_call(
        attend_back_kernel,
        grid=(H // 2,),
        in_specs=[
            pl.BlockSpec(memory_space=pltpu.SMEM),
            heads,
            heads,
            pl.BlockSpec((1, 2 * tokens, 128), lambda j: (j, 0, 0)),
            window,
        ],
        out_specs=[heads, window],
        out_shape=[
            jax.ShapeDtypeStruct((tokens, H * HEAD), jnp.bfloat16),
            jax.ShapeDtypeStruct((span, 2 * HEAD), jnp.bfloat16),
        ],
        scratch_shapes=[pltpu.VMEM((span, 2 * HEAD), jnp.float32)],
        cost_estimate=pl.CostEstimate(
            flops=10 * H * tokens * span * HEAD,
            bytes_accessed=8 * 2**20,
            transcendentals=H * tokens * span,
        ),
        compiler_params=pltpu.CompilerParams(vmem_limit_bytes=48 * 2**20),
        name="attend_back",
    )(first_token, qkv, grads, log_total, kv_window)


def rms_scale(stream, gain_row):
    mean_square = jnp.mean(stream * stream, axis=-1, keepdims=True)
    return stream * lax.rsqrt(mean_square + eps_norm) * gain_row


def gelu_product(gate_part, up_part):
    return jax.nn.gelu(gate_part, approximate=True) * up_part


def on_device(
    tokens_in,
    cotangent,
    w_qkv,
    w_out,
    w_gateup,
    w_down,
    gains,
    mom_qkv,
    mom_out,
    mom_gateup,
    mom_down,
    mom_gains,
):
    everyone = ("blk", "pair")
    bf16 = jnp.bfloat16
    f32 = jnp.float32
    blk_count = lax.axis_size("blk")
    pair_count = lax.axis_size("pair")
    device_count = blk_count * pair_count
    block_at = lax.axis_index("blk")
    half_at = lax.axis_index("pair")
    me = block_at * pair_count + half_at
    local_rows, width = tokens_in.shape
    share_rows = w_qkv.shape[0]
    span = WINDOW + local_rows
    token_count = local_rows * device_count
    large = token_count * width * 2 > 48 * 2**20
    planes = blk_count // 4
    spread = not large

    def after(value, earlier):
        return lax.optimization_barrier((value, earlier))[0] if large else value

    def exchange(packets, axes=everyone):
        return lax.all_to_all(packets, axes, split_axis=0, concat_axis=0, tiled=True)

    def swap(shard):
        return lax.ppermute(shard, "pair", [(0, 1), (1, 0)])

    def hold(value, *earlier):
        return value if large else lax.optimization_barrier((value, earlier))[0]

    def ride(packets, among="all", **options):
        sources = {"all": device_count, "plane": blk_count, "pair": pair_count}[among]
        return Exchange(packets, among, **(dict(sources=sources) | options))

    def exchanged(rides):
        results = []
        for packets, among, _, before, _, _ in rides:
            if among == "pair":
                results.append(swap(packets))
                continue
            axes, places = (everyone, device_count) if among == "all" else ("blk", blk_count)
            after_last = places - before - packets.shape[0]
            packets = jnp.pad(packets, ((before, after_last),) + ((0, 0),) * (packets.ndim - 1))
            results.append(exchange(packets, axes))
        return results

    def gather(shards, whole_slice, collective_id, rides=(), **options):
        if large:
            axes = everyone if whole_slice else "blk"
            wholes = [lax.all_gather(shard, axes, axis=0, tiled=True) for shard in shards]
            return wholes + exchanged(rides)
        return gather_now(shards, planes, whole_slice, collective_id, rides, **options)

    def scatter(partial, whole_slice, collective_id, rides=()):
        if large:
            axes = everyone if whole_slice else "blk"
            part = lax.psum_scatter(partial, axes, scatter_dimension=0, tiled=True)
            return [part] + exchanged(rides)
        return scatter_now(partial, planes, whole_slice, collective_id, rides)

    def gather_plane(shard):
        return lax.all_gather(shard, "blk", axis=0, tiled=True)

    stream = tokens_in.astype(f32)
    padded_gains = jnp.pad(gains.astype(bf16), ((0, 14), (0, 128 - share_rows)))
    full_qkv, full_gains, full_out, ffn_weights = gather(
        [w_qkv.astype(bf16), padded_gains, w_out.T.astype(bf16)],
        True,
        1,
        [ride(ffn_packets(w_gateup, w_down.T))],
        late_rows=(0, 0, share_rows),
    )
    ffn_weights = ffn_weights.reshape(width, 3 * HEAD)
    full_gains = full_gains.reshape(device_count, 16, 128)[:, :2, :share_rows].astype(f32)
    gain_attn = full_gains[:, 0].reshape(width)
    gain_mlp = full_gains[:, 1].reshape(width)
    normed_attn_f, norm_back_attn = jax.vjp(rms_scale, stream, gain_attn)
    normed_attn = normed_attn_f.astype(bf16)
    qkv = jnp.dot(normed_attn, full_qkv, preferred_element_type=f32).astype(bf16)
    (kv_all,) = gather([qkv[:, H * HEAD :]], True, 2)
    kv_window = lax.dynamic_slice_in_dim(
        jnp.pad(kv_all, ((WINDOW, 0), (0, 0))), me * local_rows, span, 0
    )
    first_token = (me * local_rows).astype(jnp.int32).reshape(1)
    mixed, log_total = attend(first_token, qkv, kv_window)
    resid = stream + jnp.einsum("tc,dc->td", mixed, full_out, preferred_element_type=f32)

    normed_mlp_f, norm_back_mlp = jax.vjp(rms_scale, resid, gain_mlp)
    normed_mlp = normed_mlp_f.astype(bf16)
    normed_mlp_plane, cotangent_plane, other_weights = gather(
        [normed_mlp, cotangent], False, 3, [ride(ffn_weights, "pair")], late_rows=(0, local_rows // 4)
    )
    pair_weights = [ffn_weights, other_weights]
    gates, ups, downs = (
        [weights[:, part * HEAD : (part + 1) * HEAD] for weights in pair_weights]
        for part in range(3)
    )
    owns_block = me < FF // HEAD
    pair_gateup = jnp.where(owns_block, jnp.concatenate(gates + ups, axis=1), 0)
    pair_down = jnp.where(owns_block, jnp.concatenate(downs, axis=1), 0)
    plane_rows = blk_count * local_rows
    both_parts = jnp.dot(normed_mlp_plane, pair_gateup, preferred_element_type=f32)
    pair_width = pair_count * HEAD
    hidden_f, geglu_back = jax.vjp(
        gelu_product, both_parts[:, :pair_width], both_parts[:, pair_width:]
    )
    hidden = hidden_f.astype(bf16)
    grad_hidden = jnp.dot(cotangent_plane, pair_down, preferred_element_type=f32)
    grad_gate, grad_up = geglu_back(grad_hidden)
    grad_gateup = jnp.concatenate([grad_gate.astype(bf16), grad_up.astype(bf16)], axis=1)
    def ffn_gradient(columns):
        gateup_right = jnp.concatenate(
            [grad_gate[:, columns].astype(bf16), grad_up[:, columns].astype(bf16)], axis=1
        )
        down_right = hidden[:, columns]
        return jnp.concatenate(
            [
                jnp.einsum("td,tf->df", normed_mlp_plane, gateup_right, preferred_element_type=f32),
                jnp.einsum("td,tf->df", cotangent_plane, down_right, preferred_element_type=f32),
            ],
            axis=1,
        )

    def pair_columns(columns):
        return columns.reshape(local_rows, -1, pair_width).transpose(1, 0, 2)

    ffn_theirs = ffn_gradient(slice(HEAD, 2 * HEAD)).astype(bf16)
    grad_normed_part = jnp.einsum("tf,df->td", grad_gateup, pair_gateup, preferred_element_type=f32)
    grad_normed_mlp, ffn_others, ffn_moms, attn_moms, out_rights = scatter(
        grad_normed_part.astype(bf16),
        False,
        4,
        [
            ride(ffn_theirs, "pair"),
            ride(ffn_packets(mom_gateup, mom_down.T)),
            ride(attn_packets(mom_qkv, mom_out.T), spread_targets=spread),
            ride(
                pair_columns(mixed), "plane", first_target=(H + 2) // 2, spread_targets=spread
            ),
        ],
    )
    grad_normed_mlp = grad_normed_mlp.astype(f32)

    ffn_grads = ffn_gradient(slice(0, HEAD))
    ffn_low, ffn_turned = orthogonalize(
        ffn_grads, ffn_others, ffn_moms.reshape(width, 3 * HEAD), 2
    )
    ffn_shape = (device_count, share_rows, 3 * HEAD)

    resid_part, gain_grad_mlp = norm_back_mlp(grad_normed_mlp)
    grad_resid = cotangent.astype(f32) + resid_part
    grad_proj = grad_resid.astype(bf16)
    grad_mixed = jnp.dot(grad_proj, full_out, preferred_element_type=f32).astype(bf16)
    grad_query, grad_kv = attend_back(first_token, qkv, grad_mixed, log_total, kv_window)
    grad_kv_all = lax.dynamic_update_slice_in_dim(
        jnp.zeros((WINDOW + token_count, 2 * HEAD), bf16), grad_kv, me * local_rows, 0
    )[WINDOW:]
    grad_kv, ffn_low = scatter(
        grad_kv_all, True, 5, [ride(ffn_low.reshape(ffn_shape), sources=FF // HEAD)]
    )
    grad_qkv = jnp.concatenate([grad_query, grad_kv], axis=1)
    grad_normed_attn = jnp.einsum("tc,dc->td", grad_qkv, full_qkv, preferred_element_type=f32)
    stream_part, gain_grad_attn = norm_back_attn(grad_normed_attn)
    input_grad = grad_resid + stream_part

    branch_part = jnp.einsum(
        "tf,df->td", after(hidden, grad_normed_mlp), pair_down, preferred_element_type=f32
    )
    branch, ffn_turned, qkv_rights = scatter(
        branch_part.astype(bf16),
        False,
        6,
        [
            ride(ffn_turned.reshape(ffn_shape), sources=FF // HEAD),
            ride(pair_columns(grad_qkv), "plane", spread_targets=spread),
        ],
    )
    block_output = (resid + branch.astype(f32)).astype(bf16)
    normed_attn_plane = gather_plane(after(hold(normed_attn, normed_mlp_plane), (ffn_grads, block_output)))
    grad_proj_plane = gather_plane(after(grad_proj, (ffn_grads, block_output)))

    pair_at = spread_place(planes, block_at) if spread else block_at

    def attn_gradient(half, qkv_rights, out_rights):
        def product(lefts, rights):
            rights = rights.reshape(plane_rows, pair_width)
            rights = lax.dynamic_slice_in_dim(rights, half * HEAD, HEAD, 1)
            return jnp.einsum("td,tf->df", lefts, rights, preferred_element_type=f32)

        return lax.cond(
            pair_at < (H + 2) // pair_count,
            lambda: product(normed_attn_plane, qkv_rights),
            lambda: product(grad_proj_plane, out_rights),
        )

    attn_theirs = attn_gradient(1 - half_at, qkv_rights, out_rights).astype(bf16)
    attn_others = swap(attn_theirs)
    attn_grads = attn_gradient(half_at, *hold((qkv_rights, out_rights), attn_theirs))
    updated_ffn = ffn_update(ffn_low, ffn_turned, w_gateup, mom_gateup, w_down.T, mom_down.T)
    (attn_results,) = orthogonalize(
        attn_grads, hold(attn_others, updated_ffn[0]), attn_moms.reshape(width, HEAD), 1
    )
    gain_grads = jnp.stack([gain_grad_attn, gain_grad_mlp], axis=0)
    gain_grads = gain_grads.reshape(2, device_count, share_rows).transpose(1, 0, 2)
    last_rides = [
        ride(
            attn_results.reshape(device_count, share_rows, 2 * HEAD),
            sources=2 * H + 2,
            spread_sources=spread,
        ),
        ride(jnp.pad(gain_grads, ((0, 0), (0, 6), (0, 128 - share_rows)))),
    ]
    if large:
        attn_results, gain_grads = exchanged(last_rides)
    else:
        attn_results, gain_grads = exchange_now(last_rides, planes, 7)
    gain_share = jnp.sum(gain_grads, axis=0)[:2, :share_rows]

    updated_qkv = attn_update(matrix_rate, 0, attn_results, w_qkv, mom_qkv)
    updated_out = attn_update(output_rate, H + 2, attn_results, w_out.T, mom_out.T)
    moment_gains = momentum_decay * mom_gains + gain_share
    new_gains = gains - gain_rate * moment_gains
    return (
        block_output,
        input_grad,
        *updated_qkv,
        *(result.T for result in updated_out),
        *updated_ffn[:3],
        *(result.T for result in updated_ffn[3:]),
        new_gains,
        moment_gains,
        new_gains.astype(bf16),
    )


def solution(mesh):
    placed = (
        P(("blk", "pair"), None),
        P(("blk", "pair"), None),
        P(("blk", "pair"), None),
        P(None, ("blk", "pair")),
        P(None, ("blk", "pair"), None),
        P(None, ("blk", "pair")),
        P(None, ("blk", "pair")),
        P(("blk", "pair"), None),
        P(None, ("blk", "pair")),
        P(None, ("blk", "pair"), None),
        P(None, ("blk", "pair")),
        P(None, ("blk", "pair")),
    )
    return jax.shard_map(
        on_device,
        mesh=mesh,
        in_specs=placed,
        out_specs=(
            P(("blk", "pair"), None),
            P(("blk", "pair"), None),
            P(("blk", "pair"), None),
            P(("blk", "pair"), None),
            P(("blk", "pair"), None),
            P(None, ("blk", "pair")),
            P(None, ("blk", "pair")),
            P(None, ("blk", "pair")),
            P(None, ("blk", "pair"), None),
            P(None, ("blk", "pair"), None),
            P(None, ("blk", "pair"), None),
            P(None, ("blk", "pair")),
            P(None, ("blk", "pair")),
            P(None, ("blk", "pair")),
            P(None, ("blk", "pair")),
            P(None, ("blk", "pair")),
            P(None, ("blk", "pair")),
        ),
        check_vma=False,
    )
```

```python
import functools
from typing import NamedTuple

import jax
import jax.numpy as jnp
from jax import lax
from jax.experimental import pallas as pl
from jax.experimental.pallas import tpu as pltpu
from jax.sharding import PartitionSpec as P

H = 10
HEAD = 256
FF = 7680
WINDOW = 2048
NS_STEPS = 5


eps_norm = 1e-06
eps_pieces = 1e-07
ns_first = 3.4445
ns_second = -4.775
ns_third = 2.0315
momentum_decay = 0.95
matrix_rate = 0.5
output_rate = 10.0
gain_rate = 0.001
weight_shrink = 0.001
masked_score = -1e30
MESH = pl.DeviceIdType.MESH


def position():
    blk, y = lax.axis_index("blk"), lax.axis_index("pair")
    return blk, lax.div(blk, 4), lax.rem(lax.div(blk, 2), 2), lax.rem(blk, 2), y


def greet(devices):
    barrier = pltpu.get_barrier_semaphore()
    for device in devices:
        pl.semaphore_signal(barrier, inc=1, device_id=device, device_id_type=MESH)
    pl.semaphore_wait(barrier, len(devices))


def remote(source, target, send_sem, recv_sem, device):
    return pltpu.make_async_remote_copy(
        src_ref=source,
        dst_ref=target,
        send_sem=send_sem,
        recv_sem=recv_sem,
        device_id=device,
        device_id_type=MESH,
    )


class Exchange(NamedTuple):
    packets: jax.Array
    among: str
    sources: int
    first_target: int = 0
    spread_sources: bool = False
    spread_targets: bool = False


def spread_place(planes, blk):
    z, x, core = lax.div(blk, 4), lax.rem(lax.div(blk, 2), 2), lax.rem(blk, 2)
    return (2 * core + lax.rem(x + z, 2)) * planes + z


def all_devices():
    blk, _, _, _, y = position()
    count = 2 * lax.axis_size("blk")
    here = 2 * blk + y
    places = [lax.rem(here + at, count) for at in range(1, count)]
    return [(lax.div(place, 2), lax.rem(place, 2)) for place in places]


def plane_devices():
    blk, _, _, _, y = position()
    count = lax.axis_size("blk")
    return [(lax.rem(blk + at, count), y) for at in range(1, count)]


def greeted(specs, nearby):
    if any(among == "all" for among, *_ in specs):
        return all_devices()
    blk, _, _, _, y = position()
    pair = [(blk, 1 - y)] * any(among == "pair" for among, *_ in specs)
    if any(among == "plane" for among, *_ in specs):
        return plane_devices() + pair
    return nearby + pair


PAIR_PARTS = 4


def exchange_count(planes, among):
    return {"all": 8 * planes, "plane": 4 * planes, "pair": PAIR_PARTS}[among]


class Ride:
    def __init__(self, planes, spec, packets, received, sems):
        self.planes, self.packets, self.received = planes, packets, received
        self.among, self.sources, self.first_target, self.from_spread, self.to_spread = spec
        self.own_sem, self.send_sems, self.recv_sems = sems
        self.count = exchange_count(planes, self.among)
        self.issued = 0
        blk, self.z, _, _, self.y = position()
        self.blk = blk
        self.here = blk if self.among == "plane" else 2 * blk + self.y

    def place(self, q):
        near = self.count // self.planes
        spot = lax.rem(self.z + 1 + lax.rem(q, self.planes), self.planes)
        return spot * near + lax.rem(self.here + lax.div(q, self.planes), near)

    def counted(self, place, spread):
        if not spread:
            return place
        if self.among == "plane":
            return spread_place(self.planes, place)
        return 2 * spread_place(self.planes, lax.div(place, 2)) + lax.rem(place, 2)

    def source(self, place):
        return self.counted(place, self.from_spread)

    def target(self, place):
        return self.counted(place, self.to_spread) - self.first_target

    def sending(self, place):
        return self.source(place) < self.sources

    def receiving(self, place):
        target = self.target(place)
        return (target >= 0) & (target < self.packets.shape[0])

    def copy(self, q):
        if self.among == "pair":
            rows = self.packets.shape[0] // PAIR_PARTS
            some = pl.ds(pl.multiple_of(q * rows, rows), rows)
            return remote(
                self.packets.at[some],
                self.received.at[some],
                self.send_sems.at[q],
                self.recv_sems.at[q],
                (self.blk, 1 - self.y),
            )
        place = self.place(q)
        device = (place, self.y)
        if self.among == "all":
            device = (lax.div(place, 2), lax.rem(place, 2))
        source = self.source(self.here)
        return remote(
            self.packets.at[self.target(place)],
            self.received.at[source],
            self.send_sems.at[q],
            self.recv_sems.at[source],
            device,
        )

    def own(self):
        return pltpu.make_async_copy(
            self.packets.at[self.target(self.here)],
            self.received.at[self.source(self.here)],
            self.own_sem.at[0],
        )

    def sends(self, q):
        away = (q < self.count) & (q != self.planes - 1)
        return away & self.sending(self.here) & self.receiving(self.place(q))

    def keeps(self):
        return self.sending(self.here) & self.receiving(self.here)

    def start_own(self):
        if self.among == "pair":
            for q in range(self.count):
                self.copy(q).start()
        else:

            @pl.when(self.keeps())
            def _():
                self.own().start()

    def issue(self, q):
        if self.among != "pair":

            @pl.when(self.sends(q))
            def _():
                self.copy(q).start()

    def issue_more(self, number):
        first, self.issued = self.issued, min(self.issued + number, self.count)

        @pl.loop(first, self.issued)
        def _(q):
            self.issue(q)

    def finish(self):
        if self.among == "pair":
            for q in range(self.count):
                self.copy(q).wait()
            return

        @pl.loop(0, self.count)
        def _(q):
            @pl.when(self.sends(q))
            def _():
                self.copy(q).wait_send()

            @pl.when((q != self.here) & self.sending(q) & self.receiving(self.here))
            def _():
                source = self.source(q)
                spot = self.received.at[source]
                remote(
                    spot, spot, self.own_sem.at[0], self.recv_sems.at[source], (self.blk, self.y)
                ).wait_recv()

        @pl.when(self.keeps())
        def _():
            self.own().wait()


def rides_of(planes, rides):
    rides = [Ride(planes, *ride) for ride in rides]
    for ride in rides:
        ride.start_own()
    return rides


def exchange_sems(exchanges, planes):
    dma = pltpu.SemaphoreType.DMA
    return [
        dma((count,))
        for exchange in exchanges
        for count in (1,) + (exchange_count(planes, exchange.among),) * 2
    ]


def exchange_specs(exchanges):
    return tuple((each.among, *each[2:]) for each in exchanges)


def communicate(
    kernel,
    operands,
    exchanges,
    outputs,
    scratch,
    planes,
    collective_id,
    cost,
    name,
    out_spec=pl.ANY,
    **options,
):
    packets = [each.packets for each in exchanges]
    received = [
        jax.ShapeDtypeStruct(
            array.shape
            if each.among == "pair"
            else (exchange_count(planes, each.among), *array.shape[1:]),
            array.dtype,
        )
        for each, array in zip(exchanges, packets)
    ]
    any_spec = pl.BlockSpec(memory_space=pl.ANY)
    return pl.pallas_call(
        kernel,
        out_shape=outputs + received,
        in_specs=[any_spec] * (len(operands) + len(packets)),
        out_specs=[pl.BlockSpec(memory_space=out_spec)] * len(outputs) + [any_spec] * len(packets),
        scratch_shapes=scratch + exchange_sems(exchanges, planes),
        compiler_params=pltpu.CompilerParams(
            collective_id=collective_id, has_side_effects=True, **options
        ),
        cost_estimate=pl.CostEstimate(flops=0, bytes_accessed=cost * 2**20, transcendentals=0),
        name=name,
    )(*operands, *packets)


def split_refs(refs, inputs, outputs, specs):
    riders = len(specs)
    ins, refs = refs[: inputs + riders], refs[inputs + riders :]
    outs, refs = refs[: outputs + riders], refs[outputs + riders :]
    scratch = refs[: len(refs) - 3 * riders]
    sems = refs[len(refs) - 3 * riders :]
    rides = [
        (spec, ins[inputs + i], outs[outputs + i], sems[3 * i : 3 * i + 3])
        for i, spec in enumerate(specs)
    ]
    return ins[:inputs], outs[:outputs], scratch, rides


def exchange_kernel(planes, specs, *refs):
    _, _, _, rides = split_refs(refs, 0, 0, specs)
    greet(greeted(specs, []))
    rides = rides_of(planes, rides)
    for ride in rides:
        ride.issue_more(ride.count)
    for ride in rides:
        ride.finish()


def exchange_now(exchanges, planes, collective_id):
    specs = exchange_specs(exchanges)
    kernel = functools.partial(exchange_kernel, planes, specs)
    return communicate(kernel, [], exchanges, [], [], planes, collective_id, 100, "exchange_now")


def gather_kernel(planes, parts, whole_slice, specs, *refs):
    arrays = 1 + max(array for array, *_ in parts)
    shard_refs, whole_refs, scratch, rides = split_refs(refs, arrays, arrays, specs)
    count = len(parts)
    shards = [shard_refs[array].at[pl.ds(start, size)] for array, start, size, _ in parts]
    late = [is_late for *_, is_late in parts]
    own_sem, line_send, second_send, first_send, core_send, recv, core_recv = scratch
    blk, z, x, core, y = position()
    firsts = 2 if whole_slice else 1
    to_core = (blk + 1 - 2 * core, y)
    if whole_slice:
        first = y * (1 - core) + x * core
        second = x * (1 - core) + y * core
        first_device = (blk + core * (2 - 4 * x), y + (1 - core) * (1 - 2 * y))
        second_device = (blk + (1 - core) * (2 - 4 * x), y + core * (1 - 2 * y))
    else:
        first, second = 0, x
        first_device, second_device = None, (blk + 2 - 4 * x, y)
    line = [(blk + 4 * (lax.rem(z + at, planes) - z), y) for at in range(1, planes)]
    nearby = [to_core, second_device] + [first_device] * whole_slice + line
    greet(greeted(specs, nearby))

    def slot(i, spot, by_first, by_second, plane):
        array, start, size, _ = parts[i]
        whole, some = whole_refs[array], pl.ds(start, size)
        if whole_slice:
            by_x = (1 - plane) * by_second + plane * by_first
            by_y = (1 - plane) * by_first + plane * by_second
            return whole.at[spot, by_x, plane, by_y, some]
        return whole.at[spot, by_second, plane, some]

    def arrive(i, spot, by_first, by_second):
        here = slot(i, spot, by_first, by_second, core)
        remote(here, here, own_sem.at[0], recv.at[i, spot, by_first, by_second], to_core).wait_recv()

    def along(i, source, spot, turn, way):
        by_second = second if turn == 0 else 1 - second
        target = slot(i, spot, first, by_second, core)
        sems = line_send.at[way, i, spot, turn], recv.at[i, spot, first, by_second]
        return remote(source, target, *sems, (blk + 4 - 8 * way, y))

    def onward(i, source, spot, own):
        target = slot(i, spot, first, second, core)
        arrived = recv.at[i, spot, first, second]
        if own or not late[i]:
            yield remote(source, target, second_send.at[i, spot], arrived, second_device)
        if whole_slice:
            yield remote(source, target, first_send.at[i, spot, 0], arrived, first_device)
        yield remote(
            source, target, core_send.at[i, spot, 0, 0], core_recv.at[i, spot, first, second], to_core
        )

    def after_second(i, spot):
        here = slot(i, spot, first, 1 - second, core)
        if whole_slice:
            yield remote(
                here, here, first_send.at[i, spot, 1], recv.at[i, spot, first, 1 - second], first_device
            )
        yield remote(
            here, here, core_send.at[i, spot, 0, 1], core_recv.at[i, spot, first, 1 - second], to_core
        )

    def after_first(i, spot, turn):
        by_second = second if turn == 0 else 1 - second
        here = slot(i, spot, 1 - first, by_second, core)
        return remote(
            here, here, core_send.at[i, spot, 1, turn], core_recv.at[i, spot, 1 - first, by_second], to_core
        )

    def line_steps():
        for far in range(1, planes):
            yield z - far, z >= far, 0, z < planes - 1
            yield z + far, z < planes - far, 1, z > 0

    ends = [(0, z < planes - 1), (1, z > 0)]
    own_copies = []
    for i in range(count):
        copy = pltpu.make_async_copy(
            shards[i], slot(i, z, first, second, core), own_sem.at[1 + i]
        )
        copy.start()
        own_copies.append(copy)

        for way, further in ends:

            @pl.when(further)
            def _():
                along(i, shards[i], z, 0, way).start()

        for copy in onward(i, shards[i], z, True):
            copy.start()
    rides = rides_of(planes, rides)

    def issue(number):
        for ride in rides:
            ride.issue_more(number)

    issue(6)
    for i in range(count):
        arrive(i, z, first, 1 - second)
        for way, further in ends * late[i]:

            @pl.when(further)
            def _():
                along(i, slot(i, z, first, 1 - second, core), z, 1, way).start()

        for copy in after_second(i, z):
            copy.start()
    issue(4)
    for spot, there, way, further in line_steps():

        @pl.when(there)
        def _():
            for i in range(count):
                here = slot(i, spot, first, second, core)
                arrive(i, spot, first, second)

                @pl.when(further)
                def _():
                    along(i, here, spot, 0, way).start()

                for copy in onward(i, here, spot, False):
                    copy.start()
            for i in range(count):
                arrive(i, spot, first, 1 - second)
                if late[i]:

                    @pl.when(further)
                    def _():
                        along(i, slot(i, spot, first, 1 - second, core), spot, 1, way).start()

                for copy in after_second(i, spot):
                    copy.start()

        issue(4)

    issue(8 * planes)
    spots = [lax.rem(z + at, planes) for at in range(planes)]
    if whole_slice:
        for spot in spots:
            for turn in range(2):
                for i in range(count):
                    arrive(i, spot, 1 - first, second if turn == 0 else 1 - second)
                    after_first(i, spot, turn).start()
    for copy in own_copies:
        copy.wait()
    for i in range(count):
        for spot in range(planes):
            for by_first in range(firsts):
                for by_second in range(2):
                    there = slot(i, spot, by_first, by_second, 1 - core)
                    arrived = core_recv.at[i, spot, by_first, by_second]
                    remote(there, there, own_sem.at[0], arrived, to_core).wait_recv()
    for ride in rides:
        ride.finish()
    for i in range(count):
        for turn in range(1 + late[i]):
            for way, further in ends:

                @pl.when(further)
                def _():
                    along(i, shards[i], z, turn, way).wait_send()

            for spot, there, way, further in line_steps():

                @pl.when(there & further)
                def _():
                    along(i, shards[i], spot, turn, way).wait_send()

        for at, spot in enumerate(spots):
            for copy in onward(i, shards[i], spot, at == 0):
                copy.wait_send()
            for copy in after_second(i, spot):
                copy.wait_send()
            for turn in range(2 * (firsts - 1)):
                after_first(i, spot, turn).wait_send()


def gather_now(shards, planes, whole_slice, collective_id, exchanges=(), late_rows=None):
    parts = []
    for array, shard in enumerate(shards):
        rows = shard.shape[0]
        early = rows - (late_rows[array] if late_rows else 0)
        parts += [(array, 0, early, False)] * (early > 0)
        parts += [(array, early, rows - early, True)] * (early < rows)
    count = len(parts)
    firsts = 2 if whole_slice else 1
    specs = exchange_specs(exchanges)
    dma = pltpu.SemaphoreType.DMA
    grid = (planes, 2, 2, 2) if whole_slice else (planes, 2, 2)
    results = communicate(
        functools.partial(gather_kernel, planes, parts, whole_slice, specs),
        list(shards),
        exchanges,
        [jax.ShapeDtypeStruct((*grid, *shard.shape), shard.dtype) for shard in shards],
        [
            dma((count + 1,)),
            dma((2, count, planes, 2)),
            dma((count, planes)),
            dma((count, planes, 2)),
            dma((count, planes, 2, 2)),
            dma((count, planes, firsts, 2)),
            dma((count, planes, firsts, 2)),
        ],
        planes,
        collective_id,
        200,
        "gather_now",
    )
    places = 4 * planes * firsts
    wholes = [
        whole.reshape(places * shard.shape[0], shard.shape[1])
        for whole, shard in zip(results, shards)
    ]
    return wholes + list(results[len(shards) :])


def scatter_kernel(planes, steps, rows, whole_slice, product, specs, *refs):
    operands, (sum_ref,), scratch, rides = split_refs(refs, 1 + product, 1, specs)
    own, from_core, from_first, from_second, from_below, from_above = scratch[:6]
    load_sem, core_sems, first_sems, second_sems, up_sems, down_sems = scratch[6:12]
    if product:
        lefts, rights, made, factor_sems = scratch[12:]
    else:
        (partial_ref,) = operands
    blk, z, x, core, y = position()
    firsts = 2 if whole_slice else 1
    to_core = (blk + 1 - 2 * core, y)
    if whole_slice:
        first = y * (1 - core) + x * core
        second = x * (1 - core) + y * core
        core_second = second
        first_device = (blk + core * (2 - 4 * x), y + (1 - core) * (1 - 2 * y))
        second_device = (blk + (1 - core) * (2 - 4 * x), y + core * (1 - 2 * y))
    else:
        first, second = 0, x
        first_device, second_device = None, (blk + 2 - 4 * x, y)
    line = [(blk + 4 * (lax.rem(z + at, planes) - z), y) for at in range(1, planes)]
    nearby = [to_core, second_device] + [first_device] * whole_slice + line
    greet(greeted(specs, nearby))

    def make(step):
        some = pl.ds(pl.multiple_of(step * rows, rows), rows)
        left = lefts[:, :, :, some, :].reshape(4 * planes * rows, lefts.shape[-1])
        wide = 2 * HEAD

        @pl.loop(0, rights.shape[0] // wide)
        def _(at):
            columns = pl.ds(pl.multiple_of(at * wide, wide), wide)
            part = lax.dot_general(
                left,
                rights[columns, :],
                (((1,), (1,)), ((), ())),
                preferred_element_type=jnp.float32,
            )
            part = part.astype(made.dtype).reshape(planes, 2, 2, rows, wide)
            made[step, :, :, :, :, columns] = part

    def piece(step, by_first, by_second, plane):
        if product:
            return made.at[step, :, by_second, plane]
        some = pl.ds(pl.multiple_of(step * rows, rows), rows)
        if whole_slice:
            by_x = (1 - plane) * by_second + plane * by_first
            by_y = (1 - plane) * by_first + plane * by_second
            return partial_ref.at[:, by_x, plane, by_y, some]
        return partial_ref.at[:, by_second, plane, some]

    def core_copy(step, by_first, by_second, plane):
        return remote(
            piece(step, by_first, by_second, plane),
            from_core.at[step, by_first, by_second],
            core_sems.at[0, step, by_first, by_second],
            core_sems.at[1, step, by_first, by_second],
            to_core,
        )

    def load(step, by_first, by_second):
        return pltpu.make_async_copy(
            piece(step, by_first, by_second, core),
            own.at[step, by_first, by_second],
            load_sem.at[step, by_first, by_second],
        )

    def first_copy(step):
        return remote(
            own.at[step, 1 - first],
            from_first.at[step],
            first_sems.at[0, step],
            first_sems.at[1, step],
            first_device,
        )

    def second_copy(step):
        return remote(
            own.at[step, first, 1 - second],
            from_second.at[step],
            second_sems.at[0, step],
            second_sems.at[1, step],
            second_device,
        )

    def up_copy(step, target):
        return remote(
            own.at[step, first, second, target],
            from_below.at[step, target],
            up_sems.at[0, step, target],
            up_sems.at[1, step, target],
            (blk + 4, y),
        )

    def down_copy(step, target):
        return remote(
            own.at[step, first, second, target],
            from_above.at[step, target],
            down_sems.at[0, step, target],
            down_sems.at[1, step, target],
            (blk - 4, y),
        )

    def halves():
        if not whole_slice:
            return [(0, 1 - second), (0, second)]
        return [(1 - first, 0), (1 - first, 1), (first, 0), (first, 1)]

    def core_halves():
        if not whole_slice:
            return [(0, 1 - second), (0, second)]
        return [(1 - core_second, 0), (1 - core_second, 1), (core_second, 0), (core_second, 1)]

    def start_loads(step):
        if product:
            make(step)
        for mine, theirs in zip(halves(), core_halves()):
            core_copy(step, *theirs, 1 - core).start()
            if not product:
                load(step, *mine).start()

    def add_core(step):
        for turn, mine in enumerate(halves()):
            if not product:
                load(step, *mine).wait()
            core_copy(step, *mine, core).wait_recv()
            if product:
                own[step, *mine] = made[step, :, mine[1], core] + from_core[step, *mine]
            else:
                own[step, *mine] += from_core[step, *mine]
            if whole_slice and turn == 1:
                first_copy(step).start()
            if not whole_slice and turn == 0:
                second_copy(step).start()

    def add_first(step):
        first_copy(step).wait_recv()
        own[step, first, 1 - second] += from_first[step, 1 - second]
        second_copy(step).start()
        own[step, first, second] += from_first[step, second]

    def add_second(step):
        second_copy(step).wait_recv()
        own[step, first, second] += from_second[step]

    def pass_up(step):
        for target in range(planes):

            @pl.when((z > 0) & (z <= target))
            def _():
                up_copy(step, target).wait_recv()

            @pl.when((z > 0) & (z < target))
            def _():
                own[step, first, second, target] += from_below[step, target]

            @pl.when(z < target)
            def _():
                up_copy(step, target).start()

    def pass_down(step):
        for target in range(planes):

            @pl.when((z < planes - 1) & (z >= target))
            def _():
                down_copy(step, target).wait_recv()

            @pl.when((z < planes - 1) & (z > target))
            def _():
                own[step, first, second, target] += from_above[step, target]

            @pl.when(z > target)
            def _():
                down_copy(step, target).start()

    def add_line(step):
        some = pl.ds(pl.multiple_of(step * rows, rows), rows)
        sum_ref[some, :] = own[step, first, second, z]

        @pl.when(z > 0)
        def _():
            sum_ref[some, :] += from_below[step, z]

        @pl.when(z < planes - 1)
        def _():
            sum_ref[some, :] += from_above[step, z]

    rides = rides_of(planes, rides)
    if product:
        factors = [
            pltpu.make_async_copy(operand, ref, factor_sems.at[i])
            for i, (operand, ref) in enumerate(zip(operands, (lefts, rights)))
        ]
        for factor in factors:
            factor.start()
        for factor in factors:
            factor.wait()

    @pl.loop(0, 2)
    def _(step):
        start_loads(step)

    early = firsts + 1
    hurry = [-(-ride.count // steps) for ride in rides]

    @pl.loop(0, steps + early + planes)
    def _(turn):
        def stage(step, work):
            @pl.when((step >= 0) & (step < steps))
            def _():
                work(step)

        @pl.when(turn < steps - 2)
        def _():
            start_loads(turn + 2)

        stage(turn, add_core)
        for ride, number in zip(rides, hurry):
            for at in range(number):
                ride.issue(turn * number + at)
        if whole_slice:
            stage(turn - 1, add_first)
        stage(turn - early + 1, add_second)
        stage(turn - early - z, pass_up)
        stage(turn - early - (planes - 1 - z), pass_down)
        stage(turn - early - planes + 1, add_line)

    @pl.loop(0, steps)
    def _(step):
        for theirs in core_halves():
            core_copy(step, *theirs, 1 - core).wait_send()
        if whole_slice:
            first_copy(step).wait_send()
        second_copy(step).wait_send()
        for target in range(planes):

            @pl.when(z < target)
            def _():
                up_copy(step, target).wait_send()

            @pl.when(z > target)
            def _():
                down_copy(step, target).wait_send()

    for ride in rides:
        ride.finish()


def scatter_now(factors, planes, whole_slice, collective_id, exchanges=()):
    firsts = 2 if whole_slice else 1
    product = len(factors) == 2
    shard_rows = factors[0].shape[0] // (4 * planes * firsts)
    width = factors[1].shape[0] if product else factors[0].shape[1]
    rows = 16
    steps = shard_rows // rows
    dtype = factors[0].dtype
    specs = exchange_specs(exchanges)
    dma = pltpu.SemaphoreType.DMA
    grid = (planes, 2, 2, 2) if whole_slice else (planes, 2, 2)
    return communicate(
        functools.partial(scatter_kernel, planes, steps, rows, whole_slice, product, specs),
        [factors[0].reshape(*grid, shard_rows, factors[0].shape[1]), *factors[1:]],
        exchanges,
        [jax.ShapeDtypeStruct((shard_rows, width), dtype)],
        [
            pltpu.VMEM((steps, firsts, 2, planes, rows, width), dtype),
            pltpu.VMEM((steps, firsts, 2, planes, rows, width), dtype),
            pltpu.VMEM((steps if whole_slice else 1, 2, planes, rows, width), dtype),
            pltpu.VMEM((steps, planes, rows, width), dtype),
            pltpu.VMEM((steps, planes, rows, width), dtype),
            pltpu.VMEM((steps, planes, rows, width), dtype),
            dma((steps, firsts, 2)),
            dma((2, steps, firsts, 2)),
            dma((2, steps)),
            dma((2, steps)),
            dma((2, steps, planes)),
            dma((2, steps, planes)),
        ]
        + [
            pltpu.VMEM((*grid, shard_rows, factors[0].shape[1]), dtype),
            pltpu.VMEM(factors[-1].shape, dtype),
            pltpu.VMEM((steps, *grid, rows, width), dtype),
            dma((2,)),
        ]
        * product,
        planes,
        collective_id,
        200,
        "scatter_now",
        out_spec=pltpu.VMEM,
        vmem_limit_bytes=56 * 2**20,
    )


def ffn_pack_kernel(gateup_ref, down_ref, packet_ref):
    for at in range(packet_ref.shape[0]):
        columns = slice(at * HEAD, (at + 1) * HEAD)
        packet_ref[at, :, :HEAD] = gateup_ref[0, :, columns].astype(jnp.bfloat16)
        packet_ref[at, :, HEAD : 2 * HEAD] = gateup_ref[1, :, columns].astype(jnp.bfloat16)
        packet_ref[at, :, 2 * HEAD :] = down_ref[:, columns].astype(jnp.bfloat16)


def ffn_packets(gateup, down):
    row_count = gateup.shape[1]
    blocks, wide = FF // HEAD, 5
    return pl.pallas_call(
        ffn_pack_kernel,
        grid=(blocks // wide,),
        in_specs=[
            pl.BlockSpec((2, row_count, wide * HEAD), lambda j: (0, 0, j)),
            pl.BlockSpec((row_count, wide * HEAD), lambda j: (0, j)),
        ],
        out_specs=pl.BlockSpec((wide, row_count, 3 * HEAD), lambda j: (j, 0, 0)),
        out_shape=jax.ShapeDtypeStruct((blocks, row_count, 3 * HEAD), jnp.bfloat16),
        cost_estimate=pl.CostEstimate(flops=0, bytes_accessed=12 * 2**20, transcendentals=0),
        compiler_params=pltpu.CompilerParams(vmem_limit_bytes=32 * 2**20),
        name="ffn_packets",
    )(gateup, down)


def attn_pack_kernel(qkv_ref, out_ref, packet_ref):
    j = pl.program_id(0)

    @pl.when(j < (H + 2) // 2)
    def _():
        for at in range(2):
            packet_ref[at] = qkv_ref[:, at * HEAD : (at + 1) * HEAD].astype(jnp.bfloat16)

    @pl.when(j >= (H + 2) // 2)
    def _():
        for at in range(2):
            packet_ref[at] = out_ref[:, at * HEAD : (at + 1) * HEAD].astype(jnp.bfloat16)


def attn_packets(qkv, out):
    row_count = qkv.shape[0]
    qkv_last, out_last = (H + 2) // 2 - 1, H // 2 - 1
    return pl.pallas_call(
        attn_pack_kernel,
        grid=(H + 1,),
        in_specs=[
            pl.BlockSpec((row_count, 2 * HEAD), lambda j: (0, jnp.minimum(j, qkv_last))),
            pl.BlockSpec((row_count, 2 * HEAD), lambda j: (0, jnp.clip(j - qkv_last - 1, 0, out_last))),
        ],
        out_specs=pl.BlockSpec((2, row_count, HEAD), lambda j: (j, 0, 0)),
        out_shape=jax.ShapeDtypeStruct((2 * H + 2, row_count, HEAD), jnp.bfloat16),
        cost_estimate=pl.CostEstimate(flops=0, bytes_accessed=4 * 2**20, transcendentals=0),
        name="attn_packets",
    )(qkv, out)


def turn_kernel(grads_ref, others_ref, mom_ref, *refs):
    *results, current_ref = refs
    if len(results) == 1:
        low_ref, turned_ref = results[0].at[:, :HEAD], results[0].at[:, HEAD:]
    else:
        low_ref, turned_ref = results
    grads = grads_ref[...] + others_ref[...].astype(jnp.float32)
    low_ref[...] = grads.astype(jnp.bfloat16)
    moment = momentum_decay * mom_ref[...].astype(jnp.float32) + grads
    moment = moment.astype(jnp.bfloat16).astype(jnp.float32)
    norm_size = jnp.sqrt(jnp.sum(moment * moment, keepdims=True))
    current_ref[...] = (moment / (norm_size + eps_pieces)).T.astype(jnp.bfloat16)

    @pl.loop(0, NS_STEPS)
    def _(sweep_index):
        current = current_ref[...]
        gram_matrix = lax.dot_general(
            current, current, (((1,), (1,)), ((), ())), preferred_element_type=jnp.float32
        ).astype(jnp.bfloat16)
        square = jnp.dot(gram_matrix, gram_matrix, preferred_element_type=jnp.float32)
        mixing = (ns_second * gram_matrix.astype(jnp.float32) + ns_third * square).astype(
            jnp.bfloat16
        )
        turned = jnp.dot(mixing, current, preferred_element_type=jnp.float32)
        current_ref[...] = (ns_first * current.astype(jnp.float32) + turned).astype(jnp.bfloat16)

    turned_ref[...] = current_ref[...].astype(jnp.float32).T.astype(jnp.bfloat16)


def orthogonalize(grads, others, moms, results):
    depth, columns = grads.shape
    block = pl.BlockSpec((depth, HEAD), lambda j: (0, j))
    pieces = columns // HEAD
    return pl.pallas_call(
        turn_kernel,
        grid=(pieces,),
        in_specs=[block] * 3,
        out_specs=[pl.BlockSpec((depth, 2 // results * HEAD), lambda j: (0, j))] * results,
        out_shape=[jax.ShapeDtypeStruct((depth, 2 // results * columns), jnp.bfloat16)] * results,
        scratch_shapes=[pltpu.VMEM((HEAD, depth), jnp.bfloat16)],
        cost_estimate=pl.CostEstimate(
            flops=pieces * 20 * depth * HEAD * HEAD, bytes_accessed=12 * depth * columns, transcendentals=0
        ),
        compiler_params=pltpu.CompilerParams(vmem_limit_bytes=48 * 2**20),
        name="orthogonalize",
    )(grads, others, moms)


def update(rate, weight, mom, grad, turn):
    moment = momentum_decay * mom + grad.astype(jnp.float32)
    new = (1.0 - weight_shrink) * weight - rate * turn.astype(jnp.float32)
    return new, moment, new.astype(jnp.bfloat16)


def ffn_update_kernel(
    grad_ref, turn_ref, w_gateup_ref, mom_gateup_ref, w_down_ref, mom_down_ref, *results
):
    for at in range(grad_ref.shape[0]):
        columns = slice(at * HEAD, (at + 1) * HEAD)
        for part in range(3):
            spot = (part, slice(None), columns) if part < 2 else (slice(None), columns)
            weight_ref, mom_ref = (
                (w_gateup_ref, mom_gateup_ref) if part < 2 else (w_down_ref, mom_down_ref)
            )
            packed = slice(part * HEAD, (part + 1) * HEAD)
            values = update(
                matrix_rate,
                weight_ref[spot],
                mom_ref[spot],
                grad_ref[at, :, packed],
                turn_ref[at, :, packed],
            )
            for ref, value in zip(results[:3] if part < 2 else results[3:], values):
                ref[spot] = value


def ffn_update(grads, turns, w_gateup, mom_gateup, w_down, mom_down):
    row_count = w_gateup.shape[1]
    wide = 3
    packet = pl.BlockSpec((wide, row_count, 3 * HEAD), lambda j: (j, 0, 0))
    gateup = pl.BlockSpec((2, row_count, wide * HEAD), lambda j: (0, 0, j))
    down = pl.BlockSpec((row_count, wide * HEAD), lambda j: (0, j))
    dtypes = (jnp.float32, jnp.float32, jnp.bfloat16)
    return pl.pallas_call(
        ffn_update_kernel,
        grid=(FF // HEAD // wide,),
        in_specs=[packet, packet, gateup, gateup, down, down],
        out_specs=[gateup] * 3 + [down] * 3,
        out_shape=[jax.ShapeDtypeStruct(w_gateup.shape, dtype) for dtype in dtypes]
        + [jax.ShapeDtypeStruct(w_down.shape, dtype) for dtype in dtypes],
        cost_estimate=pl.CostEstimate(flops=0, bytes_accessed=50 * 2**20, transcendentals=0),
        compiler_params=pltpu.CompilerParams(vmem_limit_bytes=48 * 2**20),
        name="ffn_update",
    )(grads, turns, w_gateup, mom_gateup, w_down, mom_down)


def attn_update_kernel(rate, packet_ref, w_ref, mom_ref, *results):
    for at in range(2):
        columns = slice(at * HEAD, (at + 1) * HEAD)
        values = update(
            rate,
            w_ref[:, columns],
            mom_ref[:, columns],
            packet_ref[at, :, :HEAD],
            packet_ref[at, :, HEAD:],
        )
        for ref, value in zip(results, values):
            ref[:, columns] = value


def attn_update(rate, offset, packets, weight, mom):
    row_count = packets.shape[1]
    packet = pl.BlockSpec((2, row_count, 2 * HEAD), lambda j: (j + offset // 2, 0, 0))
    block = pl.BlockSpec((row_count, 2 * HEAD), lambda j: (0, j))
    return pl.pallas_call(
        functools.partial(attn_update_kernel, rate),
        grid=(weight.shape[1] // HEAD // 2,),
        in_specs=[packet, block, block],
        out_specs=[block] * 3,
        out_shape=[
            jax.ShapeDtypeStruct(weight.shape, dtype)
            for dtype in (jnp.float32, jnp.float32, jnp.bfloat16)
        ],
        cost_estimate=pl.CostEstimate(flops=0, bytes_accessed=6 * 2**20, transcendentals=0),
        name="attn_update",
    )(packets, weight, mom)


def two_heads(ref):
    return jnp.concatenate([ref[:, :HEAD], ref[:, HEAD:]], axis=0)


def visible(tokens, first_token, shape, query_axis):
    query = lax.rem(lax.broadcasted_iota(jnp.int32, shape, query_axis), tokens)
    key = lax.broadcasted_iota(jnp.int32, shape, 1 - query_axis)
    distance = query + WINDOW - key
    return (distance >= 0) & (distance < WINDOW) & (first_token - WINDOW + key >= 0)


def attend_kernel(first_ref, queries_ref, kv_ref, mixed_ref, log_total_ref):
    tokens = queries_ref.shape[0]
    raw = lax.dot_general(
        two_heads(queries_ref),
        kv_ref[:, :HEAD],
        (((1,), (1,)), ((), ())),
        preferred_element_type=jnp.float32,
    )
    allowed = visible(tokens, first_ref[0], raw.shape, 0)
    scores = jnp.where(allowed, raw * HEAD ** (-0.5), masked_score)
    top_score = jnp.max(scores, axis=-1, keepdims=True)
    expo = jnp.exp(scores - top_score)
    total = jnp.sum(expo, axis=-1, keepdims=True)
    probs = (expo / total).astype(jnp.bfloat16)
    mixed = jnp.dot(probs, kv_ref[:, HEAD:], preferred_element_type=jnp.float32)
    mixed_ref[:, :HEAD] = mixed[:tokens].astype(jnp.bfloat16)
    mixed_ref[:, HEAD:] = mixed[tokens:].astype(jnp.bfloat16)
    log_total_ref[0] = jnp.broadcast_to(top_score + jnp.log(total), log_total_ref.shape[1:])


def attend(first_token, qkv, kv_window):
    tokens = qkv.shape[0]
    span = kv_window.shape[0]
    pairs = H // 2
    return pl.pallas_call(
        attend_kernel,
        grid=(pairs,),
        in_specs=[
            pl.BlockSpec(memory_space=pltpu.SMEM),
            pl.BlockSpec((tokens, 2 * HEAD), lambda j: (0, j)),
            pl.BlockSpec((span, 2 * HEAD), lambda j: (0, 0)),
        ],
        out_specs=[
            pl.BlockSpec((tokens, 2 * HEAD), lambda j: (0, j)),
            pl.BlockSpec((1, 2 * tokens, 128), lambda j: (j, 0, 0)),
        ],
        out_shape=[
            jax.ShapeDtypeStruct((tokens, H * HEAD), jnp.bfloat16),
            jax.ShapeDtypeStruct((pairs, 2 * tokens, 128), jnp.float32),
        ],
        cost_estimate=pl.CostEstimate(
            flops=4 * H * tokens * span * HEAD,
            bytes_accessed=4 * 2**20,
            transcendentals=H * tokens * span,
        ),
        compiler_params=pltpu.CompilerParams(vmem_limit_bytes=48 * 2**20),
        name="attend",
    )(first_token, qkv, kv_window)


def attend_back_kernel(
    first_ref, queries_ref, grads_ref, log_total_ref, kv_ref, grad_query_ref, grad_kv_ref, sums_ref
):
    tokens = queries_ref.shape[0]
    score_scale = HEAD ** (-0.5)
    keys, values = kv_ref[:, :HEAD], kv_ref[:, HEAD:]
    queries, grads = two_heads(queries_ref), two_heads(grads_ref)

    def against(left, right):
        return lax.dot_general(
            left, right, (((1,), (1,)), ((), ())), preferred_element_type=jnp.float32
        )

    raw = against(keys, queries)
    allowed = visible(tokens, first_ref[0], raw.shape, 1)
    scores = jnp.where(allowed, raw * score_scale, masked_score)
    log_total = log_total_ref[0].T[:1]
    probs = jnp.exp(scores - log_total)
    grad_probs = against(values, grads)
    row_delta = jnp.sum(probs * grad_probs, axis=0, keepdims=True)
    grad_raw = (probs * (grad_probs - row_delta) * score_scale).astype(jnp.bfloat16)
    grad_query = lax.dot_general(
        grad_raw, keys, (((0,), (0,)), ((), ())), preferred_element_type=jnp.float32
    )
    grad_query_ref[:, :HEAD] = grad_query[:tokens].astype(jnp.bfloat16)
    grad_query_ref[:, HEAD:] = grad_query[tokens:].astype(jnp.bfloat16)

    @pl.when(pl.program_id(0) == 0)
    def _():
        sums_ref[...] = jnp.zeros_like(sums_ref)

    sums_ref[:, :HEAD] += jnp.dot(grad_raw, queries, preferred_element_type=jnp.float32)
    sums_ref[:, HEAD:] += jnp.dot(
        probs.astype(jnp.bfloat16), grads, preferred_element_type=jnp.float32
    )

    @pl.when(pl.program_id(0) == pl.num_programs(0) - 1)
    def _():
        grad_kv_ref[...] = sums_ref[...].astype(jnp.bfloat16)


def attend_back(first_token, qkv, grads, log_total, kv_window):
    tokens = qkv.shape[0]
    span = kv_window.shape[0]
    heads = pl.BlockSpec((tokens, 2 * HEAD), lambda j: (0, j))
    window = pl.BlockSpec((span, 2 * HEAD), lambda j: (0, 0))
    return pl.pallas_call(
        attend_back_kernel,
        grid=(H // 2,),
        in_specs=[
            pl.BlockSpec(memory_space=pltpu.SMEM),
            heads,
            heads,
            pl.BlockSpec((1, 2 * tokens, 128), lambda j: (j, 0, 0)),
            window,
        ],
        out_specs=[heads, window],
        out_shape=[
            jax.ShapeDtypeStruct((tokens, H * HEAD), jnp.bfloat16),
            jax.ShapeDtypeStruct((span, 2 * HEAD), jnp.bfloat16),
        ],
        scratch_shapes=[pltpu.VMEM((span, 2 * HEAD), jnp.float32)],
        cost_estimate=pl.CostEstimate(
            flops=10 * H * tokens * span * HEAD,
            bytes_accessed=8 * 2**20,
            transcendentals=H * tokens * span,
        ),
        compiler_params=pltpu.CompilerParams(vmem_limit_bytes=48 * 2**20),
        name="attend_back",
    )(first_token, qkv, grads, log_total, kv_window)


def rms_scale(stream, gain_row):
    mean_square = jnp.mean(stream * stream, axis=-1, keepdims=True)
    return stream * lax.rsqrt(mean_square + eps_norm) * gain_row


def gelu_product(gate_part, up_part):
    return jax.nn.gelu(gate_part, approximate=True) * up_part


def on_device(
    tokens_in,
    cotangent,
    w_qkv,
    w_out,
    w_gateup,
    w_down,
    gains,
    mom_qkv,
    mom_out,
    mom_gateup,
    mom_down,
    mom_gains,
):
    everyone = ("blk", "pair")
    bf16 = jnp.bfloat16
    f32 = jnp.float32
    blk_count = lax.axis_size("blk")
    pair_count = lax.axis_size("pair")
    device_count = blk_count * pair_count
    block_at = lax.axis_index("blk")
    half_at = lax.axis_index("pair")
    me = block_at * pair_count + half_at
    local_rows, width = tokens_in.shape
    share_rows = w_qkv.shape[0]
    span = WINDOW + local_rows
    token_count = local_rows * device_count
    large = token_count * width * 2 > 48 * 2**20
    planes = blk_count // 4
    spread = not large

    def after(value, earlier):
        return lax.optimization_barrier((value, earlier))[0] if large else value

    def exchange(packets, axes=everyone):
        return lax.all_to_all(packets, axes, split_axis=0, concat_axis=0, tiled=True)

    def swap(shard):
        return lax.ppermute(shard, "pair", [(0, 1), (1, 0)])

    def hold(value, *earlier):
        return value if large else lax.optimization_barrier((value, earlier))[0]

    def ride(packets, among="all", **options):
        sources = {"all": device_count, "plane": blk_count, "pair": pair_count}[among]
        return Exchange(packets, among, **(dict(sources=sources) | options))

    def exchanged(rides):
        results = []
        for packets, among, _, before, _, _ in rides:
            if among == "pair":
                results.append(swap(packets))
                continue
            axes, places = (everyone, device_count) if among == "all" else ("blk", blk_count)
            after_last = places - before - packets.shape[0]
            packets = jnp.pad(packets, ((before, after_last),) + ((0, 0),) * (packets.ndim - 1))
            results.append(exchange(packets, axes))
        return results

    def gather(shards, whole_slice, collective_id, rides=(), **options):
        if large:
            axes = everyone if whole_slice else "blk"
            wholes = [lax.all_gather(shard, axes, axis=0, tiled=True) for shard in shards]
            return wholes + exchanged(rides)
        return gather_now(shards, planes, whole_slice, collective_id, rides, **options)

    def scatter(factors, whole_slice, collective_id, rides=()):
        if large:
            axes = everyone if whole_slice else "blk"
            if len(factors) == 2:
                partial = jnp.einsum("tf,df->td", *factors, preferred_element_type=f32)
                factors = [partial.astype(bf16)]
            part = lax.psum_scatter(factors[0], axes, scatter_dimension=0, tiled=True)
            return [part] + exchanged(rides)
        return scatter_now(factors, planes, whole_slice, collective_id, rides)

    def gather_plane(shard):
        return lax.all_gather(shard, "blk", axis=0, tiled=True)

    stream = tokens_in.astype(f32)
    padded_gains = jnp.pad(gains.astype(bf16), ((0, 14), (0, 128 - share_rows)))
    full_qkv, full_gains, full_out, ffn_weights = gather(
        [w_qkv.astype(bf16), padded_gains, w_out.T.astype(bf16)],
        True,
        1,
        [ride(ffn_packets(w_gateup, w_down.T))],
        late_rows=(0, 0, share_rows),
    )
    ffn_weights = ffn_weights.reshape(width, 3 * HEAD)
    full_gains = full_gains.reshape(device_count, 16, 128)[:, :2, :share_rows].astype(f32)
    gain_attn = full_gains[:, 0].reshape(width)
    gain_mlp = full_gains[:, 1].reshape(width)
    normed_attn_f, norm_back_attn = jax.vjp(rms_scale, stream, gain_attn)
    normed_attn = normed_attn_f.astype(bf16)
    qkv = jnp.dot(normed_attn, full_qkv, preferred_element_type=f32).astype(bf16)
    (kv_all,) = gather([qkv[:, H * HEAD :]], True, 2)
    kv_window = lax.dynamic_slice_in_dim(
        jnp.pad(kv_all, ((WINDOW, 0), (0, 0))), me * local_rows, span, 0
    )
    first_token = (me * local_rows).astype(jnp.int32).reshape(1)
    mixed, log_total = attend(first_token, qkv, kv_window)
    resid = stream + jnp.einsum("tc,dc->td", mixed, full_out, preferred_element_type=f32)

    normed_mlp_f, norm_back_mlp = jax.vjp(rms_scale, resid, gain_mlp)
    normed_mlp = normed_mlp_f.astype(bf16)
    normed_mlp_plane, cotangent_plane, other_weights = gather(
        [normed_mlp, cotangent], False, 3, [ride(ffn_weights, "pair")], late_rows=(0, local_rows // 4)
    )
    pair_weights = [ffn_weights, other_weights]
    gates, ups, downs = (
        [weights[:, part * HEAD : (part + 1) * HEAD] for weights in pair_weights]
        for part in range(3)
    )
    owns_block = me < FF // HEAD
    pair_gateup = jnp.where(owns_block, jnp.concatenate(gates + ups, axis=1), 0)
    pair_down = jnp.where(owns_block, jnp.concatenate(downs, axis=1), 0)
    plane_rows = blk_count * local_rows
    both_parts = jnp.dot(normed_mlp_plane, pair_gateup, preferred_element_type=f32)
    pair_width = pair_count * HEAD
    hidden_f, geglu_back = jax.vjp(
        gelu_product, both_parts[:, :pair_width], both_parts[:, pair_width:]
    )
    hidden = hidden_f.astype(bf16)
    grad_hidden = jnp.dot(cotangent_plane, pair_down, preferred_element_type=f32)
    grad_gate, grad_up = geglu_back(grad_hidden)
    grad_gateup = jnp.concatenate([grad_gate.astype(bf16), grad_up.astype(bf16)], axis=1)
    def ffn_gradient(columns):
        gateup_right = jnp.concatenate(
            [grad_gate[:, columns].astype(bf16), grad_up[:, columns].astype(bf16)], axis=1
        )
        down_right = hidden[:, columns]
        return jnp.concatenate(
            [
                jnp.einsum("td,tf->df", normed_mlp_plane, gateup_right, preferred_element_type=f32),
                jnp.einsum("td,tf->df", cotangent_plane, down_right, preferred_element_type=f32),
            ],
            axis=1,
        )

    def pair_columns(columns):
        return columns.reshape(local_rows, -1, pair_width).transpose(1, 0, 2)

    ffn_theirs = ffn_gradient(slice(HEAD, 2 * HEAD)).astype(bf16)
    grad_normed_mlp, ffn_others, ffn_moms, attn_moms, out_rights = scatter(
        [grad_gateup, pair_gateup],
        False,
        4,
        [
            ride(ffn_theirs, "pair"),
            ride(ffn_packets(mom_gateup, mom_down.T)),
            ride(attn_packets(mom_qkv, mom_out.T), spread_targets=spread),
            ride(
                pair_columns(mixed), "plane", first_target=(H + 2) // 2, spread_targets=spread
            ),
        ],
    )
    grad_normed_mlp = grad_normed_mlp.astype(f32)

    ffn_grads = ffn_gradient(slice(0, HEAD))
    ffn_low, ffn_turned = orthogonalize(
        ffn_grads, ffn_others, ffn_moms.reshape(width, 3 * HEAD), 2
    )
    ffn_shape = (device_count, share_rows, 3 * HEAD)

    resid_part, gain_grad_mlp = norm_back_mlp(grad_normed_mlp)
    grad_resid = cotangent.astype(f32) + resid_part
    grad_proj = grad_resid.astype(bf16)
    grad_mixed = jnp.dot(grad_proj, full_out, preferred_element_type=f32).astype(bf16)
    grad_query, grad_kv = attend_back(first_token, qkv, grad_mixed, log_total, kv_window)
    grad_kv_all = lax.dynamic_update_slice_in_dim(
        jnp.zeros((WINDOW + token_count, 2 * HEAD), bf16), grad_kv, me * local_rows, 0
    )[WINDOW:]
    grad_kv, ffn_low = scatter(
        [grad_kv_all], True, 5, [ride(ffn_low.reshape(ffn_shape), sources=FF // HEAD)]
    )
    grad_qkv = jnp.concatenate([grad_query, grad_kv], axis=1)
    grad_normed_attn = jnp.einsum("tc,dc->td", grad_qkv, full_qkv, preferred_element_type=f32)
    stream_part, gain_grad_attn = norm_back_attn(grad_normed_attn)
    input_grad = grad_resid + stream_part

    branch, ffn_turned, qkv_rights = scatter(
        [after(hidden, grad_normed_mlp), pair_down],
        False,
        6,
        [
            ride(ffn_turned.reshape(ffn_shape), sources=FF // HEAD),
            ride(pair_columns(grad_qkv), "plane", spread_targets=spread),
        ],
    )
    block_output = (resid + branch.astype(f32)).astype(bf16)
    normed_attn_plane = gather_plane(after(hold(normed_attn, normed_mlp_plane), (ffn_grads, block_output)))
    grad_proj_plane = gather_plane(after(grad_proj, (ffn_grads, block_output)))

    pair_at = spread_place(planes, block_at) if spread else block_at

    def attn_gradient(half, qkv_rights, out_rights):
        def product(lefts, rights):
            rights = rights.reshape(plane_rows, pair_width)
            rights = lax.dynamic_slice_in_dim(rights, half * HEAD, HEAD, 1)
            return jnp.einsum("td,tf->df", lefts, rights, preferred_element_type=f32)

        return lax.cond(
            pair_at < (H + 2) // pair_count,
            lambda: product(normed_attn_plane, qkv_rights),
            lambda: product(grad_proj_plane, out_rights),
        )

    attn_theirs = attn_gradient(1 - half_at, qkv_rights, out_rights).astype(bf16)
    attn_others = swap(attn_theirs)
    attn_grads = attn_gradient(half_at, *hold((qkv_rights, out_rights), attn_theirs))
    updated_ffn = ffn_update(ffn_low, ffn_turned, w_gateup, mom_gateup, w_down.T, mom_down.T)
    (attn_results,) = orthogonalize(
        attn_grads, hold(attn_others, updated_ffn[0]), attn_moms.reshape(width, HEAD), 1
    )
    gain_grads = jnp.stack([gain_grad_attn, gain_grad_mlp], axis=0)
    gain_grads = gain_grads.reshape(2, device_count, share_rows).transpose(1, 0, 2)
    last_rides = [
        ride(
            attn_results.reshape(device_count, share_rows, 2 * HEAD),
            sources=2 * H + 2,
            spread_sources=spread,
        ),
        ride(jnp.pad(gain_grads, ((0, 0), (0, 6), (0, 128 - share_rows)))),
    ]
    if large:
        attn_results, gain_grads = exchanged(last_rides)
    else:
        attn_results, gain_grads = exchange_now(last_rides, planes, 7)
    gain_share = jnp.sum(gain_grads, axis=0)[:2, :share_rows]

    updated_qkv = attn_update(matrix_rate, 0, attn_results, w_qkv, mom_qkv)
    updated_out = attn_update(output_rate, H + 2, attn_results, w_out.T, mom_out.T)
    moment_gains = momentum_decay * mom_gains + gain_share
    new_gains = gains - gain_rate * moment_gains
    return (
        block_output,
        input_grad,
        *updated_qkv,
        *(result.T for result in updated_out),
        *updated_ffn[:3],
        *(result.T for result in updated_ffn[3:]),
        new_gains,
        moment_gains,
        new_gains.astype(bf16),
    )


def solution(mesh):
    placed = (
        P(("blk", "pair"), None),
        P(("blk", "pair"), None),
        P(("blk", "pair"), None),
        P(None, ("blk", "pair")),
        P(None, ("blk", "pair"), None),
        P(None, ("blk", "pair")),
        P(None, ("blk", "pair")),
        P(("blk", "pair"), None),
        P(None, ("blk", "pair")),
        P(None, ("blk", "pair"), None),
        P(None, ("blk", "pair")),
        P(None, ("blk", "pair")),
    )
    return jax.shard_map(
        on_device,
        mesh=mesh,
        in_specs=placed,
        out_specs=(
            P(("blk", "pair"), None),
            P(("blk", "pair"), None),
            P(("blk", "pair"), None),
            P(("blk", "pair"), None),
            P(("blk", "pair"), None),
            P(None, ("blk", "pair")),
            P(None, ("blk", "pair")),
            P(None, ("blk", "pair")),
            P(None, ("blk", "pair"), None),
            P(None, ("blk", "pair"), None),
            P(None, ("blk", "pair"), None),
            P(None, ("blk", "pair")),
            P(None, ("blk", "pair")),
            P(None, ("blk", "pair")),
            P(None, ("blk", "pair")),
            P(None, ("blk", "pair")),
            P(None, ("blk", "pair")),
        ),
        check_vma=False,
    )
```

```python
import functools
from typing import NamedTuple

import jax
import jax.numpy as jnp
from jax import lax
from jax.experimental import pallas as pl
from jax.experimental.pallas import tpu as pltpu
from jax.sharding import PartitionSpec as P

H = 10
HEAD = 256
FF = 7680
WINDOW = 2048
NS_STEPS = 5


eps_norm = 1e-06
eps_pieces = 1e-07
ns_first = 3.4445
ns_second = -4.775
ns_third = 2.0315
momentum_decay = 0.95
matrix_rate = 0.5
output_rate = 10.0
gain_rate = 0.001
weight_shrink = 0.001
masked_score = -1e30
MESH = pl.DeviceIdType.MESH


def position():
    blk, y = lax.axis_index("blk"), lax.axis_index("pair")
    return blk, lax.div(blk, 4), lax.rem(lax.div(blk, 2), 2), lax.rem(blk, 2), y


def greet(devices):
    barrier = pltpu.get_barrier_semaphore()
    for device in devices:
        pl.semaphore_signal(barrier, inc=1, device_id=device, device_id_type=MESH)
    pl.semaphore_wait(barrier, len(devices))


def remote(source, target, send_sem, recv_sem, device):
    return pltpu.make_async_remote_copy(
        src_ref=source,
        dst_ref=target,
        send_sem=send_sem,
        recv_sem=recv_sem,
        device_id=device,
        device_id_type=MESH,
    )


class Exchange(NamedTuple):
    packets: jax.Array
    among: str
    sources: int
    first_target: int = 0
    spread_sources: bool = False
    spread_targets: bool = False


def spread_place(planes, blk):
    z, x, core = lax.div(blk, 4), lax.rem(lax.div(blk, 2), 2), lax.rem(blk, 2)
    return (2 * core + lax.rem(x + z, 2)) * planes + z


def all_devices():
    blk, _, _, _, y = position()
    count = 2 * lax.axis_size("blk")
    here = 2 * blk + y
    places = [lax.rem(here + at, count) for at in range(1, count)]
    return [(lax.div(place, 2), lax.rem(place, 2)) for place in places]


def plane_devices():
    blk, _, _, _, y = position()
    count = lax.axis_size("blk")
    return [(lax.rem(blk + at, count), y) for at in range(1, count)]


def greeted(specs, nearby):
    if any(among == "all" for among, *_ in specs):
        return all_devices()
    blk, _, _, _, y = position()
    pair = [(blk, 1 - y)] * any(among == "pair" for among, *_ in specs)
    if any(among == "plane" for among, *_ in specs):
        return plane_devices() + pair
    return nearby + pair


PAIR_PARTS = 4


def exchange_count(planes, among):
    return {"all": 8 * planes, "plane": 4 * planes, "pair": PAIR_PARTS}[among]


class Ride:
    def __init__(self, planes, spec, packets, received, sems):
        self.planes, self.packets, self.received = planes, packets, received
        self.among, self.sources, self.first_target, self.from_spread, self.to_spread = spec
        self.own_sem, self.send_sems, self.recv_sems = sems
        self.count = exchange_count(planes, self.among)
        self.issued = 0
        blk, self.z, _, _, self.y = position()
        self.blk = blk
        self.here = blk if self.among == "plane" else 2 * blk + self.y

    def place(self, q):
        near = self.count // self.planes
        spot = lax.rem(self.z + 1 + lax.rem(q, self.planes), self.planes)
        return spot * near + lax.rem(self.here + lax.div(q, self.planes), near)

    def counted(self, place, spread):
        if not spread:
            return place
        if self.among == "plane":
            return spread_place(self.planes, place)
        return 2 * spread_place(self.planes, lax.div(place, 2)) + lax.rem(place, 2)

    def source(self, place):
        return self.counted(place, self.from_spread)

    def target(self, place):
        return self.counted(place, self.to_spread) - self.first_target

    def sending(self, place):
        return self.source(place) < self.sources

    def receiving(self, place):
        target = self.target(place)
        return (target >= 0) & (target < self.packets.shape[0])

    def copy(self, q):
        if self.among == "pair":
            rows = self.packets.shape[0] // PAIR_PARTS
            some = pl.ds(pl.multiple_of(q * rows, rows), rows)
            return remote(
                self.packets.at[some],
                self.received.at[some],
                self.send_sems.at[q],
                self.recv_sems.at[q],
                (self.blk, 1 - self.y),
            )
        place = self.place(q)
        device = (place, self.y)
        if self.among == "all":
            device = (lax.div(place, 2), lax.rem(place, 2))
        source = self.source(self.here)
        return remote(
            self.packets.at[self.target(place)],
            self.received.at[source],
            self.send_sems.at[q],
            self.recv_sems.at[source],
            device,
        )

    def own(self):
        return pltpu.make_async_copy(
            self.packets.at[self.target(self.here)],
            self.received.at[self.source(self.here)],
            self.own_sem.at[0],
        )

    def sends(self, q):
        away = (q < self.count) & (q != self.planes - 1)
        return away & self.sending(self.here) & self.receiving(self.place(q))

    def keeps(self):
        return self.sending(self.here) & self.receiving(self.here)

    def start_own(self):
        if self.among == "pair":
            for q in range(self.count):
                self.copy(q).start()
        else:

            @pl.when(self.keeps())
            def _():
                self.own().start()

    def issue(self, q):
        if self.among != "pair":

            @pl.when(self.sends(q))
            def _():
                self.copy(q).start()

    def issue_more(self, number):
        first, self.issued = self.issued, min(self.issued + number, self.count)

        @pl.loop(first, self.issued)
        def _(q):
            self.issue(q)

    def finish(self):
        if self.among == "pair":
            for q in range(self.count):
                self.copy(q).wait()
            return

        @pl.loop(0, self.count)
        def _(q):
            @pl.when(self.sends(q))
            def _():
                self.copy(q).wait_send()

            @pl.when((q != self.here) & self.sending(q) & self.receiving(self.here))
            def _():
                source = self.source(q)
                spot = self.received.at[source]
                remote(
                    spot, spot, self.own_sem.at[0], self.recv_sems.at[source], (self.blk, self.y)
                ).wait_recv()

        @pl.when(self.keeps())
        def _():
            self.own().wait()


def rides_of(planes, rides):
    rides = [Ride(planes, *ride) for ride in rides]
    for ride in rides:
        ride.start_own()
    return rides


def exchange_sems(exchanges, planes):
    dma = pltpu.SemaphoreType.DMA
    return [
        dma((count,))
        for exchange in exchanges
        for count in (1,) + (exchange_count(planes, exchange.among),) * 2
    ]


def exchange_specs(exchanges):
    return tuple((each.among, *each[2:]) for each in exchanges)


def communicate(
    kernel,
    operands,
    exchanges,
    outputs,
    scratch,
    planes,
    collective_id,
    cost,
    name,
    out_spec=pl.ANY,
    **options,
):
    packets = [each.packets for each in exchanges]
    received = [
        jax.ShapeDtypeStruct(
            array.shape
            if each.among == "pair"
            else (exchange_count(planes, each.among), *array.shape[1:]),
            array.dtype,
        )
        for each, array in zip(exchanges, packets)
    ]
    any_spec = pl.BlockSpec(memory_space=pl.ANY)
    return pl.pallas_call(
        kernel,
        out_shape=outputs + received,
        in_specs=[any_spec] * (len(operands) + len(packets)),
        out_specs=[pl.BlockSpec(memory_space=out_spec)] * len(outputs) + [any_spec] * len(packets),
        scratch_shapes=scratch + exchange_sems(exchanges, planes),
        compiler_params=pltpu.CompilerParams(
            collective_id=collective_id, has_side_effects=True, **options
        ),
        cost_estimate=pl.CostEstimate(flops=0, bytes_accessed=cost * 2**20, transcendentals=0),
        name=name,
    )(*operands, *packets)


def split_refs(refs, inputs, outputs, specs):
    riders = len(specs)
    ins, refs = refs[: inputs + riders], refs[inputs + riders :]
    outs, refs = refs[: outputs + riders], refs[outputs + riders :]
    scratch = refs[: len(refs) - 3 * riders]
    sems = refs[len(refs) - 3 * riders :]
    rides = [
        (spec, ins[inputs + i], outs[outputs + i], sems[3 * i : 3 * i + 3])
        for i, spec in enumerate(specs)
    ]
    return ins[:inputs], outs[:outputs], scratch, rides


def exchange_kernel(planes, specs, *refs):
    _, _, _, rides = split_refs(refs, 0, 0, specs)
    greet(greeted(specs, []))
    rides = rides_of(planes, rides)
    for ride in rides:
        ride.issue_more(ride.count)
    for ride in rides:
        ride.finish()


def exchange_now(exchanges, planes, collective_id):
    specs = exchange_specs(exchanges)
    kernel = functools.partial(exchange_kernel, planes, specs)
    return communicate(kernel, [], exchanges, [], [], planes, collective_id, 100, "exchange_now")


def gather_kernel(planes, parts, whole_slice, specs, *refs):
    arrays = 1 + max(array for array, *_ in parts)
    shard_refs, whole_refs, scratch, rides = split_refs(refs, arrays, arrays, specs)
    count = len(parts)
    shards = [shard_refs[array].at[pl.ds(start, size)] for array, start, size, _ in parts]
    late = [is_late for *_, is_late in parts]
    own_sem, line_send, second_send, first_send, core_send, recv, core_recv = scratch
    blk, z, x, core, y = position()
    firsts = 2 if whole_slice else 1
    to_core = (blk + 1 - 2 * core, y)
    if whole_slice:
        first = y * (1 - core) + x * core
        second = x * (1 - core) + y * core
        first_device = (blk + core * (2 - 4 * x), y + (1 - core) * (1 - 2 * y))
        second_device = (blk + (1 - core) * (2 - 4 * x), y + core * (1 - 2 * y))
    else:
        first, second = 0, x
        first_device, second_device = None, (blk + 2 - 4 * x, y)
    line = [(blk + 4 * (lax.rem(z + at, planes) - z), y) for at in range(1, planes)]
    nearby = [to_core, second_device] + [first_device] * whole_slice + line
    greet(greeted(specs, nearby))

    def slot(i, spot, by_first, by_second, plane):
        array, start, size, _ = parts[i]
        whole, some = whole_refs[array], pl.ds(start, size)
        if whole_slice:
            by_x = (1 - plane) * by_second + plane * by_first
            by_y = (1 - plane) * by_first + plane * by_second
            return whole.at[spot, by_x, plane, by_y, some]
        return whole.at[spot, by_second, plane, some]

    def arrive(i, spot, by_first, by_second):
        here = slot(i, spot, by_first, by_second, core)
        remote(here, here, own_sem.at[0], recv.at[i, spot, by_first, by_second], to_core).wait_recv()

    def along(i, source, spot, turn, way):
        by_second = second if turn == 0 else 1 - second
        target = slot(i, spot, first, by_second, core)
        sems = line_send.at[way, i, spot, turn], recv.at[i, spot, first, by_second]
        return remote(source, target, *sems, (blk + 4 - 8 * way, y))

    def onward(i, source, spot, own):
        target = slot(i, spot, first, second, core)
        arrived = recv.at[i, spot, first, second]
        if own or not late[i]:
            yield remote(source, target, second_send.at[i, spot], arrived, second_device)
        if whole_slice:
            yield remote(source, target, first_send.at[i, spot, 0], arrived, first_device)
        yield remote(
            source, target, core_send.at[i, spot, 0, 0], core_recv.at[i, spot, first, second], to_core
        )

    def after_second(i, spot):
        here = slot(i, spot, first, 1 - second, core)
        if whole_slice:
            yield remote(
                here, here, first_send.at[i, spot, 1], recv.at[i, spot, first, 1 - second], first_device
            )
        yield remote(
            here, here, core_send.at[i, spot, 0, 1], core_recv.at[i, spot, first, 1 - second], to_core
        )

    def after_first(i, spot, turn):
        by_second = second if turn == 0 else 1 - second
        here = slot(i, spot, 1 - first, by_second, core)
        return remote(
            here, here, core_send.at[i, spot, 1, turn], core_recv.at[i, spot, 1 - first, by_second], to_core
        )

    def line_steps():
        for far in range(1, planes):
            yield z - far, z >= far, 0, z < planes - 1
            yield z + far, z < planes - far, 1, z > 0

    ends = [(0, z < planes - 1), (1, z > 0)]
    own_copies = []
    for i in range(count):
        copy = pltpu.make_async_copy(
            shards[i], slot(i, z, first, second, core), own_sem.at[1 + i]
        )
        copy.start()
        own_copies.append(copy)

        for way, further in ends:

            @pl.when(further)
            def _():
                along(i, shards[i], z, 0, way).start()

        for copy in onward(i, shards[i], z, True):
            copy.start()
    rides = rides_of(planes, rides)

    def issue(number):
        for ride in rides:
            ride.issue_more(number)

    issue(6)
    for i in range(count):
        arrive(i, z, first, 1 - second)
        for way, further in ends * late[i]:

            @pl.when(further)
            def _():
                along(i, slot(i, z, first, 1 - second, core), z, 1, way).start()

        for copy in after_second(i, z):
            copy.start()
    issue(4)
    for spot, there, way, further in line_steps():

        @pl.when(there)
        def _():
            for i in range(count):
                here = slot(i, spot, first, second, core)
                arrive(i, spot, first, second)

                @pl.when(further)
                def _():
                    along(i, here, spot, 0, way).start()

                for copy in onward(i, here, spot, False):
                    copy.start()
            for i in range(count):
                arrive(i, spot, first, 1 - second)
                if late[i]:

                    @pl.when(further)
                    def _():
                        along(i, slot(i, spot, first, 1 - second, core), spot, 1, way).start()

                for copy in after_second(i, spot):
                    copy.start()

        issue(4)

    issue(8 * planes)
    spots = [lax.rem(z + at, planes) for at in range(planes)]
    if whole_slice:
        for spot in spots:
            for turn in range(2):
                for i in range(count):
                    arrive(i, spot, 1 - first, second if turn == 0 else 1 - second)
                    after_first(i, spot, turn).start()
    for copy in own_copies:
        copy.wait()
    for i in range(count):
        for spot in range(planes):
            for by_first in range(firsts):
                for by_second in range(2):
                    there = slot(i, spot, by_first, by_second, 1 - core)
                    arrived = core_recv.at[i, spot, by_first, by_second]
                    remote(there, there, own_sem.at[0], arrived, to_core).wait_recv()
    for ride in rides:
        ride.finish()
    for i in range(count):
        for turn in range(1 + late[i]):
            for way, further in ends:

                @pl.when(further)
                def _():
                    along(i, shards[i], z, turn, way).wait_send()

            for spot, there, way, further in line_steps():

                @pl.when(there & further)
                def _():
                    along(i, shards[i], spot, turn, way).wait_send()

        for at, spot in enumerate(spots):
            for copy in onward(i, shards[i], spot, at == 0):
                copy.wait_send()
            for copy in after_second(i, spot):
                copy.wait_send()
            for turn in range(2 * (firsts - 1)):
                after_first(i, spot, turn).wait_send()


def gather_now(shards, planes, whole_slice, collective_id, exchanges=(), late_rows=None):
    parts = []
    for array, shard in enumerate(shards):
        rows = shard.shape[0]
        early = rows - (late_rows[array] if late_rows else 0)
        parts += [(array, 0, early, False)] * (early > 0)
        parts += [(array, early, rows - early, True)] * (early < rows)
    count = len(parts)
    firsts = 2 if whole_slice else 1
    specs = exchange_specs(exchanges)
    dma = pltpu.SemaphoreType.DMA
    grid = (planes, 2, 2, 2) if whole_slice else (planes, 2, 2)
    results = communicate(
        functools.partial(gather_kernel, planes, parts, whole_slice, specs),
        list(shards),
        exchanges,
        [jax.ShapeDtypeStruct((*grid, *shard.shape), shard.dtype) for shard in shards],
        [
            dma((count + 1,)),
            dma((2, count, planes, 2)),
            dma((count, planes)),
            dma((count, planes, 2)),
            dma((count, planes, 2, 2)),
            dma((count, planes, firsts, 2)),
            dma((count, planes, firsts, 2)),
        ],
        planes,
        collective_id,
        200,
        "gather_now",
    )
    places = 4 * planes * firsts
    wholes = [
        whole.reshape(places * shard.shape[0], shard.shape[1])
        for whole, shard in zip(results, shards)
    ]
    return wholes + list(results[len(shards) :])


def scatter_kernel(planes, steps, rows, whole_slice, product, specs, *refs):
    operands, (sum_ref,), scratch, rides = split_refs(refs, 1 + product, 1, specs)
    own, from_core, from_first, from_second, from_below, from_above = scratch[:6]
    load_sem, core_sems, first_sems, second_sems, up_sems, down_sems = scratch[6:12]
    if product:
        lefts, rights, made, factor_sems = scratch[12:]
    else:
        (partial_ref,) = operands
    blk, z, x, core, y = position()
    firsts = 2 if whole_slice else 1
    to_core = (blk + 1 - 2 * core, y)
    if whole_slice:
        first = y * (1 - core) + x * core
        second = x * (1 - core) + y * core
        core_second = second
        first_device = (blk + core * (2 - 4 * x), y + (1 - core) * (1 - 2 * y))
        second_device = (blk + (1 - core) * (2 - 4 * x), y + core * (1 - 2 * y))
    else:
        first, second = 0, x
        first_device, second_device = None, (blk + 2 - 4 * x, y)
    line = [(blk + 4 * (lax.rem(z + at, planes) - z), y) for at in range(1, planes)]
    nearby = [to_core, second_device] + [first_device] * whole_slice + line
    greet(greeted(specs, nearby))

    def make(step):
        some = pl.ds(pl.multiple_of(step * rows, rows), rows)
        left = lefts[:, :, :, some, :].reshape(4 * planes * rows, lefts.shape[-1])
        wide = 2 * HEAD

        @pl.loop(0, rights.shape[0] // wide)
        def _(at):
            columns = pl.ds(pl.multiple_of(at * wide, wide), wide)
            part = lax.dot_general(
                left,
                rights[columns, :],
                (((1,), (1,)), ((), ())),
                preferred_element_type=jnp.float32,
            )
            part = part.astype(made.dtype).reshape(planes, 2, 2, rows, wide)
            made[step, :, :, :, :, columns] = part

    def piece(step, by_first, by_second, plane):
        if product:
            return made.at[step, :, by_second, plane]
        some = pl.ds(pl.multiple_of(step * rows, rows), rows)
        if whole_slice:
            by_x = (1 - plane) * by_second + plane * by_first
            by_y = (1 - plane) * by_first + plane * by_second
            return partial_ref.at[:, by_x, plane, by_y, some]
        return partial_ref.at[:, by_second, plane, some]

    def core_copy(step, by_first, by_second, plane):
        return remote(
            piece(step, by_first, by_second, plane),
            from_core.at[step, by_first, by_second],
            core_sems.at[0, step, by_first, by_second],
            core_sems.at[1, step, by_first, by_second],
            to_core,
        )

    def load(step, by_first, by_second):
        return pltpu.make_async_copy(
            piece(step, by_first, by_second, core),
            own.at[step, by_first, by_second],
            load_sem.at[step, by_first, by_second],
        )

    def first_copy(step):
        return remote(
            own.at[step, 1 - first],
            from_first.at[step],
            first_sems.at[0, step],
            first_sems.at[1, step],
            first_device,
        )

    def second_copy(step):
        return remote(
            own.at[step, first, 1 - second],
            from_second.at[step],
            second_sems.at[0, step],
            second_sems.at[1, step],
            second_device,
        )

    def up_copy(step, target):
        return remote(
            own.at[step, first, second, target],
            from_below.at[step, target],
            up_sems.at[0, step, target],
            up_sems.at[1, step, target],
            (blk + 4, y),
        )

    def down_copy(step, target):
        return remote(
            own.at[step, first, second, target],
            from_above.at[step, target],
            down_sems.at[0, step, target],
            down_sems.at[1, step, target],
            (blk - 4, y),
        )

    def halves():
        if not whole_slice:
            return [(0, 1 - second), (0, second)]
        return [(1 - first, 0), (1 - first, 1), (first, 0), (first, 1)]

    def core_halves():
        if not whole_slice:
            return [(0, 1 - second), (0, second)]
        return [(1 - core_second, 0), (1 - core_second, 1), (core_second, 0), (core_second, 1)]

    def start_loads(step):
        if product:
            make(step)
        for mine, theirs in zip(halves(), core_halves()):
            core_copy(step, *theirs, 1 - core).start()
            if not product:
                load(step, *mine).start()

    def add_core(step):
        for turn, mine in enumerate(halves()):
            if not product:
                load(step, *mine).wait()
            core_copy(step, *mine, core).wait_recv()
            if product:
                own[step, *mine] = made[step, :, mine[1], core] + from_core[step, *mine]
            else:
                own[step, *mine] += from_core[step, *mine]
            if whole_slice and turn == 1:
                first_copy(step).start()
            if not whole_slice and turn == 0:
                second_copy(step).start()

    def add_first(step):
        first_copy(step).wait_recv()
        own[step, first, 1 - second] += from_first[step, 1 - second]
        second_copy(step).start()
        own[step, first, second] += from_first[step, second]

    def add_second(step):
        second_copy(step).wait_recv()
        own[step, first, second] += from_second[step]

    def pass_up(step):
        for target in range(planes):

            @pl.when((z > 0) & (z <= target))
            def _():
                up_copy(step, target).wait_recv()

            @pl.when((z > 0) & (z < target))
            def _():
                own[step, first, second, target] += from_below[step, target]

            @pl.when(z < target)
            def _():
                up_copy(step, target).start()

    def pass_down(step):
        for target in range(planes):

            @pl.when((z < planes - 1) & (z >= target))
            def _():
                down_copy(step, target).wait_recv()

            @pl.when((z < planes - 1) & (z > target))
            def _():
                own[step, first, second, target] += from_above[step, target]

            @pl.when(z > target)
            def _():
                down_copy(step, target).start()

    def add_line(step):
        some = pl.ds(pl.multiple_of(step * rows, rows), rows)
        sum_ref[some, :] = own[step, first, second, z]

        @pl.when(z > 0)
        def _():
            sum_ref[some, :] += from_below[step, z]

        @pl.when(z < planes - 1)
        def _():
            sum_ref[some, :] += from_above[step, z]

    rides = rides_of(planes, rides)
    hurry = [-(-ride.count // steps) for ride in rides]
    for ride, number in zip(rides, hurry):
        for at in range(number):
            ride.issue(jnp.int32(at))
    if product:
        factors = [
            pltpu.make_async_copy(operand, ref, factor_sems.at[i])
            for i, (operand, ref) in enumerate(zip(operands, (lefts, rights)))
        ]
        for factor in factors:
            factor.start()
        for factor in factors:
            factor.wait()

    @pl.loop(0, 2)
    def _(step):
        start_loads(step)

    early = firsts + 1

    @pl.loop(0, steps + early + planes)
    def _(turn):
        def stage(step, work):
            @pl.when((step >= 0) & (step < steps))
            def _():
                work(step)

        @pl.when(turn < steps - 2)
        def _():
            start_loads(turn + 2)

        stage(turn, add_core)
        for ride, number in zip(rides, hurry):
            for at in range(number):
                ride.issue((turn + 1) * number + at)
        if whole_slice:
            stage(turn - 1, add_first)
        stage(turn - early + 1, add_second)
        stage(turn - early - z, pass_up)
        stage(turn - early - (planes - 1 - z), pass_down)
        stage(turn - early - planes + 1, add_line)

    @pl.loop(0, steps)
    def _(step):
        for theirs in core_halves():
            core_copy(step, *theirs, 1 - core).wait_send()
        if whole_slice:
            first_copy(step).wait_send()
        second_copy(step).wait_send()
        for target in range(planes):

            @pl.when(z < target)
            def _():
                up_copy(step, target).wait_send()

            @pl.when(z > target)
            def _():
                down_copy(step, target).wait_send()

    for ride in rides:
        ride.finish()


def scatter_now(factors, planes, whole_slice, collective_id, exchanges=()):
    firsts = 2 if whole_slice else 1
    product = len(factors) == 2
    shard_rows = factors[0].shape[0] // (4 * planes * firsts)
    width = factors[1].shape[0] if product else factors[0].shape[1]
    rows = 16
    steps = shard_rows // rows
    dtype = factors[0].dtype
    specs = exchange_specs(exchanges)
    dma = pltpu.SemaphoreType.DMA
    grid = (planes, 2, 2, 2) if whole_slice else (planes, 2, 2)
    return communicate(
        functools.partial(scatter_kernel, planes, steps, rows, whole_slice, product, specs),
        [factors[0].reshape(*grid, shard_rows, factors[0].shape[1]), *factors[1:]],
        exchanges,
        [jax.ShapeDtypeStruct((shard_rows, width), dtype)],
        [
            pltpu.VMEM((steps, firsts, 2, planes, rows, width), dtype),
            pltpu.VMEM((steps, firsts, 2, planes, rows, width), dtype),
            pltpu.VMEM((steps if whole_slice else 1, 2, planes, rows, width), dtype),
            pltpu.VMEM((steps, planes, rows, width), dtype),
            pltpu.VMEM((steps, planes, rows, width), dtype),
            pltpu.VMEM((steps, planes, rows, width), dtype),
            dma((steps, firsts, 2)),
            dma((2, steps, firsts, 2)),
            dma((2, steps)),
            dma((2, steps)),
            dma((2, steps, planes)),
            dma((2, steps, planes)),
        ]
        + [
            pltpu.VMEM((*grid, shard_rows, factors[0].shape[1]), dtype),
            pltpu.VMEM(factors[-1].shape, dtype),
            pltpu.VMEM((steps, *grid, rows, width), dtype),
            dma((2,)),
        ]
        * product,
        planes,
        collective_id,
        200,
        "scatter_now",
        out_spec=pltpu.VMEM,
        vmem_limit_bytes=56 * 2**20,
    )


def ffn_pack_kernel(gateup_ref, down_ref, packet_ref):
    for at in range(packet_ref.shape[0]):
        columns = slice(at * HEAD, (at + 1) * HEAD)
        packet_ref[at, :, :HEAD] = gateup_ref[0, :, columns].astype(jnp.bfloat16)
        packet_ref[at, :, HEAD : 2 * HEAD] = gateup_ref[1, :, columns].astype(jnp.bfloat16)
        packet_ref[at, :, 2 * HEAD :] = down_ref[:, columns].astype(jnp.bfloat16)


def ffn_packets(gateup, down):
    row_count = gateup.shape[1]
    blocks, wide = FF // HEAD, 5
    return pl.pallas_call(
        ffn_pack_kernel,
        grid=(blocks // wide,),
        in_specs=[
            pl.BlockSpec((2, row_count, wide * HEAD), lambda j: (0, 0, j)),
            pl.BlockSpec((row_count, wide * HEAD), lambda j: (0, j)),
        ],
        out_specs=pl.BlockSpec((wide, row_count, 3 * HEAD), lambda j: (j, 0, 0)),
        out_shape=jax.ShapeDtypeStruct((blocks, row_count, 3 * HEAD), jnp.bfloat16),
        cost_estimate=pl.CostEstimate(flops=0, bytes_accessed=12 * 2**20, transcendentals=0),
        compiler_params=pltpu.CompilerParams(vmem_limit_bytes=32 * 2**20),
        name="ffn_packets",
    )(gateup, down)


def attn_pack_kernel(qkv_ref, out_ref, packet_ref):
    j = pl.program_id(0)

    @pl.when(j < (H + 2) // 2)
    def _():
        for at in range(2):
            packet_ref[at] = qkv_ref[:, at * HEAD : (at + 1) * HEAD].astype(jnp.bfloat16)

    @pl.when(j >= (H + 2) // 2)
    def _():
        for at in range(2):
            packet_ref[at] = out_ref[:, at * HEAD : (at + 1) * HEAD].astype(jnp.bfloat16)


def attn_packets(qkv, out):
    row_count = qkv.shape[0]
    qkv_last, out_last = (H + 2) // 2 - 1, H // 2 - 1
    return pl.pallas_call(
        attn_pack_kernel,
        grid=(H + 1,),
        in_specs=[
            pl.BlockSpec((row_count, 2 * HEAD), lambda j: (0, jnp.minimum(j, qkv_last))),
            pl.BlockSpec((row_count, 2 * HEAD), lambda j: (0, jnp.clip(j - qkv_last - 1, 0, out_last))),
        ],
        out_specs=pl.BlockSpec((2, row_count, HEAD), lambda j: (j, 0, 0)),
        out_shape=jax.ShapeDtypeStruct((2 * H + 2, row_count, HEAD), jnp.bfloat16),
        cost_estimate=pl.CostEstimate(flops=0, bytes_accessed=4 * 2**20, transcendentals=0),
        name="attn_packets",
    )(qkv, out)


def turn_kernel(grads_ref, others_ref, mom_ref, *refs):
    *results, current_ref = refs
    if len(results) == 1:
        low_ref, turned_ref = results[0].at[:, :HEAD], results[0].at[:, HEAD:]
    else:
        low_ref, turned_ref = results
    grads = grads_ref[...] + others_ref[...].astype(jnp.float32)
    low_ref[...] = grads.astype(jnp.bfloat16)
    moment = momentum_decay * mom_ref[...].astype(jnp.float32) + grads
    moment = moment.astype(jnp.bfloat16).astype(jnp.float32)
    norm_size = jnp.sqrt(jnp.sum(moment * moment, keepdims=True))
    current_ref[...] = (moment / (norm_size + eps_pieces)).T.astype(jnp.bfloat16)

    @pl.loop(0, NS_STEPS)
    def _(sweep_index):
        current = current_ref[...]
        gram_matrix = lax.dot_general(
            current, current, (((1,), (1,)), ((), ())), preferred_element_type=jnp.float32
        ).astype(jnp.bfloat16)
        square = jnp.dot(gram_matrix, gram_matrix, preferred_element_type=jnp.float32)
        mixing = (ns_second * gram_matrix.astype(jnp.float32) + ns_third * square).astype(
            jnp.bfloat16
        )
        turned = jnp.dot(mixing, current, preferred_element_type=jnp.float32)
        current_ref[...] = (ns_first * current.astype(jnp.float32) + turned).astype(jnp.bfloat16)

    turned_ref[...] = current_ref[...].astype(jnp.float32).T.astype(jnp.bfloat16)


def orthogonalize(grads, others, moms, results):
    depth, columns = grads.shape
    block = pl.BlockSpec((depth, HEAD), lambda j: (0, j))
    pieces = columns // HEAD
    return pl.pallas_call(
        turn_kernel,
        grid=(pieces,),
        in_specs=[block] * 3,
        out_specs=[pl.BlockSpec((depth, 2 // results * HEAD), lambda j: (0, j))] * results,
        out_shape=[jax.ShapeDtypeStruct((depth, 2 // results * columns), jnp.bfloat16)] * results,
        scratch_shapes=[pltpu.VMEM((HEAD, depth), jnp.bfloat16)],
        cost_estimate=pl.CostEstimate(
            flops=pieces * 20 * depth * HEAD * HEAD, bytes_accessed=12 * depth * columns, transcendentals=0
        ),
        compiler_params=pltpu.CompilerParams(vmem_limit_bytes=48 * 2**20),
        name="orthogonalize",
    )(grads, others, moms)


def update(rate, weight, mom, grad, turn):
    moment = momentum_decay * mom + grad.astype(jnp.float32)
    new = (1.0 - weight_shrink) * weight - rate * turn.astype(jnp.float32)
    return new, moment, new.astype(jnp.bfloat16)


def ffn_update_kernel(
    grad_ref, turn_ref, w_gateup_ref, mom_gateup_ref, w_down_ref, mom_down_ref, *results
):
    for at in range(grad_ref.shape[0]):
        columns = slice(at * HEAD, (at + 1) * HEAD)
        for part in range(3):
            spot = (part, slice(None), columns) if part < 2 else (slice(None), columns)
            weight_ref, mom_ref = (
                (w_gateup_ref, mom_gateup_ref) if part < 2 else (w_down_ref, mom_down_ref)
            )
            packed = slice(part * HEAD, (part + 1) * HEAD)
            values = update(
                matrix_rate,
                weight_ref[spot],
                mom_ref[spot],
                grad_ref[at, :, packed],
                turn_ref[at, :, packed],
            )
            for ref, value in zip(results[:3] if part < 2 else results[3:], values):
                ref[spot] = value


def ffn_update(grads, turns, w_gateup, mom_gateup, w_down, mom_down):
    row_count = w_gateup.shape[1]
    wide = 3
    packet = pl.BlockSpec((wide, row_count, 3 * HEAD), lambda j: (j, 0, 0))
    gateup = pl.BlockSpec((2, row_count, wide * HEAD), lambda j: (0, 0, j))
    down = pl.BlockSpec((row_count, wide * HEAD), lambda j: (0, j))
    dtypes = (jnp.float32, jnp.float32, jnp.bfloat16)
    return pl.pallas_call(
        ffn_update_kernel,
        grid=(FF // HEAD // wide,),
        in_specs=[packet, packet, gateup, gateup, down, down],
        out_specs=[gateup] * 3 + [down] * 3,
        out_shape=[jax.ShapeDtypeStruct(w_gateup.shape, dtype) for dtype in dtypes]
        + [jax.ShapeDtypeStruct(w_down.shape, dtype) for dtype in dtypes],
        cost_estimate=pl.CostEstimate(flops=0, bytes_accessed=50 * 2**20, transcendentals=0),
        compiler_params=pltpu.CompilerParams(vmem_limit_bytes=48 * 2**20),
        name="ffn_update",
    )(grads, turns, w_gateup, mom_gateup, w_down, mom_down)


def attn_update_kernel(rate, packet_ref, w_ref, mom_ref, *results):
    for at in range(2):
        columns = slice(at * HEAD, (at + 1) * HEAD)
        values = update(
            rate,
            w_ref[:, columns],
            mom_ref[:, columns],
            packet_ref[at, :, :HEAD],
            packet_ref[at, :, HEAD:],
        )
        for ref, value in zip(results, values):
            ref[:, columns] = value


def attn_update(rate, offset, packets, weight, mom):
    row_count = packets.shape[1]
    packet = pl.BlockSpec((2, row_count, 2 * HEAD), lambda j: (j + offset // 2, 0, 0))
    block = pl.BlockSpec((row_count, 2 * HEAD), lambda j: (0, j))
    return pl.pallas_call(
        functools.partial(attn_update_kernel, rate),
        grid=(weight.shape[1] // HEAD // 2,),
        in_specs=[packet, block, block],
        out_specs=[block] * 3,
        out_shape=[
            jax.ShapeDtypeStruct(weight.shape, dtype)
            for dtype in (jnp.float32, jnp.float32, jnp.bfloat16)
        ],
        cost_estimate=pl.CostEstimate(flops=0, bytes_accessed=6 * 2**20, transcendentals=0),
        name="attn_update",
    )(packets, weight, mom)


def two_heads(ref):
    return jnp.concatenate([ref[:, :HEAD], ref[:, HEAD:]], axis=0)


def visible(tokens, first_token, shape, query_axis):
    query = lax.rem(lax.broadcasted_iota(jnp.int32, shape, query_axis), tokens)
    key = lax.broadcasted_iota(jnp.int32, shape, 1 - query_axis)
    distance = query + WINDOW - key
    return (distance >= 0) & (distance < WINDOW) & (first_token - WINDOW + key >= 0)


def attend_kernel(first_ref, queries_ref, kv_ref, mixed_ref, log_total_ref):
    tokens = queries_ref.shape[0]
    raw = lax.dot_general(
        two_heads(queries_ref),
        kv_ref[:, :HEAD],
        (((1,), (1,)), ((), ())),
        preferred_element_type=jnp.float32,
    )
    allowed = visible(tokens, first_ref[0], raw.shape, 0)
    scores = jnp.where(allowed, raw * HEAD ** (-0.5), masked_score)
    top_score = jnp.max(scores, axis=-1, keepdims=True)
    expo = jnp.exp(scores - top_score)
    total = jnp.sum(expo, axis=-1, keepdims=True)
    probs = (expo / total).astype(jnp.bfloat16)
    mixed = jnp.dot(probs, kv_ref[:, HEAD:], preferred_element_type=jnp.float32)
    mixed_ref[:, :HEAD] = mixed[:tokens].astype(jnp.bfloat16)
    mixed_ref[:, HEAD:] = mixed[tokens:].astype(jnp.bfloat16)
    log_total_ref[0] = jnp.broadcast_to(top_score + jnp.log(total), log_total_ref.shape[1:])


def attend(first_token, qkv, kv_window):
    tokens = qkv.shape[0]
    span = kv_window.shape[0]
    pairs = H // 2
    return pl.pallas_call(
        attend_kernel,
        grid=(pairs,),
        in_specs=[
            pl.BlockSpec(memory_space=pltpu.SMEM),
            pl.BlockSpec((tokens, 2 * HEAD), lambda j: (0, j)),
            pl.BlockSpec((span, 2 * HEAD), lambda j: (0, 0)),
        ],
        out_specs=[
            pl.BlockSpec((tokens, 2 * HEAD), lambda j: (0, j)),
            pl.BlockSpec((1, 2 * tokens, 128), lambda j: (j, 0, 0)),
        ],
        out_shape=[
            jax.ShapeDtypeStruct((tokens, H * HEAD), jnp.bfloat16),
            jax.ShapeDtypeStruct((pairs, 2 * tokens, 128), jnp.float32),
        ],
        cost_estimate=pl.CostEstimate(
            flops=4 * H * tokens * span * HEAD,
            bytes_accessed=4 * 2**20,
            transcendentals=H * tokens * span,
        ),
        compiler_params=pltpu.CompilerParams(vmem_limit_bytes=48 * 2**20),
        name="attend",
    )(first_token, qkv, kv_window)


def attend_back_kernel(
    first_ref, queries_ref, grads_ref, log_total_ref, kv_ref, grad_query_ref, grad_kv_ref, sums_ref
):
    tokens = queries_ref.shape[0]
    score_scale = HEAD ** (-0.5)
    keys, values = kv_ref[:, :HEAD], kv_ref[:, HEAD:]
    queries, grads = two_heads(queries_ref), two_heads(grads_ref)

    def against(left, right):
        return lax.dot_general(
            left, right, (((1,), (1,)), ((), ())), preferred_element_type=jnp.float32
        )

    raw = against(keys, queries)
    allowed = visible(tokens, first_ref[0], raw.shape, 1)
    scores = jnp.where(allowed, raw * score_scale, masked_score)
    log_total = log_total_ref[0].T[:1]
    probs = jnp.exp(scores - log_total)
    grad_probs = against(values, grads)
    row_delta = jnp.sum(probs * grad_probs, axis=0, keepdims=True)
    grad_raw = (probs * (grad_probs - row_delta) * score_scale).astype(jnp.bfloat16)
    grad_query = lax.dot_general(
        grad_raw, keys, (((0,), (0,)), ((), ())), preferred_element_type=jnp.float32
    )
    grad_query_ref[:, :HEAD] = grad_query[:tokens].astype(jnp.bfloat16)
    grad_query_ref[:, HEAD:] = grad_query[tokens:].astype(jnp.bfloat16)

    @pl.when(pl.program_id(0) == 0)
    def _():
        sums_ref[...] = jnp.zeros_like(sums_ref)

    sums_ref[:, :HEAD] += jnp.dot(grad_raw, queries, preferred_element_type=jnp.float32)
    sums_ref[:, HEAD:] += jnp.dot(
        probs.astype(jnp.bfloat16), grads, preferred_element_type=jnp.float32
    )

    @pl.when(pl.program_id(0) == pl.num_programs(0) - 1)
    def _():
        grad_kv_ref[...] = sums_ref[...].astype(jnp.bfloat16)


def attend_back(first_token, qkv, grads, log_total, kv_window):
    tokens = qkv.shape[0]
    span = kv_window.shape[0]
    heads = pl.BlockSpec((tokens, 2 * HEAD), lambda j: (0, j))
    window = pl.BlockSpec((span, 2 * HEAD), lambda j: (0, 0))
    return pl.pallas_call(
        attend_back_kernel,
        grid=(H // 2,),
        in_specs=[
            pl.BlockSpec(memory_space=pltpu.SMEM),
            heads,
            heads,
            pl.BlockSpec((1, 2 * tokens, 128), lambda j: (j, 0, 0)),
            window,
        ],
        out_specs=[heads, window],
        out_shape=[
            jax.ShapeDtypeStruct((tokens, H * HEAD), jnp.bfloat16),
            jax.ShapeDtypeStruct((span, 2 * HEAD), jnp.bfloat16),
        ],
        scratch_shapes=[pltpu.VMEM((span, 2 * HEAD), jnp.float32)],
        cost_estimate=pl.CostEstimate(
            flops=10 * H * tokens * span * HEAD,
            bytes_accessed=8 * 2**20,
            transcendentals=H * tokens * span,
        ),
        compiler_params=pltpu.CompilerParams(vmem_limit_bytes=48 * 2**20),
        name="attend_back",
    )(first_token, qkv, grads, log_total, kv_window)


def rms_scale(stream, gain_row):
    mean_square = jnp.mean(stream * stream, axis=-1, keepdims=True)
    return stream * lax.rsqrt(mean_square + eps_norm) * gain_row


def gelu_product(gate_part, up_part):
    return jax.nn.gelu(gate_part, approximate=True) * up_part


def on_device(
    tokens_in,
    cotangent,
    w_qkv,
    w_out,
    w_gateup,
    w_down,
    gains,
    mom_qkv,
    mom_out,
    mom_gateup,
    mom_down,
    mom_gains,
):
    everyone = ("blk", "pair")
    bf16 = jnp.bfloat16
    f32 = jnp.float32
    blk_count = lax.axis_size("blk")
    pair_count = lax.axis_size("pair")
    device_count = blk_count * pair_count
    block_at = lax.axis_index("blk")
    half_at = lax.axis_index("pair")
    me = block_at * pair_count + half_at
    local_rows, width = tokens_in.shape
    share_rows = w_qkv.shape[0]
    span = WINDOW + local_rows
    token_count = local_rows * device_count
    large = token_count * width * 2 > 48 * 2**20
    planes = blk_count // 4
    spread = not large

    def after(value, earlier):
        return lax.optimization_barrier((value, earlier))[0] if large else value

    def exchange(packets, axes=everyone):
        return lax.all_to_all(packets, axes, split_axis=0, concat_axis=0, tiled=True)

    def swap(shard):
        return lax.ppermute(shard, "pair", [(0, 1), (1, 0)])

    def hold(value, *earlier):
        return value if large else lax.optimization_barrier((value, earlier))[0]

    def ride(packets, among="all", **options):
        sources = {"all": device_count, "plane": blk_count, "pair": pair_count}[among]
        return Exchange(packets, among, **(dict(sources=sources) | options))

    def exchanged(rides):
        results = []
        for packets, among, _, before, _, _ in rides:
            if among == "pair":
                results.append(swap(packets))
                continue
            axes, places = (everyone, device_count) if among == "all" else ("blk", blk_count)
            after_last = places - before - packets.shape[0]
            packets = jnp.pad(packets, ((before, after_last),) + ((0, 0),) * (packets.ndim - 1))
            results.append(exchange(packets, axes))
        return results

    def gather(shards, whole_slice, collective_id, rides=(), **options):
        if large:
            axes = everyone if whole_slice else "blk"
            wholes = [lax.all_gather(shard, axes, axis=0, tiled=True) for shard in shards]
            return wholes + exchanged(rides)
        return gather_now(shards, planes, whole_slice, collective_id, rides, **options)

    def scatter(factors, whole_slice, collective_id, rides=()):
        if large:
            axes = everyone if whole_slice else "blk"
            if len(factors) == 2:
                partial = jnp.einsum("tf,df->td", *factors, preferred_element_type=f32)
                factors = [partial.astype(bf16)]
            part = lax.psum_scatter(factors[0], axes, scatter_dimension=0, tiled=True)
            return [part] + exchanged(rides)
        return scatter_now(factors, planes, whole_slice, collective_id, rides)

    def gather_plane(shard):
        return lax.all_gather(shard, "blk", axis=0, tiled=True)

    stream = tokens_in.astype(f32)
    padded_gains = jnp.pad(gains.astype(bf16), ((0, 14), (0, 128 - share_rows)))
    full_qkv, full_gains, full_out, ffn_weights = gather(
        [w_qkv.astype(bf16), padded_gains, w_out.T.astype(bf16)],
        True,
        1,
        [ride(ffn_packets(w_gateup, w_down.T))],
        late_rows=(0, 0, share_rows),
    )
    ffn_weights = ffn_weights.reshape(width, 3 * HEAD)
    full_gains = full_gains.reshape(device_count, 16, 128)[:, :2, :share_rows].astype(f32)
    gain_attn = full_gains[:, 0].reshape(width)
    gain_mlp = full_gains[:, 1].reshape(width)
    normed_attn_f, norm_back_attn = jax.vjp(rms_scale, stream, gain_attn)
    normed_attn = normed_attn_f.astype(bf16)
    qkv = jnp.dot(normed_attn, full_qkv, preferred_element_type=f32).astype(bf16)
    (kv_all,) = gather([qkv[:, H * HEAD :]], True, 2)
    kv_window = lax.dynamic_slice_in_dim(
        jnp.pad(kv_all, ((WINDOW, 0), (0, 0))), me * local_rows, span, 0
    )
    first_token = (me * local_rows).astype(jnp.int32).reshape(1)
    mixed, log_total = attend(first_token, qkv, kv_window)
    resid = stream + jnp.einsum("tc,dc->td", mixed, full_out, preferred_element_type=f32)

    normed_mlp_f, norm_back_mlp = jax.vjp(rms_scale, resid, gain_mlp)
    normed_mlp = normed_mlp_f.astype(bf16)
    normed_mlp_plane, cotangent_plane, other_weights = gather(
        [normed_mlp, cotangent], False, 3, [ride(ffn_weights, "pair")], late_rows=(0, local_rows // 4)
    )
    pair_weights = [ffn_weights, other_weights]
    gates, ups, downs = (
        [weights[:, part * HEAD : (part + 1) * HEAD] for weights in pair_weights]
        for part in range(3)
    )
    owns_block = me < FF // HEAD
    pair_gateup = jnp.where(owns_block, jnp.concatenate(gates + ups, axis=1), 0)
    pair_down = jnp.where(owns_block, jnp.concatenate(downs, axis=1), 0)
    plane_rows = blk_count * local_rows
    both_parts = jnp.dot(normed_mlp_plane, pair_gateup, preferred_element_type=f32)
    pair_width = pair_count * HEAD
    hidden_f, geglu_back = jax.vjp(
        gelu_product, both_parts[:, :pair_width], both_parts[:, pair_width:]
    )
    hidden = hidden_f.astype(bf16)
    grad_hidden = jnp.dot(cotangent_plane, pair_down, preferred_element_type=f32)
    grad_gate, grad_up = geglu_back(grad_hidden)
    grad_gateup = jnp.concatenate([grad_gate.astype(bf16), grad_up.astype(bf16)], axis=1)
    def ffn_gradient(columns):
        gateup_right = jnp.concatenate(
            [grad_gate[:, columns].astype(bf16), grad_up[:, columns].astype(bf16)], axis=1
        )
        down_right = hidden[:, columns]
        return jnp.concatenate(
            [
                jnp.einsum("td,tf->df", normed_mlp_plane, gateup_right, preferred_element_type=f32),
                jnp.einsum("td,tf->df", cotangent_plane, down_right, preferred_element_type=f32),
            ],
            axis=1,
        )

    def pair_columns(columns):
        return columns.reshape(local_rows, -1, pair_width).transpose(1, 0, 2)

    ffn_theirs = ffn_gradient(slice(HEAD, 2 * HEAD)).astype(bf16)
    grad_normed_mlp, ffn_others, ffn_moms, attn_moms, out_rights = scatter(
        [grad_gateup, pair_gateup],
        False,
        4,
        [
            ride(ffn_theirs, "pair"),
            ride(ffn_packets(mom_gateup, mom_down.T)),
            ride(attn_packets(mom_qkv, mom_out.T), spread_targets=spread),
            ride(
                pair_columns(mixed), "plane", first_target=(H + 2) // 2, spread_targets=spread
            ),
        ],
    )
    grad_normed_mlp = grad_normed_mlp.astype(f32)

    ffn_grads = ffn_gradient(slice(0, HEAD))
    ffn_low, ffn_turned = orthogonalize(
        ffn_grads, ffn_others, ffn_moms.reshape(width, 3 * HEAD), 2
    )
    ffn_shape = (device_count, share_rows, 3 * HEAD)

    resid_part, gain_grad_mlp = norm_back_mlp(grad_normed_mlp)
    grad_resid = cotangent.astype(f32) + resid_part
    grad_proj = grad_resid.astype(bf16)
    grad_mixed = jnp.dot(grad_proj, full_out, preferred_element_type=f32).astype(bf16)
    grad_query, grad_kv = attend_back(first_token, qkv, grad_mixed, log_total, kv_window)
    grad_kv_all = lax.dynamic_update_slice_in_dim(
        jnp.zeros((WINDOW + token_count, 2 * HEAD), bf16), grad_kv, me * local_rows, 0
    )[WINDOW:]
    grad_kv, ffn_low = scatter(
        [grad_kv_all], True, 5, [ride(ffn_low.reshape(ffn_shape), sources=FF // HEAD)]
    )
    grad_qkv = jnp.concatenate([grad_query, grad_kv], axis=1)
    grad_normed_attn = jnp.einsum("tc,dc->td", grad_qkv, full_qkv, preferred_element_type=f32)
    stream_part, gain_grad_attn = norm_back_attn(grad_normed_attn)
    input_grad = grad_resid + stream_part

    branch, ffn_turned, qkv_rights = scatter(
        [after(hidden, grad_normed_mlp), pair_down],
        False,
        6,
        [
            ride(ffn_turned.reshape(ffn_shape), sources=FF // HEAD),
            ride(pair_columns(grad_qkv), "plane", spread_targets=spread),
        ],
    )
    block_output = (resid + branch.astype(f32)).astype(bf16)
    normed_attn_plane = gather_plane(after(hold(normed_attn, normed_mlp_plane), (ffn_grads, block_output)))
    grad_proj_plane = gather_plane(after(grad_proj, (ffn_grads, block_output)))

    pair_at = spread_place(planes, block_at) if spread else block_at

    def attn_gradient(half, qkv_rights, out_rights):
        def product(lefts, rights):
            rights = rights.reshape(plane_rows, pair_width)
            rights = lax.dynamic_slice_in_dim(rights, half * HEAD, HEAD, 1)
            return jnp.einsum("td,tf->df", lefts, rights, preferred_element_type=f32)

        return lax.cond(
            pair_at < (H + 2) // pair_count,
            lambda: product(normed_attn_plane, qkv_rights),
            lambda: product(grad_proj_plane, out_rights),
        )

    attn_theirs = attn_gradient(1 - half_at, qkv_rights, out_rights).astype(bf16)
    attn_others = swap(attn_theirs)
    attn_grads = attn_gradient(half_at, *hold((qkv_rights, out_rights), attn_theirs))
    updated_ffn = ffn_update(ffn_low, ffn_turned, w_gateup, mom_gateup, w_down.T, mom_down.T)
    (attn_results,) = orthogonalize(
        attn_grads, hold(attn_others, updated_ffn[0]), attn_moms.reshape(width, HEAD), 1
    )
    gain_grads = jnp.stack([gain_grad_attn, gain_grad_mlp], axis=0)
    gain_grads = gain_grads.reshape(2, device_count, share_rows).transpose(1, 0, 2)
    last_rides = [
        ride(
            attn_results.reshape(device_count, share_rows, 2 * HEAD),
            sources=2 * H + 2,
            spread_sources=spread,
        ),
        ride(jnp.pad(gain_grads, ((0, 0), (0, 6), (0, 128 - share_rows)))),
    ]
    if large:
        attn_results, gain_grads = exchanged(last_rides)
    else:
        attn_results, gain_grads = exchange_now(last_rides, planes, 7)
    gain_share = jnp.sum(gain_grads, axis=0)[:2, :share_rows]

    updated_qkv = attn_update(matrix_rate, 0, attn_results, w_qkv, mom_qkv)
    updated_out = attn_update(output_rate, H + 2, attn_results, w_out.T, mom_out.T)
    moment_gains = momentum_decay * mom_gains + gain_share
    new_gains = gains - gain_rate * moment_gains
    return (
        block_output,
        input_grad,
        *updated_qkv,
        *(result.T for result in updated_out),
        *updated_ffn[:3],
        *(result.T for result in updated_ffn[3:]),
        new_gains,
        moment_gains,
        new_gains.astype(bf16),
    )


def solution(mesh):
    placed = (
        P(("blk", "pair"), None),
        P(("blk", "pair"), None),
        P(("blk", "pair"), None),
        P(None, ("blk", "pair")),
        P(None, ("blk", "pair"), None),
        P(None, ("blk", "pair")),
        P(None, ("blk", "pair")),
        P(("blk", "pair"), None),
        P(None, ("blk", "pair")),
        P(None, ("blk", "pair"), None),
        P(None, ("blk", "pair")),
        P(None, ("blk", "pair")),
    )
    return jax.shard_map(
        on_device,
        mesh=mesh,
        in_specs=placed,
        out_specs=(
            P(("blk", "pair"), None),
            P(("blk", "pair"), None),
            P(("blk", "pair"), None),
            P(("blk", "pair"), None),
            P(("blk", "pair"), None),
            P(None, ("blk", "pair")),
            P(None, ("blk", "pair")),
            P(None, ("blk", "pair")),
            P(None, ("blk", "pair"), None),
            P(None, ("blk", "pair"), None),
            P(None, ("blk", "pair"), None),
            P(None, ("blk", "pair")),
            P(None, ("blk", "pair")),
            P(None, ("blk", "pair")),
            P(None, ("blk", "pair")),
            P(None, ("blk", "pair")),
            P(None, ("blk", "pair")),
        ),
        check_vma=False,
    )
```

```python
import functools
from typing import NamedTuple

import jax
import jax.numpy as jnp
from jax import lax
from jax.experimental import pallas as pl
from jax.experimental.pallas import tpu as pltpu
from jax.sharding import PartitionSpec as P

H = 10
HEAD = 256
FF = 7680
WINDOW = 2048
NS_STEPS = 5


eps_norm = 1e-06
eps_pieces = 1e-07
ns_first = 3.4445
ns_second = -4.775
ns_third = 2.0315
momentum_decay = 0.95
matrix_rate = 0.5
output_rate = 10.0
gain_rate = 0.001
weight_shrink = 0.001
masked_score = -1e30
MESH = pl.DeviceIdType.MESH


def position():
    blk, y = lax.axis_index("blk"), lax.axis_index("pair")
    return blk, lax.div(blk, 4), lax.rem(lax.div(blk, 2), 2), lax.rem(blk, 2), y


def greet(devices):
    barrier = pltpu.get_barrier_semaphore()
    for device in devices:
        pl.semaphore_signal(barrier, inc=1, device_id=device, device_id_type=MESH)
    pl.semaphore_wait(barrier, len(devices))


def remote(source, target, send_sem, recv_sem, device):
    return pltpu.make_async_remote_copy(
        src_ref=source,
        dst_ref=target,
        send_sem=send_sem,
        recv_sem=recv_sem,
        device_id=device,
        device_id_type=MESH,
    )


class Exchange(NamedTuple):
    packets: jax.Array
    among: str
    sources: int
    first_target: int = 0
    spread_sources: bool = False
    spread_targets: bool = False


def spread_place(planes, blk):
    z, x, core = lax.div(blk, 4), lax.rem(lax.div(blk, 2), 2), lax.rem(blk, 2)
    return (2 * core + lax.rem(x + z, 2)) * planes + z


def all_devices():
    blk, _, _, _, y = position()
    count = 2 * lax.axis_size("blk")
    here = 2 * blk + y
    places = [lax.rem(here + at, count) for at in range(1, count)]
    return [(lax.div(place, 2), lax.rem(place, 2)) for place in places]


def plane_devices():
    blk, _, _, _, y = position()
    count = lax.axis_size("blk")
    return [(lax.rem(blk + at, count), y) for at in range(1, count)]


def greeted(specs, nearby):
    if any(among == "all" for among, *_ in specs):
        return all_devices()
    blk, _, _, _, y = position()
    pair = [(blk, 1 - y)] * any(among == "pair" for among, *_ in specs)
    if any(among == "plane" for among, *_ in specs):
        return plane_devices() + pair
    return nearby + pair


PAIR_PARTS = 4


def exchange_count(planes, among):
    return {"all": 8 * planes, "plane": 4 * planes, "pair": PAIR_PARTS}[among]


class Ride:
    def __init__(self, planes, spec, packets, received, sems):
        self.planes, self.packets, self.received = planes, packets, received
        self.among, self.sources, self.first_target, self.from_spread, self.to_spread = spec
        self.own_sem, self.send_sems, self.recv_sems = sems
        self.count = exchange_count(planes, self.among)
        self.issued = 0
        blk, self.z, _, _, self.y = position()
        self.blk = blk
        self.here = blk if self.among == "plane" else 2 * blk + self.y

    def place(self, q):
        near = self.count // self.planes
        spot = lax.rem(self.z + 1 + lax.rem(q, self.planes), self.planes)
        return spot * near + lax.rem(self.here + lax.div(q, self.planes), near)

    def counted(self, place, spread):
        if not spread:
            return place
        if self.among == "plane":
            return spread_place(self.planes, place)
        return 2 * spread_place(self.planes, lax.div(place, 2)) + lax.rem(place, 2)

    def source(self, place):
        return self.counted(place, self.from_spread)

    def target(self, place):
        return self.counted(place, self.to_spread) - self.first_target

    def sending(self, place):
        return self.source(place) < self.sources

    def receiving(self, place):
        target = self.target(place)
        return (target >= 0) & (target < self.packets.shape[0])

    def copy(self, q):
        if self.among == "pair":
            rows = self.packets.shape[0] // PAIR_PARTS
            some = pl.ds(pl.multiple_of(q * rows, rows), rows)
            return remote(
                self.packets.at[some],
                self.received.at[some],
                self.send_sems.at[q],
                self.recv_sems.at[q],
                (self.blk, 1 - self.y),
            )
        place = self.place(q)
        device = (place, self.y)
        if self.among == "all":
            device = (lax.div(place, 2), lax.rem(place, 2))
        source = self.source(self.here)
        return remote(
            self.packets.at[self.target(place)],
            self.received.at[source],
            self.send_sems.at[q],
            self.recv_sems.at[source],
            device,
        )

    def own(self):
        return pltpu.make_async_copy(
            self.packets.at[self.target(self.here)],
            self.received.at[self.source(self.here)],
            self.own_sem.at[0],
        )

    def sends(self, q):
        away = (q < self.count) & (q != self.planes - 1)
        return away & self.sending(self.here) & self.receiving(self.place(q))

    def keeps(self):
        return self.sending(self.here) & self.receiving(self.here)

    def start_own(self):
        if self.among == "pair":
            for q in range(self.count):
                self.copy(q).start()
        else:

            @pl.when(self.keeps())
            def _():
                self.own().start()

    def issue(self, q):
        if self.among != "pair":

            @pl.when(self.sends(q))
            def _():
                self.copy(q).start()

    def issue_more(self, number):
        first, self.issued = self.issued, min(self.issued + number, self.count)

        @pl.loop(first, self.issued)
        def _(q):
            self.issue(q)

    def finish(self):
        if self.among == "pair":
            for q in range(self.count):
                self.copy(q).wait()
            return

        @pl.loop(0, self.count)
        def _(q):
            @pl.when(self.sends(q))
            def _():
                self.copy(q).wait_send()

            @pl.when((q != self.here) & self.sending(q) & self.receiving(self.here))
            def _():
                source = self.source(q)
                spot = self.received.at[source]
                remote(
                    spot, spot, self.own_sem.at[0], self.recv_sems.at[source], (self.blk, self.y)
                ).wait_recv()

        @pl.when(self.keeps())
        def _():
            self.own().wait()


def rides_of(planes, rides):
    rides = [Ride(planes, *ride) for ride in rides]
    for ride in rides:
        ride.start_own()
    return rides


def exchange_sems(exchanges, planes):
    dma = pltpu.SemaphoreType.DMA
    return [
        dma((count,))
        for exchange in exchanges
        for count in (1,) + (exchange_count(planes, exchange.among),) * 2
    ]


def exchange_specs(exchanges):
    return tuple((each.among, *each[2:]) for each in exchanges)


def communicate(
    kernel,
    operands,
    exchanges,
    outputs,
    scratch,
    planes,
    collective_id,
    cost,
    name,
    out_spec=pl.ANY,
    **options,
):
    packets = [each.packets for each in exchanges]
    received = [
        jax.ShapeDtypeStruct(
            array.shape
            if each.among == "pair"
            else (exchange_count(planes, each.among), *array.shape[1:]),
            array.dtype,
        )
        for each, array in zip(exchanges, packets)
    ]
    any_spec = pl.BlockSpec(memory_space=pl.ANY)
    return pl.pallas_call(
        kernel,
        out_shape=outputs + received,
        in_specs=[any_spec] * (len(operands) + len(packets)),
        out_specs=[pl.BlockSpec(memory_space=out_spec)] * len(outputs) + [any_spec] * len(packets),
        scratch_shapes=scratch + exchange_sems(exchanges, planes),
        compiler_params=pltpu.CompilerParams(
            collective_id=collective_id, has_side_effects=True, **options
        ),
        cost_estimate=pl.CostEstimate(flops=0, bytes_accessed=cost * 2**20, transcendentals=0),
        name=name,
    )(*operands, *packets)


def split_refs(refs, inputs, outputs, specs):
    riders = len(specs)
    ins, refs = refs[: inputs + riders], refs[inputs + riders :]
    outs, refs = refs[: outputs + riders], refs[outputs + riders :]
    scratch = refs[: len(refs) - 3 * riders]
    sems = refs[len(refs) - 3 * riders :]
    rides = [
        (spec, ins[inputs + i], outs[outputs + i], sems[3 * i : 3 * i + 3])
        for i, spec in enumerate(specs)
    ]
    return ins[:inputs], outs[:outputs], scratch, rides


def exchange_kernel(planes, specs, *refs):
    _, _, _, rides = split_refs(refs, 0, 0, specs)
    greet(greeted(specs, []))
    rides = rides_of(planes, rides)
    for ride in rides:
        ride.issue_more(ride.count)
    for ride in rides:
        ride.finish()


def exchange_now(exchanges, planes, collective_id):
    specs = exchange_specs(exchanges)
    kernel = functools.partial(exchange_kernel, planes, specs)
    return communicate(kernel, [], exchanges, [], [], planes, collective_id, 100, "exchange_now")


def gather_kernel(planes, parts, whole_slice, specs, *refs):
    arrays = 1 + max(array for array, *_ in parts)
    shard_refs, whole_refs, scratch, rides = split_refs(refs, arrays, arrays, specs)
    count = len(parts)
    shards = [shard_refs[array].at[pl.ds(start, size)] for array, start, size, _ in parts]
    late = [is_late for *_, is_late in parts]
    own_sem, line_send, second_send, first_send, core_send, recv, core_recv = scratch
    blk, z, x, core, y = position()
    firsts = 2 if whole_slice else 1
    to_core = (blk + 1 - 2 * core, y)
    if whole_slice:
        first = y * (1 - core) + x * core
        second = x * (1 - core) + y * core
        first_device = (blk + core * (2 - 4 * x), y + (1 - core) * (1 - 2 * y))
        second_device = (blk + (1 - core) * (2 - 4 * x), y + core * (1 - 2 * y))
    else:
        first, second = 0, x
        first_device, second_device = None, (blk + 2 - 4 * x, y)
    line = [(blk + 4 * (lax.rem(z + at, planes) - z), y) for at in range(1, planes)]
    nearby = [to_core, second_device] + [first_device] * whole_slice + line
    greet(greeted(specs, nearby))

    def slot(i, spot, by_first, by_second, plane):
        array, start, size, _ = parts[i]
        whole, some = whole_refs[array], pl.ds(start, size)
        if whole_slice:
            by_x = (1 - plane) * by_second + plane * by_first
            by_y = (1 - plane) * by_first + plane * by_second
            return whole.at[spot, by_x, plane, by_y, some]
        return whole.at[spot, by_second, plane, some]

    def arrive(i, spot, by_first, by_second):
        here = slot(i, spot, by_first, by_second, core)
        remote(here, here, own_sem.at[0], recv.at[i, spot, by_first, by_second], to_core).wait_recv()

    def along(i, source, spot, turn, way):
        by_second = second if turn == 0 else 1 - second
        target = slot(i, spot, first, by_second, core)
        sems = line_send.at[way, i, spot, turn], recv.at[i, spot, first, by_second]
        return remote(source, target, *sems, (blk + 4 - 8 * way, y))

    def onward(i, source, spot, own):
        target = slot(i, spot, first, second, core)
        arrived = recv.at[i, spot, first, second]
        if own or not late[i]:
            yield remote(source, target, second_send.at[i, spot], arrived, second_device)
        if whole_slice:
            yield remote(source, target, first_send.at[i, spot, 0], arrived, first_device)
        yield remote(
            source, target, core_send.at[i, spot, 0, 0], core_recv.at[i, spot, first, second], to_core
        )

    def after_second(i, spot):
        here = slot(i, spot, first, 1 - second, core)
        if whole_slice:
            yield remote(
                here, here, first_send.at[i, spot, 1], recv.at[i, spot, first, 1 - second], first_device
            )
        yield remote(
            here, here, core_send.at[i, spot, 0, 1], core_recv.at[i, spot, first, 1 - second], to_core
        )

    def after_first(i, spot, turn):
        by_second = second if turn == 0 else 1 - second
        here = slot(i, spot, 1 - first, by_second, core)
        return remote(
            here, here, core_send.at[i, spot, 1, turn], core_recv.at[i, spot, 1 - first, by_second], to_core
        )

    def line_steps():
        for far in range(1, planes):
            yield z - far, z >= far, 0, z < planes - 1
            yield z + far, z < planes - far, 1, z > 0

    ends = [(0, z < planes - 1), (1, z > 0)]
    own_copies = []
    for i in range(count):
        copy = pltpu.make_async_copy(
            shards[i], slot(i, z, first, second, core), own_sem.at[1 + i]
        )
        copy.start()
        own_copies.append(copy)

        for way, further in ends:

            @pl.when(further)
            def _():
                along(i, shards[i], z, 0, way).start()

        for copy in onward(i, shards[i], z, True):
            copy.start()
    rides = rides_of(planes, rides)

    def issue(number):
        for ride in rides:
            ride.issue_more(number)

    issue(6)
    for i in range(count):
        arrive(i, z, first, 1 - second)
        for way, further in ends * late[i]:

            @pl.when(further)
            def _():
                along(i, slot(i, z, first, 1 - second, core), z, 1, way).start()

        for copy in after_second(i, z):
            copy.start()
    issue(4)
    for spot, there, way, further in line_steps():

        @pl.when(there)
        def _():
            for i in range(count):
                here = slot(i, spot, first, second, core)
                arrive(i, spot, first, second)

                @pl.when(further)
                def _():
                    along(i, here, spot, 0, way).start()

                for copy in onward(i, here, spot, False):
                    copy.start()
            for i in range(count):
                arrive(i, spot, first, 1 - second)
                if late[i]:

                    @pl.when(further)
                    def _():
                        along(i, slot(i, spot, first, 1 - second, core), spot, 1, way).start()

                for copy in after_second(i, spot):
                    copy.start()

        issue(4)

    issue(8 * planes)
    spots = [lax.rem(z + at, planes) for at in range(planes)]
    if whole_slice:
        for spot in spots:
            for turn in range(2):
                for i in range(count):
                    arrive(i, spot, 1 - first, second if turn == 0 else 1 - second)
                    after_first(i, spot, turn).start()
    for copy in own_copies:
        copy.wait()
    for i in range(count):
        for spot in range(planes):
            for by_first in range(firsts):
                for by_second in range(2):
                    there = slot(i, spot, by_first, by_second, 1 - core)
                    arrived = core_recv.at[i, spot, by_first, by_second]
                    remote(there, there, own_sem.at[0], arrived, to_core).wait_recv()
    for ride in rides:
        ride.finish()
    for i in range(count):
        for turn in range(1 + late[i]):
            for way, further in ends:

                @pl.when(further)
                def _():
                    along(i, shards[i], z, turn, way).wait_send()

            for spot, there, way, further in line_steps():

                @pl.when(there & further)
                def _():
                    along(i, shards[i], spot, turn, way).wait_send()

        for at, spot in enumerate(spots):
            for copy in onward(i, shards[i], spot, at == 0):
                copy.wait_send()
            for copy in after_second(i, spot):
                copy.wait_send()
            for turn in range(2 * (firsts - 1)):
                after_first(i, spot, turn).wait_send()


def gather_now(shards, planes, whole_slice, collective_id, exchanges=(), late_rows=None):
    parts = []
    for array, shard in enumerate(shards):
        rows = shard.shape[0]
        early = rows - (late_rows[array] if late_rows else 0)
        parts += [(array, 0, early, False)] * (early > 0)
        parts += [(array, early, rows - early, True)] * (early < rows)
    count = len(parts)
    firsts = 2 if whole_slice else 1
    specs = exchange_specs(exchanges)
    dma = pltpu.SemaphoreType.DMA
    grid = (planes, 2, 2, 2) if whole_slice else (planes, 2, 2)
    results = communicate(
        functools.partial(gather_kernel, planes, parts, whole_slice, specs),
        list(shards),
        exchanges,
        [jax.ShapeDtypeStruct((*grid, *shard.shape), shard.dtype) for shard in shards],
        [
            dma((count + 1,)),
            dma((2, count, planes, 2)),
            dma((count, planes)),
            dma((count, planes, 2)),
            dma((count, planes, 2, 2)),
            dma((count, planes, firsts, 2)),
            dma((count, planes, firsts, 2)),
        ],
        planes,
        collective_id,
        200,
        "gather_now",
    )
    places = 4 * planes * firsts
    wholes = [
        whole.reshape(places * shard.shape[0], shard.shape[1])
        for whole, shard in zip(results, shards)
    ]
    return wholes + list(results[len(shards) :])


def scatter_kernel(planes, steps, rows, whole_slice, product, specs, *refs):
    operands, (sum_ref,), scratch, rides = split_refs(refs, 1 + product, 1, specs)
    own, from_core, from_first, from_second, from_below, from_above = scratch[:6]
    load_sem, core_sems, first_sems, second_sems, up_sems, down_sems = scratch[6:12]
    if product:
        lefts, rights, made, factor_sems = scratch[12:]
    else:
        (partial_ref,) = operands
    blk, z, x, core, y = position()
    firsts = 2 if whole_slice else 1
    to_core = (blk + 1 - 2 * core, y)
    if whole_slice:
        first = y * (1 - core) + x * core
        second = x * (1 - core) + y * core
        core_second = second
        first_device = (blk + core * (2 - 4 * x), y + (1 - core) * (1 - 2 * y))
        second_device = (blk + (1 - core) * (2 - 4 * x), y + core * (1 - 2 * y))
    else:
        first, second = 0, x
        first_device, second_device = None, (blk + 2 - 4 * x, y)
    line = [(blk + 4 * (lax.rem(z + at, planes) - z), y) for at in range(1, planes)]
    nearby = [to_core, second_device] + [first_device] * whole_slice + line
    greet(greeted(specs, nearby))

    def make(step):
        some = pl.ds(pl.multiple_of(step * rows, rows), rows)
        left = lefts[:, :, :, some, :].reshape(4 * planes * rows, lefts.shape[-1])
        wide = 2 * HEAD

        @pl.loop(0, rights.shape[0] // wide)
        def _(at):
            columns = pl.ds(pl.multiple_of(at * wide, wide), wide)
            part = lax.dot_general(
                left,
                rights[columns, :],
                (((1,), (1,)), ((), ())),
                preferred_element_type=jnp.float32,
            )
            part = part.astype(made.dtype).reshape(planes, 2, 2, rows, wide)
            made[step, :, :, :, :, columns] = part

    def piece(step, by_first, by_second, plane):
        if product:
            return made.at[step, :, by_second, plane]
        some = pl.ds(pl.multiple_of(step * rows, rows), rows)
        if whole_slice:
            by_x = (1 - plane) * by_second + plane * by_first
            by_y = (1 - plane) * by_first + plane * by_second
            return partial_ref.at[:, by_x, plane, by_y, some]
        return partial_ref.at[:, by_second, plane, some]

    def core_copy(step, by_first, by_second, plane):
        return remote(
            piece(step, by_first, by_second, plane),
            from_core.at[step, by_first, by_second],
            core_sems.at[0, step, by_first, by_second],
            core_sems.at[1, step, by_first, by_second],
            to_core,
        )

    def load(step, by_first, by_second):
        return pltpu.make_async_copy(
            piece(step, by_first, by_second, core),
            own.at[step, by_first, by_second],
            load_sem.at[step, by_first, by_second],
        )

    def first_copy(step):
        return remote(
            own.at[step, 1 - first],
            from_first.at[step],
            first_sems.at[0, step],
            first_sems.at[1, step],
            first_device,
        )

    def second_copy(step):
        return remote(
            own.at[step, first, 1 - second],
            from_second.at[step],
            second_sems.at[0, step],
            second_sems.at[1, step],
            second_device,
        )

    def up_copy(step, target):
        return remote(
            own.at[step, first, second, target],
            from_below.at[step, target],
            up_sems.at[0, step, target],
            up_sems.at[1, step, target],
            (blk + 4, y),
        )

    def down_copy(step, target):
        return remote(
            own.at[step, first, second, target],
            from_above.at[step, target],
            down_sems.at[0, step, target],
            down_sems.at[1, step, target],
            (blk - 4, y),
        )

    def halves():
        if not whole_slice:
            return [(0, 1 - second), (0, second)]
        return [(1 - first, 0), (1 - first, 1), (first, 0), (first, 1)]

    def core_halves():
        if not whole_slice:
            return [(0, 1 - second), (0, second)]
        return [(1 - core_second, 0), (1 - core_second, 1), (core_second, 0), (core_second, 1)]

    def start_loads(step):
        if product:
            make(step)
        for mine, theirs in zip(halves(), core_halves()):
            core_copy(step, *theirs, 1 - core).start()
            if not product:
                load(step, *mine).start()

    def add_core(step):
        for turn, mine in enumerate(halves()):
            if not product:
                load(step, *mine).wait()
            core_copy(step, *mine, core).wait_recv()
            if product:
                own[step, *mine] = made[step, :, mine[1], core] + from_core[step, *mine]
            else:
                own[step, *mine] += from_core[step, *mine]
            if whole_slice and turn == 1:
                first_copy(step).start()
            if not whole_slice and turn == 0:
                second_copy(step).start()

    def add_first(step):
        first_copy(step).wait_recv()
        own[step, first, 1 - second] += from_first[step, 1 - second]
        second_copy(step).start()
        own[step, first, second] += from_first[step, second]

    def add_second(step):
        second_copy(step).wait_recv()
        own[step, first, second] += from_second[step]

    def pass_up(step):
        for target in range(planes):

            @pl.when((z > 0) & (z <= target))
            def _():
                up_copy(step, target).wait_recv()

            @pl.when((z > 0) & (z < target))
            def _():
                own[step, first, second, target] += from_below[step, target]

            @pl.when(z < target)
            def _():
                up_copy(step, target).start()

    def pass_down(step):
        for target in range(planes):

            @pl.when((z < planes - 1) & (z >= target))
            def _():
                down_copy(step, target).wait_recv()

            @pl.when((z < planes - 1) & (z > target))
            def _():
                own[step, first, second, target] += from_above[step, target]

            @pl.when(z > target)
            def _():
                down_copy(step, target).start()

    def add_line(step):
        some = pl.ds(pl.multiple_of(step * rows, rows), rows)
        sum_ref[some, :] = own[step, first, second, z]

        @pl.when(z > 0)
        def _():
            sum_ref[some, :] += from_below[step, z]

        @pl.when(z < planes - 1)
        def _():
            sum_ref[some, :] += from_above[step, z]

    rides = rides_of(planes, rides)
    hurry = [-(-ride.count // steps) for ride in rides]
    for ride, number in zip(rides, hurry):
        for at in range(2 * number):
            ride.issue(jnp.int32(at))
    if product:
        factors = [
            pltpu.make_async_copy(operand, ref, factor_sems.at[i])
            for i, (operand, ref) in enumerate(zip(operands, (lefts, rights)))
        ]
        for factor in factors:
            factor.start()
        for factor in factors:
            factor.wait()

    @pl.loop(0, 2)
    def _(step):
        start_loads(step)

    early = firsts + 1

    @pl.loop(0, steps + early + planes)
    def _(turn):
        def stage(step, work):
            @pl.when((step >= 0) & (step < steps))
            def _():
                work(step)

        @pl.when(turn < steps - 2)
        def _():
            start_loads(turn + 2)

        stage(turn, add_core)
        for ride, number in zip(rides, hurry):
            for at in range(number):
                ride.issue((turn + 2) * number + at)
        if whole_slice:
            stage(turn - 1, add_first)
        stage(turn - early + 1, add_second)
        stage(turn - early - z, pass_up)
        stage(turn - early - (planes - 1 - z), pass_down)
        stage(turn - early - planes + 1, add_line)

    @pl.loop(0, steps)
    def _(step):
        for theirs in core_halves():
            core_copy(step, *theirs, 1 - core).wait_send()
        if whole_slice:
            first_copy(step).wait_send()
        second_copy(step).wait_send()
        for target in range(planes):

            @pl.when(z < target)
            def _():
                up_copy(step, target).wait_send()

            @pl.when(z > target)
            def _():
                down_copy(step, target).wait_send()

    for ride in rides:
        ride.finish()


def scatter_now(factors, planes, whole_slice, collective_id, exchanges=()):
    firsts = 2 if whole_slice else 1
    product = len(factors) == 2
    shard_rows = factors[0].shape[0] // (4 * planes * firsts)
    width = factors[1].shape[0] if product else factors[0].shape[1]
    rows = 16
    steps = shard_rows // rows
    dtype = factors[0].dtype
    specs = exchange_specs(exchanges)
    dma = pltpu.SemaphoreType.DMA
    grid = (planes, 2, 2, 2) if whole_slice else (planes, 2, 2)
    return communicate(
        functools.partial(scatter_kernel, planes, steps, rows, whole_slice, product, specs),
        [factors[0].reshape(*grid, shard_rows, factors[0].shape[1]), *factors[1:]],
        exchanges,
        [jax.ShapeDtypeStruct((shard_rows, width), dtype)],
        [
            pltpu.VMEM((steps, firsts, 2, planes, rows, width), dtype),
            pltpu.VMEM((steps, firsts, 2, planes, rows, width), dtype),
            pltpu.VMEM((steps if whole_slice else 1, 2, planes, rows, width), dtype),
            pltpu.VMEM((steps, planes, rows, width), dtype),
            pltpu.VMEM((steps, planes, rows, width), dtype),
            pltpu.VMEM((steps, planes, rows, width), dtype),
            dma((steps, firsts, 2)),
            dma((2, steps, firsts, 2)),
            dma((2, steps)),
            dma((2, steps)),
            dma((2, steps, planes)),
            dma((2, steps, planes)),
        ]
        + [
            pltpu.VMEM((*grid, shard_rows, factors[0].shape[1]), dtype),
            pltpu.VMEM(factors[-1].shape, dtype),
            pltpu.VMEM((steps, *grid, rows, width), dtype),
            dma((2,)),
        ]
        * product,
        planes,
        collective_id,
        200,
        "scatter_now",
        out_spec=pltpu.VMEM,
        vmem_limit_bytes=56 * 2**20,
    )


def ffn_pack_kernel(gateup_ref, down_ref, packet_ref):
    for at in range(packet_ref.shape[0]):
        columns = slice(at * HEAD, (at + 1) * HEAD)
        packet_ref[at, :, :HEAD] = gateup_ref[0, :, columns].astype(jnp.bfloat16)
        packet_ref[at, :, HEAD : 2 * HEAD] = gateup_ref[1, :, columns].astype(jnp.bfloat16)
        packet_ref[at, :, 2 * HEAD :] = down_ref[:, columns].astype(jnp.bfloat16)


def ffn_packets(gateup, down):
    row_count = gateup.shape[1]
    blocks, wide = FF // HEAD, 5
    return pl.pallas_call(
        ffn_pack_kernel,
        grid=(blocks // wide,),
        in_specs=[
            pl.BlockSpec((2, row_count, wide * HEAD), lambda j: (0, 0, j)),
            pl.BlockSpec((row_count, wide * HEAD), lambda j: (0, j)),
        ],
        out_specs=pl.BlockSpec((wide, row_count, 3 * HEAD), lambda j: (j, 0, 0)),
        out_shape=jax.ShapeDtypeStruct((blocks, row_count, 3 * HEAD), jnp.bfloat16),
        cost_estimate=pl.CostEstimate(flops=0, bytes_accessed=12 * 2**20, transcendentals=0),
        compiler_params=pltpu.CompilerParams(vmem_limit_bytes=32 * 2**20),
        name="ffn_packets",
    )(gateup, down)


def attn_pack_kernel(qkv_ref, out_ref, packet_ref):
    j = pl.program_id(0)

    @pl.when(j < (H + 2) // 2)
    def _():
        for at in range(2):
            packet_ref[at] = qkv_ref[:, at * HEAD : (at + 1) * HEAD].astype(jnp.bfloat16)

    @pl.when(j >= (H + 2) // 2)
    def _():
        for at in range(2):
            packet_ref[at] = out_ref[:, at * HEAD : (at + 1) * HEAD].astype(jnp.bfloat16)


def attn_packets(qkv, out):
    row_count = qkv.shape[0]
    qkv_last, out_last = (H + 2) // 2 - 1, H // 2 - 1
    return pl.pallas_call(
        attn_pack_kernel,
        grid=(H + 1,),
        in_specs=[
            pl.BlockSpec((row_count, 2 * HEAD), lambda j: (0, jnp.minimum(j, qkv_last))),
            pl.BlockSpec((row_count, 2 * HEAD), lambda j: (0, jnp.clip(j - qkv_last - 1, 0, out_last))),
        ],
        out_specs=pl.BlockSpec((2, row_count, HEAD), lambda j: (j, 0, 0)),
        out_shape=jax.ShapeDtypeStruct((2 * H + 2, row_count, HEAD), jnp.bfloat16),
        cost_estimate=pl.CostEstimate(flops=0, bytes_accessed=4 * 2**20, transcendentals=0),
        name="attn_packets",
    )(qkv, out)


def turn_kernel(grads_ref, others_ref, mom_ref, *refs):
    *results, current_ref = refs
    if len(results) == 1:
        low_ref, turned_ref = results[0].at[:, :HEAD], results[0].at[:, HEAD:]
    else:
        low_ref, turned_ref = results
    grads = grads_ref[...] + others_ref[...].astype(jnp.float32)
    low_ref[...] = grads.astype(jnp.bfloat16)
    moment = momentum_decay * mom_ref[...].astype(jnp.float32) + grads
    moment = moment.astype(jnp.bfloat16).astype(jnp.float32)
    norm_size = jnp.sqrt(jnp.sum(moment * moment, keepdims=True))
    current_ref[...] = (moment / (norm_size + eps_pieces)).T.astype(jnp.bfloat16)

    @pl.loop(0, NS_STEPS)
    def _(sweep_index):
        current = current_ref[...]
        gram_matrix = lax.dot_general(
            current, current, (((1,), (1,)), ((), ())), preferred_element_type=jnp.float32
        ).astype(jnp.bfloat16)
        square = jnp.dot(gram_matrix, gram_matrix, preferred_element_type=jnp.float32)
        mixing = (ns_second * gram_matrix.astype(jnp.float32) + ns_third * square).astype(
            jnp.bfloat16
        )
        turned = jnp.dot(mixing, current, preferred_element_type=jnp.float32)
        current_ref[...] = (ns_first * current.astype(jnp.float32) + turned).astype(jnp.bfloat16)

    turned_ref[...] = current_ref[...].astype(jnp.float32).T.astype(jnp.bfloat16)


def orthogonalize(grads, others, moms, results):
    depth, columns = grads.shape
    block = pl.BlockSpec((depth, HEAD), lambda j: (0, j))
    pieces = columns // HEAD
    return pl.pallas_call(
        turn_kernel,
        grid=(pieces,),
        in_specs=[block] * 3,
        out_specs=[pl.BlockSpec((depth, 2 // results * HEAD), lambda j: (0, j))] * results,
        out_shape=[jax.ShapeDtypeStruct((depth, 2 // results * columns), jnp.bfloat16)] * results,
        scratch_shapes=[pltpu.VMEM((HEAD, depth), jnp.bfloat16)],
        cost_estimate=pl.CostEstimate(
            flops=pieces * 20 * depth * HEAD * HEAD, bytes_accessed=12 * depth * columns, transcendentals=0
        ),
        compiler_params=pltpu.CompilerParams(vmem_limit_bytes=48 * 2**20),
        name="orthogonalize",
    )(grads, others, moms)


def update(rate, weight, mom, grad, turn):
    moment = momentum_decay * mom + grad.astype(jnp.float32)
    new = (1.0 - weight_shrink) * weight - rate * turn.astype(jnp.float32)
    return new, moment, new.astype(jnp.bfloat16)


def ffn_update_kernel(
    grad_ref, turn_ref, w_gateup_ref, mom_gateup_ref, w_down_ref, mom_down_ref, *results
):
    for at in range(grad_ref.shape[0]):
        columns = slice(at * HEAD, (at + 1) * HEAD)
        for part in range(3):
            spot = (part, slice(None), columns) if part < 2 else (slice(None), columns)
            weight_ref, mom_ref = (
                (w_gateup_ref, mom_gateup_ref) if part < 2 else (w_down_ref, mom_down_ref)
            )
            packed = slice(part * HEAD, (part + 1) * HEAD)
            values = update(
                matrix_rate,
                weight_ref[spot],
                mom_ref[spot],
                grad_ref[at, :, packed],
                turn_ref[at, :, packed],
            )
            for ref, value in zip(results[:3] if part < 2 else results[3:], values):
                ref[spot] = value


def ffn_update(grads, turns, w_gateup, mom_gateup, w_down, mom_down):
    row_count = w_gateup.shape[1]
    wide = 3
    packet = pl.BlockSpec((wide, row_count, 3 * HEAD), lambda j: (j, 0, 0))
    gateup = pl.BlockSpec((2, row_count, wide * HEAD), lambda j: (0, 0, j))
    down = pl.BlockSpec((row_count, wide * HEAD), lambda j: (0, j))
    dtypes = (jnp.float32, jnp.float32, jnp.bfloat16)
    return pl.pallas_call(
        ffn_update_kernel,
        grid=(FF // HEAD // wide,),
        in_specs=[packet, packet, gateup, gateup, down, down],
        out_specs=[gateup] * 3 + [down] * 3,
        out_shape=[jax.ShapeDtypeStruct(w_gateup.shape, dtype) for dtype in dtypes]
        + [jax.ShapeDtypeStruct(w_down.shape, dtype) for dtype in dtypes],
        cost_estimate=pl.CostEstimate(flops=0, bytes_accessed=50 * 2**20, transcendentals=0),
        compiler_params=pltpu.CompilerParams(vmem_limit_bytes=48 * 2**20),
        name="ffn_update",
    )(grads, turns, w_gateup, mom_gateup, w_down, mom_down)


def attn_update_kernel(rate, packet_ref, w_ref, mom_ref, *results):
    for at in range(2):
        columns = slice(at * HEAD, (at + 1) * HEAD)
        values = update(
            rate,
            w_ref[:, columns],
            mom_ref[:, columns],
            packet_ref[at, :, :HEAD],
            packet_ref[at, :, HEAD:],
        )
        for ref, value in zip(results, values):
            ref[:, columns] = value


def attn_update(rate, offset, packets, weight, mom):
    row_count = packets.shape[1]
    packet = pl.BlockSpec((2, row_count, 2 * HEAD), lambda j: (j + offset // 2, 0, 0))
    block = pl.BlockSpec((row_count, 2 * HEAD), lambda j: (0, j))
    return pl.pallas_call(
        functools.partial(attn_update_kernel, rate),
        grid=(weight.shape[1] // HEAD // 2,),
        in_specs=[packet, block, block],
        out_specs=[block] * 3,
        out_shape=[
            jax.ShapeDtypeStruct(weight.shape, dtype)
            for dtype in (jnp.float32, jnp.float32, jnp.bfloat16)
        ],
        cost_estimate=pl.CostEstimate(flops=0, bytes_accessed=6 * 2**20, transcendentals=0),
        name="attn_update",
    )(packets, weight, mom)


def two_heads(ref):
    return jnp.concatenate([ref[:, :HEAD], ref[:, HEAD:]], axis=0)


def visible(tokens, first_token, shape, query_axis):
    query = lax.rem(lax.broadcasted_iota(jnp.int32, shape, query_axis), tokens)
    key = lax.broadcasted_iota(jnp.int32, shape, 1 - query_axis)
    distance = query + WINDOW - key
    return (distance >= 0) & (distance < WINDOW) & (first_token - WINDOW + key >= 0)


def attend_kernel(first_ref, queries_ref, kv_ref, mixed_ref, log_total_ref):
    tokens = queries_ref.shape[0]
    raw = lax.dot_general(
        two_heads(queries_ref),
        kv_ref[:, :HEAD],
        (((1,), (1,)), ((), ())),
        preferred_element_type=jnp.float32,
    )
    allowed = visible(tokens, first_ref[0], raw.shape, 0)
    scores = jnp.where(allowed, raw * HEAD ** (-0.5), masked_score)
    top_score = jnp.max(scores, axis=-1, keepdims=True)
    expo = jnp.exp(scores - top_score)
    total = jnp.sum(expo, axis=-1, keepdims=True)
    probs = (expo / total).astype(jnp.bfloat16)
    mixed = jnp.dot(probs, kv_ref[:, HEAD:], preferred_element_type=jnp.float32)
    mixed_ref[:, :HEAD] = mixed[:tokens].astype(jnp.bfloat16)
    mixed_ref[:, HEAD:] = mixed[tokens:].astype(jnp.bfloat16)
    log_total_ref[0] = jnp.broadcast_to(top_score + jnp.log(total), log_total_ref.shape[1:])


def attend(first_token, qkv, kv_window):
    tokens = qkv.shape[0]
    span = kv_window.shape[0]
    pairs = H // 2
    return pl.pallas_call(
        attend_kernel,
        grid=(pairs,),
        in_specs=[
            pl.BlockSpec(memory_space=pltpu.SMEM),
            pl.BlockSpec((tokens, 2 * HEAD), lambda j: (0, j)),
            pl.BlockSpec((span, 2 * HEAD), lambda j: (0, 0)),
        ],
        out_specs=[
            pl.BlockSpec((tokens, 2 * HEAD), lambda j: (0, j)),
            pl.BlockSpec((1, 2 * tokens, 128), lambda j: (j, 0, 0)),
        ],
        out_shape=[
            jax.ShapeDtypeStruct((tokens, H * HEAD), jnp.bfloat16),
            jax.ShapeDtypeStruct((pairs, 2 * tokens, 128), jnp.float32),
        ],
        cost_estimate=pl.CostEstimate(
            flops=4 * H * tokens * span * HEAD,
            bytes_accessed=4 * 2**20,
            transcendentals=H * tokens * span,
        ),
        compiler_params=pltpu.CompilerParams(vmem_limit_bytes=48 * 2**20),
        name="attend",
    )(first_token, qkv, kv_window)


def attend_back_kernel(
    first_ref, queries_ref, grads_ref, log_total_ref, kv_ref, grad_query_ref, grad_kv_ref, sums_ref
):
    tokens = queries_ref.shape[0]
    score_scale = HEAD ** (-0.5)
    keys, values = kv_ref[:, :HEAD], kv_ref[:, HEAD:]
    queries, grads = two_heads(queries_ref), two_heads(grads_ref)

    def against(left, right):
        return lax.dot_general(
            left, right, (((1,), (1,)), ((), ())), preferred_element_type=jnp.float32
        )

    raw = against(keys, queries)
    allowed = visible(tokens, first_ref[0], raw.shape, 1)
    scores = jnp.where(allowed, raw * score_scale, masked_score)
    log_total = log_total_ref[0].T[:1]
    probs = jnp.exp(scores - log_total)
    grad_probs = against(values, grads)
    row_delta = jnp.sum(probs * grad_probs, axis=0, keepdims=True)
    grad_raw = (probs * (grad_probs - row_delta) * score_scale).astype(jnp.bfloat16)
    grad_query = lax.dot_general(
        grad_raw, keys, (((0,), (0,)), ((), ())), preferred_element_type=jnp.float32
    )
    grad_query_ref[:, :HEAD] = grad_query[:tokens].astype(jnp.bfloat16)
    grad_query_ref[:, HEAD:] = grad_query[tokens:].astype(jnp.bfloat16)

    @pl.when(pl.program_id(0) == 0)
    def _():
        sums_ref[...] = jnp.zeros_like(sums_ref)

    sums_ref[:, :HEAD] += jnp.dot(grad_raw, queries, preferred_element_type=jnp.float32)
    sums_ref[:, HEAD:] += jnp.dot(
        probs.astype(jnp.bfloat16), grads, preferred_element_type=jnp.float32
    )

    @pl.when(pl.program_id(0) == pl.num_programs(0) - 1)
    def _():
        grad_kv_ref[...] = sums_ref[...].astype(jnp.bfloat16)


def attend_back(first_token, qkv, grads, log_total, kv_window):
    tokens = qkv.shape[0]
    span = kv_window.shape[0]
    heads = pl.BlockSpec((tokens, 2 * HEAD), lambda j: (0, j))
    window = pl.BlockSpec((span, 2 * HEAD), lambda j: (0, 0))
    return pl.pallas_call(
        attend_back_kernel,
        grid=(H // 2,),
        in_specs=[
            pl.BlockSpec(memory_space=pltpu.SMEM),
            heads,
            heads,
            pl.BlockSpec((1, 2 * tokens, 128), lambda j: (j, 0, 0)),
            window,
        ],
        out_specs=[heads, window],
        out_shape=[
            jax.ShapeDtypeStruct((tokens, H * HEAD), jnp.bfloat16),
            jax.ShapeDtypeStruct((span, 2 * HEAD), jnp.bfloat16),
        ],
        scratch_shapes=[pltpu.VMEM((span, 2 * HEAD), jnp.float32)],
        cost_estimate=pl.CostEstimate(
            flops=10 * H * tokens * span * HEAD,
            bytes_accessed=8 * 2**20,
            transcendentals=H * tokens * span,
        ),
        compiler_params=pltpu.CompilerParams(vmem_limit_bytes=48 * 2**20),
        name="attend_back",
    )(first_token, qkv, grads, log_total, kv_window)


def rms_scale(stream, gain_row):
    mean_square = jnp.mean(stream * stream, axis=-1, keepdims=True)
    return stream * lax.rsqrt(mean_square + eps_norm) * gain_row


def gelu_product(gate_part, up_part):
    return jax.nn.gelu(gate_part, approximate=True) * up_part


def on_device(
    tokens_in,
    cotangent,
    w_qkv,
    w_out,
    w_gateup,
    w_down,
    gains,
    mom_qkv,
    mom_out,
    mom_gateup,
    mom_down,
    mom_gains,
):
    everyone = ("blk", "pair")
    bf16 = jnp.bfloat16
    f32 = jnp.float32
    blk_count = lax.axis_size("blk")
    pair_count = lax.axis_size("pair")
    device_count = blk_count * pair_count
    block_at = lax.axis_index("blk")
    half_at = lax.axis_index("pair")
    me = block_at * pair_count + half_at
    local_rows, width = tokens_in.shape
    share_rows = w_qkv.shape[0]
    span = WINDOW + local_rows
    token_count = local_rows * device_count
    large = token_count * width * 2 > 48 * 2**20
    planes = blk_count // 4
    spread = not large

    def after(value, earlier):
        return lax.optimization_barrier((value, earlier))[0] if large else value

    def exchange(packets, axes=everyone):
        return lax.all_to_all(packets, axes, split_axis=0, concat_axis=0, tiled=True)

    def swap(shard):
        return lax.ppermute(shard, "pair", [(0, 1), (1, 0)])

    def hold(value, *earlier):
        return value if large else lax.optimization_barrier((value, earlier))[0]

    def ride(packets, among="all", **options):
        sources = {"all": device_count, "plane": blk_count, "pair": pair_count}[among]
        return Exchange(packets, among, **(dict(sources=sources) | options))

    def exchanged(rides):
        results = []
        for packets, among, _, before, _, _ in rides:
            if among == "pair":
                results.append(swap(packets))
                continue
            axes, places = (everyone, device_count) if among == "all" else ("blk", blk_count)
            after_last = places - before - packets.shape[0]
            packets = jnp.pad(packets, ((before, after_last),) + ((0, 0),) * (packets.ndim - 1))
            results.append(exchange(packets, axes))
        return results

    def gather(shards, whole_slice, collective_id, rides=(), **options):
        if large:
            axes = everyone if whole_slice else "blk"
            wholes = [lax.all_gather(shard, axes, axis=0, tiled=True) for shard in shards]
            return wholes + exchanged(rides)
        return gather_now(shards, planes, whole_slice, collective_id, rides, **options)

    def scatter(factors, whole_slice, collective_id, rides=()):
        if large:
            axes = everyone if whole_slice else "blk"
            if len(factors) == 2:
                partial = jnp.einsum("tf,df->td", *factors, preferred_element_type=f32)
                factors = [partial.astype(bf16)]
            part = lax.psum_scatter(factors[0], axes, scatter_dimension=0, tiled=True)
            return [part] + exchanged(rides)
        return scatter_now(factors, planes, whole_slice, collective_id, rides)

    def gather_plane(shard):
        return lax.all_gather(shard, "blk", axis=0, tiled=True)

    stream = tokens_in.astype(f32)
    padded_gains = jnp.pad(gains.astype(bf16), ((0, 14), (0, 128 - share_rows)))
    full_qkv, full_gains, full_out, ffn_weights = gather(
        [w_qkv.astype(bf16), padded_gains, w_out.T.astype(bf16)],
        True,
        1,
        [ride(ffn_packets(w_gateup, w_down.T))],
        late_rows=(0, 0, share_rows),
    )
    ffn_weights = ffn_weights.reshape(width, 3 * HEAD)
    full_gains = full_gains.reshape(device_count, 16, 128)[:, :2, :share_rows].astype(f32)
    gain_attn = full_gains[:, 0].reshape(width)
    gain_mlp = full_gains[:, 1].reshape(width)
    normed_attn_f, norm_back_attn = jax.vjp(rms_scale, stream, gain_attn)
    normed_attn = normed_attn_f.astype(bf16)
    qkv = jnp.dot(normed_attn, full_qkv, preferred_element_type=f32).astype(bf16)
    (kv_all,) = gather([qkv[:, H * HEAD :]], True, 2)
    kv_window = lax.dynamic_slice_in_dim(
        jnp.pad(kv_all, ((WINDOW, 0), (0, 0))), me * local_rows, span, 0
    )
    first_token = (me * local_rows).astype(jnp.int32).reshape(1)
    mixed, log_total = attend(first_token, qkv, kv_window)
    resid = stream + jnp.einsum("tc,dc->td", mixed, full_out, preferred_element_type=f32)

    normed_mlp_f, norm_back_mlp = jax.vjp(rms_scale, resid, gain_mlp)
    normed_mlp = normed_mlp_f.astype(bf16)
    normed_mlp_plane, cotangent_plane, other_weights = gather(
        [normed_mlp, cotangent], False, 3, [ride(ffn_weights, "pair")], late_rows=(0, local_rows // 4)
    )
    pair_weights = [ffn_weights, other_weights]
    gates, ups, downs = (
        [weights[:, part * HEAD : (part + 1) * HEAD] for weights in pair_weights]
        for part in range(3)
    )
    owns_block = me < FF // HEAD
    pair_gateup = jnp.where(owns_block, jnp.concatenate(gates + ups, axis=1), 0)
    pair_down = jnp.where(owns_block, jnp.concatenate(downs, axis=1), 0)
    plane_rows = blk_count * local_rows
    both_parts = jnp.dot(normed_mlp_plane, pair_gateup, preferred_element_type=f32)
    pair_width = pair_count * HEAD
    hidden_f, geglu_back = jax.vjp(
        gelu_product, both_parts[:, :pair_width], both_parts[:, pair_width:]
    )
    hidden = hidden_f.astype(bf16)
    grad_hidden = jnp.dot(cotangent_plane, pair_down, preferred_element_type=f32)
    grad_gate, grad_up = geglu_back(grad_hidden)
    grad_gateup = jnp.concatenate([grad_gate.astype(bf16), grad_up.astype(bf16)], axis=1)
    def ffn_gradient(columns):
        gateup_right = jnp.concatenate(
            [grad_gate[:, columns].astype(bf16), grad_up[:, columns].astype(bf16)], axis=1
        )
        down_right = hidden[:, columns]
        return jnp.concatenate(
            [
                jnp.einsum("td,tf->df", normed_mlp_plane, gateup_right, preferred_element_type=f32),
                jnp.einsum("td,tf->df", cotangent_plane, down_right, preferred_element_type=f32),
            ],
            axis=1,
        )

    def pair_columns(columns):
        return columns.reshape(local_rows, -1, pair_width).transpose(1, 0, 2)

    ffn_theirs = ffn_gradient(slice(HEAD, 2 * HEAD)).astype(bf16)
    grad_normed_mlp, ffn_others, ffn_moms, attn_moms, out_rights = scatter(
        [grad_gateup, pair_gateup],
        False,
        4,
        [
            ride(ffn_theirs, "pair"),
            ride(ffn_packets(mom_gateup, mom_down.T)),
            ride(attn_packets(mom_qkv, mom_out.T), spread_targets=spread),
            ride(
                pair_columns(mixed), "plane", first_target=(H + 2) // 2, spread_targets=spread
            ),
        ],
    )
    grad_normed_mlp = grad_normed_mlp.astype(f32)

    ffn_grads = ffn_gradient(slice(0, HEAD))
    ffn_low, ffn_turned = orthogonalize(
        ffn_grads, ffn_others, ffn_moms.reshape(width, 3 * HEAD), 2
    )
    ffn_shape = (device_count, share_rows, 3 * HEAD)

    resid_part, gain_grad_mlp = norm_back_mlp(grad_normed_mlp)
    grad_resid = cotangent.astype(f32) + resid_part
    grad_proj = grad_resid.astype(bf16)
    grad_mixed = jnp.dot(grad_proj, full_out, preferred_element_type=f32).astype(bf16)
    grad_query, grad_kv = attend_back(first_token, qkv, grad_mixed, log_total, kv_window)
    grad_kv_all = lax.dynamic_update_slice_in_dim(
        jnp.zeros((WINDOW + token_count, 2 * HEAD), bf16), grad_kv, me * local_rows, 0
    )[WINDOW:]
    grad_kv, ffn_low = scatter(
        [grad_kv_all], True, 5, [ride(ffn_low.reshape(ffn_shape), sources=FF // HEAD)]
    )
    grad_qkv = jnp.concatenate([grad_query, grad_kv], axis=1)
    grad_normed_attn = jnp.einsum("tc,dc->td", grad_qkv, full_qkv, preferred_element_type=f32)
    stream_part, gain_grad_attn = norm_back_attn(grad_normed_attn)
    input_grad = grad_resid + stream_part

    branch, ffn_turned, qkv_rights = scatter(
        [after(hidden, grad_normed_mlp), pair_down],
        False,
        6,
        [
            ride(ffn_turned.reshape(ffn_shape), sources=FF // HEAD),
            ride(pair_columns(grad_qkv), "plane", spread_targets=spread),
        ],
    )
    block_output = (resid + branch.astype(f32)).astype(bf16)
    normed_attn_plane = gather_plane(after(hold(normed_attn, normed_mlp_plane), (ffn_grads, block_output)))
    grad_proj_plane = gather_plane(after(grad_proj, (ffn_grads, block_output)))

    pair_at = spread_place(planes, block_at) if spread else block_at

    def attn_gradient(half, qkv_rights, out_rights):
        def product(lefts, rights):
            rights = rights.reshape(plane_rows, pair_width)
            rights = lax.dynamic_slice_in_dim(rights, half * HEAD, HEAD, 1)
            return jnp.einsum("td,tf->df", lefts, rights, preferred_element_type=f32)

        return lax.cond(
            pair_at < (H + 2) // pair_count,
            lambda: product(normed_attn_plane, qkv_rights),
            lambda: product(grad_proj_plane, out_rights),
        )

    attn_theirs = attn_gradient(1 - half_at, qkv_rights, out_rights).astype(bf16)
    attn_others = swap(attn_theirs)
    attn_grads = attn_gradient(half_at, *hold((qkv_rights, out_rights), attn_theirs))
    updated_ffn = ffn_update(ffn_low, ffn_turned, w_gateup, mom_gateup, w_down.T, mom_down.T)
    (attn_results,) = orthogonalize(
        attn_grads, hold(attn_others, updated_ffn[0]), attn_moms.reshape(width, HEAD), 1
    )
    gain_grads = jnp.stack([gain_grad_attn, gain_grad_mlp], axis=0)
    gain_grads = gain_grads.reshape(2, device_count, share_rows).transpose(1, 0, 2)
    last_rides = [
        ride(
            attn_results.reshape(device_count, share_rows, 2 * HEAD),
            sources=2 * H + 2,
            spread_sources=spread,
        ),
        ride(jnp.pad(gain_grads, ((0, 0), (0, 6), (0, 128 - share_rows)))),
    ]
    if large:
        attn_results, gain_grads = exchanged(last_rides)
    else:
        attn_results, gain_grads = exchange_now(last_rides, planes, 7)
    gain_share = jnp.sum(gain_grads, axis=0)[:2, :share_rows]

    updated_qkv = attn_update(matrix_rate, 0, attn_results, w_qkv, mom_qkv)
    updated_out = attn_update(output_rate, H + 2, attn_results, w_out.T, mom_out.T)
    moment_gains = momentum_decay * mom_gains + gain_share
    new_gains = gains - gain_rate * moment_gains
    return (
        block_output,
        input_grad,
        *updated_qkv,
        *(result.T for result in updated_out),
        *updated_ffn[:3],
        *(result.T for result in updated_ffn[3:]),
        new_gains,
        moment_gains,
        new_gains.astype(bf16),
    )


def solution(mesh):
    placed = (
        P(("blk", "pair"), None),
        P(("blk", "pair"), None),
        P(("blk", "pair"), None),
        P(None, ("blk", "pair")),
        P(None, ("blk", "pair"), None),
        P(None, ("blk", "pair")),
        P(None, ("blk", "pair")),
        P(("blk", "pair"), None),
        P(None, ("blk", "pair")),
        P(None, ("blk", "pair"), None),
        P(None, ("blk", "pair")),
        P(None, ("blk", "pair")),
    )
    return jax.shard_map(
        on_device,
        mesh=mesh,
        in_specs=placed,
        out_specs=(
            P(("blk", "pair"), None),
            P(("blk", "pair"), None),
            P(("blk", "pair"), None),
            P(("blk", "pair"), None),
            P(("blk", "pair"), None),
            P(None, ("blk", "pair")),
            P(None, ("blk", "pair")),
            P(None, ("blk", "pair")),
            P(None, ("blk", "pair"), None),
            P(None, ("blk", "pair"), None),
            P(None, ("blk", "pair"), None),
            P(None, ("blk", "pair")),
            P(None, ("blk", "pair")),
            P(None, ("blk", "pair")),
            P(None, ("blk", "pair")),
            P(None, ("blk", "pair")),
            P(None, ("blk", "pair")),
        ),
        check_vma=False,
    )
```
